32 devices in a mesh: dp: 8 (over y, x, core), tensor: 4 (over z).
Axes of the slice: x: 2, y: 2, z: 4, core: 2. Of those that a mesh axis runs over, the one named last changes fastest.
Arguments:
- tokens: bfloat16 [2, 1024, 1536], P(None, 'dp'), may hold values from -6 to 6
- context: bfloat16 [2, 48, 1024], P(None, 'dp'), may hold values from -6 to 6
- captions: bfloat16 [2, 48, 256, 4096], P(None, 'dp'), may hold values from -6 to 6
- shapes: int32 [2, 48, 2], P(None, 'dp'), may hold values from 0 to 31, as said below
- text_len: int32 [2, 48], P(None, 'dp'), may hold values from 32 to 256, as said below
- w_query: bfloat16 [1536, 1536], P('dp', 'tensor'), may hold values from -0.15625 to 0.15625
- w_key: bfloat16 [1536, 1536], P('dp', 'tensor'), may hold values from -0.15625 to 0.15625
- w_value: bfloat16 [1536, 1536], P('dp', 'tensor'), may hold values from -0.15625 to 0.15625
- w_out: bfloat16 [1536, 1536], P('dp', 'tensor'), may hold values from -0.625 to 0.625
- w_text_key: bfloat16 [4096, 1536], P('dp', 'tensor'), may hold values from -0.09375 to 0.09375
- w_text_value: bfloat16 [4096, 1536], P('dp', 'tensor'), may hold values from -0.09375 to 0.09375
- w_gate: bfloat16 [1536, 4096], P('dp', 'tensor'), may hold values from -0.15625 to 0.15625
- w_up: bfloat16 [1536, 4096], P('dp', 'tensor'), may hold values from -0.15625 to 0.15625
- w_down: bfloat16 [1536, 4096], P('dp', 'tensor'), may hold values from -0.1875 to 0.1875
- w_adaln: bfloat16 [1024, 6144], P('dp', 'tensor'), may hold values from -0.25 to 0.25
- gain_attn: bfloat16 [1536], P('dp'), may hold values from 0.25 to 1.75
- gain_ffn: bfloat16 [1536], P('dp'), may hold values from 0.25 to 1.75
- gain_query: bfloat16 [64, 24], P('dp', 'tensor'), may hold values from 0.25 to 1.75
- gain_key: bfloat16 [64, 24], P('dp', 'tensor'), may hold values from 0.25 to 1.75
- gain_text: bfloat16 [64, 24], P('dp', 'tensor'), may hold values from 0.25 to 1.75
- cross_gate: bfloat16 [24], P('tensor'), may hold values from -1.5 to 1.5
- cotangent: bfloat16 [2, 1024, 1536], P(None, 'dp'), may hold values from -6 to 6
Outputs:
- result: bfloat16 [2, 1024, 1536], P(None, 'dp')
- grad_tokens: bfloat16 [2, 1024, 1536], P(None, 'dp')
- grad_w_query: float32 [1536, 1536], P('dp', 'tensor')
- grad_w_key: float32 [1536, 1536], P('dp', 'tensor')
- grad_w_value: float32 [1536, 1536], P('dp', 'tensor')
- grad_w_out: float32 [1536, 1536], P('dp', 'tensor')
- grad_w_text_key: float32 [4096, 1536], P('dp', 'tensor')
- grad_w_text_value: float32 [4096, 1536], P('dp', 'tensor')
- grad_w_gate: float32 [1536, 4096], P('dp', 'tensor')
- grad_w_up: float32 [1536, 4096], P('dp', 'tensor')
- grad_w_down: float32 [1536, 4096], P('dp', 'tensor')
- grad_w_adaln: float32 [1024, 6144], P('dp', 'tensor')
- grad_gain_attn: float32 [1536], P('dp')
- grad_gain_ffn: float32 [1536], P('dp')
- grad_gain_query: float32 [64, 24], P('dp', 'tensor')
- grad_gain_key: float32 [64, 24], P('dp', 'tensor')
- grad_gain_text: float32 [64, 24], P('dp', 'tensor')
- grad_cross_gate: float32 [24], P('tensor')
The draws below stay inside these ranges and needn't reach their ends.
Inputs may be any that keep to these rules, and one draw needn't show every extreme that they name: `shapes`: each slot holds an image of rows x (cols + 1) tokens (cols patch columns and one line-end token per row), packed in slot order from the first token of its device's micro-batch rows; an empty slot has rows = cols = 0, otherwise rows is 2 to 4 and cols 7 to 31. The first slot of each device is never empty; the images of one device in one micro-batch take at most 128 tokens, and in each micro-batch one device is filled exactly by one image of 4 rows and 31 columns. `text_len`: in each micro-batch some slot has all 256 caption tokens live.
All inputs are finite; a program needn't handle non-finite values.
Results may differ from the reference program's by a relative error of at most 0.035.
Values may be sent and summed in bfloat16 or wider, within the bound.
A program may use at most 256 MiB of HBM per device.

```python
import jax
import jax.numpy as jnp
from jax import lax

D = 1536
HEADS = 24
HEAD_DIM = 64
FF = 4096
DT = 4096
CD = 1024
TXT = 256
MICRO = 2
IMG_DEV = 6
MB_TOK = 128
IMGS = 48
TOK = 1024
N_DP = 8
N_TENSOR = 4


def draw_shapes(key, part):
    key = jax.random.fold_in(key, 11)
    key_rows, key_cols, key_full = jax.random.split(key, 3)
    groups = IMGS // IMG_DEV
    height = jax.random.randint(key_rows, (MICRO, groups, IMG_DEV), 2, MB_TOK // 32 + 1)
    columns = jax.random.randint(key_cols, (MICRO, groups, IMG_DEV), 7, 32)
    filled = jnp.zeros((MICRO, groups), jnp.int32)
    kept_rows = []
    kept_cols = []
    for position in range(IMG_DEV):
        extent = height[:, :, position] * (columns[:, :, position] + 1)
        fits = filled + extent <= MB_TOK
        kept_rows.append(jnp.where(fits, height[:, :, position], 0))
        kept_cols.append(jnp.where(fits, columns[:, :, position], 0))
        filled = filled + jnp.where(fits, extent, 0)
    height = jnp.stack(kept_rows, axis=2)
    columns = jnp.stack(kept_cols, axis=2)
    chosen = jax.random.randint(key_full, (MICRO,), 0, groups)
    picked = (jnp.arange(groups)[None, :] == chosen[:, None])[:, :, None]
    leading = (jnp.arange(IMG_DEV) == 0)[None, None, :]
    height = jnp.where(picked, jnp.where(leading, MB_TOK // 32, 0), height)
    columns = jnp.where(picked, jnp.where(leading, 31, 0), columns)
    return jnp.stack([height, columns], axis=-1).reshape(MICRO, IMGS, 2).astype(jnp.int32)


def draw_text_len(key, part):
    key = jax.random.fold_in(key, 23)
    key_length, key_choice = jax.random.split(key)
    lengths = jax.random.randint(key_length, (MICRO, IMGS), TXT // 8, TXT + 1)
    longest = jax.random.randint(key_choice, (MICRO,), 0, IMGS)
    return jnp.where(jnp.arange(IMGS)[None, :] == longest[:, None], TXT, lengths).astype(jnp.int32)


def block_levels(rng, shape, cuts, low, high):
    loudness, own = 1.0, jax.random.fold_in(rng, 6)
    for dim, blocks in cuts:
        draws = jnp.exp(jax.random.uniform(jax.random.fold_in(own, dim), (blocks,), jnp.float32, low / len(cuts), high / len(cuts)))
        loudness = loudness * jnp.repeat(draws, shape[dim] // blocks).reshape([-1 if axis == dim else 1 for axis in range(len(shape))])
    return loudness


def scatter_about(rng, dims, deviation, most, pieces=(), kind=jnp.bfloat16):
    level = block_levels(rng, dims, pieces, -0.22, 0.18) if pieces else 1.0
    result = jax.random.normal(rng, dims, jnp.float32) * deviation * level
    return jnp.minimum(jnp.maximum(result, -most), most).astype(kind)


def setup_inputs(seed: int = 0) -> dict:
    key_of = jax.random.split(jax.random.key(seed), 23)
    return {
        "tokens": scatter_about(key_of[0], (MICRO, TOK, D), 1.0, 6.0, ((1, 8),)),
        "context": scatter_about(key_of[1], (MICRO, IMGS, CD), 1.0, 6.0, ((1, 8),)),
        "captions": scatter_about(key_of[2], (MICRO, IMGS, TXT, DT), 1.0, 6.0, ((1, 8),)),
        "shapes": draw_shapes(jax.random.fold_in(key_of[22], 71), 0),
        "text_len": draw_text_len(jax.random.fold_in(key_of[22], 71), 0),
        "w_query": scatter_about(key_of[5], (D, D), D ** -0.5, 0.15625, ((0, 8), (1, 4))),
        "w_key": scatter_about(key_of[6], (D, D), D ** -0.5, 0.15625, ((0, 8), (1, 4))),
        "w_value": scatter_about(key_of[7], (D, D), D ** -0.5, 0.15625, ((0, 8), (1, 4))),
        "w_out": scatter_about(key_of[8], (D, D), (D // 16) ** -0.5, 0.625, ((0, 8), (1, 4))),
        "w_text_key": scatter_about(key_of[9], (DT, D), DT ** -0.5, 0.09375, ((0, 8), (1, 4))),
        "w_text_value": scatter_about(key_of[10], (DT, D), DT ** -0.5, 0.09375, ((0, 8), (1, 4))),
        "w_gate": scatter_about(key_of[11], (D, FF), D ** -0.5, 0.15625, ((0, 8), (1, 4))),
        "w_up": scatter_about(key_of[12], (D, FF), D ** -0.5, 0.15625, ((0, 8), (1, 4))),
        "w_down": scatter_about(key_of[13], (D, FF), (FF // 4) ** -0.5, 0.1875, ((0, 8), (1, 4))),
        "w_adaln": scatter_about(key_of[14], (CD, 4 * D), (CD // 2) ** -0.5, 0.25, ((0, 8), (1, 4))),
        "gain_attn": jnp.clip(1.0 + 0.15 * jax.random.normal(key_of[15], (D,), jnp.float32), 0.25, 1.75).astype(jnp.bfloat16),
        "gain_ffn": jnp.clip(1.0 + 0.15 * jax.random.normal(key_of[16], (D,), jnp.float32), 0.25, 1.75).astype(jnp.bfloat16),
        "gain_query": jnp.clip(1.0 + 0.15 * jax.random.normal(key_of[17], (HEAD_DIM, HEADS), jnp.float32), 0.25, 1.75).astype(jnp.bfloat16),
        "gain_key": jnp.clip(1.0 + 0.15 * jax.random.normal(key_of[18], (HEAD_DIM, HEADS), jnp.float32), 0.25, 1.75).astype(jnp.bfloat16),
        "gain_text": jnp.clip(1.0 + 0.15 * jax.random.normal(key_of[19], (HEAD_DIM, HEADS), jnp.float32), 0.25, 1.75).astype(jnp.bfloat16),
        "cross_gate": jnp.clip(jax.random.uniform(key_of[20], (HEADS,), jnp.float32, -1.5, 1.5) * block_levels(key_of[20], (HEADS,), ((0, 4),), -0.4, 0.0), -1.5, 1.5).astype(jnp.bfloat16),
        "cotangent": scatter_about(key_of[21], (MICRO, TOK, D), 1.0, 6.0, ((1, 8),)),
    }


@jax.custom_vjp
def low(v):
    return lax.optimization_barrier(v.astype(jnp.bfloat16)).astype(jnp.float32)

@jax.custom_vjp
def low_back(v):
    return v

def low_keep(v):
    return (low(v), None)

def low_pass(kept, grad):
    return (grad,)

def back_keep(v):
    return (v, None)

def back_low(kept, grad):
    return (low(grad),)
low.defvjp(low_keep, low_pass)
low_back.defvjp(back_keep, back_low)
EPSILON = 1e-06
MASKED = -1e+30
ROPE_BASE = 10000.0

def exact_dot(left, right):
    return jnp.dot(left, right, precision=lax.Precision.HIGHEST)

def exact_einsum(form, left, right):
    return jnp.einsum(form, left, right, precision=lax.Precision.HIGHEST)

def image_layout(shapes, count):
    height = shapes[:, 0]
    stride_all = shapes[:, 1] + 1
    extent = height * stride_all
    finish = jnp.cumsum(extent)
    begin = finish - extent
    places = jnp.arange(count, dtype=jnp.int32)
    member = (places[:, None] >= begin[None, :]) & (places[:, None] < finish[None, :])
    member_int = member.astype(jnp.int32)
    inside = lax.optimization_barrier(jnp.sum(member_int, axis=1))
    slot_ids = jnp.arange(shapes.shape[0], dtype=jnp.int32)
    segment = lax.optimization_barrier(jnp.sum(member_int * slot_ids[None, :], axis=1))
    stride = lax.optimization_barrier(jnp.sum(member_int * stride_all[None, :], axis=1)) + 1 - inside
    offset = places - lax.optimization_barrier(jnp.sum(member_int * begin[None, :], axis=1))
    return (member.astype(jnp.float32), segment, inside, offset // stride, offset % stride)

def rope_tables(row_pos, col_pos):
    quarter = HEAD_DIM // 4
    freq = ROPE_BASE ** (-jnp.arange(quarter, dtype=jnp.float32) / quarter)
    angles = jnp.stack([row_pos.astype(jnp.float32)[:, None] * freq[None, :], col_pos.astype(jnp.float32)[:, None] * freq[None, :]], axis=1)
    return (jnp.cos(angles), jnp.sin(angles))

def rotate(values, cosine_table, sine_table):
    count, heads, width = values.shape
    parts = values.reshape(count, heads, 2, 2, width // 4)
    former = parts[:, :, :, 0, :]
    latter = parts[:, :, :, 1, :]
    cos_wide = cosine_table[:, None, :, :]
    sin_wide = sine_table[:, None, :, :]
    turned = jnp.stack([former * cos_wide - latter * sin_wide, latter * cos_wide + former * sin_wide], axis=3)
    return turned.reshape(count, heads, width)

def head_norm(values, gain):
    scale = lax.rsqrt(lax.optimization_barrier(jnp.mean(values * values, axis=-1, keepdims=True)) + EPSILON)
    return values * scale * gain.T[None, :, :]

def row_norm(values):
    return values * lax.rsqrt(lax.optimization_barrier(jnp.mean(values * values, axis=-1, keepdims=True)) + EPSILON)

def attend(queries, keys, values, allowed):
    scores = low_back(exact_einsum('thd,shd->hts', queries, keys)) * HEAD_DIM ** (-0.5)
    scores = jnp.where(allowed[None], scores, MASKED)
    probs = jax.nn.softmax(scores, axis=-1)
    return low_back(exact_einsum('hts,shd->thd', low(probs), values))

def tensor_sum(left, weight):
    count = left.shape[0]
    left_parts = left.reshape(count, N_TENSOR, -1)
    weight_parts = weight.reshape(weight.shape[0], N_TENSOR, -1)
    partial_sums = exact_einsum('tnc,onc->nto', left_parts, weight_parts)
    return lax.optimization_barrier(jnp.sum(low(partial_sums), axis=0))

def block_forward(tokens, params, context, captions, shapes, text_len):
    w_query, w_key, w_value, w_out, w_text_key, w_text_value, w_gate, w_up, w_down, w_adaln, gain_attn, gain_ffn, gain_query, gain_key, gain_text, cross_gate = params
    count = tokens.shape[0]
    slots = shapes.shape[0]
    member, segment, inside, row_pos, col_pos = image_layout(shapes, count)
    cond_act = low(jax.nn.silu(context))
    modulation = low_back(exact_dot(cond_act, w_adaln))
    token_mod = exact_dot(member, modulation)
    scale_attn, gate_attn, scale_ffn, gate_ffn = jnp.split(token_mod, 4, axis=1)
    attn_in = low(row_norm(tokens) * gain_attn * (1.0 + scale_attn))
    cosine_table, sine_table = rope_tables(row_pos, col_pos)
    query = low_back(exact_dot(attn_in, w_query)).reshape(count, HEADS, HEAD_DIM)
    key_proj = low_back(exact_dot(attn_in, w_key)).reshape(count, HEADS, HEAD_DIM)
    value_proj = low(low_back(exact_dot(attn_in, w_value))).reshape(count, HEADS, HEAD_DIM)
    query_rot = low(rotate(head_norm(query, gain_query), cosine_table, sine_table))
    key_rot = low(rotate(head_norm(key_proj, gain_key), cosine_table, sine_table))
    text_flat = captions.reshape(slots * TXT, DT)
    text_raw = low_back(exact_dot(text_flat, w_text_key)).reshape(slots * TXT, HEADS, HEAD_DIM)
    text_key = low(head_norm(text_raw, gain_text))
    text_value = low(low_back(exact_dot(text_flat, w_text_value))).reshape(slots * TXT, HEADS, HEAD_DIM)
    self_id = jnp.where(inside > 0, segment, slots)
    self_mask = self_id[:, None] == self_id[None, :]
    key_slot = jnp.arange(slots * TXT, dtype=jnp.int32) // TXT
    text_live = (jnp.arange(TXT, dtype=jnp.int32)[None, :] < text_len[:, None]).reshape(slots * TXT)
    cross_mask = (segment[:, None] == key_slot[None, :]) & text_live[None, :]
    self_out = attend(query_rot, key_rot, value_proj, self_mask)
    cross_out = attend(query_rot, text_key, text_value, cross_mask)
    mixed = low((self_out + jnp.tanh(cross_gate)[None, :, None] * cross_out).reshape(count, D))
    attn_out = low_back(tensor_sum(mixed, w_out))
    hidden = tokens + jnp.tanh(gate_attn) * attn_out
    ffn_in = low(row_norm(hidden) * gain_ffn * (1.0 + scale_ffn))
    gate_proj = low_back(exact_dot(ffn_in, w_gate))
    up_proj = low_back(exact_dot(ffn_in, w_up))
    inner = low(jax.nn.silu(gate_proj) * up_proj)
    ffn_out = low_back(tensor_sum(inner, w_down))
    return hidden + jnp.tanh(gate_ffn) * ffn_out

def reference(tokens, context, captions, shapes, text_len, w_query, w_key, w_value, w_out, w_text_key, w_text_value, w_gate, w_up, w_down, w_adaln, gain_attn, gain_ffn, gain_query, gain_key, gain_text, cross_gate, cotangent):
    params = tuple((weight.astype(jnp.float32) for weight in (w_query, w_key, w_value, w_out, w_text_key, w_text_value, w_gate, w_up, w_down, w_adaln, gain_attn, gain_ffn, gain_query, gain_key, gain_text, cross_gate)))
    groups = MICRO * N_DP
    tok_groups = tokens.astype(jnp.float32).reshape(groups, MB_TOK, D)
    cot_groups = cotangent.astype(jnp.float32).reshape(groups, MB_TOK, D)
    ctx_groups = context.astype(jnp.float32).reshape(groups, IMG_DEV, CD)
    cap_groups = captions.astype(jnp.float32).reshape(groups, IMG_DEV, TXT, DT)
    shape_groups = shapes.reshape(groups, IMG_DEV, 2)
    len_groups = text_len.reshape(groups, IMG_DEV)

    def group_step(totals, group_items):
        tok_part, ctx_part, cap_part, shape_part, len_part, cot_part = group_items

        def closed(tok_in, weights):
            return block_forward(tok_in, weights, ctx_part, cap_part, shape_part, len_part)
        output, pullback = jax.vjp(closed, tok_part, params)
        tok_grad, param_grad = pullback(cot_part)
        totals = jax.tree.map(jnp.add, totals, param_grad)
        return (totals, (output.astype(jnp.bfloat16), tok_grad.astype(jnp.bfloat16)))
    zero_grads = jax.tree.map(jnp.zeros_like, params)
    totals, (outputs, tok_grads) = lax.scan(group_step, zero_grads, (tok_groups, ctx_groups, cap_groups, shape_groups, len_groups, cot_groups))
    return (outputs.reshape(MICRO, TOK, D), tok_grads.reshape(MICRO, TOK, D), totals[0], totals[1], totals[2], totals[3], totals[4], totals[5], totals[6], totals[7], totals[8], totals[9], totals[10], totals[11], totals[12], totals[13], totals[14], totals[15])
```

```python
import functools

import jax
import jax.numpy as jnp
from jax import lax
from jax.sharding import PartitionSpec as P

HEAD_DIM = 64
DT = 4096
TXT = 256


EPSILON = 1e-06
MASKED = -1e30
ROPE_BASE = 10000.0


def image_layout(shapes, count):
    height = shapes[:, 0]
    stride_all = shapes[:, 1] + 1
    extent = height * stride_all
    finish = jnp.cumsum(extent)
    begin = finish - extent
    places = jnp.arange(count, dtype=jnp.int32)
    member = (places[:, None] >= begin[None, :]) & (places[:, None] < finish[None, :])
    member_int = member.astype(jnp.int32)
    inside = jnp.sum(member_int, axis=1)
    slot_ids = jnp.arange(shapes.shape[0], dtype=jnp.int32)
    segment = jnp.sum(member_int * slot_ids[None, :], axis=1)
    stride = jnp.sum(member_int * stride_all[None, :], axis=1) + 1 - inside
    offset = places - jnp.sum(member_int * begin[None, :], axis=1)
    return (member.astype(jnp.float32), segment, inside, offset // stride, offset % stride)


def rope_tables(row_pos, col_pos):
    quarter = HEAD_DIM // 4
    freq = ROPE_BASE ** (-jnp.arange(quarter, dtype=jnp.float32) / quarter)
    angles = jnp.stack(
        [
            row_pos.astype(jnp.float32)[:, None] * freq[None, :],
            col_pos.astype(jnp.float32)[:, None] * freq[None, :],
        ],
        axis=1,
    )
    return (jnp.cos(angles), jnp.sin(angles))


def rotate(values, cosine_table, sine_table):
    count, heads, width = values.shape
    parts = values.reshape(count, heads, 2, 2, width // 4)
    former = parts[:, :, :, 0, :]
    latter = parts[:, :, :, 1, :]
    cos_wide = cosine_table[:, None, :, :]
    sin_wide = sine_table[:, None, :, :]
    turned = jnp.stack(
        [former * cos_wide - latter * sin_wide, latter * cos_wide + former * sin_wide], axis=3
    )
    return turned.reshape(count, heads, width)


def head_norm(values, gain):
    scale = lax.rsqrt(jnp.mean(values * values, axis=-1, keepdims=True) + EPSILON)
    return values * scale * gain.T[None, :, :]


def modulate(values, gain, scale):
    normed = values * lax.rsqrt(jnp.mean(values * values, axis=1, keepdims=True) + EPSILON)
    return normed * gain * (1.0 + scale)


def activate(gate_val, up_val):
    return jax.nn.silu(gate_val) * up_val


def contract_rows(left, right):
    return lax.dot_general(
        left, right, (((0,), (0,)), ((), ())), preferred_element_type=jnp.float32
    )


def contract_cols(left, right):
    return lax.dot_general(
        left, right, (((1,), (1,)), ((), ())), preferred_element_type=jnp.float32
    )


def score_block(queries, keys, allowed, scale):
    scores = jnp.einsum("thd,shd->hts", queries, keys, preferred_element_type=jnp.float32) * scale
    return jnp.where(allowed[None], scores, MASKED)


def attend_forward(queries, keys, values, allowed, scale):
    scores = score_block(queries, keys, allowed, scale)
    peak = jnp.max(scores, axis=2, keepdims=True)
    expo = jnp.exp(scores - peak)
    total = jnp.sum(expo, axis=2, keepdims=True)
    probs = (expo / total).astype(jnp.bfloat16)
    output = jnp.einsum("hts,shd->thd", probs, values, preferred_element_type=jnp.float32)
    return (output, peak + jnp.log(total))


def attend_backward(queries, keys, values, allowed, scale, log_total, grad_out):
    probs = jnp.exp(score_block(queries, keys, allowed, scale) - log_total)
    grad_probs = jnp.einsum("thd,shd->hts", grad_out, values, preferred_element_type=jnp.float32)
    grad_scores = probs * (grad_probs - jnp.sum(probs * grad_probs, axis=2, keepdims=True))
    scaled = (grad_scores * scale).astype(jnp.bfloat16)
    grad_query = jnp.einsum("hts,shd->thd", scaled, keys, preferred_element_type=jnp.float32)
    grad_key = jnp.einsum("hts,thd->shd", scaled, queries, preferred_element_type=jnp.float32)
    grad_value = jnp.einsum(
        "hts,thd->shd", probs.astype(jnp.bfloat16), grad_out, preferred_element_type=jnp.float32
    )
    return (grad_query, grad_key, grad_value)


def shards(
    n_dp,
    n_tensor,
    tokens,
    context,
    captions,
    shapes,
    text_len,
    w_query,
    w_key,
    w_value,
    w_out,
    w_text_key,
    w_text_value,
    w_gate,
    w_up,
    w_down,
    w_adaln,
    gain_attn,
    gain_ffn,
    gain_query,
    gain_key,
    gain_text,
    cross_gate,
    cotangent,
):
    parts = 8 if n_dp == 8 else 1
    micro, count, width = tokens.shape
    slots = shapes.shape[1]
    rows = micro * count
    images = micro * slots
    heads = w_query.shape[1] // HEAD_DIM
    local_width = heads * HEAD_DIM
    hidden_units = w_gate.shape[1]
    scale = HEAD_DIM ** (-0.5)
    dp_rank = lax.axis_index("dp")
    tensor_rank = lax.axis_index("tensor")
    order = dp_rank ^ jnp.arange(parts, dtype=jnp.int32) if parts > 1 else None

    def hop(value, mask):
        return lax.ppermute(value, "dp", [(i, i ^ mask) for i in range(n_dp)])

    def spread(shard, path):
        if parts == 1:
            return [lax.all_gather(shard, "dp", axis=0, tiled=True)]
        along_x = hop(shard, 2)
        along_y = hop(shard, 4)
        diagonal = hop(along_y, 2) if path == 0 else hop(along_x, 4)
        even = [shard, along_x, along_y, diagonal]
        odd = [hop(piece, 1) for piece in even]
        return [piece for pair in zip(even, odd) for piece in pair]

    def collect(even, odd, path):
        if parts == 1:
            return lax.psum_scatter(even[0].astype(jnp.float32), "dp", scatter_dimension=0, tiled=True)
        got = hop(odd, 1)
        pair = [even[i].astype(jnp.float32) + got[i].astype(jnp.float32) for i in range(4)]
        near, far, first, second = (1, 2, 2, 4) if path == 0 else (2, 1, 4, 2)
        got = hop(jnp.stack([pair[near], pair[3]]).astype(jnp.bfloat16), first)
        kept = pair[0] + got[0].astype(jnp.float32)
        passed = (pair[far] + got[1].astype(jnp.float32)).astype(jnp.bfloat16)
        return kept + hop(passed, second).astype(jnp.float32)

    def relative(value, axis):
        if parts == 1:
            return value
        shape = value.shape
        cut = shape[:axis] + (parts, shape[axis] // parts) + shape[axis + 1 :]
        return jnp.take(value.reshape(cut), order, axis=axis).reshape(shape)

    def tensor_shift(value, shift):
        return lax.ppermute(
            value, "tensor", [(i, (i + shift) % n_tensor) for i in range(n_tensor)]
        )

    def tensor_sum(partial):
        part_rows = partial.shape[0] // n_tensor
        partial = partial.astype(jnp.bfloat16)

        def block(rank):
            return lax.dynamic_slice_in_dim(partial, rank * part_rows, part_rows, 0)

        total = block(tensor_rank).astype(jnp.float32)
        for shift in range(1, n_tensor):
            got = tensor_shift(block((tensor_rank + shift) % n_tensor), shift)
            total = total + got.astype(jnp.float32)
        return tensor_gather(total.astype(jnp.bfloat16), 0)

    def tensor_gather(value, axis):
        got = [value] + [tensor_shift(value, shift) for shift in range(1, n_tensor)]
        stacked = jnp.stack(got)
        ranks = (tensor_rank - jnp.arange(n_tensor, dtype=jnp.int32)) % n_tensor
        placed = jnp.take(stacked, ranks, axis=0)
        return jnp.concatenate([placed[i] for i in range(n_tensor)], axis=axis)

    def grad_pieces(left, right):
        blocks = left.reshape(left.shape[0], parts, -1)
        even = jnp.einsum(
            "tpk,tn->pkn", blocks[:, 0::2], right, preferred_element_type=jnp.float32
        ).astype(jnp.bfloat16)
        if parts == 1:
            return even, None
        odd = jnp.einsum(
            "tpk,tn->pkn", blocks[:, 1::2], right, preferred_element_type=jnp.float32
        ).astype(jnp.bfloat16)
        return even, odd

    half = hidden_units // 2
    small = jnp.concatenate(
        [
            context.reshape(-1),
            gain_attn,
            gain_ffn,
            gain_query.reshape(-1),
            gain_key.reshape(-1),
            gain_text.reshape(-1),
        ]
    )
    small_all = lax.all_gather(small, "dp", axis=0)
    text_key_pieces = spread(w_text_key, 0)
    text_value_pieces = spread(w_text_value, 1)
    query_value_pieces = spread(jnp.concatenate([w_query, w_value], axis=1), 0)
    key_out_pieces = spread(jnp.concatenate([w_key, w_out], axis=1), 1)
    gate_down_pieces = spread(jnp.concatenate([w_gate, w_down[:, :half]], axis=1), 0)
    up_down_pieces = spread(jnp.concatenate([w_up, w_down[:, half:]], axis=1), 1)
    text_key_mat = relative(jnp.concatenate(text_key_pieces, axis=0), 0)
    text_value_mat = relative(jnp.concatenate(text_value_pieces, axis=0), 0)
    query_value_mat = jnp.concatenate(query_value_pieces, axis=0)
    query_mat, value_mat = query_value_mat[:, :local_width], query_value_mat[:, local_width:]
    key_out_mat = jnp.concatenate(key_out_pieces, axis=0)
    key_mat, out_mat = key_out_mat[:, :local_width], key_out_mat[:, local_width:]
    gate_down_mat = jnp.concatenate(gate_down_pieces, axis=0)
    up_down_mat = jnp.concatenate(up_down_pieces, axis=0)
    gate_mat, up_mat = gate_down_mat[:, :hidden_units], up_down_mat[:, :hidden_units]
    down_mat = jnp.concatenate(
        [gate_down_mat[:, hidden_units:], up_down_mat[:, hidden_units:]], axis=1
    )

    cuts = [context.size, gain_attn.size, gain_ffn.size] + [gain_query.size] * 3
    edges = [sum(cuts[:i]) for i in range(len(cuts) + 1)]
    context_all, attn_gain, ffn_gain, query_gain, key_gain, text_gain = [
        small_all[:, edges[i] : edges[i + 1]] for i in range(6)
    ]
    attn_gain = relative(attn_gain.reshape(width), 0)
    ffn_gain = relative(ffn_gain.reshape(width), 0)
    query_gain = query_gain.reshape(HEAD_DIM, heads)
    key_gain = key_gain.reshape(HEAD_DIM, heads)
    text_gain = text_gain.reshape(HEAD_DIM, heads)

    cond_all = context_all.reshape(n_dp * images, -1)
    cond_rows = w_adaln.shape[0]
    cond_cols = lax.dynamic_slice_in_dim(cond_all, dp_rank * cond_rows, cond_rows, 1)
    cond_act = jax.nn.silu(cond_cols.astype(jnp.float32)).astype(jnp.bfloat16)
    mod_partial = jnp.dot(cond_act, w_adaln, preferred_element_type=jnp.float32)
    mod_part = lax.psum_scatter(mod_partial, "dp", scatter_dimension=0, tiled=True)
    modulation = tensor_gather(mod_part.astype(jnp.bfloat16), 1)
    modulation = relative(modulation.reshape(images, 4, width), 2)

    layouts = [image_layout(shapes[i], count) for i in range(micro)]
    member, segment, inside, row_pos, col_pos = [
        jnp.stack([layout[j] for layout in layouts]) for j in range(5)
    ]
    tables = [rope_tables(row_pos[i], col_pos[i]) for i in range(micro)]
    cosine_table = jnp.concatenate([table[0] for table in tables])
    sine_table = jnp.concatenate([table[1] for table in tables])
    token_mod = jnp.einsum(
        "mts,mscd->cmtd",
        member.astype(jnp.bfloat16),
        modulation.reshape(micro, slots, 4, width),
        preferred_element_type=jnp.float32,
    ).reshape(4, rows, width)
    scale_attn, gate_attn, scale_ffn, gate_ffn = [token_mod[i] for i in range(4)]

    token_rel = relative(tokens.reshape(rows, width), 1)
    grad_y_rel = relative(cotangent.reshape(rows, width), 1)
    residual_in = token_rel.astype(jnp.float32)
    attn_in_f, norm_pull = jax.vjp(modulate, residual_in, attn_gain.astype(jnp.float32), scale_attn)
    attn_in = attn_in_f.astype(jnp.bfloat16)

    def prep_pos(values, gain):
        return rotate(head_norm(values, gain), cosine_table, sine_table)

    query_raw = jnp.dot(attn_in, query_mat, preferred_element_type=jnp.float32)
    query_rot_f, query_pull = jax.vjp(
        prep_pos, query_raw.reshape(rows, heads, HEAD_DIM), query_gain.astype(jnp.float32)
    )
    key_raw = jnp.dot(attn_in, key_mat, preferred_element_type=jnp.float32)
    key_rot_f, key_pull = jax.vjp(
        prep_pos, key_raw.reshape(rows, heads, HEAD_DIM), key_gain.astype(jnp.float32)
    )
    by_micro = (micro, count, heads, HEAD_DIM)
    query_rot = query_rot_f.astype(jnp.bfloat16).reshape(by_micro)
    key_rot = key_rot_f.astype(jnp.bfloat16).reshape(by_micro)
    value_proj = (
        jnp.dot(attn_in, value_mat, preferred_element_type=jnp.float32)
        .astype(jnp.bfloat16)
        .reshape(by_micro)
    )
    text_flat = captions.reshape(images * TXT, DT)
    text_raw = jnp.dot(text_flat, text_key_mat, preferred_element_type=jnp.float32)
    text_key_f, text_pull = jax.vjp(
        head_norm, text_raw.reshape(images * TXT, heads, HEAD_DIM), text_gain.astype(jnp.float32)
    )
    text_shape = (micro, slots * TXT, heads, HEAD_DIM)
    text_key = text_key_f.astype(jnp.bfloat16).reshape(text_shape)
    text_value = (
        jnp.dot(text_flat, text_value_mat, preferred_element_type=jnp.float32)
        .astype(jnp.bfloat16)
        .reshape(text_shape)
    )
    self_id = jnp.where(inside > 0, segment, slots)
    self_mask = self_id[:, :, None] == self_id[:, None, :]
    key_slot = jnp.arange(slots * TXT, dtype=jnp.int32) // TXT
    text_live = (jnp.arange(TXT, dtype=jnp.int32)[None, None, :] < text_len[:, :, None]).reshape(
        micro, slots * TXT
    )
    cross_mask = (segment[:, :, None] == key_slot[None, None, :]) & text_live[:, None, :]
    gate_tanh = jnp.tanh(cross_gate.astype(jnp.float32))[None, None, :, None]
    forward = jax.vmap(attend_forward, in_axes=(0, 0, 0, 0, None))
    backward = jax.vmap(attend_backward, in_axes=(0, 0, 0, 0, None, 0, 0))
    self_out, self_lse = forward(query_rot, key_rot, value_proj, self_mask, scale)
    cross_out, cross_lse = forward(query_rot, text_key, text_value, cross_mask, scale)
    mixed = (self_out + gate_tanh * cross_out).reshape(rows, -1).astype(jnp.bfloat16)
    attn_out = tensor_sum(contract_cols(mixed, out_mat)).astype(jnp.float32)
    hidden = residual_in + jnp.tanh(gate_attn) * attn_out
    ffn_in_f, ffn_pull = jax.vjp(modulate, hidden, ffn_gain.astype(jnp.float32), scale_ffn)
    ffn_in = ffn_in_f.astype(jnp.bfloat16)
    gate_proj = jnp.dot(ffn_in, gate_mat, preferred_element_type=jnp.float32)
    up_proj = jnp.dot(ffn_in, up_mat, preferred_element_type=jnp.float32)
    inner_f, act_pull = jax.vjp(activate, gate_proj, up_proj)
    inner = inner_f.astype(jnp.bfloat16)

    grad_y = grad_y_rel.astype(jnp.float32)
    tanh_ffn = jnp.tanh(gate_ffn)
    grad_ffn_out = (tanh_ffn * grad_y).astype(jnp.bfloat16)
    grad_inner = jnp.dot(grad_ffn_out, down_mat, preferred_element_type=jnp.float32)
    grad_gate_f, grad_up_f = act_pull(grad_inner)
    grad_gate_b = grad_gate_f.astype(jnp.bfloat16)
    grad_up_b = grad_up_f.astype(jnp.bfloat16)
    ffn_part = contract_cols(grad_gate_b, gate_mat) + contract_cols(grad_up_b, up_mat)
    grad_ffn_in = tensor_sum(ffn_part).astype(jnp.float32)
    down_0 = collect(*grad_pieces(grad_ffn_out, inner[:, :half]), 0)
    down_1 = collect(*grad_pieces(grad_ffn_out, inner[:, half:]), 1)
    grad_w_gate = collect(*grad_pieces(ffn_in, grad_gate_b), 0)
    grad_w_up = collect(*grad_pieces(ffn_in, grad_up_b), 1)
    ffn_out = tensor_sum(contract_cols(inner, down_mat)).astype(jnp.float32)
    output = (hidden + jnp.tanh(gate_ffn) * ffn_out).astype(jnp.bfloat16)
    grad_gate_ffn = grad_y * ffn_out * (1.0 - tanh_ffn * tanh_ffn)

    grad_hidden_norm, grad_ffn_gain, grad_scale_ffn = ffn_pull(grad_ffn_in)
    grad_hidden = grad_y + grad_hidden_norm
    tanh_attn = jnp.tanh(gate_attn)
    grad_attn_out = (tanh_attn * grad_hidden).astype(jnp.bfloat16)
    grad_gate_attn = grad_hidden * attn_out * (1.0 - tanh_attn * tanh_attn)
    grad_mixed = jnp.dot(grad_attn_out, out_mat, preferred_element_type=jnp.float32).reshape(
        by_micro
    )
    grad_w_out = collect(*grad_pieces(grad_attn_out, mixed), 1)
    grad_self = grad_mixed.astype(jnp.bfloat16)
    grad_cross = (gate_tanh * grad_mixed).astype(jnp.bfloat16)
    gate_total = jnp.sum(grad_mixed * cross_out, axis=(0, 1, 3)) * (
        1.0 - gate_tanh[0, 0, :, 0] * gate_tanh[0, 0, :, 0]
    )
    grad_q_self, grad_k_self, grad_v_self = backward(
        query_rot, key_rot, value_proj, self_mask, scale, self_lse, grad_self
    )
    grad_q_cross, grad_k_text, grad_v_text = backward(
        query_rot, text_key, text_value, cross_mask, scale, cross_lse, grad_cross
    )
    flat = (rows, heads, HEAD_DIM)
    grad_query_raw, grad_query_gain = query_pull((grad_q_self + grad_q_cross).reshape(flat))
    grad_key_raw, grad_key_gain = key_pull(grad_k_self.reshape(flat))
    grad_text_raw, grad_text_gain = text_pull(grad_k_text.reshape(-1, heads, HEAD_DIM))
    grad_query_b = grad_query_raw.reshape(rows, -1).astype(jnp.bfloat16)
    grad_key_b = grad_key_raw.reshape(rows, -1).astype(jnp.bfloat16)
    grad_value_b = grad_v_self.reshape(rows, -1).astype(jnp.bfloat16)
    grad_text_key_b = grad_text_raw.reshape(images * TXT, -1).astype(jnp.bfloat16)
    grad_text_value_b = grad_v_text.reshape(images * TXT, -1).astype(jnp.bfloat16)
    attn_part = (
        contract_cols(grad_query_b, query_mat)
        + contract_cols(grad_key_b, key_mat)
        + contract_cols(grad_value_b, value_mat)
    )
    grad_attn_in = tensor_sum(attn_part).astype(jnp.float32)
    grad_w_query = collect(*grad_pieces(attn_in, grad_query_b), 0)
    grad_w_key = collect(*grad_pieces(attn_in, grad_key_b), 1)
    grad_w_value = collect(*grad_pieces(attn_in, grad_value_b), 0)

    def text_pieces(right):
        full = relative(contract_rows(text_flat, right).astype(jnp.bfloat16), 0)
        blocks = full.reshape(parts, -1, full.shape[1])
        return (blocks[0::2], blocks[1::2]) if parts > 1 else (blocks, None)

    grad_w_text_key = collect(*text_pieces(grad_text_key_b), 0)
    grad_w_text_value = collect(*text_pieces(grad_text_value_b), 1)

    grad_resid_norm, grad_attn_gain, grad_scale_attn = norm_pull(grad_attn_in)
    grad_tokens = (grad_hidden + grad_resid_norm).astype(jnp.bfloat16)
    grad_token_mod = jnp.stack([grad_scale_attn, grad_gate_attn, grad_scale_ffn, grad_gate_ffn])
    grad_modulation = jnp.einsum(
        "mts,cmtd->mscd",
        member,
        grad_token_mod.reshape(4, micro, count, width),
        precision=lax.Precision.HIGHEST,
    ).reshape(images, 4, width)
    grad_modulation = relative(grad_modulation, 2).reshape(images, 4 * width)
    span = w_adaln.shape[1]
    grad_mod_part = lax.dynamic_slice_in_dim(grad_modulation, tensor_rank * span, span, 1).astype(
        jnp.bfloat16
    )
    grad_mod_all = lax.all_gather(grad_mod_part, "dp", axis=0, tiled=True)
    grad_w_adaln = contract_rows(cond_act, grad_mod_all)
    sums = jnp.concatenate(
        [
            relative(grad_attn_gain, 0),
            relative(grad_ffn_gain, 0),
            grad_query_gain.reshape(-1),
            grad_key_gain.reshape(-1),
            grad_text_gain.reshape(-1),
            gate_total,
        ]
    )
    sums = lax.psum(sums, "dp")
    head_size = HEAD_DIM * heads
    edge = 2 * width

    def own(flat_sum, shape):
        whole = flat_sum.reshape(shape)
        size = shape[0] // n_dp
        return lax.dynamic_slice_in_dim(whole, dp_rank * size, size, 0)

    head_shape = (HEAD_DIM, heads)
    return (
        relative(output, 1).reshape(micro, count, width),
        relative(grad_tokens, 1).reshape(micro, count, width),
        grad_w_query,
        grad_w_key,
        grad_w_value,
        grad_w_out,
        grad_w_text_key,
        grad_w_text_value,
        grad_w_gate,
        grad_w_up,
        jnp.concatenate([down_0, down_1], axis=1),
        grad_w_adaln,
        own(sums[:width], (width,)),
        own(sums[width:edge], (width,)),
        own(sums[edge : edge + head_size], head_shape),
        own(sums[edge + head_size : edge + 2 * head_size], head_shape),
        own(sums[edge + 2 * head_size : edge + 3 * head_size], head_shape),
        sums[edge + 3 * head_size :],
    )


def solution(mesh):
    return jax.shard_map(
        functools.partial(shards, mesh.shape["dp"], mesh.shape["tensor"]),
        mesh=mesh,
        in_specs=(
            P(None, "dp", None),
            P(None, "dp", None),
            P(None, "dp", None, None),
            P(None, "dp", None),
            P(None, "dp"),
            P("dp", "tensor"),
            P("dp", "tensor"),
            P("dp", "tensor"),
            P("dp", "tensor"),
            P("dp", "tensor"),
            P("dp", "tensor"),
            P("dp", "tensor"),
            P("dp", "tensor"),
            P("dp", "tensor"),
            P("dp", "tensor"),
            P("dp"),
            P("dp"),
            P("dp", "tensor"),
            P("dp", "tensor"),
            P("dp", "tensor"),
            P("tensor"),
            P(None, "dp", None),
        ),
        out_specs=(
            P(None, "dp", None),
            P(None, "dp", None),
            P("dp", "tensor"),
            P("dp", "tensor"),
            P("dp", "tensor"),
            P("dp", "tensor"),
            P("dp", "tensor"),
            P("dp", "tensor"),
            P("dp", "tensor"),
            P("dp", "tensor"),
            P("dp", "tensor"),
            P("dp", "tensor"),
            P("dp"),
            P("dp"),
            P("dp", "tensor"),
            P("dp", "tensor"),
            P("dp", "tensor"),
            P("tensor"),
        ),
        check_vma=False,
    )
```

```python
import functools

import jax
import jax.numpy as jnp
from jax import lax
from jax.experimental import pallas as pl
from jax.experimental.pallas import tpu as pltpu
from jax.sharding import PartitionSpec as P

HEAD_DIM = 64
DT = 4096
TXT = 256


EPSILON = 1e-06
MASKED = -1e30
ROPE_BASE = 10000.0
STRIP = 16
F32 = jnp.float32
BF16 = jnp.bfloat16


def image_layout(shapes, count):
    height = shapes[:, 0]
    stride_all = shapes[:, 1] + 1
    extent = height * stride_all
    finish = jnp.cumsum(extent)
    begin = finish - extent
    places = jnp.arange(count, dtype=jnp.int32)
    member = (places[:, None] >= begin[None, :]) & (places[:, None] < finish[None, :])
    member_int = member.astype(jnp.int32)
    inside = jnp.sum(member_int, axis=1)
    slot_ids = jnp.arange(shapes.shape[0], dtype=jnp.int32)
    segment = jnp.sum(member_int * slot_ids[None, :], axis=1)
    stride = jnp.sum(member_int * stride_all[None, :], axis=1) + 1 - inside
    offset = places - jnp.sum(member_int * begin[None, :], axis=1)
    return (member.astype(jnp.float32), segment, inside, offset // stride, offset % stride)


def rope_tables(row_pos, col_pos):
    quarter = HEAD_DIM // 4
    freq = ROPE_BASE ** (-jnp.arange(quarter, dtype=jnp.float32) / quarter)
    angles = jnp.stack(
        [
            row_pos.astype(jnp.float32)[:, None] * freq[None, :],
            col_pos.astype(jnp.float32)[:, None] * freq[None, :],
        ],
        axis=1,
    )
    return (jnp.cos(angles), jnp.sin(angles))


def dot_nn(left, right):
    return lax.dot_general(left, right, (((1,), (0,)), ((), ())), preferred_element_type=F32)


def dot_nt(left, right):
    return lax.dot_general(left, right, (((1,), (1,)), ((), ())), preferred_element_type=F32)


def dot_tn(left, right):
    return lax.dot_general(left, right, (((0,), (0,)), ((), ())), preferred_element_type=F32)


def struct(shape, dtype=BF16):
    return jax.ShapeDtypeStruct(shape, dtype)


def run(body, outs, ins, scratch=(), flops=0, traffic=0):
    return pl.pallas_call(
        body,
        out_shape=outs,
        in_specs=[pl.BlockSpec(memory_space=space) for _, space in ins],
        out_specs=[pl.BlockSpec(memory_space=pltpu.VMEM)] * len(outs),
        scratch_shapes=list(scratch),
        compiler_params=pltpu.CompilerParams(vmem_limit_bytes=48 * 2**20),
        cost_estimate=pl.CostEstimate(flops=flops, bytes_accessed=traffic, transcendentals=0),
    )(*[array for array, _ in ins])


def start_pieces(pieces, target, sems):
    rank = lax.axis_index("dp")
    size = pieces[0].shape[0]
    copies = []
    for index, piece in enumerate(pieces):
        owner = jnp.bitwise_xor(rank, index) if len(pieces) > 1 else 0
        place = pl.ds(pl.multiple_of(owner * size, 64), size)
        copies.append(pltpu.make_async_copy(piece, target.at[place], sems.at[index]))
    for copy in copies:
        copy.start()
    return copies


def wait_all(copies):
    for copy in copies:
        copy.wait()


def place_blocks(blocks, target, n_tensor):
    rank = lax.axis_index("tensor")
    size = blocks[0].shape[0]
    for shift, block in enumerate(blocks):
        owner = lax.rem(rank - shift + n_tensor, n_tensor)
        target[pl.ds(pl.multiple_of(owner * size, 16), size), :] = block[...]


def cut_blocks(source, outs, n_tensor):
    rank = lax.axis_index("tensor")
    size = outs[0].shape[0]
    for shift, out in enumerate(outs):
        owner = lax.rem(rank + shift, n_tensor)
        out[...] = source[pl.ds(pl.multiple_of(owner * size, 16), size), :]


def token_columns(member, mods, which, target, n_tensor):
    rank = lax.axis_index("tensor")
    chosen = mods[0][...]
    for shift in range(1, n_tensor):
        chosen = jnp.where(lax.rem(rank - shift + n_tensor, n_tensor) == which, mods[shift][...], chosen)
    target[...] = dot_nn(member[...], chosen).astype(BF16)


def over_strips(rows, step):
    @pl.loop(0, rows // STRIP)
    def _(index):
        step(pl.ds(pl.multiple_of(index * STRIP, STRIP), STRIP))


def write_pieces(left, right, even, odd, total):
    width = left.shape[1]
    step = 256
    columns = right.shape[1]
    rank = lax.axis_index("dp")
    for first in range(0, columns, step):
        span = slice(first, min(first + step, columns))
        total[:, span] = dot_tn(left[...], right[:, span]).astype(BF16)
    size = even.shape[1]
    if even.shape[0] == 1:
        even[0] = total[:, :columns]
        return
    for index in range(4):
        for out, low in ((even, 0), (odd, 1)):
            owner = jnp.bitwise_xor(rank, 2 * index + low)
            out[index] = total[pl.ds(pl.multiple_of(owner * size, 64), size), :columns]


def head_sum(values, blocks):
    high = values.astype(BF16)
    low = (values - high.astype(F32)).astype(BF16)
    return dot_nn(high, blocks) + dot_nn(low, blocks)


def head_blocks(width):
    row = lax.broadcasted_iota(jnp.int32, (width, width), 0) // HEAD_DIM
    column = lax.broadcasted_iota(jnp.int32, (width, width), 1) // HEAD_DIM
    return jnp.where(row == column, 1.0, 0.0).astype(BF16)


def swap_pairs(values):
    width = values.shape[1]
    quarter = HEAD_DIM // 4
    lane = lax.broadcasted_iota(jnp.int32, values.shape, 1)
    former = lax.rem(lane, 2 * quarter) < quarter
    return jnp.where(
        former, pltpu.roll(values, width - quarter, 1), pltpu.roll(values, quarter, 1)
    )


def head_norm(values, gain, blocks):
    scale = lax.rsqrt(head_sum(values * values, blocks) * (1.0 / HEAD_DIM) + EPSILON)
    return values * scale * gain


def head_norm_back(values, gain, grad, blocks):
    scale = lax.rsqrt(head_sum(values * values, blocks) * (1.0 / HEAD_DIM) + EPSILON)
    normed = values * scale
    grad_gain = jnp.sum(grad * normed, axis=0, keepdims=True)
    inner = grad * gain
    mean = head_sum(inner * normed, blocks) * (1.0 / HEAD_DIM)
    return scale * (inner - normed * mean), grad_gain


def row_scale(values):
    return lax.rsqrt(jnp.mean(values * values, axis=1, keepdims=True) + EPSILON)


def project_kernel(
    n_tensor, parts, tokens, member, gain, q_gain, k_gain, cosine, sine, *rest
):
    mods, rest = rest[:n_tensor], rest[n_tensor:]
    pieces_a, pieces_b, rest = rest[:parts], rest[parts : 2 * parts], rest[2 * parts :]
    attn_in, query_raw, key_raw, query_rot, key_rot, value, mat_a, mat_b, mod, sems = rest
    copies = start_pieces(pieces_a, mat_a, sems.at[0]) + start_pieces(pieces_b, mat_b, sems.at[1])
    width = q_gain.shape[1]
    token_columns(member, mods, 0, mod, n_tensor)
    blocks = head_blocks(width)

    def step(at):
        x = tokens[at, :].astype(F32)
        normed = x * row_scale(x)
        attn_in[at, :] = (normed * gain[...] * (1.0 + mod[at, :].astype(F32))).astype(BF16)

    over_strips(tokens.shape[0], step)
    wait_all(copies)
    query_raw[...] = dot_nn(attn_in[...], mat_a[:, :width])
    key_raw[...] = dot_nn(attn_in[...], mat_b[:, :width])
    value[...] = dot_nn(attn_in[...], mat_a[:, width:]).astype(BF16)
    for raw, head_gain, out in ((query_raw, q_gain, query_rot), (key_raw, k_gain, key_rot)):
        normed = head_norm(raw[...], head_gain[...], blocks)
        out[...] = (normed * cosine[...] + swap_pairs(normed) * sine[...]).astype(BF16)


def text_kernel(
    parts, live, source, captions, gain, *rest
):
    pieces_k, pieces_v, rest = rest[:parts], rest[parts : 2 * parts], rest[2 * parts :]
    text_raw, text_key, text_value, mat_k, mat_v, sems = rest
    image = pl.program_id(0)

    @pl.when(image == 0)
    def _():
        wait_all(
            start_pieces(pieces_k, mat_k, sems.at[0]) + start_pieces(pieces_v, mat_v, sems.at[1])
        )

    @pl.when(live[image] > 0)
    def _():
        raw = dot_nn(captions[0], mat_k[...])
        text_raw[0] = raw.astype(BF16)
        text_key[0] = head_norm(raw, gain[...], head_blocks(raw.shape[1])).astype(BF16)
        text_value[0] = dot_nn(captions[0], mat_v[...]).astype(BF16)


def softmax(scores, allowed, rows_live):
    scores = jnp.where(allowed, scores, MASKED)
    expo = jnp.where(allowed, jnp.exp(scores - jnp.max(scores, axis=1, keepdims=True)), 0.0)
    total = jnp.sum(expo, axis=1, keepdims=True)
    if rows_live is not None:
        total = jnp.where(rows_live, total, 1.0)
    return expo / total


def attend_kernel(
    n_tensor, parts, micro, scale, live, text_len, query, key, value, text_key, text_value,
    self_id, self_row, segment, gate, *rest
):
    pieces_b, rest = rest[:parts], rest[parts:]
    mixed, cross_out, rest = rest[0], rest[1], rest[2:]
    partials, (mat_b, whole, sems) = rest[:n_tensor], rest[n_tensor:]
    copies = start_pieces(pieces_b, mat_b, sems)
    rows, width = query.shape
    count = rows // micro
    slots = text_key.shape[0] // micro
    heads = width // HEAD_DIM
    cross_out[...] = jnp.zeros_like(cross_out)

    @pl.loop(0, micro * slots)
    def _(image):
        @pl.when(live[image] > 0)
        def _():
            at = pl.ds(pl.multiple_of((image // slots) * count, count), count)
            mine = segment[at, :] == lax.rem(image, slots)
            column = lax.broadcasted_iota(jnp.int32, (count, TXT), 1)
            allowed = mine & (column < text_len[image])
            for head in range(heads):
                lanes = slice(head * HEAD_DIM, (head + 1) * HEAD_DIM)
                scores = dot_nt(query[at, lanes], text_key[image, :, lanes]) * scale
                probs = softmax(scores, allowed, mine).astype(BF16)
                cross_out[at, lanes] += dot_nn(probs, text_value[image, :, lanes])

    for batch in range(micro):
        at = slice(batch * count, (batch + 1) * count)
        allowed = self_id[at, :] == self_row[batch : batch + 1, :]
        for head in range(heads):
            lanes = slice(head * HEAD_DIM, (head + 1) * HEAD_DIM)
            scores = dot_nt(query[at, lanes], key[at, lanes]) * scale
            probs = softmax(scores, allowed, None).astype(BF16)
            out = dot_nn(probs, value[at, lanes])
            mixed[at, lanes] = (out + gate[:, lanes] * cross_out[at, lanes]).astype(BF16)
    wait_all(copies)
    whole[...] = dot_nt(mixed[...], mat_b[:, width:]).astype(BF16)
    cut_blocks(whole, partials, n_tensor)


def feed_kernel(
    n_tensor, parts, tokens, member, gain, cotangent, *rest
):
    mods, rest = rest[:n_tensor], rest[n_tensor:]
    sums, rest = rest[:n_tensor], rest[n_tensor:]
    pieces_a, pieces_b, rest = rest[:parts], rest[parts : 2 * parts], rest[2 * parts :]
    hidden, ffn_in, inner, grad_gate, grad_up, grad_out, rest = *rest[:6], rest[6:]
    partials, rest = rest[:n_tensor], rest[n_tensor:]
    mat_a, mat_b, attn_out, mod_1, mod_2, mod_3, whole, sems = rest
    copies = start_pieces(pieces_a, mat_a, sems.at[0]) + start_pieces(pieces_b, mat_b, sems.at[1])
    place_blocks(sums, attn_out, n_tensor)
    token_columns(member, mods, 1, mod_1, n_tensor)
    token_columns(member, mods, 2, mod_2, n_tensor)
    token_columns(member, mods, 3, mod_3, n_tensor)

    def step(at):
        gate_attn = jnp.tanh(mod_1[at, :].astype(F32))
        state = tokens[at, :].astype(F32) + gate_attn * attn_out[at, :].astype(F32)
        hidden[at, :] = state
        normed = state * row_scale(state)
        ffn_in[at, :] = (normed * gain[...] * (1.0 + mod_2[at, :].astype(F32))).astype(BF16)
        gate_ffn = jnp.tanh(mod_3[at, :].astype(F32))
        grad_out[at, :] = (gate_ffn * cotangent[at, :].astype(F32)).astype(BF16)

    rows = tokens.shape[0]
    over_strips(rows, step)
    wait_all(copies)
    units = inner.shape[1]
    chunk = 256
    for first in range(0, units, chunk):
        span = slice(first, first + chunk)
        gate = dot_nn(ffn_in[...], mat_a[:, span])
        up = dot_nn(ffn_in[...], mat_b[:, span])
        half = units // 2
        down = mat_a if first < half else mat_b
        start = units + first % half
        grad_inner = dot_nn(grad_out[...], down[:, start : start + chunk])
        turn = jax.nn.sigmoid(gate)
        active = gate * turn
        inner[:, span] = (active * up).astype(BF16)
        grad_up[:, span] = (grad_inner * active).astype(BF16)
        slope = turn * (1.0 + gate * (1.0 - turn))
        grad_gate[:, span] = (grad_inner * up * slope).astype(BF16)
    width = tokens.shape[1]
    for first in range(0, width, 512):
        span = slice(first, first + 512)
        whole[:, span] = (
            dot_nt(grad_gate[...], mat_a[span, :units]) + dot_nt(grad_up[...], mat_b[span, :units])
        ).astype(BF16)
    cut_blocks(whole, partials, n_tensor)


def feed_grad_kernel(ffn_in, grad_gate, grad_up, gate_even, gate_odd, up_even, up_odd, total):
    write_pieces(ffn_in, grad_gate, gate_even, gate_odd, total)
    write_pieces(ffn_in, grad_up, up_even, up_odd, total)


def down_grad_kernel(n_tensor, parts, grad_out, inner, *rest):
    pieces_a, pieces_b, rest = rest[:parts], rest[parts : 2 * parts], rest[2 * parts :]
    even, odd, rest = rest[0], rest[1], rest[2:]
    partials, (total, mat_a, mat_b, whole, sems) = rest[:n_tensor], rest[n_tensor:]
    copies = start_pieces(pieces_a, mat_a, sems.at[0]) + start_pieces(pieces_b, mat_b, sems.at[1])
    write_pieces(grad_out, inner, even, odd, total)
    wait_all(copies)
    units = inner.shape[1]
    half = units // 2
    for first in range(0, whole.shape[1], 512):
        span = slice(first, first + 512)
        whole[:, span] = (
            dot_nt(inner[:, :half], mat_a[span, units:])
            + dot_nt(inner[:, half:], mat_b[span, units:])
        ).astype(BF16)
    cut_blocks(whole, partials, n_tensor)


def modulate_back(values, gain, shift, grad):
    scale = row_scale(values)
    normed = values * scale
    inner = grad * gain * (1.0 + shift)
    mean = jnp.mean(inner * normed, axis=1, keepdims=True)
    return scale * (inner - normed * mean), grad * normed


def mixed_grad_kernel(n_tensor, parts, hidden, member, gain, cotangent, *rest):
    mods, rest = rest[:n_tensor], rest[n_tensor:]
    sums, rest = rest[:n_tensor], rest[n_tensor:]
    pieces_b, rest = rest[:parts], rest[parts:]
    grad_hidden, grad_out, grad_mixed, mat_b, grad_in, mod_1, mod_2, sems = rest
    copies = start_pieces(pieces_b, mat_b, sems)
    place_blocks(sums, grad_in, n_tensor)
    token_columns(member, mods, 1, mod_1, n_tensor)
    token_columns(member, mods, 2, mod_2, n_tensor)

    def step(at):
        back, _ = modulate_back(
            hidden[at, :], gain[...], mod_2[at, :].astype(F32), grad_in[at, :].astype(F32)
        )
        total = cotangent[at, :].astype(F32) + back
        grad_hidden[at, :] = total
        grad_out[at, :] = (jnp.tanh(mod_1[at, :].astype(F32)) * total).astype(BF16)

    over_strips(hidden.shape[0], step)
    wait_all(copies)
    width = grad_mixed.shape[1]
    grad_mixed[...] = dot_nn(grad_out[...], mat_b[:, width:])


def attend_back_kernel(
    micro, scale, live, text_len, grad_mixed, cross_out, query, key, value, text_key, text_value,
    text_raw, query_raw, key_raw, q_gain, k_gain, t_gain, cosine, sine, self_id, self_row, segment,
    gate, grad_query_b, grad_key_b, grad_value_b, grad_text_key, grad_text_value,
    gain_sums, grad_query, grad_key, grad_cross, grad_text
):
    rows, width = query.shape
    count = rows // micro
    slots = text_key.shape[0] // micro
    heads = width // HEAD_DIM
    blocks = head_blocks(width)
    gate_sum = jnp.sum(grad_mixed[...] * cross_out[...], axis=0, keepdims=True)
    gain_sums[...] = jnp.zeros_like(gain_sums)
    gain_sums[3:4, :] = gate_sum * (1.0 - gate[...] * gate[...])
    grad_cross[...] = (gate[...] * grad_mixed[...]).astype(BF16)
    for batch in range(micro):
        at = slice(batch * count, (batch + 1) * count)
        allowed = self_id[at, :] == self_row[batch : batch + 1, :]
        for head in range(heads):
            lanes = slice(head * HEAD_DIM, (head + 1) * HEAD_DIM)
            q, k = query[at, lanes], key[at, lanes]
            grad = grad_mixed[at, lanes].astype(BF16)
            probs = softmax(dot_nt(q, k) * scale, allowed, None)
            grad_probs = dot_nt(grad, value[at, lanes])
            mean = jnp.sum(probs * grad_probs, axis=1, keepdims=True)
            scaled = (probs * (grad_probs - mean) * scale).astype(BF16)
            grad_query[at, lanes] = dot_nn(scaled, k)
            grad_key[at, lanes] = dot_tn(scaled, q)
            grad_value_b[at, lanes] = dot_tn(probs.astype(BF16), grad).astype(BF16)

    @pl.loop(0, micro * slots)
    def _(image):
        @pl.when(live[image] == 0)
        def _():
            grad_text_key[image] = jnp.zeros((TXT, width), BF16)
            grad_text_value[image] = jnp.zeros((TXT, width), BF16)

        @pl.when(live[image] > 0)
        def _():
            at = pl.ds(pl.multiple_of((image // slots) * count, count), count)
            mine = segment[at, :] == lax.rem(image, slots)
            column = lax.broadcasted_iota(jnp.int32, (count, TXT), 1)
            allowed = mine & (column < text_len[image])
            for head in range(heads):
                lanes = slice(head * HEAD_DIM, (head + 1) * HEAD_DIM)
                q, k = query[at, lanes], text_key[image, :, lanes]
                grad = grad_cross[at, lanes]
                probs = softmax(dot_nt(q, k) * scale, allowed, mine)
                grad_probs = dot_nt(grad, text_value[image, :, lanes])
                mean = jnp.sum(probs * grad_probs, axis=1, keepdims=True)
                scaled = (probs * (grad_probs - mean) * scale).astype(BF16)
                grad_query[at, lanes] += dot_nn(scaled, k)
                grad_text[:, lanes] = dot_tn(scaled, q)
                grad_text_value[image, :, lanes] = dot_tn(probs.astype(BF16), grad).astype(BF16)
            back, gain_sum = head_norm_back(
                text_raw[image].astype(F32), t_gain[...], grad_text[...], blocks
            )
            grad_text_key[image] = back.astype(BF16)
            gain_sums[2:3, :] += gain_sum

    for index, (grad, raw, gain, out) in enumerate(
        (
            (grad_query, query_raw, q_gain, grad_query_b),
            (grad_key, key_raw, k_gain, grad_key_b),
        )
    ):
        turned = grad[...] * cosine[...] + swap_pairs(grad[...] * sine[...])
        back, gain_sum = head_norm_back(raw[...], gain[...], turned, blocks)
        out[...] = back.astype(BF16)
        gain_sums[index : index + 1, :] = gain_sum


def attn_grad_kernel(
    n_tensor, parts, attn_in, grad_query, grad_key, grad_value, grad_out, mixed, *rest
):
    pieces_a, pieces_b, rest = rest[:parts], rest[parts : 2 * parts], rest[2 * parts :]
    even, odd, rest = rest[:2], rest[2:4], rest[4:]
    partials, rest = rest[:n_tensor], rest[n_tensor:]
    mat_a, mat_b, pair, whole, total, sems = rest
    copies = start_pieces(pieces_a, mat_a, sems.at[0]) + start_pieces(pieces_b, mat_b, sems.at[1])
    width = grad_query.shape[1]
    pair[:, :width] = grad_query[...]
    pair[:, width:] = grad_value[...]
    wait_all(copies)
    for first in range(0, whole.shape[1], 512):
        span = slice(first, first + 512)
        whole[:, span] = (
            dot_nt(pair[...], mat_a[span, :]) + dot_nt(grad_key[...], mat_b[span, :width])
        ).astype(BF16)
    cut_blocks(whole, partials, n_tensor)
    write_pieces(attn_in, pair, even[0], odd[0], total)
    rank = lax.axis_index("dp")
    total[:, :width] = dot_tn(attn_in[...], grad_key[...]).astype(BF16)
    total[:, width:] = dot_tn(grad_out[...], mixed[...]).astype(BF16)
    size = even[1].shape[1]
    if parts == 1:
        even[1][0] = total[...]
        return
    for index in range(4):
        for out, low in ((even[1], 0), (odd[1], 1)):
            owner = jnp.bitwise_xor(rank, 2 * index + low)
            out[index] = total[pl.ds(pl.multiple_of(owner * size, 64), size), :]


def text_grad_kernel(live, source, rank, captions, grad_key, grad_value, out_key, out_value, acc):
    image = pl.program_id(1)
    width = grad_key.shape[2]

    @pl.when(image == 0)
    def _():
        acc[...] = jnp.zeros_like(acc)

    @pl.when(live[image] > 0)
    def _():
        acc[:, :width] += dot_tn(captions[0], grad_key[image])
        acc[:, width:] += dot_tn(captions[0], grad_value[image])

    @pl.when(image == pl.num_programs(1) - 1)
    def _():
        out_key[0] = acc[:, :width].astype(BF16)
        out_value[0] = acc[:, width:].astype(BF16)


def segment_sum(member, values):
    high = values.astype(BF16)
    rest = values - high.astype(F32)
    middle = rest.astype(BF16)
    low = (rest - middle.astype(F32)).astype(BF16)
    return dot_tn(member, high) + dot_tn(member, middle) + dot_tn(member, low)


def output_kernel(n_tensor, hidden, member, gain, cotangent, *rest):
    mods, rest = rest[:n_tensor], rest[n_tensor:]
    sums, rest = rest[:n_tensor], rest[n_tensor:]
    sums_2, rest = rest[:n_tensor], rest[n_tensor:]
    result, grad_mod, grad_gain, ffn_out, grad_in, mod_2, mod_3, grad = rest
    place_blocks(sums, ffn_out, n_tensor)
    place_blocks(sums_2, grad_in, n_tensor)
    token_columns(member, mods, 2, mod_2, n_tensor)
    token_columns(member, mods, 3, mod_3, n_tensor)
    rank = lax.axis_index("tensor")
    grad_gain[...] = jnp.zeros_like(grad_gain)

    def step(at):
        state = hidden[at, :]
        gate = jnp.tanh(mod_3[at, :].astype(F32))
        out = ffn_out[at, :].astype(F32)
        result[at, :] = (state + gate * out).astype(BF16)
        up = grad_in[at, :].astype(F32)
        product = up * state * row_scale(state)
        grad_gain[...] += jnp.sum(
            product * (1.0 + mod_2[at, :].astype(F32)), axis=0, keepdims=True
        )
        grad_gate = cotangent[at, :].astype(F32) * out * (1.0 - gate * gate)
        grad[at, :] = jnp.where(rank == 2, product * gain[...], grad_gate)

    over_strips(hidden.shape[0], step)
    grad_mod[...] = segment_sum(member[...], grad[...])


def input_kernel(n_tensor, tokens, member, gain, grad_hidden, other_mod, *rest):
    mods, rest = rest[:n_tensor], rest[n_tensor:]
    sums, rest = rest[:n_tensor], rest[n_tensor:]
    sums_2, rest = rest[:n_tensor], rest[n_tensor:]
    grad_tokens, grad_mod, grad_gain, attn_out, grad_in, mod_0, mod_1, grad = rest
    place_blocks(sums, grad_in, n_tensor)
    place_blocks(sums_2, attn_out, n_tensor)
    token_columns(member, mods, 0, mod_0, n_tensor)
    token_columns(member, mods, 1, mod_1, n_tensor)
    rank = lax.axis_index("tensor")
    grad_gain[...] = jnp.zeros_like(grad_gain)

    def step(at):
        shift = mod_0[at, :].astype(F32)
        upper = grad_hidden[at, :]
        back, product = modulate_back(
            tokens[at, :].astype(F32), gain[...], shift, grad_in[at, :].astype(F32)
        )
        grad_tokens[at, :] = (upper + back).astype(BF16)
        grad_gain[...] += jnp.sum(product * (1.0 + shift), axis=0, keepdims=True)
        gate = jnp.tanh(mod_1[at, :].astype(F32))
        grad_gate = upper * attn_out[at, :].astype(F32) * (1.0 - gate * gate)
        grad[at, :] = jnp.where(rank == 0, product * gain[...], grad_gate)

    over_strips(tokens.shape[0], step)
    own = segment_sum(member[...], grad[...])
    grad_mod[...] = jnp.where(rank < 2, own, other_mod[...]).astype(BF16)


def shards(
    n_dp,
    n_tensor,
    tokens,
    context,
    captions,
    shapes,
    text_len,
    w_query,
    w_key,
    w_value,
    w_out,
    w_text_key,
    w_text_value,
    w_gate,
    w_up,
    w_down,
    w_adaln,
    gain_attn,
    gain_ffn,
    gain_query,
    gain_key,
    gain_text,
    cross_gate,
    cotangent,
):
    parts = 8 if n_dp == 8 else 1
    micro, count, width = tokens.shape
    slots = shapes.shape[1]
    rows = micro * count
    images = micro * slots
    heads = w_query.shape[1] // HEAD_DIM
    local = heads * HEAD_DIM
    units = w_gate.shape[1]
    scale = HEAD_DIM ** (-0.5)
    dp_rank = lax.axis_index("dp")
    order = dp_rank ^ jnp.arange(parts, dtype=jnp.int32) if parts > 1 else None
    vmem, smem, anywhere = pltpu.VMEM, pltpu.SMEM, pl.ANY
    dma = pltpu.SemaphoreType.DMA

    def inside(*arrays):
        return [(array, vmem) for array in arrays]

    def scalars(*arrays):
        return [(array, smem) for array in arrays]

    def outside(*arrays):
        return [(array, anywhere) for array in arrays]

    def hop(value, mask):
        return lax.ppermute(value, "dp", [(i, i ^ mask) for i in range(n_dp)])

    def spread(shard, path):
        if parts == 1:
            return [lax.all_gather(shard, "dp", axis=0, tiled=True)]
        along_x = hop(shard, 2)
        along_y = hop(shard, 4)
        diagonal = hop(along_y, 2) if path == 0 else hop(along_x, 4)
        even = [shard, along_x, along_y, diagonal]
        odd = [hop(piece, 1) for piece in even]
        return [piece for pair in zip(even, odd) for piece in pair]

    def collect(even, odd, path):
        if parts == 1:
            return lax.psum_scatter(even[0].astype(F32), "dp", scatter_dimension=0, tiled=True)
        got = hop(odd, 1)
        pair = [even[i].astype(F32) + got[i].astype(F32) for i in range(4)]
        near, far, first, second = (1, 2, 2, 4) if path == 0 else (2, 1, 4, 2)
        got = hop(jnp.stack([pair[near], pair[3]]).astype(BF16), first)
        kept = pair[0] + got[0].astype(F32)
        passed = (pair[far] + got[1].astype(F32)).astype(BF16)
        return kept + hop(passed, second).astype(F32)

    def tensor_shift(value, shift):
        return lax.ppermute(
            value, "tensor", [(i, (i + shift) % n_tensor) for i in range(n_tensor)]
        )

    def tensor_gather(value):
        return [value] + [tensor_shift(value, shift) for shift in range(1, n_tensor)]

    def tensor_sum(blocks):
        total = blocks[0].astype(F32)
        for shift in range(1, n_tensor):
            total = total + tensor_shift(blocks[shift], shift).astype(F32)
        return tensor_gather(total.astype(BF16))

    def doubled(value):
        if parts == 1:
            return lax.all_gather(value, "dp", axis=0)
        value = value[None]
        for mask in (1, 2, 4):
            value = jnp.concatenate([value, hop(value, mask)], axis=0)
        return value

    half = units // 2
    small = jnp.concatenate(
        [
            context.reshape(-1),
            gain_attn,
            gain_ffn,
            gain_query.reshape(-1),
            gain_key.reshape(-1),
            gain_text.reshape(-1),
        ]
    )
    small_all = doubled(small)
    text_key_pieces = spread(w_text_key, 0)
    text_value_pieces = spread(w_text_value, 1)
    pieces_qv = spread(jnp.concatenate([w_query, w_value], axis=1), 0)
    pieces_ko = spread(jnp.concatenate([w_key, w_out], axis=1), 1)
    pieces_gd = spread(jnp.concatenate([w_gate, w_down[:, :half]], axis=1), 0)
    pieces_ud = spread(jnp.concatenate([w_up, w_down[:, half:]], axis=1), 1)

    cuts = [context.size, gain_attn.size, gain_ffn.size] + [gain_query.size] * 3
    edges = [sum(cuts[:i]) for i in range(len(cuts) + 1)]
    context_all, *gains = [small_all[:, edges[i] : edges[i + 1]] for i in range(6)]
    if parts > 1:
        gains = [jnp.take(gain, order, axis=0) for gain in gains]
    attn_gain, ffn_gain = [gain.reshape(1, width).astype(F32) for gain in gains[:2]]
    query_gain, key_gain, text_gain = [
        gain.reshape(HEAD_DIM, heads).T.reshape(1, local).astype(F32) for gain in gains[2:]
    ]

    cond_rows = w_adaln.shape[0]
    cond_cols = lax.dynamic_slice_in_dim(
        context_all.reshape(n_dp * images, -1), dp_rank * cond_rows, cond_rows, 1
    )
    cond_act = jax.nn.silu(cond_cols.astype(F32)).astype(BF16)
    mod_partial = dot_nn(cond_act, w_adaln)
    if parts == 1:
        mod_part = lax.psum_scatter(mod_partial, "dp", scatter_dimension=0, tiled=True)
    else:
        mod_part = mod_partial.reshape(parts, images, -1)
        for mask in (4, 2, 1):
            mod_part = mod_part[:mask] + hop(mod_part[mask:], mask)
        mod_part = mod_part[0]
    mods = tensor_gather(mod_part.astype(BF16))

    layouts = [image_layout(shapes[i], count) for i in range(micro)]
    member, segment, inside_any, row_pos, col_pos = [
        jnp.stack([layout[j] for layout in layouts]) for j in range(5)
    ]
    cosine, sine = rope_tables(row_pos.reshape(rows), col_pos.reshape(rows))
    cosine = jnp.tile(jnp.stack([cosine, cosine], axis=2).reshape(rows, HEAD_DIM), (1, heads))
    sine = jnp.tile(jnp.stack([-sine, sine], axis=2).reshape(rows, HEAD_DIM), (1, heads))
    which = jnp.arange(micro, dtype=jnp.int32)
    member = jnp.where(
        (which[:, None] == which[None, :])[:, None, :, None], member[:, :, None, :], 0.0
    )
    member = member.reshape(rows, images).astype(BF16)
    self_row = jnp.where(inside_any > 0, segment, slots)
    self_id = self_row.reshape(rows, 1)
    segment = segment.reshape(rows, 1)
    lens = text_len.reshape(images)
    used = shapes[:, :, 0] * (shapes[:, :, 1] + 1) > 0
    used = used | (jnp.arange(slots)[None, :] == 0)
    live = used.reshape(images).astype(jnp.int32)
    at = jnp.arange(images, dtype=jnp.int32)
    source = lax.cummax(jnp.where(live > 0, at, 0))
    gate = jnp.repeat(jnp.tanh(cross_gate.astype(F32)), HEAD_DIM)[None, :]
    token_rows = tokens.reshape(rows, width)
    grad_y = cotangent.reshape(rows, width)
    caption_images = captions.reshape(images, TXT, DT)

    attn_in, query_raw, key_raw, query_rot, key_rot, value = run(
        functools.partial(project_kernel, n_tensor, parts),
        [struct((rows, width))]
        + [struct((rows, local), F32)] * 2
        + [struct((rows, local))] * 3,
        inside(token_rows, member, attn_gain, query_gain, key_gain, cosine, sine, *mods)
        + outside(*pieces_qv, *pieces_ko),
        [
            vmem((width, 2 * local), BF16),
            vmem((width, 2 * local), BF16),
            vmem((rows, width), BF16),
            dma((2, parts)),
        ],
        flops=6 * rows * width * local,
        traffic=10 * 2**20,
    )

    text_raw, text_key, text_value = pl.pallas_call(
        functools.partial(text_kernel, parts),
        out_shape=[struct((images, TXT, local))] * 3,
        grid_spec=pltpu.PrefetchScalarGridSpec(
            num_scalar_prefetch=2,
            grid=(images,),
            in_specs=[
                pl.BlockSpec((1, TXT, DT), lambda i, live, source: (source[i], 0, 0)),
                pl.BlockSpec((1, local), lambda i, live, source: (0, 0)),
            ]
            + [pl.BlockSpec(memory_space=anywhere)] * (2 * parts),
            out_specs=[pl.BlockSpec((1, TXT, local), lambda i, live, source: (i, 0, 0))] * 3,
            scratch_shapes=[vmem((DT, local), BF16), vmem((DT, local), BF16), dma((2, parts))],
        ),
        compiler_params=pltpu.CompilerParams(vmem_limit_bytes=40 * 2**20),
        cost_estimate=pl.CostEstimate(
            flops=2 * images * TXT * DT * local, bytes_accessed=20 * 2**20, transcendentals=0
        ),
    )(live, source, caption_images, text_gain, *text_key_pieces, *text_value_pieces)

    part_rows = rows // n_tensor
    blocks = [struct((part_rows, width))] * n_tensor
    mixed, cross_out, *attn_part = run(
        functools.partial(attend_kernel, n_tensor, parts, micro, scale),
        [struct((rows, local)), struct((rows, local), F32)] + blocks,
        scalars(live, lens)
        + inside(query_rot, key_rot, value, text_key, text_value, self_id, self_row, segment, gate)
        + outside(*pieces_ko),
        [vmem((width, 2 * local), BF16), vmem((rows, width), BF16), dma((parts,))],
        flops=2 * 2**30,
        traffic=12 * 2**20,
    )
    attn_out = tensor_sum(attn_part)

    mat = vmem((width, units + half), BF16)
    wide = vmem((rows, width), BF16)
    hidden, ffn_in, inner, grad_gate, grad_up, grad_ffn_out, *ffn_part = run(
        functools.partial(feed_kernel, n_tensor, parts),
        [struct((rows, width), F32), struct((rows, width))]
        + [struct((rows, units))] * 3
        + [struct((rows, width))]
        + blocks,
        inside(token_rows, member, ffn_gain, grad_y, *mods, *attn_out)
        + outside(*pieces_gd, *pieces_ud),
        [mat, mat, wide, wide, wide, wide, wide, dma((2, parts))],
        flops=10 * rows * width * units,
        traffic=20 * 2**20,
    )
    grad_ffn_in = tensor_sum(ffn_part)

    size = width // parts
    even_of = lambda depth, columns: struct((max(parts // 2, 1), depth, columns))
    piece = [even_of(size, units)] * 2
    down_even, down_odd, *ffn_out_part = run(
        functools.partial(down_grad_kernel, n_tensor, parts),
        piece + blocks,
        inside(grad_ffn_out, inner) + outside(*pieces_gd, *pieces_ud),
        [vmem((width, units), BF16), mat, mat, wide, dma((2, parts))],
        flops=4 * rows * width * units,
        traffic=15 * 2**20,
    )
    gate_even, gate_odd, up_even, up_odd = run(
        feed_grad_kernel,
        piece + piece,
        inside(ffn_in, grad_gate, grad_up),
        [vmem((width, units), BF16)],
        flops=4 * rows * width * units,
        traffic=8 * 2**20,
    )
    grad_down_0 = collect(down_even[:, :, :half], down_odd[:, :, :half], 0)
    grad_down_1 = collect(down_even[:, :, half:], down_odd[:, :, half:], 1)
    grad_w_gate = collect(gate_even, gate_odd, 0)
    grad_w_up = collect(up_even, up_odd, 1)

    grad_hidden, grad_attn_out, grad_mixed = run(
        functools.partial(mixed_grad_kernel, n_tensor, parts),
        [struct((rows, width), F32), struct((rows, width)), struct((rows, local), F32)],
        inside(hidden, member, ffn_gain, grad_y, *mods, *grad_ffn_in) + outside(*pieces_ko),
        [vmem((width, 2 * local), BF16), wide, wide, wide, dma((parts,))],
        flops=2 * rows * width * local,
        traffic=8 * 2**20,
    )

    tile = struct((rows, local))
    texts = struct((images, TXT, local))
    grad_query_b, grad_key_b, grad_value_b, grad_text_key, grad_text_value, gain_sums = run(
        functools.partial(attend_back_kernel, micro, scale),
        [tile, tile, tile, texts, texts, struct((8, local), F32)],
        scalars(live, lens)
        + inside(
            grad_mixed, cross_out, query_rot, key_rot, value, text_key, text_value, text_raw,
            query_raw, key_raw, query_gain, key_gain, text_gain, cosine, sine, self_id, self_row,
            segment, gate,
        ),
        [
            vmem((rows, local), F32),
            vmem((rows, local), F32),
            vmem((rows, local), BF16),
            vmem((TXT, local), F32),
        ],
        flops=4 * 2**30,
        traffic=15 * 2**20,
    )

    piece = even_of(size, 2 * local)
    qv_even, ko_even, qv_odd, ko_odd, *attn_in_part = run(
        functools.partial(attn_grad_kernel, n_tensor, parts),
        [piece] * 4 + blocks,
        inside(attn_in, grad_query_b, grad_key_b, grad_value_b, grad_attn_out, mixed)
        + outside(*pieces_qv, *pieces_ko),
        [
            vmem((width, 2 * local), BF16),
            vmem((width, 2 * local), BF16),
            vmem((rows, 2 * local), BF16),
            wide,
            vmem((width, 2 * local), BF16),
            dma((2, parts)),
        ],
        flops=14 * rows * width * local,
        traffic=15 * 2**20,
    )
    grad_attn_in = tensor_sum(attn_in_part)
    grad_qv = collect(qv_even, qv_odd, 0)
    grad_ko = collect(ko_even, ko_odd, 1)

    depth = DT // parts

    def text_grads(low):
        chosen = max(parts // 2, 1)

        def caption_place(j, i, live, source, rank):
            block = jnp.bitwise_xor(rank[0], 2 * j + low) if parts > 1 else 0
            return (source[i], 0, block)

        return pl.pallas_call(
            text_grad_kernel,
            out_shape=[even_of(depth, local)] * 2,
            grid_spec=pltpu.PrefetchScalarGridSpec(
                num_scalar_prefetch=3,
                grid=(chosen, images),
                in_specs=[
                    pl.BlockSpec((1, TXT, depth), caption_place),
                    pl.BlockSpec((images, TXT, local), lambda j, i, *_: (0, 0, 0)),
                    pl.BlockSpec((images, TXT, local), lambda j, i, *_: (0, 0, 0)),
                ],
                out_specs=[pl.BlockSpec((1, depth, local), lambda j, i, *_: (j, 0, 0))] * 2,
                scratch_shapes=[vmem((depth, 2 * local), F32)],
            ),
            compiler_params=pltpu.CompilerParams(vmem_limit_bytes=56 * 2**20),
            cost_estimate=pl.CostEstimate(
                flops=images * TXT * DT * local, bytes_accessed=10 * 2**20, transcendentals=0
            ),
        )(live, source, dp_rank[None].astype(jnp.int32), caption_images, grad_text_key, grad_text_value)

    if parts > 1:
        text_key_odd, text_value_odd = text_grads(1)
    else:
        text_key_odd, text_value_odd = None, None
    text_key_even, text_value_even = text_grads(0)
    grad_w_text_key = collect(text_key_even, text_key_odd, 0)
    grad_w_text_value = collect(text_value_even, text_value_odd, 1)

    ffn_out = tensor_sum(ffn_out_part)
    result, ffn_mod, ffn_gain_sum = run(
        functools.partial(output_kernel, n_tensor),
        [struct((rows, width)), struct((images, width), F32), struct((1, width), F32)],
        inside(hidden, member, ffn_gain, grad_y, *mods, *ffn_out, *grad_ffn_in),
        [wide, wide, wide, wide, vmem((rows, width), F32)],
        traffic=8 * 2**20,
    )
    grad_tokens, grad_mod, attn_gain_sum = run(
        functools.partial(input_kernel, n_tensor),
        [struct((rows, width)), struct((images, width)), struct((1, width), F32)],
        inside(
            token_rows, member, attn_gain, grad_hidden, ffn_mod, *mods, *grad_attn_in, *attn_out
        ),
        [wide, wide, wide, wide, vmem((rows, width), F32)],
        traffic=8 * 2**20,
    )
    grad_mod_all = doubled(grad_mod).reshape(n_dp * images, width)
    grad_w_adaln = dot_tn(cond_act, grad_mod_all)
    head_sums = gain_sums[:3].reshape(3, heads, HEAD_DIM).transpose(0, 2, 1)
    gate_sums = jnp.sum(gain_sums[3].reshape(heads, HEAD_DIM), axis=1)
    sums = jnp.concatenate(
        [attn_gain_sum[0], ffn_gain_sum[0], head_sums.reshape(-1), gate_sums]
    )
    if parts == 1:
        sums = lax.psum(sums, "dp")
    else:
        for mask in (1, 2, 4):
            sums = sums + hop(sums, mask)

    def own(first, shape):
        whole = sums[first : first + shape[0] * (shape[1] if len(shape) > 1 else 1)].reshape(shape)
        part = shape[0] // n_dp
        return lax.dynamic_slice_in_dim(whole, dp_rank * part, part, 0)

    head_shape = (HEAD_DIM, heads)
    edge = 2 * width
    return (
        result.reshape(micro, count, width),
        grad_tokens.reshape(micro, count, width),
        grad_qv[:, :local],
        grad_ko[:, :local],
        grad_qv[:, local:],
        grad_ko[:, local:],
        grad_w_text_key,
        grad_w_text_value,
        grad_w_gate,
        grad_w_up,
        jnp.concatenate([grad_down_0, grad_down_1], axis=1),
        grad_w_adaln,
        own(0, (width,)),
        own(width, (width,)),
        own(edge, head_shape),
        own(edge + local, head_shape),
        own(edge + 2 * local, head_shape),
        sums[edge + 3 * local :],
    )


def solution(mesh):
    return jax.shard_map(
        functools.partial(shards, mesh.shape["dp"], mesh.shape["tensor"]),
        mesh=mesh,
        in_specs=(
            P(None, "dp", None),
            P(None, "dp", None),
            P(None, "dp", None, None),
            P(None, "dp", None),
            P(None, "dp"),
            P("dp", "tensor"),
            P("dp", "tensor"),
            P("dp", "tensor"),
            P("dp", "tensor"),
            P("dp", "tensor"),
            P("dp", "tensor"),
            P("dp", "tensor"),
            P("dp", "tensor"),
            P("dp", "tensor"),
            P("dp", "tensor"),
            P("dp"),
            P("dp"),
            P("dp", "tensor"),
            P("dp", "tensor"),
            P("dp", "tensor"),
            P("tensor"),
            P(None, "dp", None),
        ),
        out_specs=(
            P(None, "dp", None),
            P(None, "dp", None),
            P("dp", "tensor"),
            P("dp", "tensor"),
            P("dp", "tensor"),
            P("dp", "tensor"),
            P("dp", "tensor"),
            P("dp", "tensor"),
            P("dp", "tensor"),
            P("dp", "tensor"),
            P("dp", "tensor"),
            P("dp", "tensor"),
            P("dp"),
            P("dp"),
            P("dp", "tensor"),
            P("dp", "tensor"),
            P("dp", "tensor"),
            P("tensor"),
        ),
        check_vma=False,
    )
```

```python
import functools

import jax
import jax.numpy as jnp
from jax import lax
from jax.experimental import pallas as pl
from jax.experimental.pallas import tpu as pltpu
from jax.sharding import PartitionSpec as P

HEAD_DIM = 64
DT = 4096
TXT = 256


EPSILON = 1e-06
MASKED = -1e30
ROPE_BASE = 10000.0
STRIP = 16
F32 = jnp.float32
BF16 = jnp.bfloat16


def image_layout(shapes, count):
    height = shapes[:, 0]
    stride_all = shapes[:, 1] + 1
    extent = height * stride_all
    finish = jnp.cumsum(extent)
    begin = finish - extent
    places = jnp.arange(count, dtype=jnp.int32)
    member = (places[:, None] >= begin[None, :]) & (places[:, None] < finish[None, :])
    member_int = member.astype(jnp.int32)
    inside = jnp.sum(member_int, axis=1)
    slot_ids = jnp.arange(shapes.shape[0], dtype=jnp.int32)
    segment = jnp.sum(member_int * slot_ids[None, :], axis=1)
    stride = jnp.sum(member_int * stride_all[None, :], axis=1) + 1 - inside
    offset = places - jnp.sum(member_int * begin[None, :], axis=1)
    return (member.astype(jnp.float32), segment, inside, offset // stride, offset % stride)


def rope_tables(row_pos, col_pos):
    quarter = HEAD_DIM // 4
    freq = ROPE_BASE ** (-jnp.arange(quarter, dtype=jnp.float32) / quarter)
    angles = jnp.stack(
        [
            row_pos.astype(jnp.float32)[:, None] * freq[None, :],
            col_pos.astype(jnp.float32)[:, None] * freq[None, :],
        ],
        axis=1,
    )
    return (jnp.cos(angles), jnp.sin(angles))


def dot_nn(left, right):
    return lax.dot_general(left, right, (((1,), (0,)), ((), ())), preferred_element_type=F32)


def dot_nt(left, right):
    return lax.dot_general(left, right, (((1,), (1,)), ((), ())), preferred_element_type=F32)


def dot_tn(left, right):
    return lax.dot_general(left, right, (((0,), (0,)), ((), ())), preferred_element_type=F32)


def struct(shape, dtype=BF16):
    return jax.ShapeDtypeStruct(shape, dtype)


def run(body, outs, ins, scratch=(), flops=0, traffic=0):
    return pl.pallas_call(
        body,
        out_shape=outs,
        in_specs=[pl.BlockSpec(memory_space=space) for _, space in ins],
        out_specs=[pl.BlockSpec(memory_space=pltpu.VMEM)] * len(outs),
        scratch_shapes=list(scratch),
        compiler_params=pltpu.CompilerParams(vmem_limit_bytes=48 * 2**20),
        cost_estimate=pl.CostEstimate(flops=flops, bytes_accessed=traffic, transcendentals=0),
    )(*[array for array, _ in ins])


def load(source, target, sem):
    copy = pltpu.make_async_copy(source, target, sem)
    copy.start()
    return copy


def wait_all(copies):
    for copy in copies:
        copy.wait()


def token_columns(member, mods, which, target):
    target[...] = dot_nn(member[...], mods[which]).astype(BF16)


def over_strips(rows, step):
    @pl.loop(0, rows // STRIP)
    def _(index):
        step(pl.ds(pl.multiple_of(index * STRIP, STRIP), STRIP))


def write_pieces(left, right, even, odd, total):
    width = left.shape[1]
    step = 256
    columns = right.shape[1]
    rank = lax.axis_index("dp")
    for first in range(0, columns, step):
        span = slice(first, min(first + step, columns))
        total[:, span] = dot_tn(left[...], right[:, span]).astype(BF16)
    size = even.shape[1]
    if even.shape[0] == 1:
        even[0] = total[:, :columns]
        return
    for index in range(4):
        for out, low in ((even, 0), (odd, 1)):
            owner = jnp.bitwise_xor(rank, 2 * index + low)
            out[index] = total[pl.ds(pl.multiple_of(owner * size, 64), size), :columns]


def head_sum(values, blocks):
    high = values.astype(BF16)
    low = (values - high.astype(F32)).astype(BF16)
    return dot_nn(high, blocks) + dot_nn(low, blocks)


def head_blocks(width):
    row = lax.broadcasted_iota(jnp.int32, (width, width), 0) // HEAD_DIM
    column = lax.broadcasted_iota(jnp.int32, (width, width), 1) // HEAD_DIM
    return jnp.where(row == column, 1.0, 0.0).astype(BF16)


def swap_pairs(values):
    width = values.shape[1]
    quarter = HEAD_DIM // 4
    lane = lax.broadcasted_iota(jnp.int32, values.shape, 1)
    former = lax.rem(lane, 2 * quarter) < quarter
    return jnp.where(
        former, pltpu.roll(values, width - quarter, 1), pltpu.roll(values, quarter, 1)
    )


def head_norm(values, gain, blocks):
    scale = lax.rsqrt(head_sum(values * values, blocks) * (1.0 / HEAD_DIM) + EPSILON)
    return values * scale * gain


def head_norm_back(values, gain, grad, blocks):
    scale = lax.rsqrt(head_sum(values * values, blocks) * (1.0 / HEAD_DIM) + EPSILON)
    normed = values * scale
    grad_gain = jnp.sum(grad * normed, axis=0, keepdims=True)
    inner = grad * gain
    mean = head_sum(inner * normed, blocks) * (1.0 / HEAD_DIM)
    return scale * (inner - normed * mean), grad_gain


def row_scale(values):
    return lax.rsqrt(jnp.mean(values * values, axis=1, keepdims=True) + EPSILON)


MESH = pl.DeviceIdType.MESH
PAIR, ALONG_X, ALONG_Y = 1, 2, 4


def partner(mask):
    rank = lax.axis_index("dp")
    index = rank
    for bit in (1, 2, 4):
        if mask & bit:
            index = index + bit - 2 * bit * lax.rem(rank // bit, 2)
    return index


def greet(masks, shifts, n_tensor):
    barrier = pltpu.get_barrier_semaphore()
    rank = lax.axis_index("tensor")
    for mask in masks:
        pl.semaphore_signal(
            barrier, inc=1, device_id={"dp": partner(mask)}, device_id_type=MESH
        )
    for shift in shifts:
        pl.semaphore_signal(
            barrier,
            inc=1,
            device_id={"tensor": lax.rem(rank + shift, n_tensor)},
            device_id_type=MESH,
        )
    pl.semaphore_wait(barrier, len(masks) + len(shifts))


def send(source, target, sems, index, device):
    copy = pltpu.make_async_remote_copy(
        src_ref=source,
        dst_ref=target,
        send_sem=sems.at[(0,) + index],
        recv_sem=sems.at[(1,) + index],
        device_id=device,
        device_id_type=MESH,
    )
    copy.start()
    return copy


def gather_kernel(
    n_tensor, shard_tk, shard_tv, shard_qv, shard_ko, small, w_adaln,
    tk, tv, qv, ko, small_all, cond_act, mods,
    product, sums, own_sems, shard_sems, small_sems, mod_sems, tensor_sems,
):
    rank, tensor_rank = lax.axis_index("dp"), lax.axis_index("tensor")
    masks = range(1, 8)
    shifts = range(1, n_tensor)
    greet(masks, shifts, n_tensor)
    sends = []
    small_copies = []
    for mask in masks:
        small_copies.append(
            send(
                small.at[partner(mask)], small_all.at[rank], small_sems, (mask,),
                {"dp": partner(mask)},
            )
        )
    groups = ((shard_tk, tk), (shard_tv, tv), (shard_qv, qv), (shard_ko, ko))

    def rows_of(shard, index, first, size):
        return pl.ds(pl.multiple_of(index * shard.shape[0] + first, 32), size)

    firsts, seconds, pairs, locals_ = [], [], [], []
    for number, (shard, whole) in enumerate(groups):
        size = shard.shape[0]
        mine = whole.at[rows_of(shard, rank, 0, size)]
        firsts.append(
            [
                send(shard, mine, shard_sems, (number, place), {"dp": partner(mask)})
                for place, mask in ((0, ALONG_X), (1, ALONG_Y))
            ]
        )
        pairs.append([send(shard, mine, shard_sems, (number, 4), {"dp": partner(PAIR)})])
        local = pltpu.make_async_copy(shard, mine, own_sems.at[number])
        local.start()
        locals_.append(local)

    small_all[rank] = small[rank]
    for copy in small_copies:
        copy.wait_recv()
    depth, width = w_adaln.shape
    context = small_all[:, 0:16, :].astype(F32).reshape(8 * 16, depth)
    cond_act[...] = jax.nn.silu(context).astype(BF16)
    product[...] = dot_nn(cond_act[...], w_adaln[...]).astype(BF16).reshape(8, 16, width)
    mod_copies = [
        send(
            product.at[partner(mask)], sums.at[mask], mod_sems, (mask,), {"dp": partner(mask)}
        )
        for mask in masks
    ]
    sums[0] = product[rank]
    for copy in mod_copies:
        copy.wait_recv()
    total = sums[0].astype(F32)
    for mask in masks:
        total = total + sums[mask].astype(F32)
    mods[tensor_rank] = total.astype(BF16)
    tensor_copies = [
        send(
            mods.at[tensor_rank], mods.at[tensor_rank], tensor_sems, (shift,),
            {"tensor": lax.rem(tensor_rank + shift, n_tensor)},
        )
        for shift in shifts
    ]

    for number, (shard, whole) in enumerate(groups):
        size = shard.shape[0]
        half = size // 2
        seconds.append([])
        for place, mask, onward, start in ((0, ALONG_X, ALONG_Y, half), (1, ALONG_Y, ALONG_X, 0)):
            firsts[number][place].wait_recv()
            part = whole.at[rows_of(shard, partner(mask), start, half)]
            seconds[number].append(
                send(part, part, shard_sems, (number, 2 + place), {"dp": partner(onward)})
            )
            piece = whole.at[rows_of(shard, partner(mask), 0, size)]
            pairs[number].append(
                send(piece, piece, shard_sems, (number, 5 + place), {"dp": partner(PAIR)})
            )
    for number, (shard, whole) in enumerate(groups):
        half = shard.shape[0] // 2
        for place, start in ((0, half), (1, 0)):
            seconds[number][place].wait_recv()
            part = whole.at[rows_of(shard, partner(ALONG_X + ALONG_Y), start, half)]
            pairs[number].append(
                send(part, part, shard_sems, (number, 7 + place), {"dp": partner(PAIR)})
            )
    for number in range(4):
        for copy in pairs[number]:
            copy.wait_recv()
    for copy in tensor_copies:
        copy.wait_recv()
    for number in range(4):
        for copy in firsts[number] + seconds[number] + pairs[number]:
            copy.wait_send()
        locals_[number].wait()
    for copy in small_copies + mod_copies + tensor_copies:
        copy.wait_send()


def reduce_kernel(count, *refs):
    evens, odds, refs = refs[:count], refs[count : 2 * count], refs[2 * count :]
    outs, refs = refs[:count], refs[count:]
    from_pair, out_2, in_2, out_3, in_3 = [refs[i * count : (i + 1) * count] for i in range(5)]
    sems = refs[5 * count]
    greet((PAIR, ALONG_X, ALONG_Y), (), 1)
    pairs = [
        send(odds[g], from_pair[g], sems, (g, 0), {"dp": partner(PAIR)}) for g in range(count)
    ]
    routes = ((0, 1, 2, ALONG_X, ALONG_Y), (1, 2, 1, ALONG_Y, ALONG_X))
    seconds, thirds = [], []
    strip = 32
    for g in range(count):
        half = outs[g].shape[0] // 2
        pairs[g].wait_recv()
        seconds.append([])
        for side, close, far, first, last in routes:

            @pl.loop(0, half // strip)
            def _(index):
                low = pl.multiple_of(index * strip, strip)
                here = pl.ds(low, strip)
                there = pl.ds(pl.multiple_of(low + side * half, strip), strip)
                for slot, piece in ((0, close), (1, 3)):
                    out_2[g][side, slot, here, :] = (
                        evens[g][piece, there, :].astype(F32)
                        + from_pair[g][piece, there, :].astype(F32)
                    ).astype(BF16)

            seconds[g].append(
                send(
                    out_2[g].at[side], in_2[g].at[side], sems, (g, 1 + side), {"dp": partner(first)}
                )
            )
    for g in range(count):
        half = outs[g].shape[0] // 2
        thirds.append([])
        for side, close, far, first, last in routes:
            seconds[g][side].wait_recv()

            @pl.loop(0, half // strip)
            def _(index):
                low = pl.multiple_of(index * strip, strip)
                here = pl.ds(low, strip)
                there = pl.ds(pl.multiple_of(low + side * half, strip), strip)
                out_3[g][side, here, :] = (
                    evens[g][far, there, :].astype(F32)
                    + from_pair[g][far, there, :].astype(F32)
                    + in_2[g][side, 1, here, :].astype(F32)
                ).astype(BF16)
                outs[g][there, :] = (
                    evens[g][0, there, :].astype(F32)
                    + from_pair[g][0, there, :].astype(F32)
                    + in_2[g][side, 0, here, :].astype(F32)
                )

            thirds[g].append(
                send(
                    out_3[g].at[side], in_3[g].at[side], sems, (g, 3 + side), {"dp": partner(last)}
                )
            )
    for g in range(count):
        half = outs[g].shape[0] // 2
        for side in (0, 1):
            thirds[g][side].wait_recv()

            @pl.loop(0, half // strip)
            def _(index):
                low = pl.multiple_of(index * strip, strip)
                there = pl.ds(pl.multiple_of(low + side * half, strip), strip)
                outs[g][there, :] += in_3[g][side, pl.ds(low, strip), :].astype(F32)

    for g in range(count):
        for copy in [pairs[g]] + seconds[g] + thirds[g]:
            copy.wait_send()


def tensor_kernel(n_tensor, partial, out, arrived, sems):
    rank = lax.axis_index("tensor")
    size = arrived.shape[1]
    shifts = range(1, n_tensor)
    greet((), shifts, n_tensor)

    def block(index):
        return pl.ds(pl.multiple_of(index * size, 16), size)

    firsts = []
    for shift in shifts:
        other = lax.rem(rank + shift, n_tensor)
        firsts.append(
            send(
                partial.at[block(other)], arrived.at[shift - 1], sems, (0, shift - 1),
                {"tensor": other},
            )
        )
    for copy in firsts:
        copy.wait_recv()

    @pl.loop(0, size // STRIP)
    def _(index):
        low = pl.multiple_of(index * STRIP, STRIP)
        here = pl.ds(low, STRIP)
        there = pl.ds(pl.multiple_of(rank * size + low, STRIP), STRIP)
        total = partial[there, :].astype(F32)
        for shift in shifts:
            total = total + arrived[shift - 1, here, :].astype(F32)
        out[there, :] = total.astype(BF16)

    seconds = []
    for shift in shifts:
        other = lax.rem(rank + shift, n_tensor)
        mine = out.at[block(rank)]
        seconds.append(send(mine, mine, sems, (1, shift - 1), {"tensor": other}))
    for copy in seconds:
        copy.wait_recv()
    for copy in firsts + seconds:
        copy.wait_send()


def finish_kernel(grad_mod, sums, cond_act, grad_adaln, total, all_mod, all_sums, sems):
    rank = lax.axis_index("dp")
    masks = range(1, 8)
    greet(masks, (), 1)
    copies = []
    for mask in masks:
        device = {"dp": partner(mask)}
        copies.append(send(grad_mod, all_mod.at[rank], sems, (0, mask), device))
        copies.append(send(sums, all_sums.at[mask], sems, (1, mask), device))
    all_mod[rank] = grad_mod[...]
    all_sums[0] = sums[...]
    for copy in copies:
        copy.wait_recv()
    added = all_sums[0]
    for mask in masks:
        added = added + all_sums[mask]
    total[...] = added
    grad_adaln[...] = dot_tn(cond_act[...], all_mod[...].reshape(8 * 16, all_mod.shape[2]))
    for copy in copies:
        copy.wait_send()


def exchange(body, outs, ins, scratch, collective, vmem=48):
    spaces = [space for _, space in outs]
    return pl.pallas_call(
        body,
        out_shape=[shape for shape, _ in outs],
        in_specs=[pl.BlockSpec(memory_space=space) for _, space in ins],
        out_specs=[pl.BlockSpec(memory_space=space) for space in spaces],
        scratch_shapes=scratch,
        compiler_params=pltpu.CompilerParams(
            collective_id=collective, has_side_effects=True, vmem_limit_bytes=vmem * 2**20
        ),
    )(*[array for array, _ in ins])


def project_kernel(
    tokens, member, gain, q_gain, k_gain, cosine, sine, mods, whole_a, whole_b,
    attn_in, query_raw, key_raw, query_rot, key_rot, value, mat_a, mat_b, mod, sems
):
    copies = [load(whole_a, mat_a, sems.at[0]), load(whole_b, mat_b, sems.at[1])]
    width = q_gain.shape[1]
    token_columns(member, mods, 0, mod)
    blocks = head_blocks(width)

    def step(at):
        x = tokens[at, :].astype(F32)
        normed = x * row_scale(x)
        attn_in[at, :] = (normed * gain[...] * (1.0 + mod[at, :].astype(F32))).astype(BF16)

    over_strips(tokens.shape[0], step)
    wait_all(copies)
    query_raw[...] = dot_nn(attn_in[...], mat_a[:, :width])
    key_raw[...] = dot_nn(attn_in[...], mat_b[:, :width])
    value[...] = dot_nn(attn_in[...], mat_a[:, width:]).astype(BF16)
    for raw, head_gain, out in ((query_raw, q_gain, query_rot), (key_raw, k_gain, key_rot)):
        normed = head_norm(raw[...], head_gain[...], blocks)
        out[...] = (normed * cosine[...] + swap_pairs(normed) * sine[...]).astype(BF16)


def text_kernel(
    live, source, captions, gain, whole_k, whole_v,
    text_raw, text_key, text_value, mat_k, mat_v, sems
):
    image = pl.program_id(0)

    @pl.when(image == 0)
    def _():
        wait_all([load(whole_k, mat_k, sems.at[0]), load(whole_v, mat_v, sems.at[1])])

    @pl.when(live[image] > 0)
    def _():
        raw = dot_nn(captions[0], mat_k[...])
        text_raw[0] = raw.astype(BF16)
        text_key[0] = head_norm(raw, gain[...], head_blocks(raw.shape[1])).astype(BF16)
        text_value[0] = dot_nn(captions[0], mat_v[...]).astype(BF16)


def softmax(scores, allowed, rows_live):
    scores = jnp.where(allowed, scores, MASKED)
    expo = jnp.where(allowed, jnp.exp(scores - jnp.max(scores, axis=1, keepdims=True)), 0.0)
    total = jnp.sum(expo, axis=1, keepdims=True)
    if rows_live is not None:
        total = jnp.where(rows_live, total, 1.0)
    return expo / total


def attend_kernel(
    micro, scale, live, text_len, query, key, value, text_key, text_value,
    self_id, self_row, segment, gate, whole_b, mixed, cross_out, whole, mat_b, sem
):
    copies = [load(whole_b, mat_b, sem)]
    rows, width = query.shape
    count = rows // micro
    slots = text_key.shape[0] // micro
    heads = width // HEAD_DIM
    cross_out[...] = jnp.zeros_like(cross_out)

    @pl.loop(0, micro * slots)
    def _(image):
        @pl.when(live[image] > 0)
        def _():
            at = pl.ds(pl.multiple_of((image // slots) * count, count), count)
            mine = segment[at, :] == lax.rem(image, slots)
            column = lax.broadcasted_iota(jnp.int32, (count, TXT), 1)
            allowed = mine & (column < text_len[image])
            for head in range(heads):
                lanes = slice(head * HEAD_DIM, (head + 1) * HEAD_DIM)
                scores = dot_nt(query[at, lanes], text_key[image, :, lanes]) * scale
                probs = softmax(scores, allowed, mine).astype(BF16)
                cross_out[at, lanes] += dot_nn(probs, text_value[image, :, lanes])

    for batch in range(micro):
        at = slice(batch * count, (batch + 1) * count)
        allowed = self_id[at, :] == self_row[batch : batch + 1, :]
        for head in range(heads):
            lanes = slice(head * HEAD_DIM, (head + 1) * HEAD_DIM)
            scores = dot_nt(query[at, lanes], key[at, lanes]) * scale
            probs = softmax(scores, allowed, None).astype(BF16)
            out = dot_nn(probs, value[at, lanes])
            mixed[at, lanes] = (out + gate[:, lanes] * cross_out[at, lanes]).astype(BF16)
    wait_all(copies)
    whole[...] = dot_nt(mixed[...], mat_b[:, width:]).astype(BF16)


def feed_kernel(
    tokens, member, gain, cotangent, mods, attn_out, whole_f,
    hidden, ffn_in, inner, grad_gate, grad_up, grad_out, whole,
    mat, mod_1, mod_2, mod_3, sem
):
    copies = [load(whole_f, mat, sem)]
    units = inner.shape[1]
    mat_a, mat_b, mat_c = [mat.at[:, i * units : (i + 1) * units] for i in range(3)]
    token_columns(member, mods, 1, mod_1)
    token_columns(member, mods, 2, mod_2)
    token_columns(member, mods, 3, mod_3)

    def step(at):
        gate_attn = jnp.tanh(mod_1[at, :].astype(F32))
        state = tokens[at, :].astype(F32) + gate_attn * attn_out[at, :].astype(F32)
        hidden[at, :] = state
        normed = state * row_scale(state)
        ffn_in[at, :] = (normed * gain[...] * (1.0 + mod_2[at, :].astype(F32))).astype(BF16)
        gate_ffn = jnp.tanh(mod_3[at, :].astype(F32))
        grad_out[at, :] = (gate_ffn * cotangent[at, :].astype(F32)).astype(BF16)

    rows = tokens.shape[0]
    over_strips(rows, step)
    wait_all(copies)
    chunk = 256
    for first in range(0, units, chunk):
        span = slice(first, first + chunk)
        gate = dot_nn(ffn_in[...], mat_a[:, span])
        up = dot_nn(ffn_in[...], mat_b[:, span])
        grad_inner = dot_nn(grad_out[...], mat_c[:, span])
        turn = jax.nn.sigmoid(gate)
        active = gate * turn
        inner[:, span] = (active * up).astype(BF16)
        grad_up[:, span] = (grad_inner * active).astype(BF16)
        slope = turn * (1.0 + gate * (1.0 - turn))
        grad_gate[:, span] = (grad_inner * up * slope).astype(BF16)
    width = tokens.shape[1]
    for first in range(0, width, 512):
        span = slice(first, first + 512)
        whole[:, span] = (
            dot_nt(grad_gate[...], mat_a[span, :]) + dot_nt(grad_up[...], mat_b[span, :])
        ).astype(BF16)


def feed_grad_kernel(grad_out, inner, ffn_in, grad_gate, grad_up, total):
    units = inner.shape[1]
    step = 256
    for index, (left, right) in enumerate(
        ((ffn_in, grad_gate), (ffn_in, grad_up), (grad_out, inner))
    ):
        for first in range(0, units, step):
            out = slice(index * units + first, index * units + first + step)
            total[:, out] = dot_tn(left[...], right[:, first : first + step]).astype(BF16)


def feed_out_kernel(inner, whole_f, partial, mat, sem):
    units = inner.shape[1]
    copy = load(whole_f.at[:, 2 * units : 3 * units], mat, sem)
    copy.wait()
    for first in range(0, partial.shape[1], 512):
        span = slice(first, first + 512)
        partial[:, span] = dot_nt(inner[...], mat[span, :]).astype(BF16)


def modulate_back(values, gain, shift, grad):
    scale = row_scale(values)
    normed = values * scale
    inner = grad * gain * (1.0 + shift)
    mean = jnp.mean(inner * normed, axis=1, keepdims=True)
    return scale * (inner - normed * mean), grad * normed


def mixed_grad_kernel(
    hidden, member, gain, cotangent, mods, grad_in, whole_b,
    grad_hidden, grad_out, grad_mixed, mat_b, mod_1, mod_2, sem
):
    copies = [load(whole_b, mat_b, sem)]
    token_columns(member, mods, 1, mod_1)
    token_columns(member, mods, 2, mod_2)

    def step(at):
        back, _ = modulate_back(
            hidden[at, :], gain[...], mod_2[at, :].astype(F32), grad_in[at, :].astype(F32)
        )
        total = cotangent[at, :].astype(F32) + back
        grad_hidden[at, :] = total
        grad_out[at, :] = (jnp.tanh(mod_1[at, :].astype(F32)) * total).astype(BF16)

    over_strips(hidden.shape[0], step)
    wait_all(copies)
    width = grad_mixed.shape[1]
    grad_mixed[...] = dot_nn(grad_out[...], mat_b[:, width:])


def attend_back_kernel(
    micro, scale, live, text_len, grad_mixed, cross_out, query, key, value, text_key, text_value,
    text_raw, query_raw, key_raw, q_gain, k_gain, t_gain, cosine, sine, self_id, self_row, segment,
    gate, grad_query_b, grad_key_b, grad_value_b, grad_text_key, grad_text_value,
    gain_sums, grad_query, grad_key, grad_cross, grad_text
):
    rows, width = query.shape
    count = rows // micro
    slots = text_key.shape[0] // micro
    heads = width // HEAD_DIM
    blocks = head_blocks(width)
    gate_sum = jnp.sum(grad_mixed[...] * cross_out[...], axis=0, keepdims=True)
    gain_sums[...] = jnp.zeros_like(gain_sums)
    gain_sums[3:4, :] = gate_sum * (1.0 - gate[...] * gate[...])
    grad_cross[...] = (gate[...] * grad_mixed[...]).astype(BF16)
    for batch in range(micro):
        at = slice(batch * count, (batch + 1) * count)
        allowed = self_id[at, :] == self_row[batch : batch + 1, :]
        for head in range(heads):
            lanes = slice(head * HEAD_DIM, (head + 1) * HEAD_DIM)
            q, k = query[at, lanes], key[at, lanes]
            grad = grad_mixed[at, lanes].astype(BF16)
            probs = softmax(dot_nt(q, k) * scale, allowed, None)
            grad_probs = dot_nt(grad, value[at, lanes])
            mean = jnp.sum(probs * grad_probs, axis=1, keepdims=True)
            scaled = (probs * (grad_probs - mean) * scale).astype(BF16)
            grad_query[at, lanes] = dot_nn(scaled, k)
            grad_key[at, lanes] = dot_tn(scaled, q)
            grad_value_b[at, lanes] = dot_tn(probs.astype(BF16), grad).astype(BF16)

    @pl.loop(0, micro * slots)
    def _(image):
        @pl.when(live[image] == 0)
        def _():
            grad_text_key[image] = jnp.zeros((TXT, width), BF16)
            grad_text_value[image] = jnp.zeros((TXT, width), BF16)

        @pl.when(live[image] > 0)
        def _():
            at = pl.ds(pl.multiple_of((image // slots) * count, count), count)
            mine = segment[at, :] == lax.rem(image, slots)
            column = lax.broadcasted_iota(jnp.int32, (count, TXT), 1)
            allowed = mine & (column < text_len[image])
            for head in range(heads):
                lanes = slice(head * HEAD_DIM, (head + 1) * HEAD_DIM)
                q, k = query[at, lanes], text_key[image, :, lanes]
                grad = grad_cross[at, lanes]
                probs = softmax(dot_nt(q, k) * scale, allowed, mine)
                grad_probs = dot_nt(grad, text_value[image, :, lanes])
                mean = jnp.sum(probs * grad_probs, axis=1, keepdims=True)
                scaled = (probs * (grad_probs - mean) * scale).astype(BF16)
                grad_query[at, lanes] += dot_nn(scaled, k)
                grad_text[:, lanes] = dot_tn(scaled, q)
                grad_text_value[image, :, lanes] = dot_tn(probs.astype(BF16), grad).astype(BF16)
            back, gain_sum = head_norm_back(
                text_raw[image].astype(F32), t_gain[...], grad_text[...], blocks
            )
            grad_text_key[image] = back.astype(BF16)
            gain_sums[2:3, :] += gain_sum

    for index, (grad, raw, gain, out) in enumerate(
        (
            (grad_query, query_raw, q_gain, grad_query_b),
            (grad_key, key_raw, k_gain, grad_key_b),
        )
    ):
        turned = grad[...] * cosine[...] + swap_pairs(grad[...] * sine[...])
        back, gain_sum = head_norm_back(raw[...], gain[...], turned, blocks)
        out[...] = back.astype(BF16)
        gain_sums[index : index + 1, :] = gain_sum


def attn_grad_kernel(
    parts, attn_in, grad_query, grad_key, grad_value, grad_out, mixed, whole_a, whole_b, *rest
):
    even, odd, rest = rest[:2], rest[2:4], rest[4:]
    whole, mat_a, mat_b, pair, total, sems = rest
    copies = [load(whole_a, mat_a, sems.at[0]), load(whole_b, mat_b, sems.at[1])]
    width = grad_query.shape[1]
    pair[:, :width] = grad_query[...]
    pair[:, width:] = grad_value[...]
    wait_all(copies)
    for first in range(0, whole.shape[1], 512):
        span = slice(first, first + 512)
        whole[:, span] = (
            dot_nt(pair[...], mat_a[span, :]) + dot_nt(grad_key[...], mat_b[span, :width])
        ).astype(BF16)
    write_pieces(attn_in, pair, even[0], odd[0], total)
    rank = lax.axis_index("dp")
    total[:, :width] = dot_tn(attn_in[...], grad_key[...]).astype(BF16)
    total[:, width:] = dot_tn(grad_out[...], mixed[...]).astype(BF16)
    size = even[1].shape[1]
    if parts == 1:
        even[1][0] = total[...]
        return
    for index in range(4):
        for out, low in ((even[1], 0), (odd[1], 1)):
            owner = jnp.bitwise_xor(rank, 2 * index + low)
            out[index] = total[pl.ds(pl.multiple_of(owner * size, 64), size), :]


def text_grad_kernel(live, source, rank, captions, grad_key, grad_value, out_key, out_value, acc):
    image = pl.program_id(1)
    width = grad_key.shape[2]

    @pl.when(image == 0)
    def _():
        acc[...] = jnp.zeros_like(acc)

    @pl.when(live[image] > 0)
    def _():
        acc[:, :width] += dot_tn(captions[0], grad_key[image])
        acc[:, width:] += dot_tn(captions[0], grad_value[image])

    @pl.when(image == pl.num_programs(1) - 1)
    def _():
        out_key[0] = acc[:, :width].astype(BF16)
        out_value[0] = acc[:, width:].astype(BF16)


def segment_sum(member, values):
    high = values.astype(BF16)
    rest = values - high.astype(F32)
    middle = rest.astype(BF16)
    low = (rest - middle.astype(F32)).astype(BF16)
    return dot_tn(member, high) + dot_tn(member, middle) + dot_tn(member, low)


def output_kernel(
    hidden, member, gain, cotangent, mods, ffn_out, grad_in,
    result, grad_mod, grad_gain, mod_2, mod_3, grad
):
    token_columns(member, mods, 2, mod_2)
    token_columns(member, mods, 3, mod_3)
    rank = lax.axis_index("tensor")
    grad_gain[...] = jnp.zeros_like(grad_gain)

    def step(at):
        state = hidden[at, :]
        gate = jnp.tanh(mod_3[at, :].astype(F32))
        out = ffn_out[at, :].astype(F32)
        result[at, :] = (state + gate * out).astype(BF16)
        up = grad_in[at, :].astype(F32)
        product = up * state * row_scale(state)
        grad_gain[...] += jnp.sum(
            product * (1.0 + mod_2[at, :].astype(F32)), axis=0, keepdims=True
        )
        grad_gate = cotangent[at, :].astype(F32) * out * (1.0 - gate * gate)
        grad[at, :] = jnp.where(rank == 2, product * gain[...], grad_gate)

    over_strips(hidden.shape[0], step)
    grad_mod[...] = segment_sum(member[...], grad[...])


def input_kernel(
    tokens, member, gain, grad_hidden, other_mod, mods, grad_in, attn_out,
    grad_tokens, grad_mod, grad_gain, mod_0, mod_1, grad
):
    token_columns(member, mods, 0, mod_0)
    token_columns(member, mods, 1, mod_1)
    rank = lax.axis_index("tensor")
    grad_gain[...] = jnp.zeros_like(grad_gain)

    def step(at):
        shift = mod_0[at, :].astype(F32)
        upper = grad_hidden[at, :]
        back, product = modulate_back(
            tokens[at, :].astype(F32), gain[...], shift, grad_in[at, :].astype(F32)
        )
        grad_tokens[at, :] = (upper + back).astype(BF16)
        grad_gain[...] += jnp.sum(product * (1.0 + shift), axis=0, keepdims=True)
        gate = jnp.tanh(mod_1[at, :].astype(F32))
        grad_gate = upper * attn_out[at, :].astype(F32) * (1.0 - gate * gate)
        grad[at, :] = jnp.where(rank == 0, product * gain[...], grad_gate)

    over_strips(tokens.shape[0], step)
    own = segment_sum(member[...], grad[...])
    grad_mod[...] = jnp.where(rank < 2, own, other_mod[...]).astype(BF16)


def shards(
    n_dp,
    n_tensor,
    tokens,
    context,
    captions,
    shapes,
    text_len,
    w_query,
    w_key,
    w_value,
    w_out,
    w_text_key,
    w_text_value,
    w_gate,
    w_up,
    w_down,
    w_adaln,
    gain_attn,
    gain_ffn,
    gain_query,
    gain_key,
    gain_text,
    cross_gate,
    cotangent,
):
    parts = 8 if n_dp == 8 else 1
    micro, count, width = tokens.shape
    slots = shapes.shape[1]
    rows = micro * count
    images = micro * slots
    heads = w_query.shape[1] // HEAD_DIM
    local = heads * HEAD_DIM
    units = w_gate.shape[1]
    scale = HEAD_DIM ** (-0.5)
    dp_rank = lax.axis_index("dp")
    padded = 16
    vmem, smem, anywhere = pltpu.VMEM, pltpu.SMEM, pl.ANY
    dma = pltpu.SemaphoreType.DMA

    def inside(*arrays):
        return [(array, vmem) for array in arrays]

    def scalars(*arrays):
        return [(array, smem) for array in arrays]

    def outside(*arrays):
        return [(array, anywhere) for array in arrays]

    def after(values, earlier):
        return lax.optimization_barrier((list(values), list(earlier)))[0]

    def gathered(shard):
        return lax.all_gather(shard, "dp", axis=0, tiled=True)

    def scattered(whole):
        return lax.psum_scatter(whole, "dp", scatter_dimension=0, tiled=True).astype(F32)

    part_rows = rows // n_tensor

    def tensor_sum(partial):
        (out,) = exchange(
            functools.partial(tensor_kernel, n_tensor),
            [(struct((rows, width)), vmem)],
            inside(partial),
            [vmem((n_tensor - 1, part_rows, width), BF16), dma((2, 2, n_tensor - 1))],
            1,
        )
        return out

    gain_list = (gain_attn, gain_ffn, gain_query, gain_key, gain_text)
    gain_rows = jnp.concatenate([gain.reshape(-1) for gain in gain_list])
    cond_rows, span = w_adaln.shape
    shard_qv = jnp.concatenate([w_query, w_value], axis=1)
    shard_ko = jnp.concatenate([w_key, w_out], axis=1)
    shard_f = jnp.concatenate([w_gate, w_up, w_down], axis=1)
    if parts == 1:
        whole_tk, whole_tv = gathered(w_text_key), gathered(w_text_value)
        whole_qv, whole_ko = gathered(shard_qv), gathered(shard_ko)
        gain_rows = lax.all_gather(gain_rows, "dp", axis=0)
        context_all = gathered(context.reshape(images, -1))
        cond_cols = lax.dynamic_slice_in_dim(context_all, dp_rank * cond_rows, cond_rows, 1)
        cond_act = jax.nn.silu(cond_cols.astype(F32)).astype(BF16)
        mod_part = scattered(dot_nn(cond_act, w_adaln)).astype(BF16)
        mods = lax.all_gather(mod_part, "tensor", axis=0)
        mods = jnp.pad(mods, ((0, 0), (0, padded - images), (0, 0)))
    else:
        gain_size = gain_rows.size
        small = jnp.pad(
            context.reshape(images, parts, -1).transpose(1, 0, 2),
            ((0, 0), (0, padded - images), (0, 0)),
        )
        packed = jnp.pad(gain_rows, (0, padded * cond_rows - gain_size))
        packed = jnp.broadcast_to(packed.reshape(1, padded, cond_rows), small.shape)
        small = jnp.concatenate([small, packed], axis=1)
        whole_tk, whole_tv, whole_qv, whole_ko, small_all, cond_act, mods = exchange(
            functools.partial(gather_kernel, n_tensor),
            [(struct((DT, local)), anywhere)] * 2
            + [(struct((width, 2 * local)), anywhere)] * 2
            + [
                (struct(small.shape), vmem),
                (struct((parts * padded, cond_rows)), vmem),
                (struct((n_tensor, padded, span)), vmem),
            ],
            outside(w_text_key, w_text_value, shard_qv, shard_ko) + inside(small, w_adaln),
            [
                vmem((parts, padded, span), BF16),
                vmem((parts, padded, span), BF16),
                dma((4,)),
                dma((2, 4, 9)),
                dma((2, 8)),
                dma((2, 8)),
                dma((2, n_tensor)),
            ],
            2,
        )
        gain_rows = small_all[:, padded:].reshape(parts, -1)[:, :gain_size]
        (shard_f,) = after([shard_f], [mods])
    whole_f = gathered(shard_f)
    sizes = [gain.size for gain in gain_list]
    edges = [sum(sizes[:i]) for i in range(len(sizes) + 1)]
    gains = [gain_rows[:, edges[i] : edges[i + 1]] for i in range(5)]
    attn_gain, ffn_gain = [gain.reshape(1, width).astype(F32) for gain in gains[:2]]
    query_gain, key_gain, text_gain = [
        gain.reshape(HEAD_DIM, heads).T.reshape(1, local).astype(F32) for gain in gains[2:]
    ]

    layouts = [image_layout(shapes[i], count) for i in range(micro)]
    member, segment, inside_any, row_pos, col_pos = [
        jnp.stack([layout[j] for layout in layouts]) for j in range(5)
    ]
    cosine, sine = rope_tables(row_pos.reshape(rows), col_pos.reshape(rows))
    cosine = jnp.tile(jnp.stack([cosine, cosine], axis=2).reshape(rows, HEAD_DIM), (1, heads))
    sine = jnp.tile(jnp.stack([-sine, sine], axis=2).reshape(rows, HEAD_DIM), (1, heads))
    which = jnp.arange(micro, dtype=jnp.int32)
    member = jnp.where(
        (which[:, None] == which[None, :])[:, None, :, None], member[:, :, None, :], 0.0
    )
    member = jnp.pad(member.reshape(rows, images), ((0, 0), (0, padded - images))).astype(BF16)
    self_row = jnp.where(inside_any > 0, segment, slots)
    self_id = self_row.reshape(rows, 1)
    segment = segment.reshape(rows, 1)
    lens = text_len.reshape(images)
    used = shapes[:, :, 0] * (shapes[:, :, 1] + 1) > 0
    used = used | (jnp.arange(slots)[None, :] == 0)
    live = used.reshape(images).astype(jnp.int32)
    at = jnp.arange(images, dtype=jnp.int32)
    source = lax.cummax(jnp.where(live > 0, at, 0))
    gate = jnp.repeat(jnp.tanh(cross_gate.astype(F32)), HEAD_DIM)[None, :]
    token_rows = tokens.reshape(rows, width)
    grad_y = cotangent.reshape(rows, width)
    caption_images = captions.reshape(images, TXT, DT)

    attn_in, query_raw, key_raw, query_rot, key_rot, value = run(
        project_kernel,
        [struct((rows, width))]
        + [struct((rows, local), F32)] * 2
        + [struct((rows, local))] * 3,
        inside(token_rows, member, attn_gain, query_gain, key_gain, cosine, sine, mods)
        + outside(whole_qv, whole_ko),
        [
            vmem((width, 2 * local), BF16),
            vmem((width, 2 * local), BF16),
            vmem((rows, width), BF16),
            dma((2,)),
        ],
        flops=6 * rows * width * local,
        traffic=10 * 2**20,
    )

    text_raw, text_key, text_value = pl.pallas_call(
        text_kernel,
        out_shape=[struct((images, TXT, local))] * 3,
        grid_spec=pltpu.PrefetchScalarGridSpec(
            num_scalar_prefetch=2,
            grid=(images,),
            in_specs=[
                pl.BlockSpec((1, TXT, DT), lambda i, live, source: (source[i], 0, 0)),
                pl.BlockSpec((1, local), lambda i, live, source: (0, 0)),
            ]
            + [pl.BlockSpec(memory_space=anywhere)] * 2,
            out_specs=[pl.BlockSpec((1, TXT, local), lambda i, live, source: (i, 0, 0))] * 3,
            scratch_shapes=[vmem((DT, local), BF16), vmem((DT, local), BF16), dma((2,))],
        ),
        compiler_params=pltpu.CompilerParams(vmem_limit_bytes=40 * 2**20),
        cost_estimate=pl.CostEstimate(
            flops=2 * images * TXT * DT * local, bytes_accessed=20 * 2**20, transcendentals=0
        ),
    )(live, source, caption_images, text_gain, whole_tk, whole_tv)

    wide = vmem((rows, width), BF16)
    mixed, cross_out, attn_part = run(
        functools.partial(attend_kernel, micro, scale),
        [struct((rows, local)), struct((rows, local), F32), struct((rows, width))],
        scalars(live, lens)
        + inside(query_rot, key_rot, value, text_key, text_value, self_id, self_row, segment, gate)
        + outside(whole_ko),
        [vmem((width, 2 * local), BF16), dma],
        flops=2 * 2**30,
        traffic=12 * 2**20,
    )
    attn_out = tensor_sum(attn_part)

    mat = vmem((width, 3 * units), BF16)
    hidden, ffn_in, inner, grad_gate, grad_up, grad_ffn_out, ffn_part = run(
        feed_kernel,
        [struct((rows, width), F32), struct((rows, width))]
        + [struct((rows, units))] * 3
        + [struct((rows, width))] * 2,
        inside(token_rows, member, ffn_gain, grad_y, mods, attn_out) + outside(whole_f),
        [mat, wide, wide, wide, dma],
        flops=10 * rows * width * units,
        traffic=20 * 2**20,
    )
    (grad_f,) = run(
        feed_grad_kernel,
        [struct((width, 3 * units))],
        inside(grad_ffn_out, inner, ffn_in, grad_gate, grad_up),
        flops=6 * rows * width * units,
        traffic=12 * 2**20,
    )
    (ffn_part,) = after([ffn_part], [grad_f])
    grad_ffn_in = tensor_sum(ffn_part)
    grad_f = scattered(grad_f)
    (ffn_out_part,) = run(
        feed_out_kernel,
        [struct((rows, width))],
        inside(inner) + outside(whole_f),
        [vmem((width, units), BF16), dma],
        flops=2 * rows * width * units,
        traffic=5 * 2**20,
    )
    ffn_out = lax.psum(ffn_out_part, "tensor")

    grad_hidden, grad_attn_out, grad_mixed = run(
        mixed_grad_kernel,
        [struct((rows, width), F32), struct((rows, width)), struct((rows, local), F32)],
        inside(hidden, member, ffn_gain, grad_y, mods, grad_ffn_in) + outside(whole_ko),
        [vmem((width, 2 * local), BF16), wide, wide, dma],
        flops=2 * rows * width * local,
        traffic=8 * 2**20,
    )

    tile = struct((rows, local))
    texts = struct((images, TXT, local))
    grad_query_b, grad_key_b, grad_value_b, grad_text_key, grad_text_value, gain_sums = run(
        functools.partial(attend_back_kernel, micro, scale),
        [tile, tile, tile, texts, texts, struct((8, local), F32)],
        scalars(live, lens)
        + inside(
            grad_mixed, cross_out, query_rot, key_rot, value, text_key, text_value, text_raw,
            query_raw, key_raw, query_gain, key_gain, text_gain, cosine, sine, self_id, self_row,
            segment, gate,
        ),
        [
            vmem((rows, local), F32),
            vmem((rows, local), F32),
            vmem((rows, local), BF16),
            vmem((TXT, local), F32),
        ],
        flops=4 * 2**30,
        traffic=15 * 2**20,
    )

    size = width // parts

    def even_of(depth, columns):
        return struct((max(parts // 2, 1), depth, columns))

    qv_even, ko_even, qv_odd, ko_odd, attn_in_part = run(
        functools.partial(attn_grad_kernel, parts),
        [even_of(size, 2 * local)] * 4 + [struct((rows, width))],
        inside(attn_in, grad_query_b, grad_key_b, grad_value_b, grad_attn_out, mixed)
        + outside(whole_qv, whole_ko),
        [
            vmem((width, 2 * local), BF16),
            vmem((width, 2 * local), BF16),
            vmem((rows, 2 * local), BF16),
            vmem((width, 2 * local), BF16),
            dma((2,)),
        ],
        flops=14 * rows * width * local,
        traffic=15 * 2**20,
    )
    (attn_in_part,) = after([attn_in_part], [ffn_out])
    grad_attn_in = lax.psum(attn_in_part, "tensor")

    depth = DT // parts

    def text_grads(low):
        chosen = max(parts // 2, 1)

        def caption_place(j, i, live, source, rank):
            block = jnp.bitwise_xor(rank[0], 2 * j + low) if parts > 1 else 0
            return (source[i], 0, block)

        return pl.pallas_call(
            text_grad_kernel,
            out_shape=[even_of(depth, local)] * 2,
            grid_spec=pltpu.PrefetchScalarGridSpec(
                num_scalar_prefetch=3,
                grid=(chosen, images),
                in_specs=[
                    pl.BlockSpec((1, TXT, depth), caption_place),
                    pl.BlockSpec((images, TXT, local), lambda j, i, *_: (0, 0, 0)),
                    pl.BlockSpec((images, TXT, local), lambda j, i, *_: (0, 0, 0)),
                ],
                out_specs=[pl.BlockSpec((1, depth, local), lambda j, i, *_: (j, 0, 0))] * 2,
                scratch_shapes=[vmem((depth, 2 * local), F32)],
            ),
            compiler_params=pltpu.CompilerParams(vmem_limit_bytes=56 * 2**20),
            cost_estimate=pl.CostEstimate(
                flops=images * TXT * DT * local, bytes_accessed=10 * 2**20, transcendentals=0
            ),
        )(live, source, dp_rank[None].astype(jnp.int32), caption_images, grad_text_key, grad_text_value)

    key_even, value_even = text_grads(0)
    if parts == 1:
        pieces = (key_even, value_even, qv_even, ko_even)
        grad_tk, grad_tv, grad_qv, grad_ko = [scattered(piece[0].astype(F32)) for piece in pieces]
    else:
        key_odd, value_odd = text_grads(1)
        evens = (qv_even, ko_even, key_even, value_even)
        shapes_of = [piece.shape[1:] for piece in evens]
        grad_qv, grad_ko, grad_tk, grad_tv = exchange(
            functools.partial(reduce_kernel, 4),
            [(struct(shape, F32), vmem) for shape in shapes_of],
            inside(*evens, qv_odd, ko_odd, key_odd, value_odd),
            [vmem((4,) + shape, BF16) for shape in shapes_of]
            + [vmem((2, 2, shape[0] // 2, shape[1]), BF16) for shape in shapes_of] * 2
            + [vmem((2, shape[0] // 2, shape[1]), BF16) for shape in shapes_of] * 2
            + [dma((2, 4, 5))],
            3,
        )

    result, ffn_mod, ffn_gain_sum = run(
        output_kernel,
        [struct((rows, width)), struct((padded, width), F32), struct((1, width), F32)],
        inside(hidden, member, ffn_gain, grad_y, mods, ffn_out, grad_ffn_in),
        [wide, wide, vmem((rows, width), F32)],
        traffic=8 * 2**20,
    )
    grad_tokens, grad_mod, attn_gain_sum = run(
        input_kernel,
        [struct((rows, width)), struct((padded, width)), struct((1, width), F32)],
        inside(token_rows, member, attn_gain, grad_hidden, ffn_mod, mods, grad_attn_in, attn_out),
        [wide, wide, vmem((rows, width), F32)],
        traffic=8 * 2**20,
    )
    head_sums = gain_sums[:3].reshape(3, heads, HEAD_DIM).transpose(0, 2, 1)
    gate_sums = jnp.sum(gain_sums[3].reshape(heads, HEAD_DIM), axis=1)
    sums = jnp.concatenate(
        [attn_gain_sum[0], ffn_gain_sum[0], head_sums.reshape(-1), gate_sums]
    )
    if parts == 1:
        sums = lax.psum(sums, "dp")
        grad_w_adaln = dot_tn(cond_act, gathered(grad_mod[:images]))
    else:
        flat_size = sums.size
        tall = -(-flat_size // 1024) * 8
        sums = jnp.pad(sums, (0, tall * 128 - flat_size)).reshape(tall, 128)
        grad_w_adaln, sums = exchange(
            finish_kernel,
            [(struct((cond_rows, span), F32), vmem), (struct((tall, 128), F32), vmem)],
            inside(grad_mod, sums, cond_act),
            [vmem((parts, padded, span), BF16), vmem((parts, tall, 128), F32), dma((2, 2, 8))],
            4,
        )
        sums = sums.reshape(-1)[:flat_size]

    def own(first, shape):
        whole = sums[first : first + shape[0] * (shape[1] if len(shape) > 1 else 1)].reshape(shape)
        part = shape[0] // n_dp
        return lax.dynamic_slice_in_dim(whole, dp_rank * part, part, 0)

    head_shape = (HEAD_DIM, heads)
    edge = 2 * width
    return (
        result.reshape(micro, count, width),
        grad_tokens.reshape(micro, count, width),
        grad_qv[:, :local],
        grad_ko[:, :local],
        grad_qv[:, local:],
        grad_ko[:, local:],
        grad_tk,
        grad_tv,
        grad_f[:, :units],
        grad_f[:, units : 2 * units],
        grad_f[:, 2 * units :],
        grad_w_adaln,
        own(0, (width,)),
        own(width, (width,)),
        own(edge, head_shape),
        own(edge + local, head_shape),
        own(edge + 2 * local, head_shape),
        sums[edge + 3 * local :],
    )


def solution(mesh):
    return jax.shard_map(
        functools.partial(shards, mesh.shape["dp"], mesh.shape["tensor"]),
        mesh=mesh,
        in_specs=(
            P(None, "dp", None),
            P(None, "dp", None),
            P(None, "dp", None, None),
            P(None, "dp", None),
            P(None, "dp"),
            P("dp", "tensor"),
            P("dp", "tensor"),
            P("dp", "tensor"),
            P("dp", "tensor"),
            P("dp", "tensor"),
            P("dp", "tensor"),
            P("dp", "tensor"),
            P("dp", "tensor"),
            P("dp", "tensor"),
            P("dp", "tensor"),
            P("dp"),
            P("dp"),
            P("dp", "tensor"),
            P("dp", "tensor"),
            P("dp", "tensor"),
            P("tensor"),
            P(None, "dp", None),
        ),
        out_specs=(
            P(None, "dp", None),
            P(None, "dp", None),
            P("dp", "tensor"),
            P("dp", "tensor"),
            P("dp", "tensor"),
            P("dp", "tensor"),
            P("dp", "tensor"),
            P("dp", "tensor"),
            P("dp", "tensor"),
            P("dp", "tensor"),
            P("dp", "tensor"),
            P("dp", "tensor"),
            P("dp"),
            P("dp"),
            P("dp", "tensor"),
            P("dp", "tensor"),
            P("dp", "tensor"),
            P("tensor"),
        ),
        check_vma=False,
    )
```

```python
import functools

import jax
import jax.numpy as jnp
from jax import lax
from jax.experimental import pallas as pl
from jax.experimental.pallas import tpu as pltpu
from jax.sharding import PartitionSpec as P

HEAD_DIM = 64
DT = 4096
TXT = 256


EPSILON = 1e-06
MASKED = -1e30
ROPE_BASE = 10000.0
STRIP = 16
F32 = jnp.float32
BF16 = jnp.bfloat16


def image_layout(shapes, count):
    height = shapes[:, 0]
    stride_all = shapes[:, 1] + 1
    extent = height * stride_all
    finish = jnp.cumsum(extent)
    begin = finish - extent
    places = jnp.arange(count, dtype=jnp.int32)
    member = (places[:, None] >= begin[None, :]) & (places[:, None] < finish[None, :])
    member_int = member.astype(jnp.int32)
    inside = jnp.sum(member_int, axis=1)
    slot_ids = jnp.arange(shapes.shape[0], dtype=jnp.int32)
    segment = jnp.sum(member_int * slot_ids[None, :], axis=1)
    stride = jnp.sum(member_int * stride_all[None, :], axis=1) + 1 - inside
    offset = places - jnp.sum(member_int * begin[None, :], axis=1)
    return (member.astype(jnp.float32), segment, inside, offset // stride, offset % stride)


def rope_tables(row_pos, col_pos):
    quarter = HEAD_DIM // 4
    freq = ROPE_BASE ** (-jnp.arange(quarter, dtype=jnp.float32) / quarter)
    angles = jnp.stack(
        [
            row_pos.astype(jnp.float32)[:, None] * freq[None, :],
            col_pos.astype(jnp.float32)[:, None] * freq[None, :],
        ],
        axis=1,
    )
    return (jnp.cos(angles), jnp.sin(angles))


def dot_nn(left, right):
    return lax.dot_general(left, right, (((1,), (0,)), ((), ())), preferred_element_type=F32)


def dot_nt(left, right):
    return lax.dot_general(left, right, (((1,), (1,)), ((), ())), preferred_element_type=F32)


def dot_tn(left, right):
    return lax.dot_general(left, right, (((0,), (0,)), ((), ())), preferred_element_type=F32)


def struct(shape, dtype=BF16):
    return jax.ShapeDtypeStruct(shape, dtype)


def run(body, outs, ins, scratch=(), flops=0, traffic=0):
    return pl.pallas_call(
        body,
        out_shape=outs,
        in_specs=[pl.BlockSpec(memory_space=space) for _, space in ins],
        out_specs=[pl.BlockSpec(memory_space=pltpu.VMEM)] * len(outs),
        scratch_shapes=list(scratch),
        compiler_params=pltpu.CompilerParams(vmem_limit_bytes=48 * 2**20),
        cost_estimate=pl.CostEstimate(flops=flops, bytes_accessed=traffic, transcendentals=0),
    )(*[array for array, _ in ins])


def load(source, target, sem):
    copy = pltpu.make_async_copy(source, target, sem)
    copy.start()
    return copy


def wait_all(copies):
    for copy in copies:
        copy.wait()


def token_columns(member, mods, which, target):
    target[...] = dot_nn(member[...], mods[which]).astype(BF16)


def over_strips(rows, step):
    @pl.loop(0, rows // STRIP)
    def _(index):
        step(pl.ds(pl.multiple_of(index * STRIP, STRIP), STRIP))


def head_sum(values, blocks):
    high = values.astype(BF16)
    low = (values - high.astype(F32)).astype(BF16)
    return dot_nn(high, blocks) + dot_nn(low, blocks)


def head_blocks(width):
    row = lax.broadcasted_iota(jnp.int32, (width, width), 0) // HEAD_DIM
    column = lax.broadcasted_iota(jnp.int32, (width, width), 1) // HEAD_DIM
    return jnp.where(row == column, 1.0, 0.0).astype(BF16)


def swap_pairs(values):
    width = values.shape[1]
    quarter = HEAD_DIM // 4
    lane = lax.broadcasted_iota(jnp.int32, values.shape, 1)
    former = lax.rem(lane, 2 * quarter) < quarter
    return jnp.where(
        former, pltpu.roll(values, width - quarter, 1), pltpu.roll(values, quarter, 1)
    )


def head_norm(values, gain, blocks):
    scale = lax.rsqrt(head_sum(values * values, blocks) * (1.0 / HEAD_DIM) + EPSILON)
    return values * scale * gain


def head_norm_back(values, gain, grad, blocks):
    scale = lax.rsqrt(head_sum(values * values, blocks) * (1.0 / HEAD_DIM) + EPSILON)
    normed = values * scale
    grad_gain = jnp.sum(grad * normed, axis=0, keepdims=True)
    inner = grad * gain
    mean = head_sum(inner * normed, blocks) * (1.0 / HEAD_DIM)
    return scale * (inner - normed * mean), grad_gain


def row_scale(values):
    return lax.rsqrt(jnp.mean(values * values, axis=1, keepdims=True) + EPSILON)


MESH = pl.DeviceIdType.MESH
PAIR, ALONG_X, ALONG_Y = 1, 2, 4


def partner(mask):
    rank = lax.axis_index("dp")
    index = rank
    for bit in (1, 2, 4):
        flip = lax.rem(mask // bit, 2)
        index = index + flip * (bit - 2 * bit * lax.rem(rank // bit, 2))
    return index


def greet(masks, shifts, n_tensor):
    barrier = pltpu.get_barrier_semaphore()
    rank = lax.axis_index("tensor")
    for mask in masks:
        pl.semaphore_signal(
            barrier, inc=1, device_id={"dp": partner(mask)}, device_id_type=MESH
        )
    for shift in shifts:
        pl.semaphore_signal(
            barrier,
            inc=1,
            device_id={"tensor": lax.rem(rank + shift, n_tensor)},
            device_id_type=MESH,
        )
    pl.semaphore_wait(barrier, len(masks) + len(shifts))


def send(source, target, sems, index, device):
    copy = pltpu.make_async_remote_copy(
        src_ref=source,
        dst_ref=target,
        send_sem=sems.at[(0,) + index],
        recv_sem=sems.at[(1,) + index],
        device_id=device,
        device_id_type=MESH,
    )
    copy.start()
    return copy


def gather_kernel(
    n_tensor, shard_tk, shard_tv, shard_qv, shard_ko, small, w_adaln,
    tk, tv, qv, ko, small_all, cond_act, mods,
    product, sums, own_sems, shard_sems, small_sems, mod_sems, tensor_sems,
):
    rank, tensor_rank = lax.axis_index("dp"), lax.axis_index("tensor")
    masks = range(1, 8)
    shifts = range(1, n_tensor)
    greet(masks, shifts, n_tensor)
    sends = []
    small_copies = []
    for mask in masks:
        small_copies.append(
            send(
                small.at[partner(mask)], small_all.at[rank], small_sems, (mask,),
                {"dp": partner(mask)},
            )
        )
    groups = ((shard_tk, tk), (shard_tv, tv), (shard_qv, qv), (shard_ko, ko))

    def rows_of(shard, index, first, size):
        return pl.ds(pl.multiple_of(index * shard.shape[0] + first, 32), size)

    firsts, seconds, pairs, locals_ = [], [], [], []
    for number, (shard, whole) in enumerate(groups):
        size = shard.shape[0]
        mine = whole.at[rows_of(shard, rank, 0, size)]
        firsts.append(
            [
                send(shard, mine, shard_sems, (number, place), {"dp": partner(mask)})
                for place, mask in ((0, ALONG_X), (1, ALONG_Y))
            ]
        )
        pairs.append([send(shard, mine, shard_sems, (number, 4), {"dp": partner(PAIR)})])
        local = pltpu.make_async_copy(shard, mine, own_sems.at[number])
        local.start()
        locals_.append(local)

    small_all[rank] = small[rank]
    for copy in small_copies:
        copy.wait_recv()
    depth, width = w_adaln.shape
    context = small_all[:, 0:16, :].astype(F32).reshape(8 * 16, depth)
    cond_act[...] = jax.nn.silu(context).astype(BF16)
    product[...] = dot_nn(cond_act[...], w_adaln[...]).astype(BF16).reshape(8, 16, width)
    mod_copies = [
        send(
            product.at[partner(mask)], sums.at[mask], mod_sems, (mask,), {"dp": partner(mask)}
        )
        for mask in masks
    ]
    for number, (shard, whole) in enumerate(groups):
        size = shard.shape[0]
        half = size // 2
        seconds.append([])
        for place, mask, onward, start in ((0, ALONG_X, ALONG_Y, half), (1, ALONG_Y, ALONG_X, 0)):
            firsts[number][place].wait_recv()
            part = whole.at[rows_of(shard, partner(mask), start, half)]
            seconds[number].append(
                send(part, part, shard_sems, (number, 2 + place), {"dp": partner(onward)})
            )
            piece = whole.at[rows_of(shard, partner(mask), 0, size)]
            pairs[number].append(
                send(piece, piece, shard_sems, (number, 5 + place), {"dp": partner(PAIR)})
            )
    sums[0] = product[rank]
    for copy in mod_copies:
        copy.wait_recv()
    total = sums[0].astype(F32)
    for mask in masks:
        total = total + sums[mask].astype(F32)
    mods[tensor_rank] = total.astype(BF16)
    tensor_copies = [
        send(
            mods.at[tensor_rank], mods.at[tensor_rank], tensor_sems, (shift,),
            {"tensor": lax.rem(tensor_rank + shift, n_tensor)},
        )
        for shift in shifts
    ]

    for number, (shard, whole) in enumerate(groups):
        half = shard.shape[0] // 2
        for place, start in ((0, half), (1, 0)):
            seconds[number][place].wait_recv()
            part = whole.at[rows_of(shard, partner(ALONG_X + ALONG_Y), start, half)]
            pairs[number].append(
                send(part, part, shard_sems, (number, 7 + place), {"dp": partner(PAIR)})
            )
    for number in range(4):
        for copy in pairs[number]:
            copy.wait_recv()
    for copy in tensor_copies:
        copy.wait_recv()
    for number in range(4):
        for copy in firsts[number] + seconds[number] + pairs[number]:
            copy.wait_send()
        locals_[number].wait()
    for copy in small_copies + mod_copies + tensor_copies:
        copy.wait_send()


ROUTES = ((0, 1, 2, ALONG_X, ALONG_Y), (1, 2, 1, ALONG_Y, ALONG_X))
REDUCE_STRIP = 32


def over_half(half, step):
    @pl.loop(0, half // REDUCE_STRIP)
    def _(index):
        step(pl.multiple_of(index * REDUCE_STRIP, REDUCE_STRIP))


class Reduce:
    def __init__(self, number, read, out, from_pair, out_2, in_2, out_3, in_3, sems):
        self.number, self.read, self.out, self.sems = number, read, out, sems
        self.from_pair, self.out_2, self.in_2, self.out_3, self.in_3 = (
            from_pair, out_2, in_2, out_3, in_3
        )
        self.half = out.shape[0] // 2
        self.copies = []

    def pair_term(self, piece, low):
        there = pl.ds(low, REDUCE_STRIP)
        return self.read(piece, low) + self.from_pair[piece, there, :].astype(F32)

    def first(self, piece, source):
        return send(
            source, self.from_pair.at[piece], self.sems, (self.number, piece),
            {"dp": partner(PAIR)},
        )

    def second(self, firsts):
        for copy in firsts:
            copy.wait_recv()
        self.copies = list(firsts)
        self.arriving = []
        for side, close, far, first, last in ROUTES:

            def step(low):
                for slot, piece in ((0, close), (1, 3)):
                    self.out_2[side, slot, pl.ds(low, REDUCE_STRIP), :] = self.pair_term(
                        piece, pl.multiple_of(low + side * self.half, REDUCE_STRIP)
                    ).astype(BF16)

            over_half(self.half, step)
            self.arriving.append(
                send(
                    self.out_2.at[side], self.in_2.at[side], self.sems, (self.number, 4 + side),
                    {"dp": partner(first)},
                )
            )
        self.copies += self.arriving

    def third(self):
        last_arriving = []
        for side, close, far, first, last in ROUTES:
            self.arriving[side].wait_recv()

            def step(low):
                here = pl.ds(low, REDUCE_STRIP)
                there = pl.multiple_of(low + side * self.half, REDUCE_STRIP)
                self.out_3[side, here, :] = (
                    self.pair_term(far, there) + self.in_2[side, 1, here, :].astype(F32)
                ).astype(BF16)
                self.out[pl.ds(there, REDUCE_STRIP), :] = (
                    self.pair_term(0, there) + self.in_2[side, 0, here, :].astype(F32)
                )

            over_half(self.half, step)
            last_arriving.append(
                send(
                    self.out_3.at[side], self.in_3.at[side], self.sems, (self.number, 6 + side),
                    {"dp": partner(last)},
                )
            )
        self.arriving = last_arriving
        self.copies += self.arriving

    def last(self):
        for side in (0, 1):
            self.arriving[side].wait_recv()

            def step(low):
                there = pl.ds(pl.multiple_of(low + side * self.half, REDUCE_STRIP), REDUCE_STRIP)
                self.out[there, :] += self.in_3[side, pl.ds(low, REDUCE_STRIP), :].astype(F32)

            over_half(self.half, step)
        for copy in self.copies:
            copy.wait_send()


def reduce_scratch(depth, columns):
    half = depth // 2
    return [
        pltpu.VMEM((4, depth, columns), BF16),
        pltpu.VMEM((2, 2, half, columns), BF16),
        pltpu.VMEM((2, 2, half, columns), BF16),
        pltpu.VMEM((2, half, columns), BF16),
        pltpu.VMEM((2, half, columns), BF16),
    ]


def piece_reader(total, size):
    def read(piece, low):
        first = partner(2 * piece) * size + low
        return total[pl.ds(pl.multiple_of(first, 32), REDUCE_STRIP), :].astype(F32)

    return read


def piece_of(total, mask, size):
    return total.at[pl.ds(pl.multiple_of(partner(mask) * size, 64), size)]


class TensorSum:
    def __init__(self, number, n_tensor, arrived, sems):
        self.number, self.n_tensor, self.arrived, self.sems = number, n_tensor, arrived, sems
        self.rank = lax.axis_index("tensor")
        self.size = arrived.shape[1]
        self.others = [
            (shift - 1, lax.rem(self.rank + shift, n_tensor)) for shift in range(1, n_tensor)
        ]

    def block(self, index):
        return pl.ds(pl.multiple_of(index * self.size, 16), self.size)

    def scatter(self, partial):
        self.partial = partial
        self.firsts = [
            send(
                partial.at[self.block(other)], self.arrived.at[place], self.sems,
                (2 * self.number, place), {"tensor": other},
            )
            for place, other in self.others
        ]

    def add(self, out, whole):
        for copy in self.firsts:
            copy.wait_recv()

        @pl.loop(0, self.size // STRIP)
        def _(index):
            low = pl.multiple_of(index * STRIP, STRIP)
            there = pl.ds(pl.multiple_of(self.rank * self.size + low, STRIP), STRIP)
            total = self.partial[there, :].astype(F32)
            for place, _ in self.others:
                total = total + self.arrived[place, pl.ds(low, STRIP), :].astype(F32)
            out[there if whole else pl.ds(low, STRIP), :] = total.astype(BF16)

        for copy in self.firsts:
            copy.wait_send()

    def gather(self, out):
        mine = out.at[self.block(self.rank)]
        self.seconds = [
            send(mine, mine, self.sems, (2 * self.number + 1, place), {"tensor": other})
            for place, other in self.others
        ]

    def finish(self):
        for copy in self.seconds:
            copy.wait()


def tensor_kernel(n_tensor, partial, out, arrived, sems):
    greet((), range(1, n_tensor), n_tensor)
    total = TensorSum(0, n_tensor, arrived, sems)
    total.scatter(partial)
    total.add(out, True)
    total.gather(out)
    total.finish()


def finish_kernel(grad_mod, sums, cond_act, grad_adaln, total, all_mod, all_sums, sems):
    rank = lax.axis_index("dp")
    masks = range(1, 8)
    greet(masks, (), 1)
    copies = []
    for mask in masks:
        device = {"dp": partner(mask)}
        copies.append(send(grad_mod, all_mod.at[rank], sems, (0, mask), device))
        copies.append(send(sums, all_sums.at[mask], sems, (1, mask), device))
    all_mod[rank] = grad_mod[...]
    all_sums[0] = sums[...]
    for copy in copies:
        copy.wait_recv()
    added = all_sums[0]
    for mask in masks:
        added = added + all_sums[mask]
    total[...] = added
    grad_adaln[...] = dot_tn(cond_act[...], all_mod[...].reshape(8 * 16, all_mod.shape[2]))
    for copy in copies:
        copy.wait_send()


def exchange(body, outs, ins, scratch, collective, vmem=48):
    spaces = [space for _, space in outs]
    return pl.pallas_call(
        body,
        out_shape=[shape for shape, _ in outs],
        in_specs=[pl.BlockSpec(memory_space=space) for _, space in ins],
        out_specs=[pl.BlockSpec(memory_space=space) for space in spaces],
        scratch_shapes=scratch,
        compiler_params=pltpu.CompilerParams(
            collective_id=collective, has_side_effects=True, vmem_limit_bytes=vmem * 2**20
        ),
    )(*[array for array, _ in ins])


def project_kernel(
    tokens, member, gain, q_gain, k_gain, cosine, sine, mods, whole_a, whole_b,
    attn_in, query_raw, key_raw, query_rot, key_rot, value, mat_a, mat_b, mod, sems
):
    copies = [load(whole_a, mat_a, sems.at[0]), load(whole_b, mat_b, sems.at[1])]
    width = q_gain.shape[1]
    token_columns(member, mods, 0, mod)
    blocks = head_blocks(width)

    def step(at):
        x = tokens[at, :].astype(F32)
        normed = x * row_scale(x)
        attn_in[at, :] = (normed * gain[...] * (1.0 + mod[at, :].astype(F32))).astype(BF16)

    over_strips(tokens.shape[0], step)
    wait_all(copies)
    query_raw[...] = dot_nn(attn_in[...], mat_a[:, :width])
    key_raw[...] = dot_nn(attn_in[...], mat_b[:, :width])
    value[...] = dot_nn(attn_in[...], mat_a[:, width:]).astype(BF16)
    for raw, head_gain, out in ((query_raw, q_gain, query_rot), (key_raw, k_gain, key_rot)):
        normed = head_norm(raw[...], head_gain[...], blocks)
        out[...] = (normed * cosine[...] + swap_pairs(normed) * sine[...]).astype(BF16)


def text_kernel(
    live, source, captions, gain, whole_k, whole_v,
    text_raw, text_key, text_value, mat_k, mat_v, sems
):
    image = pl.program_id(0)

    @pl.when(image == 0)
    def _():
        wait_all([load(whole_k, mat_k, sems.at[0]), load(whole_v, mat_v, sems.at[1])])

    @pl.when(live[image] > 0)
    def _():
        raw = dot_nn(captions[0], mat_k[...])
        text_raw[0] = raw.astype(BF16)
        text_key[0] = head_norm(raw, gain[...], head_blocks(raw.shape[1])).astype(BF16)
        text_value[0] = dot_nn(captions[0], mat_v[...]).astype(BF16)


def softmax(scores, allowed, rows_live):
    scores = jnp.where(allowed, scores, MASKED)
    expo = jnp.where(allowed, jnp.exp(scores - jnp.max(scores, axis=1, keepdims=True)), 0.0)
    total = jnp.sum(expo, axis=1, keepdims=True)
    if rows_live is not None:
        total = jnp.where(rows_live, total, 1.0)
    return expo / total


def attend_kernel(
    micro, scale, live, text_len, query, key, value, text_key, text_value,
    self_id, self_row, segment, gate, whole_b, mixed, cross_out, whole, mat_b, sem
):
    copies = [load(whole_b, mat_b, sem)]
    rows, width = query.shape
    count = rows // micro
    slots = text_key.shape[0] // micro
    heads = width // HEAD_DIM
    cross_out[...] = jnp.zeros_like(cross_out)

    @pl.loop(0, micro * slots)
    def _(image):
        @pl.when(live[image] > 0)
        def _():
            at = pl.ds(pl.multiple_of((image // slots) * count, count), count)
            mine = segment[at, :] == lax.rem(image, slots)
            column = lax.broadcasted_iota(jnp.int32, (count, TXT), 1)
            allowed = mine & (column < text_len[image])
            for head in range(heads):
                lanes = slice(head * HEAD_DIM, (head + 1) * HEAD_DIM)
                scores = dot_nt(query[at, lanes], text_key[image, :, lanes]) * scale
                probs = softmax(scores, allowed, mine).astype(BF16)
                cross_out[at, lanes] += dot_nn(probs, text_value[image, :, lanes])

    for batch in range(micro):
        at = slice(batch * count, (batch + 1) * count)
        allowed = self_id[at, :] == self_row[batch : batch + 1, :]
        for head in range(heads):
            lanes = slice(head * HEAD_DIM, (head + 1) * HEAD_DIM)
            scores = dot_nt(query[at, lanes], key[at, lanes]) * scale
            probs = softmax(scores, allowed, None).astype(BF16)
            out = dot_nn(probs, value[at, lanes])
            mixed[at, lanes] = (out + gate[:, lanes] * cross_out[at, lanes]).astype(BF16)
    wait_all(copies)
    whole[...] = dot_nt(mixed[...], mat_b[:, width:]).astype(BF16)


def feed_kernel(
    tokens, member, gain, cotangent, mods, attn_out, whole_f,
    hidden, ffn_in, inner, grad_gate, grad_up, grad_out, whole,
    mat, mod_1, mod_2, mod_3, sem
):
    copies = [load(whole_f, mat, sem)]
    units = inner.shape[1]
    mat_a, mat_b, mat_c = [mat.at[:, i * units : (i + 1) * units] for i in range(3)]
    token_columns(member, mods, 1, mod_1)
    token_columns(member, mods, 2, mod_2)
    token_columns(member, mods, 3, mod_3)

    def step(at):
        gate_attn = jnp.tanh(mod_1[at, :].astype(F32))
        state = tokens[at, :].astype(F32) + gate_attn * attn_out[at, :].astype(F32)
        hidden[at, :] = state
        normed = state * row_scale(state)
        ffn_in[at, :] = (normed * gain[...] * (1.0 + mod_2[at, :].astype(F32))).astype(BF16)
        gate_ffn = jnp.tanh(mod_3[at, :].astype(F32))
        grad_out[at, :] = (gate_ffn * cotangent[at, :].astype(F32)).astype(BF16)

    rows = tokens.shape[0]
    over_strips(rows, step)
    wait_all(copies)
    chunk = 256
    for first in range(0, units, chunk):
        span = slice(first, first + chunk)
        gate = dot_nn(ffn_in[...], mat_a[:, span])
        up = dot_nn(ffn_in[...], mat_b[:, span])
        grad_inner = dot_nn(grad_out[...], mat_c[:, span])
        turn = jax.nn.sigmoid(gate)
        active = gate * turn
        inner[:, span] = (active * up).astype(BF16)
        grad_up[:, span] = (grad_inner * active).astype(BF16)
        slope = turn * (1.0 + gate * (1.0 - turn))
        grad_gate[:, span] = (grad_inner * up * slope).astype(BF16)
    width = tokens.shape[1]
    for first in range(0, width, 512):
        span = slice(first, first + 512)
        whole[:, span] = (
            dot_nt(grad_gate[...], mat_a[span, :]) + dot_nt(grad_up[...], mat_b[span, :])
        ).astype(BF16)


def feed_grad_kernel(grad_out, inner, ffn_in, grad_gate, grad_up, total):
    units = inner.shape[1]
    step = 256
    for index, (left, right) in enumerate(
        ((ffn_in, grad_gate), (ffn_in, grad_up), (grad_out, inner))
    ):
        for first in range(0, units, step):
            out = slice(index * units + first, index * units + first + step)
            total[:, out] = dot_tn(left[...], right[:, first : first + step]).astype(BF16)


def feed_out_kernel(inner, whole_f, partial, mat, sem):
    units = inner.shape[1]
    copy = load(whole_f.at[:, 2 * units : 3 * units], mat, sem)
    copy.wait()
    for first in range(0, partial.shape[1], 512):
        span = slice(first, first + 512)
        partial[:, span] = dot_nt(inner[...], mat[span, :]).astype(BF16)


def modulate_back(values, gain, shift, grad):
    scale = row_scale(values)
    normed = values * scale
    inner = grad * gain * (1.0 + shift)
    mean = jnp.mean(inner * normed, axis=1, keepdims=True)
    return scale * (inner - normed * mean), grad * normed


def mixed_grad_kernel(
    hidden, member, gain, cotangent, mods, grad_in, whole_b,
    grad_hidden, grad_out, grad_mixed, mat_b, mod_1, mod_2, sem
):
    copies = [load(whole_b, mat_b, sem)]
    token_columns(member, mods, 1, mod_1)
    token_columns(member, mods, 2, mod_2)

    def step(at):
        back, _ = modulate_back(
            hidden[at, :], gain[...], mod_2[at, :].astype(F32), grad_in[at, :].astype(F32)
        )
        total = cotangent[at, :].astype(F32) + back
        grad_hidden[at, :] = total
        grad_out[at, :] = (jnp.tanh(mod_1[at, :].astype(F32)) * total).astype(BF16)

    over_strips(hidden.shape[0], step)
    wait_all(copies)
    width = grad_mixed.shape[1]
    grad_mixed[...] = dot_nn(grad_out[...], mat_b[:, width:])


def feed_exchange_kernel(
    n_tensor, tokens, member, gain, cotangent, mods, attn_out, whole_f, whole_ko,
    hidden, grad_hidden, grad_attn_out, grad_mixed, grad_in, ffn_out_rows, *rest
):
    outs, rest = rest[:3], rest[3:]
    (
        ffn_in, inner, grad_gate, grad_up, grad_out, ffn_part, out_part,
        mat, mod_1, mod_2, mod_3, *rest
    ) = rest
    totals, rest = rest[:3], rest[3:]
    buffers, (arrived_1, arrived_2, sem, mat_sem, sems, tensor_sems) = rest[:15], rest[15:]
    greet((PAIR, ALONG_X, ALONG_Y), range(1, n_tensor), n_tensor)
    feed_kernel(
        tokens, member, gain, cotangent, mods, attn_out, whole_f,
        hidden, ffn_in, inner, grad_gate, grad_up, grad_out, ffn_part,
        mat, mod_1, mod_2, mod_3, sem,
    )
    sum_in = TensorSum(0, n_tensor, arrived_1, tensor_sems)
    sum_in.scatter(ffn_part)
    size = outs[0].shape[0]
    reduces, firsts = [], []
    for number, (left, right) in enumerate(
        ((ffn_in, grad_gate), (ffn_in, grad_up), (grad_out, inner))
    ):
        total = totals[number]
        for first in range(0, total.shape[1], 256):
            span = slice(first, first + 256)
            total[:, span] = dot_tn(left[...], right[:, span]).astype(BF16)
        reduce = Reduce(
            number, piece_reader(total, size), outs[number],
            *buffers[5 * number : 5 * number + 5], sems,
        )
        reduces.append(reduce)
        firsts.append(
            [reduce.first(piece, piece_of(total, 2 * piece + 1, size)) for piece in range(4)]
        )
    units = inner.shape[1]
    for first in range(0, out_part.shape[1], 512):
        span = slice(first, first + 512)
        out_part[:, span] = dot_nt(inner[...], mat[span, 2 * units :]).astype(BF16)
    sum_out = TensorSum(1, n_tensor, arrived_2, tensor_sems)
    for number in range(3):
        reduces[number].second(firsts[number])
    sum_in.add(grad_in, True)
    sum_in.gather(grad_in)
    sum_out.scatter(out_part)
    for reduce in reduces:
        reduce.third()
    sum_in.finish()
    head_width = grad_mixed.shape[1]
    copy = load(whole_ko.at[:, head_width:], mat.at[:, :head_width], mat_sem)

    def step(at):
        back, _ = modulate_back(
            hidden[at, :], gain[...], mod_2[at, :].astype(F32), grad_in[at, :].astype(F32)
        )
        total = cotangent[at, :].astype(F32) + back
        grad_hidden[at, :] = total
        grad_attn_out[at, :] = (jnp.tanh(mod_1[at, :].astype(F32)) * total).astype(BF16)

    over_strips(hidden.shape[0], step)
    copy.wait()
    grad_mixed[...] = dot_nn(grad_attn_out[...], mat[:, :head_width])
    for reduce in reduces:
        reduce.last()
    sum_out.add(ffn_out_rows, False)


def attend_back_kernel(
    micro, scale, live, text_len, grad_mixed, cross_out, query, key, value, text_key, text_value,
    text_raw, query_raw, key_raw, q_gain, k_gain, t_gain, cosine, sine, self_id, self_row, segment,
    gate, grad_query_b, grad_key_b, grad_value_b, grad_text_key, grad_text_value,
    gain_sums, grad_query, grad_key, grad_cross, grad_text
):
    rows, width = query.shape
    count = rows // micro
    slots = text_key.shape[0] // micro
    heads = width // HEAD_DIM
    blocks = head_blocks(width)
    gate_sum = jnp.sum(grad_mixed[...] * cross_out[...], axis=0, keepdims=True)
    gain_sums[...] = jnp.zeros_like(gain_sums)
    gain_sums[3:4, :] = gate_sum * (1.0 - gate[...] * gate[...])
    grad_cross[...] = (gate[...] * grad_mixed[...]).astype(BF16)
    for batch in range(micro):
        at = slice(batch * count, (batch + 1) * count)
        allowed = self_id[at, :] == self_row[batch : batch + 1, :]
        for head in range(heads):
            lanes = slice(head * HEAD_DIM, (head + 1) * HEAD_DIM)
            q, k = query[at, lanes], key[at, lanes]
            grad = grad_mixed[at, lanes].astype(BF16)
            probs = softmax(dot_nt(q, k) * scale, allowed, None)
            grad_probs = dot_nt(grad, value[at, lanes])
            mean = jnp.sum(probs * grad_probs, axis=1, keepdims=True)
            scaled = (probs * (grad_probs - mean) * scale).astype(BF16)
            grad_query[at, lanes] = dot_nn(scaled, k)
            grad_key[at, lanes] = dot_tn(scaled, q)
            grad_value_b[at, lanes] = dot_tn(probs.astype(BF16), grad).astype(BF16)

    @pl.loop(0, micro * slots)
    def _(image):
        @pl.when(live[image] == 0)
        def _():
            grad_text_key[image] = jnp.zeros((TXT, width), BF16)
            grad_text_value[image] = jnp.zeros((TXT, width), BF16)

        @pl.when(live[image] > 0)
        def _():
            at = pl.ds(pl.multiple_of((image // slots) * count, count), count)
            mine = segment[at, :] == lax.rem(image, slots)
            column = lax.broadcasted_iota(jnp.int32, (count, TXT), 1)
            allowed = mine & (column < text_len[image])
            for head in range(heads):
                lanes = slice(head * HEAD_DIM, (head + 1) * HEAD_DIM)
                q, k = query[at, lanes], text_key[image, :, lanes]
                grad = grad_cross[at, lanes]
                probs = softmax(dot_nt(q, k) * scale, allowed, mine)
                grad_probs = dot_nt(grad, text_value[image, :, lanes])
                mean = jnp.sum(probs * grad_probs, axis=1, keepdims=True)
                scaled = (probs * (grad_probs - mean) * scale).astype(BF16)
                grad_query[at, lanes] += dot_nn(scaled, k)
                grad_text[:, lanes] = dot_tn(scaled, q)
                grad_text_value[image, :, lanes] = dot_tn(probs.astype(BF16), grad).astype(BF16)
            back, gain_sum = head_norm_back(
                text_raw[image].astype(F32), t_gain[...], grad_text[...], blocks
            )
            grad_text_key[image] = back.astype(BF16)
            gain_sums[2:3, :] += gain_sum

    for index, (grad, raw, gain, out) in enumerate(
        (
            (grad_query, query_raw, q_gain, grad_query_b),
            (grad_key, key_raw, k_gain, grad_key_b),
        )
    ):
        turned = grad[...] * cosine[...] + swap_pairs(grad[...] * sine[...])
        back, gain_sum = head_norm_back(raw[...], gain[...], turned, blocks)
        out[...] = back.astype(BF16)
        gain_sums[index : index + 1, :] = gain_sum


def attn_grad_kernel(
    attn_in, grad_query, grad_key, grad_value, grad_out, mixed, whole_a, whole_b,
    total_a, total_b, whole, mat_a, mat_b, pair, sems
):
    copies = [load(whole_a, mat_a, sems.at[0]), load(whole_b, mat_b, sems.at[1])]
    width = grad_query.shape[1]
    pair[:, :width] = grad_query[...]
    pair[:, width:] = grad_value[...]
    wait_all(copies)
    for first in range(0, whole.shape[1], 512):
        span = slice(first, first + 512)
        whole[:, span] = (
            dot_nt(pair[...], mat_a[span, :]) + dot_nt(grad_key[...], mat_b[span, :width])
        ).astype(BF16)
    for first in range(0, 2 * width, 256):
        span = slice(first, first + 256)
        total_a[:, span] = dot_tn(attn_in[...], pair[:, span]).astype(BF16)
    total_b[:, :width] = dot_tn(attn_in[...], grad_key[...]).astype(BF16)
    total_b[:, width:] = dot_tn(grad_out[...], mixed[...]).astype(BF16)


def last_exchange_kernel(
    n_tensor, captions, grad_key, grad_value, total_qv, total_ko, attn_part, ffn_rows,
    out_qv, out_ko, out_text, grad_in, ffn_out, *rest
):
    buffers, rest = rest[:15], rest[15:]
    text_total, block, pair, arrived, block_sems, sems, tensor_sems = rest
    greet((PAIR, ALONG_X, ALONG_Y), range(1, n_tensor), n_tensor)
    sum_in = TensorSum(0, n_tensor, arrived, tensor_sems)
    sum_in.scatter(attn_part)
    sum_out = TensorSum(1, n_tensor, arrived, tensor_sems)
    ffn_out[sum_out.block(sum_out.rank), :] = ffn_rows[...]
    size = out_qv.shape[0]
    depth = out_text.shape[0]
    images, length, width = grad_key.shape
    reduces, firsts = [], []
    for number, (total, out) in enumerate(((total_qv, out_qv), (total_ko, out_ko))):
        reduce = Reduce(
            number, piece_reader(total, size), out, *buffers[5 * number : 5 * number + 5], sems
        )
        reduces.append(reduce)
        firsts.append(
            [reduce.first(piece, piece_of(total, 2 * piece + 1, size)) for piece in range(4)]
        )
    tall = images * length

    def fetch(mask, slot):
        columns = pl.ds(pl.multiple_of(partner(mask) * depth, 128), depth)
        return pltpu.make_async_copy(
            captions.at[:, columns], block.at[slot], block_sems.at[slot]
        )

    fetch(1, 0).start()
    pair[:, :width] = grad_key[...].reshape(tall, width)
    pair[:, width:] = grad_value[...].reshape(tall, width)

    def read_text(piece, low):
        return text_total[2 * piece, pl.ds(low, REDUCE_STRIP), :].astype(F32)

    text = Reduce(2, read_text, out_text, *buffers[10:], sems)

    def work(low):
        @pl.loop(0, 4)
        def _(index):
            slot = lax.rem(index, 2)
            mask = 2 * index + low

            @pl.when(index < 3)
            def _():
                fetch(mask + 2, 1 - slot).start()

            if low:

                @pl.when(index == 3)
                def _():
                    fetch(0, 1 - slot).start()

            fetch(mask, slot).wait()
            for first in range(0, 2 * width, 256):
                span = slice(first, first + 256)
                text_total[mask, :, span] = dot_tn(block[slot], pair[:, span]).astype(BF16)

    work(1)
    text_firsts = [text.first(piece, text_total.at[2 * piece + 1]) for piece in range(4)]
    for number in range(2):
        reduces[number].second(firsts[number])
    work(0)
    text.second(text_firsts)
    sum_in.add(grad_in, True)
    sum_in.gather(grad_in)
    sum_out.gather(ffn_out)
    for reduce in reduces:
        reduce.third()
    text.third()
    for reduce in reduces:
        reduce.last()
    text.last()
    sum_in.finish()
    sum_out.finish()


def segment_sum(member, values):
    high = values.astype(BF16)
    rest = values - high.astype(F32)
    middle = rest.astype(BF16)
    low = (rest - middle.astype(F32)).astype(BF16)
    return dot_tn(member, high) + dot_tn(member, middle) + dot_tn(member, low)


def output_kernel(
    hidden, member, gain, cotangent, mods, ffn_out, grad_in,
    result, grad_mod, grad_gain, mod_2, mod_3, grad
):
    token_columns(member, mods, 2, mod_2)
    token_columns(member, mods, 3, mod_3)
    rank = lax.axis_index("tensor")
    grad_gain[...] = jnp.zeros_like(grad_gain)

    def step(at):
        state = hidden[at, :]
        gate = jnp.tanh(mod_3[at, :].astype(F32))
        out = ffn_out[at, :].astype(F32)
        result[at, :] = (state + gate * out).astype(BF16)
        up = grad_in[at, :].astype(F32)
        product = up * state * row_scale(state)
        grad_gain[...] += jnp.sum(
            product * (1.0 + mod_2[at, :].astype(F32)), axis=0, keepdims=True
        )
        grad_gate = cotangent[at, :].astype(F32) * out * (1.0 - gate * gate)
        grad[at, :] = jnp.where(rank == 2, product * gain[...], grad_gate)

    over_strips(hidden.shape[0], step)
    grad_mod[...] = segment_sum(member[...], grad[...])


def input_kernel(
    tokens, member, gain, grad_hidden, other_mod, mods, grad_in, attn_out,
    grad_tokens, grad_mod, grad_gain, mod_0, mod_1, grad
):
    token_columns(member, mods, 0, mod_0)
    token_columns(member, mods, 1, mod_1)
    rank = lax.axis_index("tensor")
    grad_gain[...] = jnp.zeros_like(grad_gain)

    def step(at):
        shift = mod_0[at, :].astype(F32)
        upper = grad_hidden[at, :]
        back, product = modulate_back(
            tokens[at, :].astype(F32), gain[...], shift, grad_in[at, :].astype(F32)
        )
        grad_tokens[at, :] = (upper + back).astype(BF16)
        grad_gain[...] += jnp.sum(product * (1.0 + shift), axis=0, keepdims=True)
        gate = jnp.tanh(mod_1[at, :].astype(F32))
        grad_gate = upper * attn_out[at, :].astype(F32) * (1.0 - gate * gate)
        grad[at, :] = jnp.where(rank == 0, product * gain[...], grad_gate)

    over_strips(tokens.shape[0], step)
    own = segment_sum(member[...], grad[...])
    grad_mod[...] = jnp.where(rank < 2, own, other_mod[...]).astype(BF16)


def shards(
    n_dp,
    n_tensor,
    tokens,
    context,
    captions,
    shapes,
    text_len,
    w_query,
    w_key,
    w_value,
    w_out,
    w_text_key,
    w_text_value,
    w_gate,
    w_up,
    w_down,
    w_adaln,
    gain_attn,
    gain_ffn,
    gain_query,
    gain_key,
    gain_text,
    cross_gate,
    cotangent,
):
    parts = 8 if n_dp == 8 else 1
    micro, count, width = tokens.shape
    slots = shapes.shape[1]
    rows = micro * count
    images = micro * slots
    heads = w_query.shape[1] // HEAD_DIM
    local = heads * HEAD_DIM
    units = w_gate.shape[1]
    scale = HEAD_DIM ** (-0.5)
    dp_rank = lax.axis_index("dp")
    padded = 16
    vmem, smem, anywhere = pltpu.VMEM, pltpu.SMEM, pl.ANY
    dma = pltpu.SemaphoreType.DMA

    def inside(*arrays):
        return [(array, vmem) for array in arrays]

    def scalars(*arrays):
        return [(array, smem) for array in arrays]

    def outside(*arrays):
        return [(array, anywhere) for array in arrays]

    def after(values, earlier):
        return lax.optimization_barrier((list(values), list(earlier)))[0]

    def gathered(shard):
        return lax.all_gather(shard, "dp", axis=0, tiled=True)

    def scattered(whole):
        return lax.psum_scatter(whole, "dp", scatter_dimension=0, tiled=True).astype(F32)

    part_rows = rows // n_tensor
    arrived = vmem((n_tensor - 1, part_rows, width), BF16)

    def tensor_sum(partial):
        (out,) = exchange(
            functools.partial(tensor_kernel, n_tensor),
            [(struct((rows, width)), vmem)],
            inside(partial),
            [arrived, dma((2, 2, n_tensor - 1))],
            1,
        )
        return out

    gain_list = (gain_attn, gain_ffn, gain_query, gain_key, gain_text)
    gain_rows = jnp.concatenate([gain.reshape(-1) for gain in gain_list])
    cond_rows, span = w_adaln.shape
    shard_qv = jnp.concatenate([w_query, w_value], axis=1)
    shard_ko = jnp.concatenate([w_key, w_out], axis=1)
    shard_f = jnp.concatenate([w_gate, w_up, w_down], axis=1)
    if parts == 1:
        whole_tk, whole_tv = gathered(w_text_key), gathered(w_text_value)
        whole_qv, whole_ko = gathered(shard_qv), gathered(shard_ko)
        gain_rows = lax.all_gather(gain_rows, "dp", axis=0)
        context_all = gathered(context.reshape(images, -1))
        cond_cols = lax.dynamic_slice_in_dim(context_all, dp_rank * cond_rows, cond_rows, 1)
        cond_act = jax.nn.silu(cond_cols.astype(F32)).astype(BF16)
        mod_part = scattered(dot_nn(cond_act, w_adaln)).astype(BF16)
        mods = lax.all_gather(mod_part, "tensor", axis=0)
        mods = jnp.pad(mods, ((0, 0), (0, padded - images), (0, 0)))
    else:
        gain_size = gain_rows.size
        small = jnp.pad(
            context.reshape(images, parts, -1).transpose(1, 0, 2),
            ((0, 0), (0, padded - images), (0, 0)),
        )
        packed = jnp.pad(gain_rows, (0, padded * cond_rows - gain_size))
        packed = jnp.broadcast_to(packed.reshape(1, padded, cond_rows), small.shape)
        small = jnp.concatenate([small, packed], axis=1)
        whole_tk, whole_tv, whole_qv, whole_ko, small_all, cond_act, mods = exchange(
            functools.partial(gather_kernel, n_tensor),
            [(struct((DT, local)), anywhere)] * 2
            + [(struct((width, 2 * local)), anywhere)] * 2
            + [
                (struct(small.shape), vmem),
                (struct((parts * padded, cond_rows)), vmem),
                (struct((n_tensor, padded, span)), vmem),
            ],
            outside(w_text_key, w_text_value, shard_qv, shard_ko) + inside(small, w_adaln),
            [
                vmem((parts, padded, span), BF16),
                vmem((parts, padded, span), BF16),
                dma((4,)),
                dma((2, 4, 9)),
                dma((2, 8)),
                dma((2, 8)),
                dma((2, n_tensor)),
            ],
            2,
        )
        gain_rows = small_all[:, padded:].reshape(parts, -1)[:, :gain_size]
        (shard_f,) = after([shard_f], [mods])
    whole_f = gathered(shard_f)
    sizes = [gain.size for gain in gain_list]
    edges = [sum(sizes[:i]) for i in range(len(sizes) + 1)]
    gains = [gain_rows[:, edges[i] : edges[i + 1]] for i in range(5)]
    attn_gain, ffn_gain = [gain.reshape(1, width).astype(F32) for gain in gains[:2]]
    query_gain, key_gain, text_gain = [
        gain.reshape(HEAD_DIM, heads).T.reshape(1, local).astype(F32) for gain in gains[2:]
    ]

    layouts = [image_layout(shapes[i], count) for i in range(micro)]
    member, segment, inside_any, row_pos, col_pos = [
        jnp.stack([layout[j] for layout in layouts]) for j in range(5)
    ]
    cosine, sine = rope_tables(row_pos.reshape(rows), col_pos.reshape(rows))
    cosine = jnp.tile(jnp.stack([cosine, cosine], axis=2).reshape(rows, HEAD_DIM), (1, heads))
    sine = jnp.tile(jnp.stack([-sine, sine], axis=2).reshape(rows, HEAD_DIM), (1, heads))
    which = jnp.arange(micro, dtype=jnp.int32)
    member = jnp.where(
        (which[:, None] == which[None, :])[:, None, :, None], member[:, :, None, :], 0.0
    )
    member = jnp.pad(member.reshape(rows, images), ((0, 0), (0, padded - images))).astype(BF16)
    self_row = jnp.where(inside_any > 0, segment, slots)
    self_id = self_row.reshape(rows, 1)
    segment = segment.reshape(rows, 1)
    lens = text_len.reshape(images)
    used = shapes[:, :, 0] * (shapes[:, :, 1] + 1) > 0
    used = used | (jnp.arange(slots)[None, :] == 0)
    live = used.reshape(images).astype(jnp.int32)
    at = jnp.arange(images, dtype=jnp.int32)
    source = lax.cummax(jnp.where(live > 0, at, 0))
    gate = jnp.repeat(jnp.tanh(cross_gate.astype(F32)), HEAD_DIM)[None, :]
    token_rows = tokens.reshape(rows, width)
    grad_y = cotangent.reshape(rows, width)
    caption_images = captions.reshape(images, TXT, DT)

    attn_in, query_raw, key_raw, query_rot, key_rot, value = run(
        project_kernel,
        [struct((rows, width))]
        + [struct((rows, local), F32)] * 2
        + [struct((rows, local))] * 3,
        inside(token_rows, member, attn_gain, query_gain, key_gain, cosine, sine, mods)
        + outside(whole_qv, whole_ko),
        [
            vmem((width, 2 * local), BF16),
            vmem((width, 2 * local), BF16),
            vmem((rows, width), BF16),
            dma((2,)),
        ],
        flops=6 * rows * width * local,
        traffic=10 * 2**20,
    )

    text_raw, text_key, text_value = pl.pallas_call(
        text_kernel,
        out_shape=[struct((images, TXT, local))] * 3,
        grid_spec=pltpu.PrefetchScalarGridSpec(
            num_scalar_prefetch=2,
            grid=(images,),
            in_specs=[
                pl.BlockSpec((1, TXT, DT), lambda i, live, source: (source[i], 0, 0)),
                pl.BlockSpec((1, local), lambda i, live, source: (0, 0)),
            ]
            + [pl.BlockSpec(memory_space=anywhere)] * 2,
            out_specs=[pl.BlockSpec((1, TXT, local), lambda i, live, source: (i, 0, 0))] * 3,
            scratch_shapes=[vmem((DT, local), BF16), vmem((DT, local), BF16), dma((2,))],
        ),
        compiler_params=pltpu.CompilerParams(vmem_limit_bytes=40 * 2**20),
        cost_estimate=pl.CostEstimate(
            flops=2 * images * TXT * DT * local, bytes_accessed=20 * 2**20, transcendentals=0
        ),
    )(live, source, caption_images, text_gain, whole_tk, whole_tv)

    wide = vmem((rows, width), BF16)
    mixed, cross_out, attn_part = run(
        functools.partial(attend_kernel, micro, scale),
        [struct((rows, local)), struct((rows, local), F32), struct((rows, width))],
        scalars(live, lens)
        + inside(query_rot, key_rot, value, text_key, text_value, self_id, self_row, segment, gate)
        + outside(whole_ko),
        [vmem((width, 2 * local), BF16), dma],
        flops=2 * 2**30,
        traffic=12 * 2**20,
    )
    attn_out = tensor_sum(attn_part)

    size = width // parts
    if parts == 1:
        mat = vmem((width, 3 * units), BF16)
        hidden, ffn_in, inner, grad_gate, grad_up, grad_ffn_out, ffn_part = run(
            feed_kernel,
            [struct((rows, width), F32), struct((rows, width))]
            + [struct((rows, units))] * 3
            + [struct((rows, width))] * 2,
            inside(token_rows, member, ffn_gain, grad_y, mods, attn_out) + outside(whole_f),
            [mat, wide, wide, wide, dma],
            flops=10 * rows * width * units,
            traffic=20 * 2**20,
        )
        (grad_f,) = run(
            feed_grad_kernel,
            [struct((width, 3 * units))],
            inside(grad_ffn_out, inner, ffn_in, grad_gate, grad_up),
            flops=6 * rows * width * units,
            traffic=12 * 2**20,
        )
        (ffn_part,) = after([ffn_part], [grad_f])
        grad_ffn_in = tensor_sum(ffn_part)
        grad_f = scattered(grad_f)
        (ffn_out_part,) = run(
            feed_out_kernel,
            [struct((rows, width))],
            inside(inner) + outside(whole_f),
            [vmem((width, units), BF16), dma],
            flops=2 * rows * width * units,
            traffic=5 * 2**20,
        )
        ffn_out = lax.psum(ffn_out_part, "tensor")

        grad_hidden, grad_attn_out, grad_mixed = run(
            mixed_grad_kernel,
            [struct((rows, width), F32), struct((rows, width)), struct((rows, local), F32)],
            inside(hidden, member, ffn_gain, grad_y, mods, grad_ffn_in) + outside(whole_ko),
            [vmem((width, 2 * local), BF16), wide, wide, dma],
            flops=2 * rows * width * local,
            traffic=8 * 2**20,
        )
    else:
        hidden, grad_hidden, grad_attn_out, grad_mixed, grad_ffn_in, ffn_out_rows, *grad_f = exchange(
            functools.partial(feed_exchange_kernel, n_tensor),
            [
                (struct((rows, width), F32), vmem),
                (struct((rows, width), F32), vmem),
                (struct((rows, width)), vmem),
                (struct((rows, local), F32), vmem),
                (struct((rows, width)), vmem),
                (struct((part_rows, width)), vmem),
            ]
            + [(struct((size, units), F32), vmem)] * 3,
            inside(token_rows, member, ffn_gain, grad_y, mods, attn_out)
            + outside(whole_f, whole_ko),
            [wide]
            + [vmem((rows, units), BF16)] * 3
            + [wide] * 3
            + [vmem((width, 3 * units), BF16), wide, wide, wide]
            + [vmem((width, units), BF16)] * 3
            + reduce_scratch(size, units) * 3
            + [arrived, arrived, dma, dma, dma((2, 3, 8)), dma((2, 4, n_tensor - 1))],
            5,
            vmem=60,
        )

    tile = struct((rows, local))
    texts = struct((images, TXT, local))
    grad_query_b, grad_key_b, grad_value_b, grad_text_key, grad_text_value, gain_sums = run(
        functools.partial(attend_back_kernel, micro, scale),
        [tile, tile, tile, texts, texts, struct((8, local), F32)],
        scalars(live, lens)
        + inside(
            grad_mixed, cross_out, query_rot, key_rot, value, text_key, text_value, text_raw,
            query_raw, key_raw, query_gain, key_gain, text_gain, cosine, sine, self_id, self_row,
            segment, gate,
        ),
        [
            vmem((rows, local), F32),
            vmem((rows, local), F32),
            vmem((rows, local), BF16),
            vmem((TXT, local), F32),
        ],
        flops=4 * 2**30,
        traffic=15 * 2**20,
    )

    total_qv, total_ko, attn_in_part = run(
        attn_grad_kernel,
        [struct((width, 2 * local))] * 2 + [struct((rows, width))],
        inside(attn_in, grad_query_b, grad_key_b, grad_value_b, grad_attn_out, mixed)
        + outside(whole_qv, whole_ko),
        [
            vmem((width, 2 * local), BF16),
            vmem((width, 2 * local), BF16),
            vmem((rows, 2 * local), BF16),
            dma((2,)),
        ],
        flops=14 * rows * width * local,
        traffic=15 * 2**20,
    )
    depth = DT // parts
    caption_rows = captions.reshape(images * TXT, DT)
    if parts == 1:
        grad_attn_in = lax.psum(attn_in_part, "tensor")
        grads_text = jnp.concatenate([grad_text_key, grad_text_value], axis=2)
        grad_text = dot_tn(caption_rows, grads_text.reshape(images * TXT, 2 * local))
        wholes = (total_qv, total_ko, grad_text)
        grad_qv, grad_ko, grad_text = [scattered(whole.astype(F32)) for whole in wholes]
        grad_f = [grad_f[:, i * units : (i + 1) * units] for i in range(3)]
    else:
        grad_qv, grad_ko, grad_text, grad_attn_in, ffn_out = exchange(
            functools.partial(last_exchange_kernel, n_tensor),
            [
                (struct((size, 2 * local), F32), vmem),
                (struct((size, 2 * local), F32), vmem),
                (struct((depth, 2 * local), F32), vmem),
                (struct((rows, width)), vmem),
                (struct((rows, width)), vmem),
            ],
            outside(caption_rows)
            + inside(grad_text_key, grad_text_value, total_qv, total_ko, attn_in_part, ffn_out_rows),
            reduce_scratch(size, 2 * local) * 2
            + reduce_scratch(depth, 2 * local)
            + [
                vmem((parts, depth, 2 * local), BF16),
                vmem((2, images * TXT, depth), BF16),
                vmem((images * TXT, 2 * local), BF16),
                arrived,
                dma((2,)),
                dma((2, 3, 8)),
                dma((2, 4, n_tensor - 1)),
            ],
            3,
            vmem=60,
        )

    result, ffn_mod, ffn_gain_sum = run(
        output_kernel,
        [struct((rows, width)), struct((padded, width), F32), struct((1, width), F32)],
        inside(hidden, member, ffn_gain, grad_y, mods, ffn_out, grad_ffn_in),
        [wide, wide, vmem((rows, width), F32)],
        traffic=8 * 2**20,
    )
    grad_tokens, grad_mod, attn_gain_sum = run(
        input_kernel,
        [struct((rows, width)), struct((padded, width)), struct((1, width), F32)],
        inside(token_rows, member, attn_gain, grad_hidden, ffn_mod, mods, grad_attn_in, attn_out),
        [wide, wide, vmem((rows, width), F32)],
        traffic=8 * 2**20,
    )
    head_sums = gain_sums[:3].reshape(3, heads, HEAD_DIM).transpose(0, 2, 1)
    gate_sums = jnp.sum(gain_sums[3].reshape(heads, HEAD_DIM), axis=1)
    sums = jnp.concatenate(
        [attn_gain_sum[0], ffn_gain_sum[0], head_sums.reshape(-1), gate_sums]
    )
    if parts == 1:
        sums = lax.psum(sums, "dp")
        grad_w_adaln = dot_tn(cond_act, gathered(grad_mod[:images]))
    else:
        flat_size = sums.size
        tall = -(-flat_size // 1024) * 8
        sums = jnp.pad(sums, (0, tall * 128 - flat_size)).reshape(tall, 128)
        grad_w_adaln, sums = exchange(
            finish_kernel,
            [(struct((cond_rows, span), F32), vmem), (struct((tall, 128), F32), vmem)],
            inside(grad_mod, sums, cond_act),
            [vmem((parts, padded, span), BF16), vmem((parts, tall, 128), F32), dma((2, 2, 8))],
            4,
        )
        sums = sums.reshape(-1)[:flat_size]

    def own(first, shape):
        whole = sums[first : first + shape[0] * (shape[1] if len(shape) > 1 else 1)].reshape(shape)
        part = shape[0] // n_dp
        return lax.dynamic_slice_in_dim(whole, dp_rank * part, part, 0)

    head_shape = (HEAD_DIM, heads)
    edge = 2 * width
    return (
        result.reshape(micro, count, width),
        grad_tokens.reshape(micro, count, width),
        grad_qv[:, :local],
        grad_ko[:, :local],
        grad_qv[:, local:],
        grad_ko[:, local:],
        grad_text[:, :local],
        grad_text[:, local:],
        *grad_f,
        grad_w_adaln,
        own(0, (width,)),
        own(width, (width,)),
        own(edge, head_shape),
        own(edge + local, head_shape),
        own(edge + 2 * local, head_shape),
        sums[edge + 3 * local :],
    )


def solution(mesh):
    return jax.shard_map(
        functools.partial(shards, mesh.shape["dp"], mesh.shape["tensor"]),
        mesh=mesh,
        in_specs=(
            P(None, "dp", None),
            P(None, "dp", None),
            P(None, "dp", None, None),
            P(None, "dp", None),
            P(None, "dp"),
            P("dp", "tensor"),
            P("dp", "tensor"),
            P("dp", "tensor"),
            P("dp", "tensor"),
            P("dp", "tensor"),
            P("dp", "tensor"),
            P("dp", "tensor"),
            P("dp", "tensor"),
            P("dp", "tensor"),
            P("dp", "tensor"),
            P("dp"),
            P("dp"),
            P("dp", "tensor"),
            P("dp", "tensor"),
            P("dp", "tensor"),
            P("tensor"),
            P(None, "dp", None),
        ),
        out_specs=(
            P(None, "dp", None),
            P(None, "dp", None),
            P("dp", "tensor"),
            P("dp", "tensor"),
            P("dp", "tensor"),
            P("dp", "tensor"),
            P("dp", "tensor"),
            P("dp", "tensor"),
            P("dp", "tensor"),
            P("dp", "tensor"),
            P("dp", "tensor"),
            P("dp", "tensor"),
            P("dp"),
            P("dp"),
            P("dp", "tensor"),
            P("dp", "tensor"),
            P("dp", "tensor"),
            P("tensor"),
        ),
        check_vma=False,
    )
```

```python
import functools

import jax
import jax.numpy as jnp
from jax import lax
from jax.experimental import pallas as pl
from jax.experimental.pallas import tpu as pltpu
from jax.sharding import PartitionSpec as P

HEAD_DIM = 64
DT = 4096
TXT = 256


EPSILON = 1e-06
MASKED = -1e30
ROPE_BASE = 10000.0
STRIP = 16
F32 = jnp.float32
BF16 = jnp.bfloat16


def image_layout(shapes, count):
    height = shapes[:, 0]
    stride_all = shapes[:, 1] + 1
    extent = height * stride_all
    finish = jnp.cumsum(extent)
    begin = finish - extent
    places = jnp.arange(count, dtype=jnp.int32)
    member = (places[:, None] >= begin[None, :]) & (places[:, None] < finish[None, :])
    member_int = member.astype(jnp.int32)
    inside = jnp.sum(member_int, axis=1)
    slot_ids = jnp.arange(shapes.shape[0], dtype=jnp.int32)
    segment = jnp.sum(member_int * slot_ids[None, :], axis=1)
    stride = jnp.sum(member_int * stride_all[None, :], axis=1) + 1 - inside
    offset = places - jnp.sum(member_int * begin[None, :], axis=1)
    return (member.astype(jnp.float32), segment, inside, offset // stride, offset % stride)


def rope_tables(row_pos, col_pos):
    quarter = HEAD_DIM // 4
    freq = ROPE_BASE ** (-jnp.arange(quarter, dtype=jnp.float32) / quarter)
    angles = jnp.stack(
        [
            row_pos.astype(jnp.float32)[:, None] * freq[None, :],
            col_pos.astype(jnp.float32)[:, None] * freq[None, :],
        ],
        axis=1,
    )
    return (jnp.cos(angles), jnp.sin(angles))


def dot_nn(left, right):
    return lax.dot_general(left, right, (((1,), (0,)), ((), ())), preferred_element_type=F32)


def dot_nt(left, right):
    return lax.dot_general(left, right, (((1,), (1,)), ((), ())), preferred_element_type=F32)


def dot_tn(left, right):
    return lax.dot_general(left, right, (((0,), (0,)), ((), ())), preferred_element_type=F32)


def struct(shape, dtype=BF16):
    return jax.ShapeDtypeStruct(shape, dtype)


def run(body, outs, ins, scratch=(), flops=0, traffic=0):
    return pl.pallas_call(
        body,
        out_shape=outs,
        in_specs=[pl.BlockSpec(memory_space=space) for _, space in ins],
        out_specs=[pl.BlockSpec(memory_space=pltpu.VMEM)] * len(outs),
        scratch_shapes=list(scratch),
        compiler_params=pltpu.CompilerParams(vmem_limit_bytes=48 * 2**20),
        cost_estimate=pl.CostEstimate(flops=flops, bytes_accessed=traffic, transcendentals=0),
    )(*[array for array, _ in ins])


def load(source, target, sem):
    copy = pltpu.make_async_copy(source, target, sem)
    copy.start()
    return copy


def wait_all(copies):
    for copy in copies:
        copy.wait()


def token_columns(member, mods, which, target):
    target[...] = dot_nn(member[...], mods[which]).astype(BF16)


def over_strips(rows, step):
    @pl.loop(0, rows // STRIP)
    def _(index):
        step(pl.ds(pl.multiple_of(index * STRIP, STRIP), STRIP))


def head_sum(values, blocks):
    high = values.astype(BF16)
    low = (values - high.astype(F32)).astype(BF16)
    return dot_nn(high, blocks) + dot_nn(low, blocks)


def head_blocks(width):
    row = lax.broadcasted_iota(jnp.int32, (width, width), 0) // HEAD_DIM
    column = lax.broadcasted_iota(jnp.int32, (width, width), 1) // HEAD_DIM
    return jnp.where(row == column, 1.0, 0.0).astype(BF16)


def swap_pairs(values):
    width = values.shape[1]
    quarter = HEAD_DIM // 4
    lane = lax.broadcasted_iota(jnp.int32, values.shape, 1)
    former = lax.rem(lane, 2 * quarter) < quarter
    return jnp.where(
        former, pltpu.roll(values, width - quarter, 1), pltpu.roll(values, quarter, 1)
    )


def head_norm(values, gain, blocks):
    scale = lax.rsqrt(head_sum(values * values, blocks) * (1.0 / HEAD_DIM) + EPSILON)
    return values * scale * gain


def head_norm_back(values, gain, grad, blocks):
    scale = lax.rsqrt(head_sum(values * values, blocks) * (1.0 / HEAD_DIM) + EPSILON)
    normed = values * scale
    grad_gain = jnp.sum(grad * normed, axis=0, keepdims=True)
    inner = grad * gain
    mean = head_sum(inner * normed, blocks) * (1.0 / HEAD_DIM)
    return scale * (inner - normed * mean), grad_gain


def row_scale(values):
    return lax.rsqrt(jnp.mean(values * values, axis=1, keepdims=True) + EPSILON)


MESH = pl.DeviceIdType.MESH
PAIR, ALONG_X, ALONG_Y = 1, 2, 4


def partner(mask):
    rank = lax.axis_index("dp")
    index = rank
    for bit in (1, 2, 4):
        flip = lax.rem(mask // bit, 2)
        index = index + flip * (bit - 2 * bit * lax.rem(rank // bit, 2))
    return index


def announce(masks, shifts, n_tensor):
    barrier = pltpu.get_barrier_semaphore()
    rank = lax.axis_index("tensor")
    for mask in masks:
        pl.semaphore_signal(
            barrier, inc=1, device_id={"dp": partner(mask)}, device_id_type=MESH
        )
    for shift in shifts:
        pl.semaphore_signal(
            barrier,
            inc=1,
            device_id={"tensor": lax.rem(rank + shift, n_tensor)},
            device_id_type=MESH,
        )


def greet(masks, shifts, n_tensor):
    announce(masks, shifts, n_tensor)
    pl.semaphore_wait(pltpu.get_barrier_semaphore(), len(masks) + len(shifts))


def send(source, target, sems, index, device):
    copy = pltpu.make_async_remote_copy(
        src_ref=source,
        dst_ref=target,
        send_sem=sems.at[(0,) + index],
        recv_sem=sems.at[(1,) + index],
        device_id=device,
        device_id_type=MESH,
    )
    copy.start()
    return copy


def gather_kernel(
    n_tensor, shard_tk, shard_tv, shard_qv, shard_ko, context, attn_own, ffn_own, q_own, k_own,
    t_own, w_adaln, captions,
    text_raw, text_key, text_value, qv, ko, cond_act, mods, attn_gain, ffn_gain, q_gain, k_gain, t_gain,
    small, small_all, product, sums, tk, tv, block, stage, block_sems, stage_sems, own_sems, shard_sems, small_sems, mod_sems, tensor_sems,
):
    rank, tensor_rank = lax.axis_index("dp"), lax.axis_index("tensor")
    masks = range(1, 8)
    shifts = range(1, n_tensor)
    greet(masks, shifts, n_tensor)
    small_copies = []
    images, slots = context.shape[0] * context.shape[1], context.shape[1]
    depth = w_adaln.shape[0]
    gain_size = attn_own.shape[1]
    heads = q_own.shape[1]
    small[...] = jnp.zeros_like(small)
    for index in range(8):
        for first in range(0, images, slots):
            small[index, first : first + slots, :] = context[
                first // slots, :, index * depth : (index + 1) * depth
            ]
        for row, own in ((16, attn_own), (18, ffn_own)):
            for place, first in enumerate(range(0, gain_size, depth)):
                size = min(depth, gain_size - first)
                small[index, row + place : row + place + 1, :size] = own[:, first : first + size]
        for place, own in enumerate((q_own, k_own, t_own)):
            small[index, 24:32, 8 * place : 8 * place + heads] = own[...]
    for mask in masks:
        small_copies.append(
            send(
                small.at[partner(mask)], small_all.at[rank], small_sems, (mask,),
                {"dp": partner(mask)},
            )
        )
    groups = ((shard_tk, tk), (shard_tv, tv), (shard_qv, qv), (shard_ko, ko))

    def rows_of(shard, index, first, size):
        return pl.ds(pl.multiple_of(index * shard.shape[0] + first, 32), size)

    firsts, seconds, pairs, locals_ = {}, {}, {}, []

    def step_1(number):
        shard, whole = groups[number]
        mine = whole.at[rows_of(shard, rank, 0, shard.shape[0])]
        firsts[number] = [
            send(shard, mine, shard_sems, (number, place), {"dp": partner(mask)})
            for place, mask in ((0, ALONG_X), (1, ALONG_Y))
        ]
        pairs[number] = [send(shard, mine, shard_sems, (number, 4), {"dp": partner(PAIR)})]
        local = pltpu.make_async_copy(shard, mine, own_sems.at[number])
        local.start()
        locals_.append(local)

    def step_2(number):
        shard, whole = groups[number]
        size = shard.shape[0]
        half = size // 2
        seconds[number] = []
        for place, mask, onward, start in ((0, ALONG_X, ALONG_Y, half), (1, ALONG_Y, ALONG_X, 0)):
            firsts[number][place].wait_recv()
            part = whole.at[rows_of(shard, partner(mask), start, half)]
            seconds[number].append(
                send(part, part, shard_sems, (number, 2 + place), {"dp": partner(onward)})
            )
            piece = whole.at[rows_of(shard, partner(mask), 0, size)]
            pairs[number].append(
                send(piece, piece, shard_sems, (number, 5 + place), {"dp": partner(PAIR)})
            )

    def step_3(number):
        shard, whole = groups[number]
        half = shard.shape[0] // 2
        for place, start in ((0, half), (1, 0)):
            seconds[number][place].wait_recv()
            part = whole.at[rows_of(shard, partner(ALONG_X + ALONG_Y), start, half)]
            pairs[number].append(
                send(part, part, shard_sems, (number, 7 + place), {"dp": partner(PAIR)})
            )

    def step_4(number):
        for copy in pairs[number]:
            copy.wait_recv()
        locals_[number].wait()

    count = captions.shape[0]

    def fetch(image, slot):
        return pltpu.make_async_copy(captions.at[image], block.at[slot], block_sems.at[slot])

    def store(image, slot):
        return [
            pltpu.make_async_copy(
                stage.at[slot, index], out.at[image], stage_sems.at[slot, index]
            )
            for index, out in enumerate((text_raw, text_key, text_value))
        ]

    def text_images(low, high):
        @pl.loop(low, high)
        def _(image):
            slot = lax.rem(image, 2)

            @pl.when(image < count - 1)
            def _():
                fetch(image + 1, 1 - slot).start()

            fetch(image, slot).wait()

            @pl.when(image >= 2)
            def _():
                wait_all(store(image - 2, slot))

            raw = dot_nn(block[slot], tk[...])
            stage[slot, 0] = raw.astype(BF16)
            stage[slot, 1] = head_norm(raw, t_gain[...], head_blocks(raw.shape[1])).astype(BF16)
            stage[slot, 2] = dot_nn(block[slot], tv[...]).astype(BF16)
            for copy in store(image, slot):
                copy.start()

    step_1(0)
    step_1(1)
    fetch(0, 0).start()
    small_all[rank] = small[rank]
    for copy in small_copies:
        copy.wait_recv()
    width = w_adaln.shape[1]
    contexts = small_all[:, 0:16, :].astype(F32).reshape(8 * 16, depth)
    cond_act[...] = jax.nn.silu(contexts).astype(BF16)
    product[...] = dot_nn(cond_act[...], w_adaln[...]).astype(BF16).reshape(8, 16, width)
    mod_copies = [
        send(
            product.at[partner(mask)], sums.at[mask], mod_sems, (mask,), {"dp": partner(mask)}
        )
        for mask in masks
    ]
    for row, out in ((16, attn_gain), (18, ffn_gain)):
        for index in range(8):
            for place, first in enumerate(range(0, gain_size, depth)):
                size = min(depth, gain_size - first)
                start = index * gain_size + first
                out[:, start : start + size] = small_all[
                    index, row + place : row + place + 1, :size
                ].astype(F32)
    turned = jnp.transpose(small_all[:, 24:32, :].astype(F32).reshape(HEAD_DIM, depth))
    for place, out in enumerate((q_gain, k_gain, t_gain)):
        for head in range(heads):
            out[:, head * HEAD_DIM : (head + 1) * HEAD_DIM] = turned[
                8 * place + head : 8 * place + head + 1, :
            ]
    step_2(0)
    step_2(1)
    sums[0] = product[rank]
    for copy in mod_copies:
        copy.wait_recv()
    total = sums[0].astype(F32)
    for mask in masks:
        total = total + sums[mask].astype(F32)
    mods[tensor_rank] = total.astype(BF16)
    tensor_copies = [
        send(
            mods.at[tensor_rank], mods.at[tensor_rank], tensor_sems, (shift,),
            {"tensor": lax.rem(tensor_rank + shift, n_tensor)},
        )
        for shift in shifts
    ]

    for number in (0, 1):
        step_3(number)
    step_1(2)
    step_1(3)
    for number in (0, 1):
        step_4(number)
    text_images(0, count // 3)
    step_2(2)
    step_2(3)
    text_images(count // 3, 2 * count // 3)
    step_3(2)
    step_3(3)
    text_images(2 * count // 3, count)
    step_4(2)
    step_4(3)
    for image in (count - 2, count - 1):
        wait_all(store(image, image % 2))
    for copy in tensor_copies:
        copy.wait_recv()
    for number in range(4):
        for copy in firsts[number] + seconds[number] + pairs[number]:
            copy.wait_send()
    for copy in small_copies + mod_copies + tensor_copies:
        copy.wait_send()


ROUTES = ((0, 1, 2, ALONG_X, ALONG_Y), (1, 2, 1, ALONG_Y, ALONG_X))
REDUCE_STRIP = 32


def over_half(half, step):
    @pl.loop(0, half // REDUCE_STRIP)
    def _(index):
        step(pl.multiple_of(index * REDUCE_STRIP, REDUCE_STRIP))


class Reduce:
    def __init__(self, number, read, out, from_pair, out_2, in_2, out_3, in_3, sems):
        self.number, self.read, self.out, self.sems = number, read, out, sems
        self.from_pair, self.out_2, self.in_2, self.out_3, self.in_3 = (
            from_pair, out_2, in_2, out_3, in_3
        )
        self.half = out.shape[0] // 2
        self.copies, self.arriving = [], {}

    def pair_term(self, piece, low):
        there = pl.ds(low, REDUCE_STRIP)
        return self.read(piece, low) + self.from_pair[piece, there, :].astype(F32)

    def move(self, source, target, index, mask):
        return pltpu.make_async_remote_copy(
            src_ref=source,
            dst_ref=target,
            send_sem=self.sems.at[0, self.number, index],
            recv_sem=self.sems.at[1, self.number, index],
            device_id={"dp": partner(mask)},
            device_id_type=MESH,
        )

    def first(self, piece, source):
        return self.move(source, self.from_pair.at[piece], piece, PAIR)

    def second(self, piece, copy):
        copy.wait_recv()
        self.copies.append(copy)
        for side, close, far, first, last in ROUTES:
            if piece not in (close, 3):
                continue
            slot = 1 if piece == 3 else 0

            def step(low):
                self.out_2[side, slot, pl.ds(low, REDUCE_STRIP), :] = self.pair_term(
                    piece, pl.multiple_of(low + side * self.half, REDUCE_STRIP)
                ).astype(BF16)

            over_half(self.half, step)
            moved = self.move(
                self.out_2.at[side, slot], self.in_2.at[side, slot], 4 + 2 * side + slot, first
            )
            moved.start()
            self.arriving[side, slot] = moved
            self.copies.append(moved)

    def third(self):
        for side, close, far, first, last in ROUTES:
            self.arriving[side, 1].wait_recv()

            def step(low):
                here = pl.ds(low, REDUCE_STRIP)
                there = pl.multiple_of(low + side * self.half, REDUCE_STRIP)
                self.out_3[side, here, :] = (
                    self.pair_term(far, there) + self.in_2[side, 1, here, :].astype(F32)
                ).astype(BF16)

            over_half(self.half, step)
            moved = self.move(self.out_3.at[side], self.in_3.at[side], 8 + side, last)
            moved.start()
            self.arriving[side, 2] = moved
            self.copies.append(moved)

    def last(self):
        for side in (0, 1):
            self.arriving[side, 0].wait_recv()
            self.arriving[side, 2].wait_recv()

            def step(low):
                here = pl.ds(low, REDUCE_STRIP)
                there = pl.multiple_of(low + side * self.half, REDUCE_STRIP)
                self.out[pl.ds(there, REDUCE_STRIP), :] = (
                    self.pair_term(0, there)
                    + self.in_2[side, 0, here, :].astype(F32)
                    + self.in_3[side, here, :].astype(F32)
                )

            over_half(self.half, step)
        for copy in self.copies:
            copy.wait_send()


def reduce_scratch(depth, columns):
    half = depth // 2
    return [
        pltpu.VMEM((4, depth, columns), BF16),
        pltpu.VMEM((2, 2, half, columns), BF16),
        pltpu.VMEM((2, 2, half, columns), BF16),
        pltpu.VMEM((2, half, columns), BF16),
        pltpu.VMEM((2, half, columns), BF16),
    ]


def piece_reader(total, size):
    def read(piece, low):
        first = partner(2 * piece) * size + low
        return total[pl.ds(pl.multiple_of(first, 32), REDUCE_STRIP), :].astype(F32)

    return read


def reduce_firsts(reduce, total, size):
    copies = {}
    for piece in (3, 2, 1, 0):
        copies[piece] = reduce.first(piece, piece_of(total, 2 * piece + 1, size))
        copies[piece].start()
    return copies


def piece_of(total, mask, size):
    return total.at[pl.ds(pl.multiple_of(partner(mask) * size, 64), size)]


class TensorSum:
    def __init__(self, number, n_tensor, arrived, sems):
        self.number, self.n_tensor, self.arrived, self.sems = number, n_tensor, arrived, sems
        self.rank = lax.axis_index("tensor")
        self.size = arrived.shape[1]
        self.others = [
            (shift - 1, lax.rem(self.rank + shift, n_tensor)) for shift in range(1, n_tensor)
        ]

    def block(self, index):
        return pl.ds(pl.multiple_of(index * self.size, 16), self.size)

    def scatter(self, partial):
        self.partial = partial
        self.firsts = [
            send(
                partial.at[self.block(other)], self.arrived.at[place], self.sems,
                (2 * self.number, place), {"tensor": other},
            )
            for place, other in self.others
        ]

    def add(self, out, whole):
        for copy in self.firsts:
            copy.wait_recv()

        @pl.loop(0, self.size // STRIP)
        def _(index):
            low = pl.multiple_of(index * STRIP, STRIP)
            there = pl.ds(pl.multiple_of(self.rank * self.size + low, STRIP), STRIP)
            total = self.partial[there, :].astype(F32)
            for place, _ in self.others:
                total = total + self.arrived[place, pl.ds(low, STRIP), :].astype(F32)
            out[there if whole else pl.ds(low, STRIP), :] = total.astype(BF16)

        for copy in self.firsts:
            copy.wait_send()

    def gather(self, out):
        mine = out.at[self.block(self.rank)]
        self.seconds = [
            send(mine, mine, self.sems, (2 * self.number + 1, place), {"tensor": other})
            for place, other in self.others
        ]

    def finish(self):
        for copy in self.seconds:
            copy.wait()


def tensor_kernel(n_tensor, partial, out, arrived, sems):
    greet((), range(1, n_tensor), n_tensor)
    total = TensorSum(0, n_tensor, arrived, sems)
    total.scatter(partial)
    total.add(out, True)
    total.gather(out)
    total.finish()


def emit_kernel(qv, ko, text, *rest):
    count = (len(rest) - 11) // 2
    plain, rest = rest[:count], rest[count:]
    query, key, value, out, text_key, text_value = rest[:6]
    plain_out, (held, turned_key, turned_value, first, sems) = rest[6 : 6 + count], rest[6 + count :]
    width = query.shape[1]
    incoming = load(text, held, first)
    pairs = [
        (qv.at[:, :width], query), (ko.at[:, :width], key), (qv.at[:, width:], value),
        (ko.at[:, width:], out),
    ] + list(zip(plain, plain_out))
    copies = [load(source, target, sems.at[i]) for i, (source, target) in enumerate(pairs)]
    incoming.wait()
    turned_key[...] = jnp.transpose(held[:width, :])
    turned_value[...] = jnp.transpose(held[width:, :])
    copies.append(load(turned_key, text_key, sems.at[len(pairs)]))
    copies.append(load(turned_value, text_value, sems.at[len(pairs) + 1]))
    wait_all(copies)


def exchange(body, outs, ins, scratch, collective, vmem=48):
    spaces = [space for _, space in outs]
    return pl.pallas_call(
        body,
        out_shape=[shape for shape, _ in outs],
        in_specs=[pl.BlockSpec(memory_space=space) for _, space in ins],
        out_specs=[pl.BlockSpec(memory_space=space) for space in spaces],
        scratch_shapes=scratch,
        compiler_params=pltpu.CompilerParams(
            collective_id=collective, has_side_effects=True, vmem_limit_bytes=vmem * 2**20
        ),
    )(*[array for array, _ in ins])


def project_kernel(
    tokens, member, gain, q_gain, k_gain, cosine, sine, mods, whole_a, whole_b,
    attn_in, query_raw, key_raw, query_rot, key_rot, value, mat_a, mat_b, mod, sems
):
    copies = [load(whole_a, mat_a, sems.at[0]), load(whole_b, mat_b, sems.at[1])]
    width = q_gain.shape[1]
    token_columns(member, mods, 0, mod)
    blocks = head_blocks(width)

    def step(at):
        x = tokens[at, :].astype(F32)
        normed = x * row_scale(x)
        attn_in[at, :] = (normed * gain[...] * (1.0 + mod[at, :].astype(F32))).astype(BF16)

    over_strips(tokens.shape[0], step)
    wait_all(copies)
    query_raw[...] = dot_nn(attn_in[...], mat_a[:, :width])
    key_raw[...] = dot_nn(attn_in[...], mat_b[:, :width])
    value[...] = dot_nn(attn_in[...], mat_a[:, width:]).astype(BF16)
    for raw, head_gain, out in ((query_raw, q_gain, query_rot), (key_raw, k_gain, key_rot)):
        normed = head_norm(raw[...], head_gain[...], blocks)
        out[...] = (normed * cosine[...] + swap_pairs(normed) * sine[...]).astype(BF16)


def text_kernel(
    live, source, captions, gain, whole_k, whole_v,
    text_raw, text_key, text_value, mat_k, mat_v, sems
):
    image = pl.program_id(0)

    @pl.when(image == 0)
    def _():
        wait_all([load(whole_k, mat_k, sems.at[0]), load(whole_v, mat_v, sems.at[1])])

    @pl.when(live[image] > 0)
    def _():
        raw = dot_nn(captions[0], mat_k[...])
        text_raw[0] = raw.astype(BF16)
        text_key[0] = head_norm(raw, gain[...], head_blocks(raw.shape[1])).astype(BF16)
        text_value[0] = dot_nn(captions[0], mat_v[...]).astype(BF16)


def softmax(scores, allowed, rows_live):
    scores = jnp.where(allowed, scores, MASKED)
    expo = jnp.where(allowed, jnp.exp(scores - jnp.max(scores, axis=1, keepdims=True)), 0.0)
    total = jnp.sum(expo, axis=1, keepdims=True)
    if rows_live is not None:
        total = jnp.where(rows_live, total, 1.0)
    return expo / total


def attend_kernel(
    micro, scale, live, text_len, query, key, value, text_key_far, text_value_far,
    self_id, self_row, segment, gate, whole_b, mixed, cross_out, whole,
    mat_b, text_key, text_value, self_out, sem, sems
):
    text_copies = [
        load(text_key_far, text_key, sems.at[0]), load(text_value_far, text_value, sems.at[1])
    ]
    copies = [load(whole_b, mat_b, sem)]
    rows, width = query.shape
    count = rows // micro
    slots = text_key.shape[0] // micro
    heads = width // HEAD_DIM
    cross_out[...] = jnp.zeros_like(cross_out)

    for batch in range(micro):
        at = slice(batch * count, (batch + 1) * count)
        allowed = self_id[at, :] == self_row[batch : batch + 1, :]
        for head in range(heads):
            lanes = slice(head * HEAD_DIM, (head + 1) * HEAD_DIM)
            scores = dot_nt(query[at, lanes], key[at, lanes]) * scale
            probs = softmax(scores, allowed, None).astype(BF16)
            self_out[at, lanes] = dot_nn(probs, value[at, lanes])
    wait_all(text_copies)

    @pl.loop(0, micro * slots)
    def _(image):
        @pl.when(live[image] > 0)
        def _():
            at = pl.ds(pl.multiple_of((image // slots) * count, count), count)
            mine = segment[at, :] == lax.rem(image, slots)
            column = lax.broadcasted_iota(jnp.int32, (count, TXT), 1)
            allowed = mine & (column < text_len[image])
            for head in range(heads):
                lanes = slice(head * HEAD_DIM, (head + 1) * HEAD_DIM)
                scores = dot_nt(query[at, lanes], text_key[image, :, lanes]) * scale
                probs = softmax(scores, allowed, mine).astype(BF16)
                cross_out[at, lanes] += dot_nn(probs, text_value[image, :, lanes])

    mixed[...] = (self_out[...] + gate[...] * cross_out[...]).astype(BF16)
    wait_all(copies)
    whole[...] = dot_nt(mixed[...], mat_b[:, width:]).astype(BF16)


def feed_kernel(
    tokens, member, gain, cotangent, mods, attn_out, whole_f,
    hidden, ffn_in, inner, grad_gate, grad_up, grad_out, whole,
    mat, mod_1, mod_2, mod_3, sem
):
    copies = [load(whole_f, mat, sem)]
    units = inner.shape[1]
    mat_a, mat_b, mat_c = [mat.at[:, i * units : (i + 1) * units] for i in range(3)]
    token_columns(member, mods, 1, mod_1)
    token_columns(member, mods, 2, mod_2)
    token_columns(member, mods, 3, mod_3)

    def step(at):
        gate_attn = jnp.tanh(mod_1[at, :].astype(F32))
        state = tokens[at, :].astype(F32) + gate_attn * attn_out[at, :].astype(F32)
        hidden[at, :] = state
        normed = state * row_scale(state)
        ffn_in[at, :] = (normed * gain[...] * (1.0 + mod_2[at, :].astype(F32))).astype(BF16)
        gate_ffn = jnp.tanh(mod_3[at, :].astype(F32))
        grad_out[at, :] = (gate_ffn * cotangent[at, :].astype(F32)).astype(BF16)

    rows = tokens.shape[0]
    over_strips(rows, step)
    wait_all(copies)
    chunk = 256
    for first in range(0, units, chunk):
        span = slice(first, first + chunk)
        gate = dot_nn(ffn_in[...], mat_a[:, span])
        up = dot_nn(ffn_in[...], mat_b[:, span])
        grad_inner = dot_nn(grad_out[...], mat_c[:, span])
        turn = jax.nn.sigmoid(gate)
        active = gate * turn
        inner[:, span] = (active * up).astype(BF16)
        grad_up[:, span] = (grad_inner * active).astype(BF16)
        slope = turn * (1.0 + gate * (1.0 - turn))
        grad_gate[:, span] = (grad_inner * up * slope).astype(BF16)
    width = tokens.shape[1]
    for first in range(0, width, 512):
        span = slice(first, first + 512)
        whole[:, span] = (
            dot_nt(grad_gate[...], mat_a[span, :]) + dot_nt(grad_up[...], mat_b[span, :])
        ).astype(BF16)


def feed_grad_kernel(grad_out, inner, ffn_in, grad_gate, grad_up, total):
    units = inner.shape[1]
    step = 256
    for index, (left, right) in enumerate(
        ((ffn_in, grad_gate), (ffn_in, grad_up), (grad_out, inner))
    ):
        for first in range(0, units, step):
            out = slice(index * units + first, index * units + first + step)
            total[:, out] = dot_tn(left[...], right[:, first : first + step]).astype(BF16)


def feed_out_kernel(inner, whole_f, partial, mat, sem):
    units = inner.shape[1]
    copy = load(whole_f.at[:, 2 * units : 3 * units], mat, sem)
    copy.wait()
    for first in range(0, partial.shape[1], 512):
        span = slice(first, first + 512)
        partial[:, span] = dot_nt(inner[...], mat[span, :]).astype(BF16)


def modulate_back(values, gain, shift, grad):
    scale = row_scale(values)
    normed = values * scale
    inner = grad * gain * (1.0 + shift)
    mean = jnp.mean(inner * normed, axis=1, keepdims=True)
    return scale * (inner - normed * mean), grad * normed


def mixed_grad_kernel(
    hidden, member, gain, cotangent, mods, grad_in, whole_b,
    grad_hidden, grad_out, grad_mixed, mat_b, mod_1, mod_2, sem
):
    copies = [load(whole_b, mat_b, sem)]
    token_columns(member, mods, 1, mod_1)
    token_columns(member, mods, 2, mod_2)

    def step(at):
        back, _ = modulate_back(
            hidden[at, :], gain[...], mod_2[at, :].astype(F32), grad_in[at, :].astype(F32)
        )
        total = cotangent[at, :].astype(F32) + back
        grad_hidden[at, :] = total
        grad_out[at, :] = (jnp.tanh(mod_1[at, :].astype(F32)) * total).astype(BF16)

    over_strips(hidden.shape[0], step)
    wait_all(copies)
    width = grad_mixed.shape[1]
    grad_mixed[...] = dot_nn(grad_out[...], mat_b[:, width:])


def feed_exchange_kernel(
    n_tensor, tokens, member, gain, cotangent, mods, attn_out, whole_f, whole_ko,
    hidden, grad_hidden, grad_attn_out, grad_mixed, grad_in, ffn_out_rows, *rest
):
    outs, rest = rest[:3], rest[3:]
    (
        ffn_in, inner, grad_gate, grad_up, grad_out, ffn_part, out_part,
        mat, mod_1, mod_2, mod_3, *rest
    ) = rest
    totals, rest = rest[:3], rest[3:]
    buffers, (arrived_1, arrived_2, sem, mat_sem, sems, tensor_sems) = rest[:15], rest[15:]
    announce((PAIR, ALONG_X, ALONG_Y), range(1, n_tensor), n_tensor)
    feed_kernel(
        tokens, member, gain, cotangent, mods, attn_out, whole_f,
        hidden, ffn_in, inner, grad_gate, grad_up, grad_out, ffn_part,
        mat, mod_1, mod_2, mod_3, sem,
    )
    pl.semaphore_wait(pltpu.get_barrier_semaphore(), 3 + n_tensor - 1)
    sum_in = TensorSum(0, n_tensor, arrived_1, tensor_sems)
    sum_in.scatter(ffn_part)
    size = outs[0].shape[0]
    reduces, firsts = [], []
    for number, (left, right) in enumerate(
        ((ffn_in, grad_gate), (ffn_in, grad_up), (grad_out, inner))
    ):
        total = totals[number]
        for first in range(0, total.shape[1], 256):
            span = slice(first, first + 256)
            total[:, span] = dot_tn(left[...], right[:, span]).astype(BF16)
        reduce = Reduce(
            number, piece_reader(total, size), outs[number],
            *buffers[5 * number : 5 * number + 5], sems,
        )
        reduces.append(reduce)
        firsts.append(reduce_firsts(reduce, total, size))
    units = inner.shape[1]
    for first in range(0, out_part.shape[1], 512):
        span = slice(first, first + 512)
        out_part[:, span] = dot_nt(inner[...], mat[span, 2 * units :]).astype(BF16)
    sum_out = TensorSum(1, n_tensor, arrived_2, tensor_sems)
    for piece in (3, 2, 1, 0):
        for number in range(3):
            reduces[number].second(piece, firsts[number][piece])
    sum_in.add(grad_in, True)
    sum_in.gather(grad_in)
    for reduce in reduces:
        reduce.third()
    sum_in.finish()
    sum_out.scatter(out_part)
    head_width = grad_mixed.shape[1]
    copy = load(whole_ko.at[:, head_width:], mat.at[:, :head_width], mat_sem)

    def step(at):
        back, _ = modulate_back(
            hidden[at, :], gain[...], mod_2[at, :].astype(F32), grad_in[at, :].astype(F32)
        )
        total = cotangent[at, :].astype(F32) + back
        grad_hidden[at, :] = total
        grad_attn_out[at, :] = (jnp.tanh(mod_1[at, :].astype(F32)) * total).astype(BF16)

    over_strips(hidden.shape[0], step)
    copy.wait()
    grad_mixed[...] = dot_nn(grad_attn_out[...], mat[:, :head_width])
    for reduce in reduces:
        reduce.last()
    sum_out.add(ffn_out_rows, False)


def attend_back_kernel(
    micro, scale, live, text_len, grad_mixed, cross_out, query, key, value, text_key_far,
    text_value_far, text_raw_far, query_raw, key_raw, q_gain, k_gain, t_gain, cosine, sine, self_id, self_row, segment,
    gate, grad_query_b, grad_key_b, grad_value_b, grad_text, gain_sums,
    grad_query, grad_key, grad_cross, grad_turned, gain_turned, text_key, text_value, text_raw, sems,
    *held
):
    held, held_sems = held[:-1], held[-1]
    early = (grad_mixed, cross_out, query, key, value, query_raw, key_raw, cosine, sine)
    copies = [load(far, here, held_sems.at[i]) for i, (far, here) in enumerate(zip(early, held))]
    grad_mixed, cross_out, query, key, value, query_raw, key_raw, cosine, sine = held
    text_copies = [
        load(far, here, sems.at[index])
        for index, (far, here) in enumerate(
            ((text_key_far, text_key), (text_value_far, text_value), (text_raw_far, text_raw))
        )
    ]
    rows, width = query.shape
    count = rows // micro
    slots = text_key.shape[0] // micro
    heads = width // HEAD_DIM
    blocks = head_blocks(width)
    wait_all(copies)
    gate_sum = jnp.sum(grad_mixed[...] * cross_out[...], axis=0, keepdims=True)
    gain_sums[...] = jnp.zeros_like(gain_sums)
    gain_sums[3:4, :] = gate_sum * (1.0 - gate[...] * gate[...])
    grad_cross[...] = (gate[...] * grad_mixed[...]).astype(BF16)
    gain_turned[...] = jnp.zeros_like(gain_turned)
    gain_column = jnp.transpose(jnp.broadcast_to(t_gain[...], (8, width)))[:, :1]
    for batch in range(micro):
        at = slice(batch * count, (batch + 1) * count)
        allowed = self_id[at, :] == self_row[batch : batch + 1, :]
        for head in range(heads):
            lanes = slice(head * HEAD_DIM, (head + 1) * HEAD_DIM)
            q, k = query[at, lanes], key[at, lanes]
            grad = grad_mixed[at, lanes].astype(BF16)
            probs = softmax(dot_nt(q, k) * scale, allowed, None)
            grad_probs = dot_nt(grad, value[at, lanes])
            mean = jnp.sum(probs * grad_probs, axis=1, keepdims=True)
            scaled = (probs * (grad_probs - mean) * scale).astype(BF16)
            grad_query[at, lanes] = dot_nn(scaled, k)
            grad_key[at, lanes] = dot_tn(scaled, q)
            grad_value_b[at, lanes] = dot_tn(probs.astype(BF16), grad).astype(BF16)

    wait_all(text_copies)

    @pl.loop(0, micro * slots)
    def _(image):
        @pl.when(live[image] == 0)
        def _():
            grad_text[:, pl.ds(pl.multiple_of(image * TXT, TXT), TXT)] = jnp.zeros(
                (2 * width, TXT), BF16
            )

        @pl.when(live[image] > 0)
        def _():
            at = pl.ds(pl.multiple_of((image // slots) * count, count), count)
            tokens = pl.ds(pl.multiple_of(image * TXT, TXT), TXT)
            mine = segment[at, :] == lax.rem(image, slots)
            column = lax.broadcasted_iota(jnp.int32, (count, TXT), 1)
            allowed = mine & (column < text_len[image])
            for head in range(heads):
                lanes = slice(head * HEAD_DIM, (head + 1) * HEAD_DIM)
                q, k = query[at, lanes], text_key[image, :, lanes]
                grad = grad_cross[at, lanes]
                probs = softmax(dot_nt(q, k) * scale, allowed, mine)
                grad_probs = dot_nt(grad, text_value[image, :, lanes])
                mean = jnp.sum(probs * grad_probs, axis=1, keepdims=True)
                scaled = (probs * (grad_probs - mean) * scale).astype(BF16)
                grad_query[at, lanes] += dot_nn(scaled, k)
                grad_turned[lanes, :] = dot_tn(q, scaled)
                grad_text[width + head * HEAD_DIM : width + (head + 1) * HEAD_DIM, tokens] = dot_tn(
                    grad, probs.astype(BF16)
                ).astype(BF16)
            by_head = (heads, HEAD_DIM, TXT)
            raw = jnp.transpose(text_raw[image].astype(F32)).reshape(by_head)
            norm = lax.rsqrt(jnp.mean(raw * raw, axis=1, keepdims=True) + EPSILON)
            normed = raw * norm
            upper = grad_turned[...].reshape(by_head)
            gain_turned[...] += (upper * normed).reshape(width, TXT)
            inner = upper * gain_column.reshape(heads, HEAD_DIM, 1)
            mean = jnp.mean(inner * normed, axis=1, keepdims=True)
            back = norm * (inner - normed * mean)
            grad_text[:width, tokens] = back.reshape(width, TXT).astype(BF16)

    for index, (grad, raw, gain, out) in enumerate(
        (
            (grad_query, query_raw, q_gain, grad_query_b),
            (grad_key, key_raw, k_gain, grad_key_b),
        )
    ):
        turned = grad[...] * cosine[...] + swap_pairs(grad[...] * sine[...])
        back, gain_sum = head_norm_back(raw[...], gain[...], turned, blocks)
        out[...] = back.astype(BF16)
        gain_sums[index : index + 1, :] = gain_sum
    text_sums = jnp.sum(gain_turned[...], axis=1, keepdims=True)
    gain_sums[2:3, :] = jnp.transpose(jnp.broadcast_to(text_sums, (width, 128)))[:1, :]


def attn_grad_kernel(
    attn_in, grad_query, grad_key, grad_value, grad_out, mixed, whole_a, whole_b,
    total_a, total_b, whole, mat_a, mat_b, pair, sems
):
    copies = [load(whole_a, mat_a, sems.at[0]), load(whole_b, mat_b, sems.at[1])]
    width = grad_query.shape[1]
    pair[:, :width] = grad_query[...]
    pair[:, width:] = grad_value[...]
    wait_all(copies)
    for first in range(0, whole.shape[1], 512):
        span = slice(first, first + 512)
        whole[:, span] = (
            dot_nt(pair[...], mat_a[span, :]) + dot_nt(grad_key[...], mat_b[span, :width])
        ).astype(BF16)
    for first in range(0, 2 * width, 256):
        span = slice(first, first + 256)
        total_a[:, span] = dot_tn(attn_in[...], pair[:, span]).astype(BF16)
    total_b[:, :width] = dot_tn(attn_in[...], grad_key[...]).astype(BF16)
    total_b[:, width:] = dot_tn(grad_out[...], mixed[...]).astype(BF16)


def last_exchange_kernel(
    n_tensor, captions, grad_text, total_qv, total_ko, attn_part, tokens, hidden, grad_hidden, member, attn_gain, ffn_gain, cotangent, mods, ffn_grad, attn_out,
    cond_act, gain_sums, ffn_rows,
    out_qv, out_ko, out_text, result, grad_tokens, grad_adaln,
    own_attn, own_ffn, own_query, own_key, own_text, own_gate, *rest
):
    buffers, rest = rest[:15], rest[15:]
    (
        text_total, block, grad_in, ffn_out, ffn_mod, grad_mod, arrived, mod_a, mod_b, work_grad,
        sums, all_mod, all_sums, heads_turned,
        block_sems, sems, tensor_sems, small_sems,
    ) = rest
    masks = range(1, 8)
    greet(masks, range(1, n_tensor), n_tensor)
    sum_in = TensorSum(0, n_tensor, arrived, tensor_sems)
    sum_in.scatter(attn_part)
    sum_out = TensorSum(1, n_tensor, arrived, tensor_sems)
    ffn_out[sum_out.block(sum_out.rank), :] = ffn_rows[...]
    sum_out.gather(ffn_out)
    size = out_qv.shape[0]
    depth = out_text.shape[1]
    reduces, firsts = [], []
    for number, (total, out) in enumerate(((total_qv, out_qv), (total_ko, out_ko))):
        reduce = Reduce(
            number, piece_reader(total, size), out, *buffers[5 * number : 5 * number + 5], sems
        )
        reduces.append(reduce)
        firsts.append(reduce_firsts(reduce, total, size))

    def fetch(mask, slot):
        columns = pl.ds(pl.multiple_of(partner(mask) * depth, 128), depth)
        return pltpu.make_async_copy(
            captions.at[:, columns], block.at[slot], block_sems.at[slot]
        )

    def mask_at(place):
        return 7 - 2 * place + 7 * (place // 4)

    fetch(7, 0).start()

    def read_text(piece, low):
        return text_total[2 * piece, pl.ds(low, REDUCE_STRIP), :].astype(F32)

    text = Reduce(2, read_text, out_text, *buffers[10:], sems)

    def work(low, high):
        @pl.loop(low, high)
        def _(place):
            slot = lax.rem(place, 2)
            mask = mask_at(place)

            @pl.when(place < 7)
            def _():
                fetch(mask_at(place + 1), 1 - slot).start()

            fetch(mask, slot).wait()
            for first in range(0, grad_text.shape[0], 256):
                span = slice(first, first + 256)
                text_total[mask, span, :] = dot_nn(grad_text[span, :], block[slot]).astype(BF16)

    work(0, 2)
    for piece in (3, 2):
        text.first(piece, text_total.at[2 * piece + 1]).start()
    for piece in (3, 2, 1, 0):
        for number in range(2):
            reduces[number].second(piece, firsts[number][piece])
    work(2, 4)
    text_firsts = {}
    for piece in (3, 2, 1, 0):
        text_firsts[piece] = text.first(piece, text_total.at[2 * piece + 1])
    text_firsts[1].start()
    text_firsts[0].start()
    sum_in.add(grad_in, True)
    sum_in.gather(grad_in)
    for reduce in reduces:
        reduce.third()
    work(4, 5)
    text.second(3, text_firsts[3])
    work(5, 6)
    text.second(2, text_firsts[2])
    work(6, 7)
    text.second(1, text_firsts[1])
    work(7, 8)
    text.second(0, text_firsts[0])
    text.third()
    sums[...] = jnp.zeros_like(sums)
    sum_in.finish()
    sum_out.finish()
    output_kernel(
        hidden, member, ffn_gain, cotangent, mods, ffn_out, ffn_grad,
        result, ffn_mod, sums.at[1:2, :], mod_a, mod_b, work_grad,
    )
    input_kernel(
        tokens, member, attn_gain, grad_hidden, ffn_mod, mods, grad_in, attn_out,
        grad_tokens, grad_mod, sums.at[0:1, :], mod_a, mod_b, work_grad,
    )
    head_width = gain_sums.shape[1]
    for row in range(4):
        sums[2:3, row * head_width : (row + 1) * head_width] = gain_sums[row : row + 1, :]
    rank = lax.axis_index("dp")
    copies = []
    for mask in masks:
        device = {"dp": partner(mask)}
        copies.append(send(grad_mod, all_mod.at[rank], small_sems, (0, mask), device))
        copies.append(send(sums, all_sums.at[mask], small_sems, (1, mask), device))
    all_mod[rank] = grad_mod[...]
    for reduce in reduces:
        reduce.last()
    text.last()
    for copy in copies:
        copy.wait_recv()
    added = sums[...]
    for mask in masks:
        added = added + all_sums[mask]
    grad_adaln[...] = dot_tn(cond_act[...], all_mod[...].reshape(8 * 16, all_mod.shape[2]))
    gain_size = own_attn.shape[1]
    for row, out in ((0, own_attn), (1, own_ffn)):
        out[...] = added[row : row + 1, :gain_size]
        for index in range(1, 8):
            part = added[row : row + 1, index * gain_size : (index + 1) * gain_size]
            out[...] = jnp.where(rank == index, part, out[...])
    heads = own_query.shape[1]
    for place, out in enumerate((own_query, own_key, own_text)):
        for head in range(heads):
            first = place * head_width + head * HEAD_DIM
            heads_turned[head : head + 1, :HEAD_DIM] = added[2:3, first : first + HEAD_DIM]
        turned = jnp.transpose(heads_turned[...])
        part = out.shape[0]
        out[...] = turned[:part, :heads]
        for index in range(1, 8):
            here = turned[index * part : (index + 1) * part, :heads]
            out[...] = jnp.where(rank == index, here, out[...])
    for head in range(heads):
        first = 3 * head_width + head * HEAD_DIM
        own_gate[head : head + 1, :] = jnp.sum(
            added[2:3, first : first + HEAD_DIM], axis=1, keepdims=True
        )
    for copy in copies:
        copy.wait_send()


def segment_sum(member, values):
    high = values.astype(BF16)
    rest = values - high.astype(F32)
    middle = rest.astype(BF16)
    low = (rest - middle.astype(F32)).astype(BF16)
    return dot_tn(member, high) + dot_tn(member, middle) + dot_tn(member, low)


def output_kernel(
    hidden, member, gain, cotangent, mods, ffn_out, grad_in,
    result, grad_mod, grad_gain, mod_2, mod_3, grad
):
    token_columns(member, mods, 2, mod_2)
    token_columns(member, mods, 3, mod_3)
    rank = lax.axis_index("tensor")
    grad_gain[...] = jnp.zeros_like(grad_gain)

    def step(at):
        state = hidden[at, :]
        gate = jnp.tanh(mod_3[at, :].astype(F32))
        out = ffn_out[at, :].astype(F32)
        result[at, :] = (state + gate * out).astype(BF16)
        up = grad_in[at, :].astype(F32)
        product = up * state * row_scale(state)
        grad_gain[...] += jnp.sum(
            product * (1.0 + mod_2[at, :].astype(F32)), axis=0, keepdims=True
        )
        grad_gate = cotangent[at, :].astype(F32) * out * (1.0 - gate * gate)
        grad[at, :] = jnp.where(rank == 2, product * gain[...], grad_gate)

    over_strips(hidden.shape[0], step)
    grad_mod[...] = segment_sum(member[...], grad[...])


def input_kernel(
    tokens, member, gain, grad_hidden, other_mod, mods, grad_in, attn_out,
    grad_tokens, grad_mod, grad_gain, mod_0, mod_1, grad
):
    token_columns(member, mods, 0, mod_0)
    token_columns(member, mods, 1, mod_1)
    rank = lax.axis_index("tensor")
    grad_gain[...] = jnp.zeros_like(grad_gain)

    def step(at):
        shift = mod_0[at, :].astype(F32)
        upper = grad_hidden[at, :]
        back, product = modulate_back(
            tokens[at, :].astype(F32), gain[...], shift, grad_in[at, :].astype(F32)
        )
        grad_tokens[at, :] = (upper + back).astype(BF16)
        grad_gain[...] += jnp.sum(product * (1.0 + shift), axis=0, keepdims=True)
        gate = jnp.tanh(mod_1[at, :].astype(F32))
        grad_gate = upper * attn_out[at, :].astype(F32) * (1.0 - gate * gate)
        grad[at, :] = jnp.where(rank == 0, product * gain[...], grad_gate)

    over_strips(tokens.shape[0], step)
    own = segment_sum(member[...], grad[...])
    grad_mod[...] = jnp.where(rank < 2, own, other_mod[...]).astype(BF16)


def shards(
    n_dp,
    n_tensor,
    tokens,
    context,
    captions,
    shapes,
    text_len,
    w_query,
    w_key,
    w_value,
    w_out,
    w_text_key,
    w_text_value,
    w_gate,
    w_up,
    w_down,
    w_adaln,
    gain_attn,
    gain_ffn,
    gain_query,
    gain_key,
    gain_text,
    cross_gate,
    cotangent,
):
    parts = 8 if n_dp == 8 else 1
    micro, count, width = tokens.shape
    slots = shapes.shape[1]
    rows = micro * count
    images = micro * slots
    heads = w_query.shape[1] // HEAD_DIM
    local = heads * HEAD_DIM
    units = w_gate.shape[1]
    scale = HEAD_DIM ** (-0.5)
    dp_rank = lax.axis_index("dp")
    padded = 16
    vmem, smem, anywhere = pltpu.VMEM, pltpu.SMEM, pl.ANY
    dma = pltpu.SemaphoreType.DMA

    def inside(*arrays):
        return [(array, vmem) for array in arrays]

    def scalars(*arrays):
        return [(array, smem) for array in arrays]

    def outside(*arrays):
        return [(array, anywhere) for array in arrays]

    def after(values, earlier):
        return lax.optimization_barrier((list(values), list(earlier)))[0]

    def gathered(shard):
        return lax.all_gather(shard, "dp", axis=0, tiled=True)

    def scattered(whole):
        return lax.psum_scatter(whole, "dp", scatter_dimension=0, tiled=True).astype(F32)

    part_rows = rows // n_tensor
    arrived = vmem((n_tensor - 1, part_rows, width), BF16)

    def tensor_sum(partial):
        (out,) = exchange(
            functools.partial(tensor_kernel, n_tensor),
            [(struct((rows, width)), vmem)],
            inside(partial),
            [arrived, dma((2, 2, n_tensor - 1))],
            1,
        )
        return out

    gain_list = (gain_attn, gain_ffn, gain_query, gain_key, gain_text)
    cond_rows, span = w_adaln.shape
    shard_qv = jnp.concatenate([w_query, w_value], axis=1)
    shard_ko = jnp.concatenate([w_key, w_out], axis=1)
    shard_f = jnp.concatenate([w_gate, w_up, w_down], axis=1)
    if parts == 1:
        whole_tk, whole_tv = gathered(w_text_key), gathered(w_text_value)
        whole_qv, whole_ko = gathered(shard_qv), gathered(shard_ko)
        gains = [lax.all_gather(gain.astype(F32), "dp", axis=0, tiled=True) for gain in gain_list]
        attn_gain, ffn_gain = [gain.reshape(1, width) for gain in gains[:2]]
        query_gain, key_gain, text_gain = [gain.T.reshape(1, local) for gain in gains[2:]]
        context_all = gathered(context.reshape(images, -1))
        cond_cols = lax.dynamic_slice_in_dim(context_all, dp_rank * cond_rows, cond_rows, 1)
        cond_act = jax.nn.silu(cond_cols.astype(F32)).astype(BF16)
        mod_part = scattered(dot_nn(cond_act, w_adaln)).astype(BF16)
        mods = lax.all_gather(mod_part, "tensor", axis=0)
        mods = jnp.pad(mods, ((0, 0), (0, padded - images), (0, 0)))
    else:
        text_raw, text_key, text_value, whole_qv, whole_ko, cond_act, mods, *gains = exchange(
            functools.partial(gather_kernel, n_tensor),
            [(struct((images, TXT, local)), anywhere)] * 3
            + [(struct((width, 2 * local)), anywhere)] * 2
            + [
                (struct((parts * padded, cond_rows)), vmem),
                (struct((n_tensor, padded, span)), vmem),
            ]
            + [(struct((1, width), F32), vmem)] * 2
            + [(struct((1, local), F32), vmem)] * 3,
            outside(w_text_key, w_text_value, shard_qv, shard_ko)
            + inside(
                context, gain_attn[None], gain_ffn[None], gain_query, gain_key, gain_text, w_adaln
            )
            + outside(captions.reshape(images, TXT, DT)),
            [
                vmem((parts, 2 * padded, cond_rows), BF16),
                vmem((parts, 2 * padded, cond_rows), BF16),
                vmem((parts, padded, span), BF16),
                vmem((parts, padded, span), BF16),
                vmem((DT, local), BF16),
                vmem((DT, local), BF16),
                vmem((2, TXT, DT), BF16),
                vmem((2, 3, TXT, local), BF16),
                dma((2,)),
                dma((2, 3)),
                dma((4,)),
                dma((2, 4, 9)),
                dma((2, 8)),
                dma((2, 8)),
                dma((2, n_tensor)),
            ],
            2,
        )
        attn_gain, ffn_gain, query_gain, key_gain, text_gain = gains
        (shard_f,) = after([shard_f], [mods])
    whole_f = gathered(shard_f)
    layouts = [image_layout(shapes[i], count) for i in range(micro)]
    member, segment, inside_any, row_pos, col_pos = [
        jnp.stack([layout[j] for layout in layouts]) for j in range(5)
    ]
    cosine, sine = rope_tables(row_pos.reshape(rows), col_pos.reshape(rows))
    cosine = jnp.tile(jnp.stack([cosine, cosine], axis=2).reshape(rows, HEAD_DIM), (1, heads))
    sine = jnp.tile(jnp.stack([-sine, sine], axis=2).reshape(rows, HEAD_DIM), (1, heads))
    which = jnp.arange(micro, dtype=jnp.int32)
    member = jnp.where(
        (which[:, None] == which[None, :])[:, None, :, None], member[:, :, None, :], 0.0
    )
    member = jnp.pad(member.reshape(rows, images), ((0, 0), (0, padded - images))).astype(BF16)
    self_row = jnp.where(inside_any > 0, segment, slots)
    self_id = self_row.reshape(rows, 1)
    segment = segment.reshape(rows, 1)
    lens = text_len.reshape(images)
    used = shapes[:, :, 0] * (shapes[:, :, 1] + 1) > 0
    used = used | (jnp.arange(slots)[None, :] == 0)
    live = used.reshape(images).astype(jnp.int32)
    at = jnp.arange(images, dtype=jnp.int32)
    source = lax.cummax(jnp.where(live > 0, at, 0))
    gate = jnp.repeat(jnp.tanh(cross_gate.astype(F32)), HEAD_DIM)[None, :]
    token_rows = tokens.reshape(rows, width)
    grad_y = cotangent.reshape(rows, width)
    caption_images = captions.reshape(images, TXT, DT)

    attn_in, query_raw, key_raw, query_rot, key_rot, value = run(
        project_kernel,
        [struct((rows, width))]
        + [struct((rows, local), F32)] * 2
        + [struct((rows, local))] * 3,
        inside(token_rows, member, attn_gain, query_gain, key_gain, cosine, sine, mods)
        + outside(whole_qv, whole_ko),
        [
            vmem((width, 2 * local), BF16),
            vmem((width, 2 * local), BF16),
            vmem((rows, width), BF16),
            dma((2,)),
        ],
        flops=6 * rows * width * local,
        traffic=10 * 2**20,
    )

    if parts == 1:
        text_raw, text_key, text_value = pl.pallas_call(
            text_kernel,
            out_shape=[struct((images, TXT, local))] * 3,
            grid_spec=pltpu.PrefetchScalarGridSpec(
                num_scalar_prefetch=2,
                grid=(images,),
                in_specs=[
                    pl.BlockSpec((1, TXT, DT), lambda i, live, source: (source[i], 0, 0)),
                    pl.BlockSpec((1, local), lambda i, live, source: (0, 0)),
                ]
                + [pl.BlockSpec(memory_space=anywhere)] * 2,
                out_specs=[pl.BlockSpec((1, TXT, local), lambda i, live, source: (i, 0, 0))] * 3,
                scratch_shapes=[vmem((DT, local), BF16), vmem((DT, local), BF16), dma((2,))],
            ),
            compiler_params=pltpu.CompilerParams(vmem_limit_bytes=40 * 2**20),
            cost_estimate=pl.CostEstimate(
                flops=2 * images * TXT * DT * local, bytes_accessed=20 * 2**20, transcendentals=0
            ),
        )(live, source, caption_images, text_gain, whole_tk, whole_tv)

    wide = vmem((rows, width), BF16)
    mixed, cross_out, attn_part = run(
        functools.partial(attend_kernel, micro, scale),
        [struct((rows, local)), struct((rows, local), F32), struct((rows, width))],
        scalars(live, lens)
        + inside(query_rot, key_rot, value)
        + outside(text_key, text_value)
        + inside(self_id, self_row, segment, gate)
        + outside(whole_ko),
        [
            vmem((width, 2 * local), BF16),
            vmem((images, TXT, local), BF16),
            vmem((images, TXT, local), BF16),
            vmem((rows, local), F32),
            dma,
            dma((2,)),
        ],
        flops=2 * 2**30,
        traffic=12 * 2**20,
    )
    attn_out = tensor_sum(attn_part)

    size = width // parts
    if parts == 1:
        mat = vmem((width, 3 * units), BF16)
        hidden, ffn_in, inner, grad_gate, grad_up, grad_ffn_out, ffn_part = run(
            feed_kernel,
            [struct((rows, width), F32), struct((rows, width))]
            + [struct((rows, units))] * 3
            + [struct((rows, width))] * 2,
            inside(token_rows, member, ffn_gain, grad_y, mods, attn_out) + outside(whole_f),
            [mat, wide, wide, wide, dma],
            flops=10 * rows * width * units,
            traffic=20 * 2**20,
        )
        (grad_f,) = run(
            feed_grad_kernel,
            [struct((width, 3 * units))],
            inside(grad_ffn_out, inner, ffn_in, grad_gate, grad_up),
            flops=6 * rows * width * units,
            traffic=12 * 2**20,
        )
        (ffn_part,) = after([ffn_part], [grad_f])
        grad_ffn_in = tensor_sum(ffn_part)
        grad_f = scattered(grad_f)
        (ffn_out_part,) = run(
            feed_out_kernel,
            [struct((rows, width))],
            inside(inner) + outside(whole_f),
            [vmem((width, units), BF16), dma],
            flops=2 * rows * width * units,
            traffic=5 * 2**20,
        )
        ffn_out = lax.psum(ffn_out_part, "tensor")

        grad_hidden, grad_attn_out, grad_mixed = run(
            mixed_grad_kernel,
            [struct((rows, width), F32), struct((rows, width)), struct((rows, local), F32)],
            inside(hidden, member, ffn_gain, grad_y, mods, grad_ffn_in) + outside(whole_ko),
            [vmem((width, 2 * local), BF16), wide, wide, dma],
            flops=2 * rows * width * local,
            traffic=8 * 2**20,
        )
    else:
        hidden, grad_hidden, grad_attn_out, grad_mixed, grad_ffn_in, ffn_out_rows, *grad_f = exchange(
            functools.partial(feed_exchange_kernel, n_tensor),
            [
                (struct((rows, width), F32), vmem),
                (struct((rows, width), F32), vmem),
                (struct((rows, width)), vmem),
                (struct((rows, local), F32), vmem),
                (struct((rows, width)), vmem),
                (struct((part_rows, width)), vmem),
            ]
            + [(struct((size, units), F32), vmem)] * 3,
            inside(token_rows, member, ffn_gain, grad_y, mods, attn_out)
            + outside(whole_f, whole_ko),
            [wide]
            + [vmem((rows, units), BF16)] * 3
            + [wide] * 3
            + [vmem((width, 3 * units), BF16), wide, wide, wide]
            + [vmem((width, units), BF16)] * 3
            + reduce_scratch(size, units) * 3
            + [arrived, arrived, dma, dma, dma((2, 3, 10)), dma((2, 4, n_tensor - 1))],
            5,
            vmem=60,
        )

    tile = struct((rows, local))
    grad_query_b, grad_key_b, grad_value_b, grad_text_all, gain_sums = run(
        functools.partial(attend_back_kernel, micro, scale),
        [tile, tile, tile, struct((2 * local, images * TXT)), struct((8, local), F32)],
        scalars(live, lens)
        + outside(
            grad_mixed, cross_out, query_rot, key_rot, value, text_key, text_value, text_raw,
            query_raw, key_raw,
        )
        + inside(query_gain, key_gain, text_gain)
        + outside(cosine, sine)
        + inside(self_id, self_row, segment, gate),
        [
            vmem((rows, local), F32),
            vmem((rows, local), F32),
            vmem((rows, local), BF16),
            vmem((local, TXT), F32),
            vmem((local, TXT), F32),
            vmem((images, TXT, local), BF16),
            vmem((images, TXT, local), BF16),
            vmem((images, TXT, local), BF16),
            dma((3,)),
        ]
        + [vmem((rows, local), F32)] * 2
        + [vmem((rows, local), BF16)] * 3
        + [vmem((rows, local), F32)] * 4
        + [
            dma((9,)),
        ],
        flops=4 * 2**30,
        traffic=15 * 2**20,
    )

    total_qv, total_ko, attn_in_part = run(
        attn_grad_kernel,
        [struct((width, 2 * local))] * 2 + [struct((rows, width))],
        inside(attn_in, grad_query_b, grad_key_b, grad_value_b, grad_attn_out, mixed)
        + outside(whole_qv, whole_ko),
        [
            vmem((width, 2 * local), BF16),
            vmem((width, 2 * local), BF16),
            vmem((rows, 2 * local), BF16),
            dma((2,)),
        ],
        flops=14 * rows * width * local,
        traffic=15 * 2**20,
    )
    depth = DT // parts
    caption_rows = captions.reshape(images * TXT, DT)
    if parts == 1:
        grad_attn_in = lax.psum(attn_in_part, "tensor")
        grad_text = dot_nn(grad_text_all, caption_rows)
        wholes = (total_qv, total_ko, grad_text.T)
        grad_qv, grad_ko, grad_text = [scattered(whole.astype(F32)) for whole in wholes]
        grad_query, grad_value = grad_qv[:, :local], grad_qv[:, local:]
        grad_key, grad_out = grad_ko[:, :local], grad_ko[:, local:]
        grad_tk, grad_tv = grad_text[:, :local], grad_text[:, local:]
        grad_f = [grad_f[:, i * units : (i + 1) * units] for i in range(3)]
        result, ffn_mod, ffn_gain_sum = run(
            output_kernel,
            [struct((rows, width)), struct((padded, width), F32), struct((1, width), F32)],
            inside(hidden, member, ffn_gain, grad_y, mods, ffn_out, grad_ffn_in),
            [wide, wide, vmem((rows, width), F32)],
        )
        grad_tokens, grad_mod, attn_gain_sum = run(
            input_kernel,
            [struct((rows, width)), struct((padded, width)), struct((1, width), F32)],
            inside(
                token_rows, member, attn_gain, grad_hidden, ffn_mod, mods, grad_attn_in, attn_out
            ),
            [wide, wide, vmem((rows, width), F32)],
        )
        grad_w_adaln = dot_tn(cond_act, gathered(grad_mod[:images]))
        sums = [attn_gain_sum[0], ffn_gain_sum[0]]
        sums += [row.reshape(heads, HEAD_DIM).T for row in gain_sums[:3]]
        sums = lax.psum(sums, "dp")
        own = [
            lax.dynamic_slice_in_dim(whole, dp_rank * (whole.shape[0] // n_dp), whole.shape[0] // n_dp, 0)
            for whole in sums
        ]
        own.append(lax.psum(jnp.sum(gain_sums[3].reshape(heads, HEAD_DIM), axis=1), "dp"))
    else:
        grad_qv, grad_ko, grad_text, result, grad_tokens, grad_w_adaln, *own = exchange(
            functools.partial(last_exchange_kernel, n_tensor),
            [
                (struct((size, 2 * local), F32), vmem),
                (struct((size, 2 * local), F32), vmem),
                (struct((2 * local, depth), F32), vmem),
                (struct((rows, width)), vmem),
                (struct((rows, width)), vmem),
                (struct((cond_rows, span), F32), vmem),
            ]
            + [(struct((1, gain_attn.size), F32), vmem)] * 2
            + [(struct(gain_query.shape, F32), vmem)] * 3
            + [(struct((heads, 1), F32), vmem)],
            outside(caption_rows)
            + inside(
                grad_text_all, total_qv, total_ko, attn_in_part, token_rows, hidden,
                grad_hidden, member, attn_gain, ffn_gain, grad_y, mods, grad_ffn_in, attn_out,
                cond_act, gain_sums, ffn_out_rows,
            ),
            reduce_scratch(size, 2 * local) * 2
            + reduce_scratch(2 * local, depth)
            + [
                vmem((parts, 2 * local, depth), BF16),
                vmem((2, images * TXT, depth), BF16),
                wide,
                wide,
                vmem((padded, width), F32),
                vmem((padded, width), BF16),
                arrived,
                wide,
                wide,
                vmem((rows, width), F32),
                vmem((8, width), F32),
                vmem((parts, padded, width), BF16),
                vmem((parts, 8, width), F32),
                vmem((8, 128), F32),
                dma((2,)),
                dma((2, 3, 10)),
                dma((2, 4, n_tensor - 1)),
                dma((2, 2, 8)),
            ],
            3,
            vmem=62,
        )
        own[:2] = [part[0] for part in own[:2]]
        own[5] = own[5][:, 0]
        plain = [*grad_f, grad_w_adaln, result, grad_tokens]
        square, tall = struct((size, local), F32), struct((depth, local), F32)
        (
            grad_query, grad_key, grad_value, grad_out, grad_tk, grad_tv, *plain
        ) = pl.pallas_call(
            emit_kernel,
            out_shape=[square] * 4 + [tall] * 2 + [struct(x.shape, x.dtype) for x in plain],
            in_specs=[pl.BlockSpec(memory_space=anywhere)] * (3 + len(plain)),
            out_specs=[pl.BlockSpec(memory_space=anywhere)] * (6 + len(plain)),
            scratch_shapes=[
                vmem((2 * local, depth), F32),
                vmem((depth, local), F32),
                vmem((depth, local), F32),
                dma,
                dma((6 + len(plain),)),
            ],
            compiler_params=pltpu.CompilerParams(vmem_limit_bytes=16 * 2**20),
        )(grad_qv, grad_ko, grad_text, *plain)
        *grad_f, grad_w_adaln, result, grad_tokens = plain

    return (
        result.reshape(micro, count, width),
        grad_tokens.reshape(micro, count, width),
        grad_query,
        grad_key,
        grad_value,
        grad_out,
        grad_tk,
        grad_tv,
        *grad_f,
        grad_w_adaln,
        *own,
    )


def solution(mesh):
    return jax.shard_map(
        functools.partial(shards, mesh.shape["dp"], mesh.shape["tensor"]),
        mesh=mesh,
        in_specs=(
            P(None, "dp", None),
            P(None, "dp", None),
            P(None, "dp", None, None),
            P(None, "dp", None),
            P(None, "dp"),
            P("dp", "tensor"),
            P("dp", "tensor"),
            P("dp", "tensor"),
            P("dp", "tensor"),
            P("dp", "tensor"),
            P("dp", "tensor"),
            P("dp", "tensor"),
            P("dp", "tensor"),
            P("dp", "tensor"),
            P("dp", "tensor"),
            P("dp"),
            P("dp"),
            P("dp", "tensor"),
            P("dp", "tensor"),
            P("dp", "tensor"),
            P("tensor"),
            P(None, "dp", None),
        ),
        out_specs=(
            P(None, "dp", None),
            P(None, "dp", None),
            P("dp", "tensor"),
            P("dp", "tensor"),
            P("dp", "tensor"),
            P("dp", "tensor"),
            P("dp", "tensor"),
            P("dp", "tensor"),
            P("dp", "tensor"),
            P("dp", "tensor"),
            P("dp", "tensor"),
            P("dp", "tensor"),
            P("dp"),
            P("dp"),
            P("dp", "tensor"),
            P("dp", "tensor"),
            P("dp", "tensor"),
            P("tensor"),
        ),
        check_vma=False,
    )
```

```python
import functools

import jax
import jax.numpy as jnp
from jax import lax
from jax.experimental import pallas as pl
from jax.experimental.pallas import tpu as pltpu
from jax.sharding import PartitionSpec as P

HEAD_DIM = 64
DT = 4096
TXT = 256


EPSILON = 1e-06
MASKED = -1e30
ROPE_BASE = 10000.0
STRIP = 16
F32 = jnp.float32
BF16 = jnp.bfloat16


def image_layout(shapes, count):
    height = shapes[:, 0]
    stride_all = shapes[:, 1] + 1
    extent = height * stride_all
    finish = jnp.cumsum(extent)
    begin = finish - extent
    places = jnp.arange(count, dtype=jnp.int32)
    member = (places[:, None] >= begin[None, :]) & (places[:, None] < finish[None, :])
    member_int = member.astype(jnp.int32)
    inside = jnp.sum(member_int, axis=1)
    slot_ids = jnp.arange(shapes.shape[0], dtype=jnp.int32)
    segment = jnp.sum(member_int * slot_ids[None, :], axis=1)
    stride = jnp.sum(member_int * stride_all[None, :], axis=1) + 1 - inside
    offset = places - jnp.sum(member_int * begin[None, :], axis=1)
    return (member.astype(jnp.float32), segment, inside, offset // stride, offset % stride)


def rope_tables(row_pos, col_pos):
    quarter = HEAD_DIM // 4
    freq = ROPE_BASE ** (-jnp.arange(quarter, dtype=jnp.float32) / quarter)
    angles = jnp.stack(
        [
            row_pos.astype(jnp.float32)[:, None] * freq[None, :],
            col_pos.astype(jnp.float32)[:, None] * freq[None, :],
        ],
        axis=1,
    )
    return (jnp.cos(angles), jnp.sin(angles))


def dot_nn(left, right):
    return lax.dot_general(left, right, (((1,), (0,)), ((), ())), preferred_element_type=F32)


def dot_nt(left, right):
    return lax.dot_general(left, right, (((1,), (1,)), ((), ())), preferred_element_type=F32)


def dot_tn(left, right):
    return lax.dot_general(left, right, (((0,), (0,)), ((), ())), preferred_element_type=F32)


def struct(shape, dtype=BF16):
    return jax.ShapeDtypeStruct(shape, dtype)


def run(body, outs, ins, scratch=(), flops=0, traffic=0):
    return pl.pallas_call(
        body,
        out_shape=outs,
        in_specs=[pl.BlockSpec(memory_space=space) for _, space in ins],
        out_specs=[pl.BlockSpec(memory_space=pltpu.VMEM)] * len(outs),
        scratch_shapes=list(scratch),
        compiler_params=pltpu.CompilerParams(vmem_limit_bytes=48 * 2**20),
        cost_estimate=pl.CostEstimate(flops=flops, bytes_accessed=traffic, transcendentals=0),
    )(*[array for array, _ in ins])


def load(source, target, sem):
    copy = pltpu.make_async_copy(source, target, sem)
    copy.start()
    return copy


def wait_all(copies):
    for copy in copies:
        copy.wait()


def token_columns(member, mods, which, target):
    target[...] = dot_nn(member[...], mods[which]).astype(BF16)


def over_strips(rows, step):
    @pl.loop(0, rows // STRIP)
    def _(index):
        step(pl.ds(pl.multiple_of(index * STRIP, STRIP), STRIP))


def head_sum(values, blocks):
    high = values.astype(BF16)
    low = (values - high.astype(F32)).astype(BF16)
    return dot_nn(high, blocks) + dot_nn(low, blocks)


def head_blocks(width):
    row = lax.broadcasted_iota(jnp.int32, (width, width), 0) // HEAD_DIM
    column = lax.broadcasted_iota(jnp.int32, (width, width), 1) // HEAD_DIM
    return jnp.where(row == column, 1.0, 0.0).astype(BF16)


def swap_pairs(values):
    width = values.shape[1]
    quarter = HEAD_DIM // 4
    lane = lax.broadcasted_iota(jnp.int32, values.shape, 1)
    former = lax.rem(lane, 2 * quarter) < quarter
    return jnp.where(
        former, pltpu.roll(values, width - quarter, 1), pltpu.roll(values, quarter, 1)
    )


def head_norm(values, gain, blocks):
    scale = lax.rsqrt(head_sum(values * values, blocks) * (1.0 / HEAD_DIM) + EPSILON)
    return values * scale * gain


def head_norm_back(values, gain, grad, blocks):
    scale = lax.rsqrt(head_sum(values * values, blocks) * (1.0 / HEAD_DIM) + EPSILON)
    normed = values * scale
    grad_gain = jnp.sum(grad * normed, axis=0, keepdims=True)
    inner = grad * gain
    mean = head_sum(inner * normed, blocks) * (1.0 / HEAD_DIM)
    return scale * (inner - normed * mean), grad_gain


def row_scale(values):
    return lax.rsqrt(jnp.mean(values * values, axis=1, keepdims=True) + EPSILON)


MESH = pl.DeviceIdType.MESH
PAIR, ALONG_X, ALONG_Y = 1, 2, 4


def partner(mask):
    rank = lax.axis_index("dp")
    index = rank
    for bit in (1, 2, 4):
        flip = lax.rem(mask // bit, 2)
        index = index + flip * (bit - 2 * bit * lax.rem(rank // bit, 2))
    return index


def announce(masks, shifts, n_tensor):
    barrier = pltpu.get_barrier_semaphore()
    rank = lax.axis_index("tensor")
    for mask in masks:
        pl.semaphore_signal(
            barrier, inc=1, device_id={"dp": partner(mask)}, device_id_type=MESH
        )
    for shift in shifts:
        pl.semaphore_signal(
            barrier,
            inc=1,
            device_id={"tensor": lax.rem(rank + shift, n_tensor)},
            device_id_type=MESH,
        )


def greet(masks, shifts, n_tensor):
    announce(masks, shifts, n_tensor)
    pl.semaphore_wait(pltpu.get_barrier_semaphore(), len(masks) + len(shifts))


def send(source, target, sems, index, device):
    copy = pltpu.make_async_remote_copy(
        src_ref=source,
        dst_ref=target,
        send_sem=sems.at[(0,) + index],
        recv_sem=sems.at[(1,) + index],
        device_id=device,
        device_id_type=MESH,
    )
    copy.start()
    return copy


def gather_kernel(
    n_tensor, shard_tk, shard_tv, shard_qv, shard_ko, context, attn_own, ffn_own, q_own, k_own,
    t_own, w_adaln, captions,
    text_raw, text_key, text_value, qv, ko, cond_act, mods, attn_gain, ffn_gain, q_gain, k_gain, t_gain,
    small, small_all, product, sums, tk, tv, blocks, block, stage, block_sems, stage_sems, own_sems, shard_sems, small_sems, mod_sems, tensor_sems,
):
    rank, tensor_rank = lax.axis_index("dp"), lax.axis_index("tensor")
    masks = range(1, 8)
    shifts = range(1, n_tensor)
    greet(masks, shifts, n_tensor)
    groups = ((shard_tk, tk), (shard_tv, tv), (shard_qv, qv), (shard_ko, ko))

    def rows_of(shard, index, first, size):
        return pl.ds(pl.multiple_of(index * shard.shape[0] + first, 32), size)

    firsts, seconds, pairs, locals_ = {}, {}, {}, []

    def step_1(number):
        shard, whole = groups[number]
        mine = whole.at[rows_of(shard, rank, 0, shard.shape[0])]
        firsts[number] = [
            send(shard, mine, shard_sems, (number, place), {"dp": partner(mask)})
            for place, mask in ((0, ALONG_X), (1, ALONG_Y))
        ]
        pairs[number] = [send(shard, mine, shard_sems, (number, 4), {"dp": partner(PAIR)})]
        local = pltpu.make_async_copy(shard, mine, own_sems.at[number])
        local.start()
        locals_.append(local)

    def step_2(number):
        shard, whole = groups[number]
        size = shard.shape[0]
        half = size // 2
        seconds[number] = []
        for place, mask, onward, start in ((0, ALONG_X, ALONG_Y, half), (1, ALONG_Y, ALONG_X, 0)):
            firsts[number][place].wait_recv()
            part = whole.at[rows_of(shard, partner(mask), start, half)]
            seconds[number].append(
                send(part, part, shard_sems, (number, 2 + place), {"dp": partner(onward)})
            )
            piece = whole.at[rows_of(shard, partner(mask), 0, size)]
            pairs[number].append(
                send(piece, piece, shard_sems, (number, 5 + place), {"dp": partner(PAIR)})
            )

    def step_3(number):
        shard, whole = groups[number]
        half = shard.shape[0] // 2
        for place, start in ((0, half), (1, 0)):
            seconds[number][place].wait_recv()
            part = whole.at[rows_of(shard, partner(ALONG_X + ALONG_Y), start, half)]
            pairs[number].append(
                send(part, part, shard_sems, (number, 7 + place), {"dp": partner(PAIR)})
            )

    def step_4(number):
        for copy in pairs[number]:
            copy.wait_recv()
        locals_[number].wait()

    count = captions.shape[0]

    def fetch(image, slot):
        return pltpu.make_async_copy(captions.at[image], block.at[slot], block_sems.at[slot])

    outputs = (text_raw, text_key, text_value)
    kinds = ((0, 1), (2,))

    def store(image, slot, kind):
        return [
            pltpu.make_async_copy(
                stage.at[slot, index], outputs[index].at[image], stage_sems.at[slot, index]
            )
            for index in kinds[kind]
        ]

    def text_images(low, high, kind):
        @pl.loop(low, high)
        def _(image):
            slot = lax.rem(image, 2)

            @pl.when(image < count - 1)
            def _():
                fetch(image + 1, 1 - slot).start()

            if kind == 0:

                @pl.when(image == count - 1)
                def _():
                    fetch(0, 1 - slot).start()

            fetch(image, slot).wait()

            @pl.when(image >= 2)
            def _():
                wait_all(store(image - 2, slot, kind))

            if kind == 0:
                raw = dot_nn(block[slot], tk[...])
                stage[slot, 0] = raw.astype(BF16)
                stage[slot, 1] = head_norm(raw, t_gain[...], blocks[...]).astype(BF16)
            else:
                stage[slot, 2] = dot_nn(block[slot], tv[...]).astype(BF16)
            for copy in store(image, slot, kind):
                copy.start()

    fetch(0, 0).start()
    step_1(0)
    blocks[...] = head_blocks(tk.shape[1])
    small_copies = []
    images, slots = context.shape[0] * context.shape[1], context.shape[1]
    depth = w_adaln.shape[0]
    gain_size = attn_own.shape[1]
    heads = q_own.shape[1]
    small[...] = jnp.zeros_like(small)
    for index in range(8):
        for first in range(0, images, slots):
            small[index, first : first + slots, :] = context[
                first // slots, :, index * depth : (index + 1) * depth
            ]
        for row, own in ((16, attn_own), (18, ffn_own)):
            for place, first in enumerate(range(0, gain_size, depth)):
                size = min(depth, gain_size - first)
                small[index, row + place : row + place + 1, :size] = own[:, first : first + size]
        for place, own in enumerate((q_own, k_own, t_own)):
            small[index, 24:32, 8 * place : 8 * place + heads] = own[...]
    for mask in masks:
        small_copies.append(
            send(
                small.at[partner(mask)], small_all.at[rank], small_sems, (mask,),
                {"dp": partner(mask)},
            )
        )
    small_all[rank] = small[rank]
    for copy in small_copies:
        copy.wait_recv()
    width = w_adaln.shape[1]
    contexts = small_all[:, 0:16, :].astype(F32).reshape(8 * 16, depth)
    cond_act[...] = jax.nn.silu(contexts).astype(BF16)
    product[...] = dot_nn(cond_act[...], w_adaln[...]).astype(BF16).reshape(8, 16, width)
    mod_copies = [
        send(
            product.at[partner(mask)], sums.at[mask], mod_sems, (mask,), {"dp": partner(mask)}
        )
        for mask in masks
    ]
    step_2(0)
    step_1(1)
    for row, out in ((16, attn_gain), (18, ffn_gain)):
        for index in range(8):
            for place, first in enumerate(range(0, gain_size, depth)):
                size = min(depth, gain_size - first)
                start = index * gain_size + first
                out[:, start : start + size] = small_all[
                    index, row + place : row + place + 1, :size
                ].astype(F32)
    turned = jnp.transpose(small_all[:, 24:32, :].astype(F32).reshape(HEAD_DIM, depth))
    for place, out in enumerate((q_gain, k_gain, t_gain)):
        for head in range(heads):
            out[:, head * HEAD_DIM : (head + 1) * HEAD_DIM] = turned[
                8 * place + head : 8 * place + head + 1, :
            ]
    sums[0] = product[rank]
    for copy in mod_copies:
        copy.wait_recv()
    total = sums[0].astype(F32)
    for mask in masks:
        total = total + sums[mask].astype(F32)
    mods[tensor_rank] = total.astype(BF16)
    tensor_copies = [
        send(
            mods.at[tensor_rank], mods.at[tensor_rank], tensor_sems, (shift,),
            {"tensor": lax.rem(tensor_rank + shift, n_tensor)},
        )
        for shift in shifts
    ]

    step_3(0)
    step_4(0)
    third = count // 3
    text_images(0, third, 0)
    step_2(1)
    step_1(2)
    step_1(3)
    text_images(third, 2 * third, 0)
    step_3(1)
    text_images(2 * third, count, 0)
    step_4(1)
    text_images(0, third, 1)
    step_2(2)
    step_2(3)
    text_images(third, 2 * third, 1)
    text_images(2 * third, count, 1)
    step_3(2)
    step_3(3)
    step_4(2)
    step_4(3)
    for image in (count - 2, count - 1):
        for kind in (0, 1):
            wait_all(store(image, image % 2, kind))
    for copy in tensor_copies:
        copy.wait_recv()
    for number in range(4):
        for copy in firsts[number] + seconds[number] + pairs[number]:
            copy.wait_send()
    for copy in small_copies + mod_copies + tensor_copies:
        copy.wait_send()


ROUTES = ((0, 1, 2, ALONG_X, ALONG_Y), (1, 2, 1, ALONG_Y, ALONG_X))
REDUCE_STRIP = 32


def over_half(half, step):
    @pl.loop(0, half // REDUCE_STRIP)
    def _(index):
        step(pl.multiple_of(index * REDUCE_STRIP, REDUCE_STRIP))


class Reduce:
    def __init__(self, number, read, out, from_pair, out_2, in_2, out_3, in_3, sems):
        self.number, self.read, self.out, self.sems = number, read, out, sems
        self.from_pair, self.out_2, self.in_2, self.out_3, self.in_3 = (
            from_pair, out_2, in_2, out_3, in_3
        )
        self.half = out.shape[0] // 2
        self.copies, self.arriving = [], {}

    def pair_term(self, piece, low):
        there = pl.ds(low, REDUCE_STRIP)
        return self.read(piece, low) + self.from_pair[piece, there, :].astype(F32)

    def move(self, source, target, index, mask):
        return pltpu.make_async_remote_copy(
            src_ref=source,
            dst_ref=target,
            send_sem=self.sems.at[0, self.number, index],
            recv_sem=self.sems.at[1, self.number, index],
            device_id={"dp": partner(mask)},
            device_id_type=MESH,
        )

    def first(self, piece, source):
        return self.move(source, self.from_pair.at[piece], piece, PAIR)

    def second(self, piece, copy):
        copy.wait_recv()
        self.copies.append(copy)
        for side, close, far, first, last in ROUTES:
            if piece not in (close, 3):
                continue
            slot = 1 if piece == 3 else 0

            def step(low):
                self.out_2[side, slot, pl.ds(low, REDUCE_STRIP), :] = self.pair_term(
                    piece, pl.multiple_of(low + side * self.half, REDUCE_STRIP)
                ).astype(BF16)

            over_half(self.half, step)
            moved = self.move(
                self.out_2.at[side, slot], self.in_2.at[side, slot], 4 + 2 * side + slot, first
            )
            moved.start()
            self.arriving[side, slot] = moved
            self.copies.append(moved)

    def third(self):
        for side, close, far, first, last in ROUTES:
            self.arriving[side, 1].wait_recv()

            def step(low):
                here = pl.ds(low, REDUCE_STRIP)
                there = pl.multiple_of(low + side * self.half, REDUCE_STRIP)
                self.out_3[side, here, :] = (
                    self.pair_term(far, there) + self.in_2[side, 1, here, :].astype(F32)
                ).astype(BF16)

            over_half(self.half, step)
            moved = self.move(self.out_3.at[side], self.in_3.at[side], 8 + side, last)
            moved.start()
            self.arriving[side, 2] = moved
            self.copies.append(moved)

    def last(self):
        for side in (0, 1):
            self.arriving[side, 0].wait_recv()
            self.arriving[side, 2].wait_recv()

            def step(low):
                here = pl.ds(low, REDUCE_STRIP)
                there = pl.multiple_of(low + side * self.half, REDUCE_STRIP)
                self.out[pl.ds(there, REDUCE_STRIP), :] = (
                    self.pair_term(0, there)
                    + self.in_2[side, 0, here, :].astype(F32)
                    + self.in_3[side, here, :].astype(F32)
                )

            over_half(self.half, step)
        for copy in self.copies:
            copy.wait_send()


def reduce_scratch(depth, columns):
    half = depth // 2
    return [
        pltpu.VMEM((4, depth, columns), BF16),
        pltpu.VMEM((2, 2, half, columns), BF16),
        pltpu.VMEM((2, 2, half, columns), BF16),
        pltpu.VMEM((2, half, columns), BF16),
        pltpu.VMEM((2, half, columns), BF16),
    ]


def piece_reader(total, size):
    def read(piece, low):
        first = partner(2 * piece) * size + low
        return total[pl.ds(pl.multiple_of(first, 32), REDUCE_STRIP), :].astype(F32)

    return read


def reduce_firsts(reduce, total, size):
    copies = {}
    for piece in (3, 2, 1, 0):
        copies[piece] = reduce.first(piece, piece_of(total, 2 * piece + 1, size))
        copies[piece].start()
    return copies


def piece_of(total, mask, size):
    return total.at[pl.ds(pl.multiple_of(partner(mask) * size, 64), size)]


class TensorSum:
    def __init__(self, number, n_tensor, arrived, sems):
        self.number, self.n_tensor, self.arrived, self.sems = number, n_tensor, arrived, sems
        self.rank = lax.axis_index("tensor")
        self.size = arrived.shape[1]
        self.others = [
            (shift - 1, lax.rem(self.rank + shift, n_tensor)) for shift in range(1, n_tensor)
        ]

    def block(self, index):
        return pl.ds(pl.multiple_of(index * self.size, 16), self.size)

    def scatter(self, partial):
        self.partial = partial
        self.firsts = [
            send(
                partial.at[self.block(other)], self.arrived.at[place], self.sems,
                (2 * self.number, place), {"tensor": other},
            )
            for place, other in self.others
        ]

    def add(self, out, whole):
        for copy in self.firsts:
            copy.wait_recv()

        @pl.loop(0, self.size // STRIP)
        def _(index):
            low = pl.multiple_of(index * STRIP, STRIP)
            there = pl.ds(pl.multiple_of(self.rank * self.size + low, STRIP), STRIP)
            total = self.partial[there, :].astype(F32)
            for place, _ in self.others:
                total = total + self.arrived[place, pl.ds(low, STRIP), :].astype(F32)
            out[there if whole else pl.ds(low, STRIP), :] = total.astype(BF16)

        for copy in self.firsts:
            copy.wait_send()

    def gather(self, out):
        mine = out.at[self.block(self.rank)]
        self.seconds = [
            send(mine, mine, self.sems, (2 * self.number + 1, place), {"tensor": other})
            for place, other in self.others
        ]

    def finish(self):
        for copy in self.seconds:
            copy.wait()


def tensor_kernel(n_tensor, partial, out, arrived, sems):
    greet((), range(1, n_tensor), n_tensor)
    total = TensorSum(0, n_tensor, arrived, sems)
    total.scatter(partial)
    total.add(out, True)
    total.gather(out)
    total.finish()


def emit_kernel(qv, ko, text, *rest):
    count = (len(rest) - 11) // 2
    plain, rest = rest[:count], rest[count:]
    query, key, value, out, text_key, text_value = rest[:6]
    plain_out, (held, turned_key, turned_value, first, sems) = rest[6 : 6 + count], rest[6 + count :]
    width = query.shape[1]
    incoming = load(text, held, first)
    pairs = [
        (qv.at[:, :width], query), (ko.at[:, :width], key), (qv.at[:, width:], value),
        (ko.at[:, width:], out),
    ] + list(zip(plain, plain_out))
    copies = [load(source, target, sems.at[i]) for i, (source, target) in enumerate(pairs)]
    incoming.wait()
    turned_key[...] = jnp.transpose(held[:width, :])
    turned_value[...] = jnp.transpose(held[width:, :])
    copies.append(load(turned_key, text_key, sems.at[len(pairs)]))
    copies.append(load(turned_value, text_value, sems.at[len(pairs) + 1]))
    wait_all(copies)


def exchange(body, outs, ins, scratch, collective, vmem=48):
    spaces = [space for _, space in outs]
    return pl.pallas_call(
        body,
        out_shape=[shape for shape, _ in outs],
        in_specs=[pl.BlockSpec(memory_space=space) for _, space in ins],
        out_specs=[pl.BlockSpec(memory_space=space) for space in spaces],
        scratch_shapes=scratch,
        compiler_params=pltpu.CompilerParams(
            collective_id=collective, has_side_effects=True, vmem_limit_bytes=vmem * 2**20
        ),
    )(*[array for array, _ in ins])


def project_kernel(
    tokens, member, gain, q_gain, k_gain, cosine, sine, mods, whole_a, whole_b,
    attn_in, query_raw, key_raw, query_rot, key_rot, value, mat_a, mat_b, mod, sems
):
    copies = [load(whole_a, mat_a, sems.at[0]), load(whole_b, mat_b, sems.at[1])]
    width = q_gain.shape[1]
    token_columns(member, mods, 0, mod)
    blocks = head_blocks(width)

    def step(at):
        x = tokens[at, :].astype(F32)
        normed = x * row_scale(x)
        attn_in[at, :] = (normed * gain[...] * (1.0 + mod[at, :].astype(F32))).astype(BF16)

    over_strips(tokens.shape[0], step)
    wait_all(copies)
    query_raw[...] = dot_nn(attn_in[...], mat_a[:, :width])
    key_raw[...] = dot_nn(attn_in[...], mat_b[:, :width])
    value[...] = dot_nn(attn_in[...], mat_a[:, width:]).astype(BF16)
    for raw, head_gain, out in ((query_raw, q_gain, query_rot), (key_raw, k_gain, key_rot)):
        normed = head_norm(raw[...], head_gain[...], blocks)
        out[...] = (normed * cosine[...] + swap_pairs(normed) * sine[...]).astype(BF16)


def text_kernel(
    live, source, captions, gain, whole_k, whole_v,
    text_raw, text_key, text_value, mat_k, mat_v, sems
):
    image = pl.program_id(0)

    @pl.when(image == 0)
    def _():
        wait_all([load(whole_k, mat_k, sems.at[0]), load(whole_v, mat_v, sems.at[1])])

    @pl.when(live[image] > 0)
    def _():
        raw = dot_nn(captions[0], mat_k[...])
        text_raw[0] = raw.astype(BF16)
        text_key[0] = head_norm(raw, gain[...], head_blocks(raw.shape[1])).astype(BF16)
        text_value[0] = dot_nn(captions[0], mat_v[...]).astype(BF16)


def stack_pair(values):
    lane = lax.broadcasted_iota(jnp.int32, (1, 2 * HEAD_DIM), 1)
    first = jnp.where(lane < HEAD_DIM, 1.0, 0.0).astype(values.dtype)
    second = jnp.where(lane < HEAD_DIM, 0.0, 1.0).astype(values.dtype)
    return jnp.concatenate([values * first, values * second], axis=0)


def unstack_pair(values):
    count = values.shape[0] // 2
    lane = lax.broadcasted_iota(jnp.int32, (count, 2 * HEAD_DIM), 1)
    return jnp.where(lane < HEAD_DIM, values[:count], values[count:])


def twice(values):
    return jnp.concatenate([values, values], axis=0)


def softmax(scores, allowed, rows_live):
    scores = jnp.where(allowed, scores, MASKED)
    expo = jnp.where(allowed, jnp.exp(scores - jnp.max(scores, axis=1, keepdims=True)), 0.0)
    total = jnp.sum(expo, axis=1, keepdims=True)
    if rows_live is not None:
        total = jnp.where(rows_live, total, 1.0)
    return expo * (1.0 / total)


def attend_kernel(
    micro, scale, live, text_len, query, key, value, text_key_far, text_value_far,
    self_id, self_row, segment, gate, whole_b, mixed, cross_out, whole,
    mat_b, text_key, text_value, self_out, sem, sems
):
    text_copies = [
        load(text_key_far, text_key, sems.at[0]), load(text_value_far, text_value, sems.at[1])
    ]
    copies = [load(whole_b, mat_b, sem)]
    rows, width = query.shape
    count = rows // micro
    slots = text_key.shape[0] // micro
    heads = width // HEAD_DIM
    cross_out[...] = jnp.zeros_like(cross_out)

    for batch in range(micro):
        at = slice(batch * count, (batch + 1) * count)
        allowed = twice(self_id[at, :]) == self_row[batch : batch + 1, :]
        for first in range(0, width, 2 * HEAD_DIM):
            lanes = slice(first, first + 2 * HEAD_DIM)
            scores = dot_nt(stack_pair(query[at, lanes]), key[at, lanes]) * scale
            probs = softmax(scores, allowed, None).astype(BF16)
            self_out[at, lanes] = unstack_pair(dot_nn(probs, value[at, lanes]))
    wait_all(text_copies)

    @pl.loop(0, micro * slots)
    def _(image):
        @pl.when(live[image] > 0)
        def _():
            at = pl.ds(pl.multiple_of((image // slots) * count, count), count)
            mine = twice(segment[at, :]) == lax.rem(image, slots)
            column = lax.broadcasted_iota(jnp.int32, (2 * count, TXT), 1)
            allowed = mine & (column < text_len[image])
            for first in range(0, width, 2 * HEAD_DIM):
                lanes = slice(first, first + 2 * HEAD_DIM)
                scores = dot_nt(stack_pair(query[at, lanes]), text_key[image, :, lanes]) * scale
                probs = softmax(scores, allowed, mine).astype(BF16)
                cross_out[at, lanes] += unstack_pair(dot_nn(probs, text_value[image, :, lanes]))

    mixed[...] = (self_out[...] + gate[...] * cross_out[...]).astype(BF16)
    wait_all(copies)
    whole[...] = dot_nt(mixed[...], mat_b[:, width:]).astype(BF16)


def feed_kernel(
    tokens, member, gain, cotangent, mods, attn_out, whole_f,
    hidden, ffn_in, inner, grad_gate, grad_up, grad_out, whole,
    mat, mod_1, mod_2, mod_3, sem
):
    copies = [load(whole_f, mat, sem)]
    units = inner.shape[1]
    mat_a, mat_b, mat_c = [mat.at[:, i * units : (i + 1) * units] for i in range(3)]
    token_columns(member, mods, 1, mod_1)
    token_columns(member, mods, 2, mod_2)
    token_columns(member, mods, 3, mod_3)

    def step(at):
        gate_attn = jnp.tanh(mod_1[at, :].astype(F32))
        state = tokens[at, :].astype(F32) + gate_attn * attn_out[at, :].astype(F32)
        hidden[at, :] = state
        normed = state * row_scale(state)
        ffn_in[at, :] = (normed * gain[...] * (1.0 + mod_2[at, :].astype(F32))).astype(BF16)
        gate_ffn = jnp.tanh(mod_3[at, :].astype(F32))
        grad_out[at, :] = (gate_ffn * cotangent[at, :].astype(F32)).astype(BF16)

    rows = tokens.shape[0]
    over_strips(rows, step)
    wait_all(copies)
    chunk = 256
    for first in range(0, units, chunk):
        span = slice(first, first + chunk)
        gate = dot_nn(ffn_in[...], mat_a[:, span])
        up = dot_nn(ffn_in[...], mat_b[:, span])
        grad_inner = dot_nn(grad_out[...], mat_c[:, span])
        turn = jax.nn.sigmoid(gate)
        active = gate * turn
        inner[:, span] = (active * up).astype(BF16)
        grad_up[:, span] = (grad_inner * active).astype(BF16)
        slope = turn * (1.0 + gate * (1.0 - turn))
        grad_gate[:, span] = (grad_inner * up * slope).astype(BF16)
    width = tokens.shape[1]
    for first in range(0, width, 512):
        span = slice(first, first + 512)
        whole[:, span] = (
            dot_nt(grad_gate[...], mat_a[span, :]) + dot_nt(grad_up[...], mat_b[span, :])
        ).astype(BF16)


def feed_grad_kernel(grad_out, inner, ffn_in, grad_gate, grad_up, total):
    units = inner.shape[1]
    step = 256
    for index, (left, right) in enumerate(
        ((ffn_in, grad_gate), (ffn_in, grad_up), (grad_out, inner))
    ):
        for first in range(0, units, step):
            out = slice(index * units + first, index * units + first + step)
            total[:, out] = dot_tn(left[...], right[:, first : first + step]).astype(BF16)


def feed_out_kernel(inner, whole_f, partial, mat, sem):
    units = inner.shape[1]
    copy = load(whole_f.at[:, 2 * units : 3 * units], mat, sem)
    copy.wait()
    for first in range(0, partial.shape[1], 512):
        span = slice(first, first + 512)
        partial[:, span] = dot_nt(inner[...], mat[span, :]).astype(BF16)


def modulate_back(values, gain, shift, grad):
    scale = row_scale(values)
    normed = values * scale
    inner = grad * gain * (1.0 + shift)
    mean = jnp.mean(inner * normed, axis=1, keepdims=True)
    return scale * (inner - normed * mean), grad * normed


def mixed_grad_kernel(
    hidden, member, gain, cotangent, mods, grad_in, whole_b,
    grad_hidden, grad_out, grad_mixed, mat_b, mod_1, mod_2, sem
):
    copies = [load(whole_b, mat_b, sem)]
    token_columns(member, mods, 1, mod_1)
    token_columns(member, mods, 2, mod_2)

    def step(at):
        back, _ = modulate_back(
            hidden[at, :], gain[...], mod_2[at, :].astype(F32), grad_in[at, :].astype(F32)
        )
        total = cotangent[at, :].astype(F32) + back
        grad_hidden[at, :] = total
        grad_out[at, :] = (jnp.tanh(mod_1[at, :].astype(F32)) * total).astype(BF16)

    over_strips(hidden.shape[0], step)
    wait_all(copies)
    width = grad_mixed.shape[1]
    grad_mixed[...] = dot_nn(grad_out[...], mat_b[:, width:])


def feed_exchange_kernel(
    n_tensor, tokens, member, gain, cotangent, mods, attn_out, whole_f, whole_ko,
    hidden, grad_hidden, grad_attn_out, grad_mixed, result_rows, gate_part, ffn_mod, gain_sum, *rest
):
    outs, rest = rest[:3], rest[3:]
    (
        ffn_in, inner, grad_gate, grad_up, grad_out, ffn_part, out_part,
        mat, mod_1, mod_2, mod_3, grad_in, ffn_rows, wide_grad, rows_grad, *rest
    ) = rest
    totals, rest = rest[:3], rest[3:]
    buffers, (arrived_1, arrived_2, sem, mat_sem, sems, tensor_sems) = rest[:15], rest[15:]
    announce((PAIR, ALONG_X, ALONG_Y), range(1, n_tensor), n_tensor)
    feed_kernel(
        tokens, member, gain, cotangent, mods, attn_out, whole_f,
        hidden, ffn_in, inner, grad_gate, grad_up, grad_out, ffn_part,
        mat, mod_1, mod_2, mod_3, sem,
    )
    pl.semaphore_wait(pltpu.get_barrier_semaphore(), 3 + n_tensor - 1)
    sum_in = TensorSum(0, n_tensor, arrived_1, tensor_sems)
    sum_in.scatter(ffn_part)
    size = outs[0].shape[0]
    reduces, firsts = [], []
    for number, (left, right) in enumerate(
        ((ffn_in, grad_gate), (ffn_in, grad_up), (grad_out, inner))
    ):
        total = totals[number]
        for first in range(0, total.shape[1], 256):
            span = slice(first, first + 256)
            total[:, span] = dot_tn(left[...], right[:, span]).astype(BF16)
        reduce = Reduce(
            number, piece_reader(total, size), outs[number],
            *buffers[5 * number : 5 * number + 5], sems,
        )
        reduces.append(reduce)
        firsts.append(reduce_firsts(reduce, total, size))
    units = inner.shape[1]
    for first in range(0, out_part.shape[1], 512):
        span = slice(first, first + 512)
        out_part[:, span] = dot_nt(inner[...], mat[span, 2 * units :]).astype(BF16)
    sum_out = TensorSum(1, n_tensor, arrived_2, tensor_sems)
    for piece in (3, 2, 1, 0):
        for number in range(3):
            reduces[number].second(piece, firsts[number][piece])
    sum_in.add(grad_in, True)
    sum_in.gather(grad_in)
    for reduce in reduces:
        reduce.third()
    sum_in.finish()
    sum_out.scatter(out_part)
    head_width = grad_mixed.shape[1]
    copy = load(whole_ko.at[:, head_width:], mat.at[:, :head_width], mat_sem)

    def step(at):
        back, _ = modulate_back(
            hidden[at, :], gain[...], mod_2[at, :].astype(F32), grad_in[at, :].astype(F32)
        )
        total = cotangent[at, :].astype(F32) + back
        grad_hidden[at, :] = total
        grad_attn_out[at, :] = (jnp.tanh(mod_1[at, :].astype(F32)) * total).astype(BF16)

    over_strips(hidden.shape[0], step)
    copy.wait()
    grad_mixed[...] = dot_nn(grad_attn_out[...], mat[:, :head_width])
    gain_sum[...] = jnp.zeros_like(gain_sum)

    def scale_step(at):
        state = hidden[at, :]
        product = grad_in[at, :].astype(F32) * state * row_scale(state)
        gain_sum[...] += jnp.sum(
            product * (1.0 + mod_2[at, :].astype(F32)), axis=0, keepdims=True
        )
        wide_grad[at, :] = product * gain[...]

    over_strips(hidden.shape[0], scale_step)
    ffn_mod[...] = segment_sum(member[...], wide_grad[...])
    for reduce in reduces:
        reduce.last()
    sum_out.add(ffn_rows, False)
    first = sum_out.rank * sum_out.size

    def row_step(here):
        at = pl.ds(pl.multiple_of(first + here.start, STRIP), STRIP)
        gate = jnp.tanh(mod_3[at, :].astype(F32))
        out = ffn_rows[here, :].astype(F32)
        result_rows[here, :] = (hidden[at, :] + gate * out).astype(BF16)
        rows_grad[here, :] = cotangent[at, :].astype(F32) * out * (1.0 - gate * gate)

    over_strips(sum_out.size, row_step)
    gate_part[...] = segment_sum(member[sum_out.block(sum_out.rank), :], rows_grad[...]).astype(BF16)


def attend_back_kernel(
    micro, scale, live, text_len, grad_mixed, cross_out, query, key, value, text_key_far,
    text_value_far, text_raw_far, query_raw, key_raw, q_gain, k_gain, t_gain, cosine, sine, self_id, self_row, segment,
    gate, grad_query_b, grad_key_b, grad_value_b, grad_text, gain_sums,
    grad_query, grad_key, grad_cross, grad_turned, gain_turned, text_key, text_value, text_raw, sems,
    *held
):
    held, held_sems = held[:-1], held[-1]
    early = (grad_mixed, cross_out, query, key, value, query_raw, key_raw, cosine, sine)
    copies = [load(far, here, held_sems.at[i]) for i, (far, here) in enumerate(zip(early, held))]
    grad_mixed, cross_out, query, key, value, query_raw, key_raw, cosine, sine = held
    text_copies = [
        load(far, here, sems.at[index])
        for index, (far, here) in enumerate(
            ((text_key_far, text_key), (text_value_far, text_value), (text_raw_far, text_raw))
        )
    ]
    rows, width = query.shape
    count = rows // micro
    slots = text_key.shape[0] // micro
    heads = width // HEAD_DIM
    blocks = head_blocks(width)
    wait_all(copies)
    gate_sum = jnp.sum(grad_mixed[...] * cross_out[...], axis=0, keepdims=True)
    gain_sums[...] = jnp.zeros_like(gain_sums)
    gain_sums[3:4, :] = gate_sum * (1.0 - gate[...] * gate[...])
    grad_cross[...] = (gate[...] * grad_mixed[...]).astype(BF16)
    gain_turned[...] = jnp.zeros_like(gain_turned)
    gain_column = jnp.transpose(jnp.broadcast_to(t_gain[...], (8, width)))[:, :1]
    for batch in range(micro):
        at = slice(batch * count, (batch + 1) * count)
        allowed = twice(self_id[at, :]) == self_row[batch : batch + 1, :]
        for first in range(0, width, 2 * HEAD_DIM):
            lanes = slice(first, first + 2 * HEAD_DIM)
            q, k = stack_pair(query[at, lanes]), key[at, lanes]
            grad = stack_pair(grad_mixed[at, lanes].astype(BF16))
            probs = softmax(dot_nt(q, k) * scale, allowed, None)
            grad_probs = dot_nt(grad, value[at, lanes])
            mean = jnp.sum(probs * grad_probs, axis=1, keepdims=True)
            scaled = (probs * (grad_probs - mean) * scale).astype(BF16)
            grad_query[at, lanes] = unstack_pair(dot_nn(scaled, k))
            grad_key[at, lanes] = dot_tn(scaled, q)
            grad_value_b[at, lanes] = dot_tn(probs.astype(BF16), grad).astype(BF16)

    wait_all(text_copies)

    @pl.loop(0, micro * slots)
    def _(image):
        @pl.when(live[image] == 0)
        def _():
            grad_text[:, pl.ds(pl.multiple_of(image * TXT, TXT), TXT)] = jnp.zeros(
                (2 * width, TXT), BF16
            )

        @pl.when(live[image] > 0)
        def _():
            at = pl.ds(pl.multiple_of((image // slots) * count, count), count)
            tokens = pl.ds(pl.multiple_of(image * TXT, TXT), TXT)
            mine = twice(segment[at, :]) == lax.rem(image, slots)
            column = lax.broadcasted_iota(jnp.int32, (2 * count, TXT), 1)
            allowed = mine & (column < text_len[image])
            for first in range(0, width, 2 * HEAD_DIM):
                lanes = slice(first, first + 2 * HEAD_DIM)
                q, k = stack_pair(query[at, lanes]), text_key[image, :, lanes]
                grad = stack_pair(grad_cross[at, lanes])
                probs = softmax(dot_nt(q, k) * scale, allowed, mine)
                grad_probs = dot_nt(grad, text_value[image, :, lanes])
                mean = jnp.sum(probs * grad_probs, axis=1, keepdims=True)
                scaled = (probs * (grad_probs - mean) * scale).astype(BF16)
                grad_query[at, lanes] += unstack_pair(dot_nn(scaled, k))
                grad_turned[lanes, :] = dot_tn(q, scaled)
                grad_text[width + first : width + first + 2 * HEAD_DIM, tokens] = dot_tn(
                    grad, probs.astype(BF16)
                ).astype(BF16)
            by_head = (heads, HEAD_DIM, TXT)
            raw = jnp.transpose(text_raw[image].astype(F32)).reshape(by_head)
            norm = lax.rsqrt(jnp.mean(raw * raw, axis=1, keepdims=True) + EPSILON)
            normed = raw * norm
            upper = grad_turned[...].reshape(by_head)
            gain_turned[...] += (upper * normed).reshape(width, TXT)
            inner = upper * gain_column.reshape(heads, HEAD_DIM, 1)
            mean = jnp.mean(inner * normed, axis=1, keepdims=True)
            back = norm * (inner - normed * mean)
            grad_text[:width, tokens] = back.reshape(width, TXT).astype(BF16)

    for index, (grad, raw, gain, out) in enumerate(
        (
            (grad_query, query_raw, q_gain, grad_query_b),
            (grad_key, key_raw, k_gain, grad_key_b),
        )
    ):
        turned = grad[...] * cosine[...] + swap_pairs(grad[...] * sine[...])
        back, gain_sum = head_norm_back(raw[...], gain[...], turned, blocks)
        out[...] = back.astype(BF16)
        gain_sums[index : index + 1, :] = gain_sum
    text_sums = jnp.sum(gain_turned[...], axis=1, keepdims=True)
    gain_sums[2:3, :] = jnp.transpose(jnp.broadcast_to(text_sums, (width, 128)))[:1, :]


def attn_grad_kernel(
    attn_in, grad_query, grad_key, grad_value, grad_out, mixed, whole_a, whole_b,
    total_a, total_b, whole, mat_a, mat_b, pair, sems
):
    copies = [load(whole_a, mat_a, sems.at[0]), load(whole_b, mat_b, sems.at[1])]
    width = grad_query.shape[1]
    pair[:, :width] = grad_query[...]
    pair[:, width:] = grad_value[...]
    wait_all(copies)
    for first in range(0, whole.shape[1], 512):
        span = slice(first, first + 512)
        whole[:, span] = (
            dot_nt(pair[...], mat_a[span, :]) + dot_nt(grad_key[...], mat_b[span, :width])
        ).astype(BF16)
    for first in range(0, 2 * width, 256):
        span = slice(first, first + 256)
        total_a[:, span] = dot_tn(attn_in[...], pair[:, span]).astype(BF16)
    total_b[:, :width] = dot_tn(attn_in[...], grad_key[...]).astype(BF16)
    total_b[:, width:] = dot_tn(grad_out[...], mixed[...]).astype(BF16)


def last_exchange_kernel(
    n_tensor, captions, grad_text, total_qv, total_ko, attn_part, tokens, grad_hidden, member,
    attn_gain, mods, attn_out, cond_act, gain_sums, result_rows, gate_part, ffn_mod, ffn_gain_sum,
    out_qv, out_ko, out_text, result, grad_tokens, grad_adaln,
    own_attn, own_ffn, own_query, own_key, own_text, own_gate, *rest
):
    buffers, rest = rest[:15], rest[15:]
    (
        text_total, block, grad_in, gate_parts, other_mod, grad_mod, arrived, mod_a, mod_b, work_grad,
        sums, all_mod, all_sums, heads_turned,
        block_sems, sems, tensor_sems, small_sems,
    ) = rest
    masks = range(1, 8)
    greet(masks, range(1, n_tensor), n_tensor)
    sum_in = TensorSum(0, n_tensor, arrived, tensor_sems)
    sum_in.scatter(attn_part)
    sum_out = TensorSum(1, n_tensor, arrived, tensor_sems)
    result[sum_out.block(sum_out.rank), :] = result_rows[...]
    gate_parts[0] = gate_part[...]
    gate_copies = [
        send(gate_part, gate_parts.at[place + 1], tensor_sems, (2, place), {"tensor": other})
        for place, other in sum_in.others
    ]
    size = out_qv.shape[0]
    depth = out_text.shape[1]
    reduces, firsts = [], []
    for number, (total, out) in enumerate(((total_qv, out_qv), (total_ko, out_ko))):
        reduce = Reduce(
            number, piece_reader(total, size), out, *buffers[5 * number : 5 * number + 5], sems
        )
        reduces.append(reduce)
        firsts.append(reduce_firsts(reduce, total, size))

    def fetch(mask, slot):
        columns = pl.ds(pl.multiple_of(partner(mask) * depth, 128), depth)
        return pltpu.make_async_copy(
            captions.at[:, columns], block.at[slot], block_sems.at[slot]
        )

    def mask_at(place):
        return 7 - 2 * place + 7 * (place // 4)

    fetch(7, 0).start()

    def read_text(piece, low):
        return text_total[2 * piece, pl.ds(low, REDUCE_STRIP), :].astype(F32)

    text = Reduce(2, read_text, out_text, *buffers[10:], sems)

    def work(low, high):
        @pl.loop(low, high)
        def _(place):
            slot = lax.rem(place, 2)
            mask = mask_at(place)

            @pl.when(place < 7)
            def _():
                fetch(mask_at(place + 1), 1 - slot).start()

            fetch(mask, slot).wait()
            for first in range(0, grad_text.shape[0], 256):
                span = slice(first, first + 256)
                text_total[mask, span, :] = dot_nn(grad_text[span, :], block[slot]).astype(BF16)

    work(0, 2)
    for piece in (3, 2):
        text.first(piece, text_total.at[2 * piece + 1]).start()
    for piece in (3, 2, 1, 0):
        for number in range(2):
            reduces[number].second(piece, firsts[number][piece])
    work(2, 4)
    text_firsts = {}
    for piece in (3, 2, 1, 0):
        text_firsts[piece] = text.first(piece, text_total.at[2 * piece + 1])
    text_firsts[1].start()
    text_firsts[0].start()
    sum_in.add(grad_in, True)
    sum_in.gather(grad_in)
    sum_out.gather(result)
    for reduce in reduces:
        reduce.third()
    work(4, 5)
    text.second(3, text_firsts[3])
    work(5, 6)
    text.second(2, text_firsts[2])
    work(6, 7)
    text.second(1, text_firsts[1])
    work(7, 8)
    text.second(0, text_firsts[0])
    text.third()
    sums[...] = jnp.zeros_like(sums)
    sums[1:2, :] = ffn_gain_sum[...]
    for copy in gate_copies:
        copy.wait()
    gate_mod = gate_parts[0].astype(F32)
    for place, _ in sum_in.others:
        gate_mod = gate_mod + gate_parts[place + 1].astype(F32)
    other_mod[...] = jnp.where(sum_in.rank == 3, gate_mod, ffn_mod[...])
    sum_in.finish()
    input_kernel(
        tokens, member, attn_gain, grad_hidden, other_mod, mods, grad_in, attn_out,
        grad_tokens, grad_mod, sums.at[0:1, :], mod_a, mod_b, work_grad,
    )
    head_width = gain_sums.shape[1]
    for row in range(4):
        sums[2:3, row * head_width : (row + 1) * head_width] = gain_sums[row : row + 1, :]
    rank = lax.axis_index("dp")
    copies = []
    for mask in masks:
        device = {"dp": partner(mask)}
        copies.append(send(grad_mod, all_mod.at[rank], small_sems, (0, mask), device))
        copies.append(send(sums, all_sums.at[mask], small_sems, (1, mask), device))
    all_mod[rank] = grad_mod[...]
    for reduce in reduces:
        reduce.last()
    text.last()
    for copy in copies:
        copy.wait_recv()
    added = sums[...]
    for mask in masks:
        added = added + all_sums[mask]
    grad_adaln[...] = dot_tn(cond_act[...], all_mod[...].reshape(8 * 16, all_mod.shape[2]))
    gain_size = own_attn.shape[1]
    for row, out in ((0, own_attn), (1, own_ffn)):
        out[...] = added[row : row + 1, :gain_size]
        for index in range(1, 8):
            part = added[row : row + 1, index * gain_size : (index + 1) * gain_size]
            out[...] = jnp.where(rank == index, part, out[...])
    heads = own_query.shape[1]
    for place, out in enumerate((own_query, own_key, own_text)):
        for head in range(heads):
            first = place * head_width + head * HEAD_DIM
            heads_turned[head : head + 1, :HEAD_DIM] = added[2:3, first : first + HEAD_DIM]
        turned = jnp.transpose(heads_turned[...])
        part = out.shape[0]
        out[...] = turned[:part, :heads]
        for index in range(1, 8):
            here = turned[index * part : (index + 1) * part, :heads]
            out[...] = jnp.where(rank == index, here, out[...])
    for head in range(heads):
        first = 3 * head_width + head * HEAD_DIM
        own_gate[head : head + 1, :] = jnp.sum(
            added[2:3, first : first + HEAD_DIM], axis=1, keepdims=True
        )
    for copy in copies:
        copy.wait_send()
    sum_out.finish()


def segment_sum(member, values):
    high = values.astype(BF16)
    rest = values - high.astype(F32)
    middle = rest.astype(BF16)
    low = (rest - middle.astype(F32)).astype(BF16)
    return dot_tn(member, high) + dot_tn(member, middle) + dot_tn(member, low)


def output_kernel(
    hidden, member, gain, cotangent, mods, ffn_out, grad_in,
    result, grad_mod, grad_gain, mod_2, mod_3, grad
):
    token_columns(member, mods, 2, mod_2)
    token_columns(member, mods, 3, mod_3)
    rank = lax.axis_index("tensor")
    grad_gain[...] = jnp.zeros_like(grad_gain)

    def step(at):
        state = hidden[at, :]
        gate = jnp.tanh(mod_3[at, :].astype(F32))
        out = ffn_out[at, :].astype(F32)
        result[at, :] = (state + gate * out).astype(BF16)
        up = grad_in[at, :].astype(F32)
        product = up * state * row_scale(state)
        grad_gain[...] += jnp.sum(
            product * (1.0 + mod_2[at, :].astype(F32)), axis=0, keepdims=True
        )
        grad_gate = cotangent[at, :].astype(F32) * out * (1.0 - gate * gate)
        grad[at, :] = jnp.where(rank == 2, product * gain[...], grad_gate)

    over_strips(hidden.shape[0], step)
    grad_mod[...] = segment_sum(member[...], grad[...])


def input_kernel(
    tokens, member, gain, grad_hidden, other_mod, mods, grad_in, attn_out,
    grad_tokens, grad_mod, grad_gain, mod_0, mod_1, grad
):
    token_columns(member, mods, 0, mod_0)
    token_columns(member, mods, 1, mod_1)
    rank = lax.axis_index("tensor")
    grad_gain[...] = jnp.zeros_like(grad_gain)

    def step(at):
        shift = mod_0[at, :].astype(F32)
        upper = grad_hidden[at, :]
        back, product = modulate_back(
            tokens[at, :].astype(F32), gain[...], shift, grad_in[at, :].astype(F32)
        )
        grad_tokens[at, :] = (upper + back).astype(BF16)
        grad_gain[...] += jnp.sum(product * (1.0 + shift), axis=0, keepdims=True)
        gate = jnp.tanh(mod_1[at, :].astype(F32))
        grad_gate = upper * attn_out[at, :].astype(F32) * (1.0 - gate * gate)
        grad[at, :] = jnp.where(rank == 0, product * gain[...], grad_gate)

    over_strips(tokens.shape[0], step)
    own = segment_sum(member[...], grad[...])
    grad_mod[...] = jnp.where(rank < 2, own, other_mod[...]).astype(BF16)


def shards(
    n_dp,
    n_tensor,
    tokens,
    context,
    captions,
    shapes,
    text_len,
    w_query,
    w_key,
    w_value,
    w_out,
    w_text_key,
    w_text_value,
    w_gate,
    w_up,
    w_down,
    w_adaln,
    gain_attn,
    gain_ffn,
    gain_query,
    gain_key,
    gain_text,
    cross_gate,
    cotangent,
):
    parts = 8 if n_dp == 8 else 1
    micro, count, width = tokens.shape
    slots = shapes.shape[1]
    rows = micro * count
    images = micro * slots
    heads = w_query.shape[1] // HEAD_DIM
    local = heads * HEAD_DIM
    units = w_gate.shape[1]
    scale = HEAD_DIM ** (-0.5)
    dp_rank = lax.axis_index("dp")
    padded = 16
    vmem, smem, anywhere = pltpu.VMEM, pltpu.SMEM, pl.ANY
    dma = pltpu.SemaphoreType.DMA

    def inside(*arrays):
        return [(array, vmem) for array in arrays]

    def scalars(*arrays):
        return [(array, smem) for array in arrays]

    def outside(*arrays):
        return [(array, anywhere) for array in arrays]

    def after(values, earlier):
        return lax.optimization_barrier((list(values), list(earlier)))[0]

    def gathered(shard):
        return lax.all_gather(shard, "dp", axis=0, tiled=True)

    def scattered(whole):
        return lax.psum_scatter(whole, "dp", scatter_dimension=0, tiled=True).astype(F32)

    part_rows = rows // n_tensor
    arrived = vmem((n_tensor - 1, part_rows, width), BF16)

    def tensor_sum(partial):
        (out,) = exchange(
            functools.partial(tensor_kernel, n_tensor),
            [(struct((rows, width)), vmem)],
            inside(partial),
            [arrived, dma((2, 2, n_tensor - 1))],
            1,
        )
        return out

    gain_list = (gain_attn, gain_ffn, gain_query, gain_key, gain_text)
    cond_rows, span = w_adaln.shape
    shard_qv = jnp.concatenate([w_query, w_value], axis=1)
    shard_ko = jnp.concatenate([w_key, w_out], axis=1)
    shard_f = jnp.concatenate([w_gate, w_up, w_down], axis=1)
    if parts == 1:
        whole_tk, whole_tv = gathered(w_text_key), gathered(w_text_value)
        whole_qv, whole_ko = gathered(shard_qv), gathered(shard_ko)
        gains = [lax.all_gather(gain.astype(F32), "dp", axis=0, tiled=True) for gain in gain_list]
        attn_gain, ffn_gain = [gain.reshape(1, width) for gain in gains[:2]]
        query_gain, key_gain, text_gain = [gain.T.reshape(1, local) for gain in gains[2:]]
        context_all = gathered(context.reshape(images, -1))
        cond_cols = lax.dynamic_slice_in_dim(context_all, dp_rank * cond_rows, cond_rows, 1)
        cond_act = jax.nn.silu(cond_cols.astype(F32)).astype(BF16)
        mod_part = scattered(dot_nn(cond_act, w_adaln)).astype(BF16)
        mods = lax.all_gather(mod_part, "tensor", axis=0)
        mods = jnp.pad(mods, ((0, 0), (0, padded - images), (0, 0)))
    else:
        text_raw, text_key, text_value, whole_qv, whole_ko, cond_act, mods, *gains = exchange(
            functools.partial(gather_kernel, n_tensor),
            [(struct((images, TXT, local)), anywhere)] * 3
            + [(struct((width, 2 * local)), anywhere)] * 2
            + [
                (struct((parts * padded, cond_rows)), vmem),
                (struct((n_tensor, padded, span)), vmem),
            ]
            + [(struct((1, width), F32), vmem)] * 2
            + [(struct((1, local), F32), vmem)] * 3,
            outside(w_text_key, w_text_value, shard_qv, shard_ko)
            + inside(
                context, gain_attn[None], gain_ffn[None], gain_query, gain_key, gain_text, w_adaln
            )
            + outside(captions.reshape(images, TXT, DT)),
            [
                vmem((parts, 2 * padded, cond_rows), BF16),
                vmem((parts, 2 * padded, cond_rows), BF16),
                vmem((parts, padded, span), BF16),
                vmem((parts, padded, span), BF16),
                vmem((DT, local), BF16),
                vmem((DT, local), BF16),
                vmem((local, local), BF16),
                vmem((2, TXT, DT), BF16),
                vmem((2, 3, TXT, local), BF16),
                dma((2,)),
                dma((2, 3)),
                dma((4,)),
                dma((2, 4, 9)),
                dma((2, 8)),
                dma((2, 8)),
                dma((2, n_tensor)),
            ],
            2,
        )
        attn_gain, ffn_gain, query_gain, key_gain, text_gain = gains
        (shard_f,) = after([shard_f], [mods])
    whole_f = gathered(shard_f)
    layouts = [image_layout(shapes[i], count) for i in range(micro)]
    member, segment, inside_any, row_pos, col_pos = [
        jnp.stack([layout[j] for layout in layouts]) for j in range(5)
    ]
    cosine, sine = rope_tables(row_pos.reshape(rows), col_pos.reshape(rows))
    cosine = jnp.tile(jnp.stack([cosine, cosine], axis=2).reshape(rows, HEAD_DIM), (1, heads))
    sine = jnp.tile(jnp.stack([-sine, sine], axis=2).reshape(rows, HEAD_DIM), (1, heads))
    which = jnp.arange(micro, dtype=jnp.int32)
    member = jnp.where(
        (which[:, None] == which[None, :])[:, None, :, None], member[:, :, None, :], 0.0
    )
    member = jnp.pad(member.reshape(rows, images), ((0, 0), (0, padded - images))).astype(BF16)
    self_row = jnp.where(inside_any > 0, segment, slots)
    self_id = self_row.reshape(rows, 1)
    segment = segment.reshape(rows, 1)
    lens = text_len.reshape(images)
    used = shapes[:, :, 0] * (shapes[:, :, 1] + 1) > 0
    used = used | (jnp.arange(slots)[None, :] == 0)
    live = used.reshape(images).astype(jnp.int32)
    at = jnp.arange(images, dtype=jnp.int32)
    source = lax.cummax(jnp.where(live > 0, at, 0))
    gate = jnp.repeat(jnp.tanh(cross_gate.astype(F32)), HEAD_DIM)[None, :]
    token_rows = tokens.reshape(rows, width)
    grad_y = cotangent.reshape(rows, width)
    caption_images = captions.reshape(images, TXT, DT)

    attn_in, query_raw, key_raw, query_rot, key_rot, value = run(
        project_kernel,
        [struct((rows, width))]
        + [struct((rows, local), F32)] * 2
        + [struct((rows, local))] * 3,
        inside(token_rows, member, attn_gain, query_gain, key_gain, cosine, sine, mods)
        + outside(whole_qv, whole_ko),
        [
            vmem((width, 2 * local), BF16),
            vmem((width, 2 * local), BF16),
            vmem((rows, width), BF16),
            dma((2,)),
        ],
        flops=6 * rows * width * local,
        traffic=10 * 2**20,
    )

    if parts == 1:
        text_raw, text_key, text_value = pl.pallas_call(
            text_kernel,
            out_shape=[struct((images, TXT, local))] * 3,
            grid_spec=pltpu.PrefetchScalarGridSpec(
                num_scalar_prefetch=2,
                grid=(images,),
                in_specs=[
                    pl.BlockSpec((1, TXT, DT), lambda i, live, source: (source[i], 0, 0)),
                    pl.BlockSpec((1, local), lambda i, live, source: (0, 0)),
                ]
                + [pl.BlockSpec(memory_space=anywhere)] * 2,
                out_specs=[pl.BlockSpec((1, TXT, local), lambda i, live, source: (i, 0, 0))] * 3,
                scratch_shapes=[vmem((DT, local), BF16), vmem((DT, local), BF16), dma((2,))],
            ),
            compiler_params=pltpu.CompilerParams(vmem_limit_bytes=40 * 2**20),
            cost_estimate=pl.CostEstimate(
                flops=2 * images * TXT * DT * local, bytes_accessed=20 * 2**20, transcendentals=0
            ),
        )(live, source, caption_images, text_gain, whole_tk, whole_tv)

    wide = vmem((rows, width), BF16)
    mixed, cross_out, attn_part = run(
        functools.partial(attend_kernel, micro, scale),
        [struct((rows, local)), struct((rows, local), F32), struct((rows, width))],
        scalars(live, lens)
        + inside(query_rot, key_rot, value)
        + outside(text_key, text_value)
        + inside(self_id, self_row, segment, gate)
        + outside(whole_ko),
        [
            vmem((width, 2 * local), BF16),
            vmem((images, TXT, local), BF16),
            vmem((images, TXT, local), BF16),
            vmem((rows, local), F32),
            dma,
            dma((2,)),
        ],
        flops=2 * 2**30,
        traffic=12 * 2**20,
    )
    attn_out = tensor_sum(attn_part)

    size = width // parts
    if parts == 1:
        mat = vmem((width, 3 * units), BF16)
        hidden, ffn_in, inner, grad_gate, grad_up, grad_ffn_out, ffn_part = run(
            feed_kernel,
            [struct((rows, width), F32), struct((rows, width))]
            + [struct((rows, units))] * 3
            + [struct((rows, width))] * 2,
            inside(token_rows, member, ffn_gain, grad_y, mods, attn_out) + outside(whole_f),
            [mat, wide, wide, wide, dma],
            flops=10 * rows * width * units,
            traffic=20 * 2**20,
        )
        (grad_f,) = run(
            feed_grad_kernel,
            [struct((width, 3 * units))],
            inside(grad_ffn_out, inner, ffn_in, grad_gate, grad_up),
            flops=6 * rows * width * units,
            traffic=12 * 2**20,
        )
        (ffn_part,) = after([ffn_part], [grad_f])
        grad_ffn_in = tensor_sum(ffn_part)
        grad_f = scattered(grad_f)
        (ffn_out_part,) = run(
            feed_out_kernel,
            [struct((rows, width))],
            inside(inner) + outside(whole_f),
            [vmem((width, units), BF16), dma],
            flops=2 * rows * width * units,
            traffic=5 * 2**20,
        )
        ffn_out = lax.psum(ffn_out_part, "tensor")

        grad_hidden, grad_attn_out, grad_mixed = run(
            mixed_grad_kernel,
            [struct((rows, width), F32), struct((rows, width)), struct((rows, local), F32)],
            inside(hidden, member, ffn_gain, grad_y, mods, grad_ffn_in) + outside(whole_ko),
            [vmem((width, 2 * local), BF16), wide, wide, dma],
            flops=2 * rows * width * local,
            traffic=8 * 2**20,
        )
    else:
        (
            hidden, grad_hidden, grad_attn_out, grad_mixed, result_rows, gate_part, ffn_mod,
            ffn_gain_sum, *grad_f
        ) = exchange(
            functools.partial(feed_exchange_kernel, n_tensor),
            [
                (struct((rows, width), F32), vmem),
                (struct((rows, width), F32), vmem),
                (struct((rows, width)), vmem),
                (struct((rows, local), F32), vmem),
                (struct((part_rows, width)), vmem),
                (struct((padded, width)), vmem),
                (struct((padded, width), F32), vmem),
                (struct((1, width), F32), vmem),
            ]
            + [(struct((size, units), F32), vmem)] * 3,
            inside(token_rows, member, ffn_gain, grad_y, mods, attn_out)
            + outside(whole_f, whole_ko),
            [wide]
            + [vmem((rows, units), BF16)] * 3
            + [wide] * 3
            + [vmem((width, 3 * units), BF16), wide, wide, wide, wide]
            + [
                vmem((part_rows, width), BF16),
                vmem((rows, width), F32),
                vmem((part_rows, width), F32),
            ]
            + [vmem((width, units), BF16)] * 3
            + reduce_scratch(size, units) * 3
            + [arrived, arrived, dma, dma, dma((2, 3, 10)), dma((2, 4, n_tensor - 1))],
            5,
            vmem=60,
        )

    tile = struct((rows, local))
    grad_query_b, grad_key_b, grad_value_b, grad_text_all, gain_sums = run(
        functools.partial(attend_back_kernel, micro, scale),
        [tile, tile, tile, struct((2 * local, images * TXT)), struct((8, local), F32)],
        scalars(live, lens)
        + outside(
            grad_mixed, cross_out, query_rot, key_rot, value, text_key, text_value, text_raw,
            query_raw, key_raw,
        )
        + inside(query_gain, key_gain, text_gain)
        + outside(cosine, sine)
        + inside(self_id, self_row, segment, gate),
        [
            vmem((rows, local), F32),
            vmem((rows, local), F32),
            vmem((rows, local), BF16),
            vmem((local, TXT), F32),
            vmem((local, TXT), F32),
            vmem((images, TXT, local), BF16),
            vmem((images, TXT, local), BF16),
            vmem((images, TXT, local), BF16),
            dma((3,)),
        ]
        + [vmem((rows, local), F32)] * 2
        + [vmem((rows, local), BF16)] * 3
        + [vmem((rows, local), F32)] * 4
        + [
            dma((9,)),
        ],
        flops=4 * 2**30,
        traffic=15 * 2**20,
    )

    total_qv, total_ko, attn_in_part = run(
        attn_grad_kernel,
        [struct((width, 2 * local))] * 2 + [struct((rows, width))],
        inside(attn_in, grad_query_b, grad_key_b, grad_value_b, grad_attn_out, mixed)
        + outside(whole_qv, whole_ko),
        [
            vmem((width, 2 * local), BF16),
            vmem((width, 2 * local), BF16),
            vmem((rows, 2 * local), BF16),
            dma((2,)),
        ],
        flops=14 * rows * width * local,
        traffic=15 * 2**20,
    )
    depth = DT // parts
    caption_rows = captions.reshape(images * TXT, DT)
    if parts == 1:
        grad_attn_in = lax.psum(attn_in_part, "tensor")
        grad_text = dot_nn(grad_text_all, caption_rows)
        wholes = (total_qv, total_ko, grad_text.T)
        grad_qv, grad_ko, grad_text = [scattered(whole.astype(F32)) for whole in wholes]
        grad_query, grad_value = grad_qv[:, :local], grad_qv[:, local:]
        grad_key, grad_out = grad_ko[:, :local], grad_ko[:, local:]
        grad_tk, grad_tv = grad_text[:, :local], grad_text[:, local:]
        grad_f = [grad_f[:, i * units : (i + 1) * units] for i in range(3)]
        result, ffn_mod, ffn_gain_sum = run(
            output_kernel,
            [struct((rows, width)), struct((padded, width), F32), struct((1, width), F32)],
            inside(hidden, member, ffn_gain, grad_y, mods, ffn_out, grad_ffn_in),
            [wide, wide, vmem((rows, width), F32)],
        )
        grad_tokens, grad_mod, attn_gain_sum = run(
            input_kernel,
            [struct((rows, width)), struct((padded, width)), struct((1, width), F32)],
            inside(
                token_rows, member, attn_gain, grad_hidden, ffn_mod, mods, grad_attn_in, attn_out
            ),
            [wide, wide, vmem((rows, width), F32)],
        )
        grad_w_adaln = dot_tn(cond_act, gathered(grad_mod[:images]))
        sums = [attn_gain_sum[0], ffn_gain_sum[0]]
        sums += [row.reshape(heads, HEAD_DIM).T for row in gain_sums[:3]]
        sums = lax.psum(sums, "dp")
        own = [
            lax.dynamic_slice_in_dim(whole, dp_rank * (whole.shape[0] // n_dp), whole.shape[0] // n_dp, 0)
            for whole in sums
        ]
        own.append(lax.psum(jnp.sum(gain_sums[3].reshape(heads, HEAD_DIM), axis=1), "dp"))
    else:
        grad_qv, grad_ko, grad_text, result, grad_tokens, grad_w_adaln, *own = exchange(
            functools.partial(last_exchange_kernel, n_tensor),
            [
                (struct((size, 2 * local), F32), vmem),
                (struct((size, 2 * local), F32), vmem),
                (struct((2 * local, depth), F32), vmem),
                (struct((rows, width)), vmem),
                (struct((rows, width)), vmem),
                (struct((cond_rows, span), F32), vmem),
            ]
            + [(struct((1, gain_attn.size), F32), vmem)] * 2
            + [(struct(gain_query.shape, F32), vmem)] * 3
            + [(struct((heads, 1), F32), vmem)],
            outside(caption_rows)
            + inside(
                grad_text_all, total_qv, total_ko, attn_in_part, token_rows, grad_hidden, member,
                attn_gain, mods, attn_out, cond_act, gain_sums, result_rows, gate_part, ffn_mod,
                ffn_gain_sum,
            ),
            reduce_scratch(size, 2 * local) * 2
            + reduce_scratch(2 * local, depth)
            + [
                vmem((parts, 2 * local, depth), BF16),
                vmem((2, images * TXT, depth), BF16),
                wide,
                vmem((n_tensor, padded, width), BF16),
                vmem((padded, width), F32),
                vmem((padded, width), BF16),
                arrived,
                wide,
                wide,
                vmem((rows, width), F32),
                vmem((8, width), F32),
                vmem((parts, padded, width), BF16),
                vmem((parts, 8, width), F32),
                vmem((8, 128), F32),
                dma((2,)),
                dma((2, 3, 10)),
                dma((2, 4, n_tensor - 1)),
                dma((2, 2, 8)),
            ],
            3,
            vmem=62,
        )
        own[:2] = [part[0] for part in own[:2]]
        own[5] = own[5][:, 0]
        plain = [*grad_f, grad_w_adaln, result, grad_tokens]
        square, tall = struct((size, local), F32), struct((depth, local), F32)
        (
            grad_query, grad_key, grad_value, grad_out, grad_tk, grad_tv, *plain
        ) = pl.pallas_call(
            emit_kernel,
            out_shape=[square] * 4 + [tall] * 2 + [struct(x.shape, x.dtype) for x in plain],
            in_specs=[pl.BlockSpec(memory_space=anywhere)] * (3 + len(plain)),
            out_specs=[pl.BlockSpec(memory_space=anywhere)] * (6 + len(plain)),
            scratch_shapes=[
                vmem((2 * local, depth), F32),
                vmem((depth, local), F32),
                vmem((depth, local), F32),
                dma,
                dma((6 + len(plain),)),
            ],
            compiler_params=pltpu.CompilerParams(vmem_limit_bytes=16 * 2**20),
        )(grad_qv, grad_ko, grad_text, *plain)
        *grad_f, grad_w_adaln, result, grad_tokens = plain

    return (
        result.reshape(micro, count, width),
        grad_tokens.reshape(micro, count, width),
        grad_query,
        grad_key,
        grad_value,
        grad_out,
        grad_tk,
        grad_tv,
        *grad_f,
        grad_w_adaln,
        *own,
    )


def solution(mesh):
    return jax.shard_map(
        functools.partial(shards, mesh.shape["dp"], mesh.shape["tensor"]),
        mesh=mesh,
        in_specs=(
            P(None, "dp", None),
            P(None, "dp", None),
            P(None, "dp", None, None),
            P(None, "dp", None),
            P(None, "dp"),
            P("dp", "tensor"),
            P("dp", "tensor"),
            P("dp", "tensor"),
            P("dp", "tensor"),
            P("dp", "tensor"),
            P("dp", "tensor"),
            P("dp", "tensor"),
            P("dp", "tensor"),
            P("dp", "tensor"),
            P("dp", "tensor"),
            P("dp"),
            P("dp"),
            P("dp", "tensor"),
            P("dp", "tensor"),
            P("dp", "tensor"),
            P("tensor"),
            P(None, "dp", None),
        ),
        out_specs=(
            P(None, "dp", None),
            P(None, "dp", None),
            P("dp", "tensor"),
            P("dp", "tensor"),
            P("dp", "tensor"),
            P("dp", "tensor"),
            P("dp", "tensor"),
            P("dp", "tensor"),
            P("dp", "tensor"),
            P("dp", "tensor"),
            P("dp", "tensor"),
            P("dp", "tensor"),
            P("dp"),
            P("dp"),
            P("dp", "tensor"),
            P("dp", "tensor"),
            P("dp", "tensor"),
            P("tensor"),
        ),
        check_vma=False,
    )
```

```python
import functools

import jax
import jax.numpy as jnp
from jax import lax
from jax.experimental import pallas as pl
from jax.experimental.pallas import tpu as pltpu
from jax.sharding import PartitionSpec as P

HEAD_DIM = 64
DT = 4096
TXT = 256


EPSILON = 1e-06
MASKED = -1e30
ROPE_BASE = 10000.0
STRIP = 16
F32 = jnp.float32
BF16 = jnp.bfloat16


def image_layout(shapes, count):
    height = shapes[:, 0]
    stride_all = shapes[:, 1] + 1
    extent = height * stride_all
    finish = jnp.cumsum(extent)
    begin = finish - extent
    places = jnp.arange(count, dtype=jnp.int32)
    member = (places[:, None] >= begin[None, :]) & (places[:, None] < finish[None, :])
    member_int = member.astype(jnp.int32)
    inside = jnp.sum(member_int, axis=1)
    slot_ids = jnp.arange(shapes.shape[0], dtype=jnp.int32)
    segment = jnp.sum(member_int * slot_ids[None, :], axis=1)
    stride = jnp.sum(member_int * stride_all[None, :], axis=1) + 1 - inside
    offset = places - jnp.sum(member_int * begin[None, :], axis=1)
    return (member.astype(jnp.float32), segment, inside, offset // stride, offset % stride)


def rope_tables(row_pos, col_pos):
    quarter = HEAD_DIM // 4
    freq = ROPE_BASE ** (-jnp.arange(quarter, dtype=jnp.float32) / quarter)
    angles = jnp.stack(
        [
            row_pos.astype(jnp.float32)[:, None] * freq[None, :],
            col_pos.astype(jnp.float32)[:, None] * freq[None, :],
        ],
        axis=1,
    )
    return (jnp.cos(angles), jnp.sin(angles))


def dot_nn(left, right):
    return lax.dot_general(left, right, (((1,), (0,)), ((), ())), preferred_element_type=F32)


def dot_nt(left, right):
    return lax.dot_general(left, right, (((1,), (1,)), ((), ())), preferred_element_type=F32)


def dot_tn(left, right):
    return lax.dot_general(left, right, (((0,), (0,)), ((), ())), preferred_element_type=F32)


def struct(shape, dtype=BF16):
    return jax.ShapeDtypeStruct(shape, dtype)


def run(body, outs, ins, scratch=(), flops=0, traffic=0):
    return pl.pallas_call(
        body,
        out_shape=outs,
        in_specs=[pl.BlockSpec(memory_space=space) for _, space in ins],
        out_specs=[pl.BlockSpec(memory_space=pltpu.VMEM)] * len(outs),
        scratch_shapes=list(scratch),
        compiler_params=pltpu.CompilerParams(vmem_limit_bytes=48 * 2**20),
        cost_estimate=pl.CostEstimate(flops=flops, bytes_accessed=traffic, transcendentals=0),
    )(*[array for array, _ in ins])


def load(source, target, sem):
    copy = pltpu.make_async_copy(source, target, sem)
    copy.start()
    return copy


def wait_all(copies):
    for copy in copies:
        copy.wait()


def token_columns(member, mods, which, target):
    target[...] = dot_nn(member[...], mods[which]).astype(BF16)


def over_strips(rows, step):
    @pl.loop(0, rows // STRIP)
    def _(index):
        step(pl.ds(pl.multiple_of(index * STRIP, STRIP), STRIP))


def head_sum(values, blocks):
    high = values.astype(BF16)
    low = (values - high.astype(F32)).astype(BF16)
    return dot_nn(high, blocks) + dot_nn(low, blocks)


def head_blocks(width):
    row = lax.broadcasted_iota(jnp.int32, (width, width), 0) // HEAD_DIM
    column = lax.broadcasted_iota(jnp.int32, (width, width), 1) // HEAD_DIM
    return jnp.where(row == column, 1.0, 0.0).astype(BF16)


def swap_pairs(values):
    width = values.shape[1]
    quarter = HEAD_DIM // 4
    lane = lax.broadcasted_iota(jnp.int32, values.shape, 1)
    former = lax.rem(lane, 2 * quarter) < quarter
    return jnp.where(
        former, pltpu.roll(values, width - quarter, 1), pltpu.roll(values, quarter, 1)
    )


def head_norm(values, gain, blocks):
    scale = lax.rsqrt(head_sum(values * values, blocks) * (1.0 / HEAD_DIM) + EPSILON)
    return values * scale * gain


def head_norm_back(values, gain, grad, blocks):
    scale = lax.rsqrt(head_sum(values * values, blocks) * (1.0 / HEAD_DIM) + EPSILON)
    normed = values * scale
    grad_gain = jnp.sum(grad * normed, axis=0, keepdims=True)
    inner = grad * gain
    mean = head_sum(inner * normed, blocks) * (1.0 / HEAD_DIM)
    return scale * (inner - normed * mean), grad_gain


def row_scale(values):
    return lax.rsqrt(jnp.mean(values * values, axis=1, keepdims=True) + EPSILON)


MESH = pl.DeviceIdType.MESH
PAIR, ALONG_X, ALONG_Y = 1, 2, 4


def partner(mask):
    rank = lax.axis_index("dp")
    index = rank
    for bit in (1, 2, 4):
        flip = lax.rem(mask // bit, 2)
        index = index + flip * (bit - 2 * bit * lax.rem(rank // bit, 2))
    return index


def announce(masks, shifts, n_tensor):
    barrier = pltpu.get_barrier_semaphore()
    rank = lax.axis_index("tensor")
    for mask in masks:
        pl.semaphore_signal(
            barrier, inc=1, device_id={"dp": partner(mask)}, device_id_type=MESH
        )
    for shift in shifts:
        pl.semaphore_signal(
            barrier,
            inc=1,
            device_id={"tensor": lax.rem(rank + shift, n_tensor)},
            device_id_type=MESH,
        )


def greet(masks, shifts, n_tensor):
    announce(masks, shifts, n_tensor)
    pl.semaphore_wait(pltpu.get_barrier_semaphore(), len(masks) + len(shifts))


def send(source, target, sems, index, device):
    copy = pltpu.make_async_remote_copy(
        src_ref=source,
        dst_ref=target,
        send_sem=sems.at[(0,) + index],
        recv_sem=sems.at[(1,) + index],
        device_id=device,
        device_id_type=MESH,
    )
    copy.start()
    return copy


def gather_kernel(
    n_tensor, shard_tk, shard_tv, shard_qv, shard_ko, context, attn_own, ffn_own, q_own, k_own,
    t_own, w_adaln, captions,
    text_raw, text_key, text_value, qv, ko, cond_act, mods, attn_gain, ffn_gain, q_gain, k_gain, t_gain,
    small, small_all, product, sums, tk, tv, blocks, block, stage, block_sems, stage_sems, own_sems, shard_sems, small_sems, mod_sems, tensor_sems,
):
    rank, tensor_rank = lax.axis_index("dp"), lax.axis_index("tensor")
    masks = range(1, 8)
    shifts = range(1, n_tensor)
    greet(masks, shifts, n_tensor)
    groups = ((shard_tk, tk), (shard_tv, tv), (shard_qv, qv), (shard_ko, ko))

    def rows_of(shard, index, first, size):
        return pl.ds(pl.multiple_of(index * shard.shape[0] + first, 32), size)

    firsts, seconds, pairs, locals_ = {}, {}, {}, []

    def step_1(number):
        shard, whole = groups[number]
        mine = whole.at[rows_of(shard, rank, 0, shard.shape[0])]
        firsts[number] = [
            send(shard, mine, shard_sems, (number, place), {"dp": partner(mask)})
            for place, mask in ((0, ALONG_X), (1, ALONG_Y))
        ]
        pairs[number] = [send(shard, mine, shard_sems, (number, 4), {"dp": partner(PAIR)})]
        local = pltpu.make_async_copy(shard, mine, own_sems.at[number])
        local.start()
        locals_.append(local)

    def step_2(number):
        shard, whole = groups[number]
        size = shard.shape[0]
        half = size // 2
        seconds[number] = []
        for place, mask, onward, start in ((0, ALONG_X, ALONG_Y, half), (1, ALONG_Y, ALONG_X, 0)):
            firsts[number][place].wait_recv()
            part = whole.at[rows_of(shard, partner(mask), start, half)]
            seconds[number].append(
                send(part, part, shard_sems, (number, 2 + place), {"dp": partner(onward)})
            )
            piece = whole.at[rows_of(shard, partner(mask), 0, size)]
            pairs[number].append(
                send(piece, piece, shard_sems, (number, 5 + place), {"dp": partner(PAIR)})
            )

    def step_3(number):
        shard, whole = groups[number]
        half = shard.shape[0] // 2
        for place, start in ((0, half), (1, 0)):
            seconds[number][place].wait_recv()
            part = whole.at[rows_of(shard, partner(ALONG_X + ALONG_Y), start, half)]
            pairs[number].append(
                send(part, part, shard_sems, (number, 7 + place), {"dp": partner(PAIR)})
            )

    def step_4(number):
        for copy in pairs[number]:
            copy.wait_recv()
        locals_[number].wait()

    count = captions.shape[0]

    def fetch(image, slot):
        return pltpu.make_async_copy(captions.at[image], block.at[slot], block_sems.at[slot])

    outputs = (text_raw, text_key, text_value)
    kinds = ((0, 1), (2,))

    def store(image, slot, kind):
        return [
            pltpu.make_async_copy(
                stage.at[slot, index], outputs[index].at[image], stage_sems.at[slot, index]
            )
            for index in kinds[kind]
        ]

    def text_images(low, high, kind):
        @pl.loop(low, high)
        def _(image):
            slot = lax.rem(image, 2)

            @pl.when(image < count - 1)
            def _():
                fetch(image + 1, 1 - slot).start()

            if kind == 0:

                @pl.when(image == count - 1)
                def _():
                    fetch(0, 1 - slot).start()

            fetch(image, slot).wait()

            @pl.when(image >= 2)
            def _():
                wait_all(store(image - 2, slot, kind))

            if kind == 0:
                raw = dot_nn(block[slot], tk[...])
                stage[slot, 0] = raw.astype(BF16)
                stage[slot, 1] = head_norm(raw, t_gain[...], blocks[...]).astype(BF16)
            else:
                stage[slot, 2] = dot_nn(block[slot], tv[...]).astype(BF16)
            for copy in store(image, slot, kind):
                copy.start()

    fetch(0, 0).start()
    step_1(0)
    blocks[...] = head_blocks(tk.shape[1])
    small_copies = []
    images, slots = context.shape[0] * context.shape[1], context.shape[1]
    depth = w_adaln.shape[0]
    gain_size = attn_own.shape[1]
    heads = q_own.shape[1]
    small[...] = jnp.zeros_like(small)
    for index in range(8):
        for first in range(0, images, slots):
            small[index, first : first + slots, :] = context[
                first // slots, :, index * depth : (index + 1) * depth
            ]
        for row, own in ((16, attn_own), (18, ffn_own)):
            for place, first in enumerate(range(0, gain_size, depth)):
                size = min(depth, gain_size - first)
                small[index, row + place : row + place + 1, :size] = own[:, first : first + size]
        for place, own in enumerate((q_own, k_own, t_own)):
            small[index, 24:32, 8 * place : 8 * place + heads] = own[...]
    for mask in masks:
        small_copies.append(
            send(
                small.at[partner(mask)], small_all.at[rank], small_sems, (mask,),
                {"dp": partner(mask)},
            )
        )
    small_all[rank] = small[rank]
    for copy in small_copies:
        copy.wait_recv()
    width = w_adaln.shape[1]
    contexts = small_all[:, 0:16, :].astype(F32).reshape(8 * 16, depth)
    cond_act[...] = jax.nn.silu(contexts).astype(BF16)
    product[...] = dot_nn(cond_act[...], w_adaln[...]).astype(BF16).reshape(8, 16, width)
    mod_copies = [
        send(
            product.at[partner(mask)], sums.at[mask], mod_sems, (mask,), {"dp": partner(mask)}
        )
        for mask in masks
    ]
    step_2(0)
    step_1(1)
    for row, out in ((16, attn_gain), (18, ffn_gain)):
        for index in range(8):
            for place, first in enumerate(range(0, gain_size, depth)):
                size = min(depth, gain_size - first)
                start = index * gain_size + first
                out[:, start : start + size] = small_all[
                    index, row + place : row + place + 1, :size
                ].astype(F32)
    turned = jnp.transpose(small_all[:, 24:32, :].astype(F32).reshape(HEAD_DIM, depth))
    for place, out in enumerate((q_gain, k_gain, t_gain)):
        for head in range(heads):
            out[:, head * HEAD_DIM : (head + 1) * HEAD_DIM] = turned[
                8 * place + head : 8 * place + head + 1, :
            ]
    sums[0] = product[rank]
    for copy in mod_copies:
        copy.wait_recv()
    total = sums[0].astype(F32)
    for mask in masks:
        total = total + sums[mask].astype(F32)
    mods[tensor_rank] = total.astype(BF16)
    tensor_copies = [
        send(
            mods.at[tensor_rank], mods.at[tensor_rank], tensor_sems, (shift,),
            {"tensor": lax.rem(tensor_rank + shift, n_tensor)},
        )
        for shift in shifts
    ]

    step_3(0)
    step_4(0)
    third = count // 3
    text_images(0, third, 0)
    step_2(1)
    step_1(2)
    step_1(3)
    text_images(third, 2 * third, 0)
    step_3(1)
    text_images(2 * third, count, 0)
    step_4(1)
    text_images(0, third, 1)
    step_2(2)
    step_2(3)
    text_images(third, 2 * third, 1)
    text_images(2 * third, count, 1)
    step_3(2)
    step_3(3)
    step_4(2)
    step_4(3)
    for image in (count - 2, count - 1):
        for kind in (0, 1):
            wait_all(store(image, image % 2, kind))
    for copy in tensor_copies:
        copy.wait_recv()
    for number in range(4):
        for copy in firsts[number] + seconds[number] + pairs[number]:
            copy.wait_send()
    for copy in small_copies + mod_copies + tensor_copies:
        copy.wait_send()


ROUTES = ((0, 1, 2, ALONG_X, ALONG_Y), (1, 2, 1, ALONG_Y, ALONG_X))
REDUCE_STRIP = 32


def over_half(half, step):
    @pl.loop(0, half // REDUCE_STRIP)
    def _(index):
        step(pl.multiple_of(index * REDUCE_STRIP, REDUCE_STRIP))


class Reduce:
    def __init__(self, number, read, out, from_pair, out_2, in_2, out_3, in_3, sems):
        self.number, self.read, self.out, self.sems = number, read, out, sems
        self.from_pair, self.out_2, self.in_2, self.out_3, self.in_3 = (
            from_pair, out_2, in_2, out_3, in_3
        )
        self.half = out.shape[0] // 2
        self.copies, self.arriving = [], {}

    def pair_term(self, piece, low):
        there = pl.ds(low, REDUCE_STRIP)
        return self.read(piece, low) + self.from_pair[piece, there, :].astype(F32)

    def move(self, source, target, index, mask):
        return pltpu.make_async_remote_copy(
            src_ref=source,
            dst_ref=target,
            send_sem=self.sems.at[0, self.number, index],
            recv_sem=self.sems.at[1, self.number, index],
            device_id={"dp": partner(mask)},
            device_id_type=MESH,
        )

    def first(self, piece, source):
        return self.move(source, self.from_pair.at[piece], piece, PAIR)

    def second(self, piece, copy):
        copy.wait_recv()
        self.copies.append(copy)
        for side, close, far, first, last in ROUTES:
            if piece not in (close, 3):
                continue
            slot = 1 if piece == 3 else 0

            def step(low):
                self.out_2[side, slot, pl.ds(low, REDUCE_STRIP), :] = self.pair_term(
                    piece, pl.multiple_of(low + side * self.half, REDUCE_STRIP)
                ).astype(BF16)

            over_half(self.half, step)
            moved = self.move(
                self.out_2.at[side, slot], self.in_2.at[side, slot], 4 + 2 * side + slot, first
            )
            moved.start()
            self.arriving[side, slot] = moved
            self.copies.append(moved)

    def third(self):
        for side, close, far, first, last in ROUTES:
            self.arriving[side, 1].wait_recv()

            def step(low):
                here = pl.ds(low, REDUCE_STRIP)
                there = pl.multiple_of(low + side * self.half, REDUCE_STRIP)
                self.out_3[side, here, :] = (
                    self.pair_term(far, there) + self.in_2[side, 1, here, :].astype(F32)
                ).astype(BF16)

            over_half(self.half, step)
            moved = self.move(self.out_3.at[side], self.in_3.at[side], 8 + side, last)
            moved.start()
            self.arriving[side, 2] = moved
            self.copies.append(moved)

    def last(self):
        for side in (0, 1):
            self.arriving[side, 0].wait_recv()
            self.arriving[side, 2].wait_recv()

            def step(low):
                here = pl.ds(low, REDUCE_STRIP)
                there = pl.multiple_of(low + side * self.half, REDUCE_STRIP)
                self.out[pl.ds(there, REDUCE_STRIP), :] = (
                    self.pair_term(0, there)
                    + self.in_2[side, 0, here, :].astype(F32)
                    + self.in_3[side, here, :].astype(F32)
                )

            over_half(self.half, step)
        for copy in self.copies:
            copy.wait_send()


def reduce_scratch(depth, columns):
    half = depth // 2
    return [
        pltpu.VMEM((4, depth, columns), BF16),
        pltpu.VMEM((2, 2, half, columns), BF16),
        pltpu.VMEM((2, 2, half, columns), BF16),
        pltpu.VMEM((2, half, columns), BF16),
        pltpu.VMEM((2, half, columns), BF16),
    ]


def piece_reader(total, size):
    def read(piece, low):
        first = partner(2 * piece) * size + low
        return total[pl.ds(pl.multiple_of(first, 32), REDUCE_STRIP), :].astype(F32)

    return read


def reduce_firsts(reduce, total, size):
    copies = {}
    for piece in (3, 2, 1, 0):
        copies[piece] = reduce.first(piece, piece_of(total, 2 * piece + 1, size))
        copies[piece].start()
    return copies


def piece_of(total, mask, size):
    return total.at[pl.ds(pl.multiple_of(partner(mask) * size, 64), size)]


class TensorSum:
    def __init__(self, number, n_tensor, arrived, sems):
        self.number, self.n_tensor, self.arrived, self.sems = number, n_tensor, arrived, sems
        self.rank = lax.axis_index("tensor")
        self.size = arrived.shape[1]
        self.others = [
            (shift - 1, lax.rem(self.rank + shift, n_tensor)) for shift in range(1, n_tensor)
        ]

    def block(self, index):
        return pl.ds(pl.multiple_of(index * self.size, 16), self.size)

    def scatter(self, partial):
        self.partial = partial
        self.firsts = [
            send(
                partial.at[self.block(other)], self.arrived.at[place], self.sems,
                (2 * self.number, place), {"tensor": other},
            )
            for place, other in self.others
        ]

    def add(self, out, whole):
        for copy in self.firsts:
            copy.wait_recv()

        @pl.loop(0, self.size // STRIP)
        def _(index):
            low = pl.multiple_of(index * STRIP, STRIP)
            there = pl.ds(pl.multiple_of(self.rank * self.size + low, STRIP), STRIP)
            total = self.partial[there, :].astype(F32)
            for place, _ in self.others:
                total = total + self.arrived[place, pl.ds(low, STRIP), :].astype(F32)
            out[there if whole else pl.ds(low, STRIP), :] = total.astype(BF16)

        for copy in self.firsts:
            copy.wait_send()

    def gather(self, out):
        mine = out.at[self.block(self.rank)]
        self.seconds = [
            send(mine, mine, self.sems, (2 * self.number + 1, place), {"tensor": other})
            for place, other in self.others
        ]

    def finish(self):
        for copy in self.seconds:
            copy.wait()


def tensor_kernel(n_tensor, partial, out, arrived, sems):
    greet((), range(1, n_tensor), n_tensor)
    total = TensorSum(0, n_tensor, arrived, sems)
    total.scatter(partial)
    total.add(out, True)
    total.gather(out)
    total.finish()


def emit_kernel(*refs):
    count = (len(refs) - 16) // 3
    sources, refs = refs[: 3 + count], refs[3 + count :]
    outs, refs = refs[: 6 + count], refs[6 + count :]
    held, (turned_key, turned_value, in_sems, sems) = refs[: 3 + count], refs[3 + count :]
    loads = [load(far, here, in_sems.at[i]) for i, (far, here) in enumerate(zip(sources, held))]
    query, key, value, out, text_key, text_value = outs[:6]
    width = query.shape[1]
    copies = []

    def put(here, target):
        copies.append(load(here, target, sems.at[len(copies)]))

    for index in range(3, 3 + count):
        loads[index].wait()
        put(held[index], outs[3 + index])
    for index, first, second in ((0, query, value), (1, key, out)):
        loads[index].wait()
        put(held[index].at[:, :width], first)
        put(held[index].at[:, width:], second)
    loads[2].wait()
    turned_key[...] = jnp.transpose(held[2][:width, :])
    put(turned_key, text_key)
    turned_value[...] = jnp.transpose(held[2][width:, :])
    put(turned_value, text_value)
    wait_all(copies)


def exchange(body, outs, ins, scratch, collective, vmem=48):
    spaces = [space for _, space in outs]
    return pl.pallas_call(
        body,
        out_shape=[shape for shape, _ in outs],
        in_specs=[pl.BlockSpec(memory_space=space) for _, space in ins],
        out_specs=[pl.BlockSpec(memory_space=space) for space in spaces],
        scratch_shapes=scratch,
        compiler_params=pltpu.CompilerParams(
            collective_id=collective, has_side_effects=True, vmem_limit_bytes=vmem * 2**20
        ),
    )(*[array for array, _ in ins])


def project_kernel(
    tokens, member, gain, q_gain, k_gain, cosine, sine, mods, whole_a, whole_b,
    attn_in, query_raw, key_raw, query_rot, key_rot, value, mat_a, mat_b, mod, sems
):
    copies = [load(whole_a, mat_a, sems.at[0]), load(whole_b, mat_b, sems.at[1])]
    width = q_gain.shape[1]
    token_columns(member, mods, 0, mod)
    blocks = head_blocks(width)

    def step(at):
        x = tokens[at, :].astype(F32)
        normed = x * row_scale(x)
        attn_in[at, :] = (normed * gain[...] * (1.0 + mod[at, :].astype(F32))).astype(BF16)

    over_strips(tokens.shape[0], step)
    wait_all(copies)
    query_raw[...] = dot_nn(attn_in[...], mat_a[:, :width])
    key_raw[...] = dot_nn(attn_in[...], mat_b[:, :width])
    value[...] = dot_nn(attn_in[...], mat_a[:, width:]).astype(BF16)
    for raw, head_gain, out in ((query_raw, q_gain, query_rot), (key_raw, k_gain, key_rot)):
        normed = head_norm(raw[...], head_gain[...], blocks)
        out[...] = (normed * cosine[...] + swap_pairs(normed) * sine[...]).astype(BF16)


def text_kernel(
    live, source, captions, gain, whole_k, whole_v,
    text_raw, text_key, text_value, mat_k, mat_v, sems
):
    image = pl.program_id(0)

    @pl.when(image == 0)
    def _():
        wait_all([load(whole_k, mat_k, sems.at[0]), load(whole_v, mat_v, sems.at[1])])

    @pl.when(live[image] > 0)
    def _():
        raw = dot_nn(captions[0], mat_k[...])
        text_raw[0] = raw.astype(BF16)
        text_key[0] = head_norm(raw, gain[...], head_blocks(raw.shape[1])).astype(BF16)
        text_value[0] = dot_nn(captions[0], mat_v[...]).astype(BF16)


def stack_pair(values):
    lane = lax.broadcasted_iota(jnp.int32, (1, 2 * HEAD_DIM), 1)
    first = jnp.where(lane < HEAD_DIM, 1.0, 0.0).astype(values.dtype)
    second = jnp.where(lane < HEAD_DIM, 0.0, 1.0).astype(values.dtype)
    return jnp.concatenate([values * first, values * second], axis=0)


def unstack_pair(values):
    count = values.shape[0] // 2
    lane = lax.broadcasted_iota(jnp.int32, (count, 2 * HEAD_DIM), 1)
    return jnp.where(lane < HEAD_DIM, values[:count], values[count:])


def twice(values):
    return jnp.concatenate([values, values], axis=0)


def softmax(scores, allowed, rows_live):
    scores = jnp.where(allowed, scores, MASKED)
    expo = jnp.where(allowed, jnp.exp(scores - jnp.max(scores, axis=1, keepdims=True)), 0.0)
    total = jnp.sum(expo, axis=1, keepdims=True)
    if rows_live is not None:
        total = jnp.where(rows_live, total, 1.0)
    return expo * (1.0 / total)


def attend_kernel(
    micro, scale, live, text_len, query, key, value, text_key_far, text_value_far,
    self_id, self_row, segment, gate, whole_b, mixed, cross_out, whole,
    mat_b, text_key, text_value, self_out, sem, sems
):
    text_copies = [
        load(text_key_far, text_key, sems.at[0]), load(text_value_far, text_value, sems.at[1])
    ]
    copies = [load(whole_b, mat_b, sem)]
    rows, width = query.shape
    count = rows // micro
    slots = text_key.shape[0] // micro
    heads = width // HEAD_DIM
    cross_out[...] = jnp.zeros_like(cross_out)

    for batch in range(micro):
        at = slice(batch * count, (batch + 1) * count)
        allowed = twice(self_id[at, :]) == self_row[batch : batch + 1, :]
        for first in range(0, width, 2 * HEAD_DIM):
            lanes = slice(first, first + 2 * HEAD_DIM)
            scores = dot_nt(stack_pair(query[at, lanes]), key[at, lanes]) * scale
            probs = softmax(scores, allowed, None).astype(BF16)
            self_out[at, lanes] = unstack_pair(dot_nn(probs, value[at, lanes]))
    wait_all(text_copies)

    @pl.loop(0, micro * slots)
    def _(image):
        @pl.when(live[image] > 0)
        def _():
            at = pl.ds(pl.multiple_of((image // slots) * count, count), count)
            mine = twice(segment[at, :]) == lax.rem(image, slots)
            column = lax.broadcasted_iota(jnp.int32, (2 * count, TXT), 1)
            allowed = mine & (column < text_len[image])
            for first in range(0, width, 2 * HEAD_DIM):
                lanes = slice(first, first + 2 * HEAD_DIM)
                scores = dot_nt(stack_pair(query[at, lanes]), text_key[image, :, lanes]) * scale
                probs = softmax(scores, allowed, mine).astype(BF16)
                cross_out[at, lanes] += unstack_pair(dot_nn(probs, text_value[image, :, lanes]))

    mixed[...] = (self_out[...] + gate[...] * cross_out[...]).astype(BF16)
    wait_all(copies)
    whole[...] = dot_nt(mixed[...], mat_b[:, width:]).astype(BF16)


def feed_kernel(
    tokens, member, gain, cotangent, mods, attn_out, whole_f,
    hidden, ffn_in, inner, grad_gate, grad_up, grad_out, whole,
    mat, mod_1, mod_2, mod_3, sem
):
    copies = [load(whole_f, mat, sem)]
    units = inner.shape[1]
    mat_a, mat_b, mat_c = [mat.at[:, i * units : (i + 1) * units] for i in range(3)]
    token_columns(member, mods, 1, mod_1)
    token_columns(member, mods, 2, mod_2)
    token_columns(member, mods, 3, mod_3)

    def step(at):
        gate_attn = jnp.tanh(mod_1[at, :].astype(F32))
        state = tokens[at, :].astype(F32) + gate_attn * attn_out[at, :].astype(F32)
        hidden[at, :] = state
        normed = state * row_scale(state)
        ffn_in[at, :] = (normed * gain[...] * (1.0 + mod_2[at, :].astype(F32))).astype(BF16)
        gate_ffn = jnp.tanh(mod_3[at, :].astype(F32))
        grad_out[at, :] = (gate_ffn * cotangent[at, :].astype(F32)).astype(BF16)

    rows = tokens.shape[0]
    over_strips(rows, step)
    wait_all(copies)
    chunk = 256
    for first in range(0, units, chunk):
        span = slice(first, first + chunk)
        gate = dot_nn(ffn_in[...], mat_a[:, span])
        up = dot_nn(ffn_in[...], mat_b[:, span])
        grad_inner = dot_nn(grad_out[...], mat_c[:, span])
        turn = jax.nn.sigmoid(gate)
        active = gate * turn
        inner[:, span] = (active * up).astype(BF16)
        grad_up[:, span] = (grad_inner * active).astype(BF16)
        slope = turn * (1.0 + gate * (1.0 - turn))
        grad_gate[:, span] = (grad_inner * up * slope).astype(BF16)
    width = tokens.shape[1]
    for first in range(0, width, 512):
        span = slice(first, first + 512)
        whole[:, span] = (
            dot_nt(grad_gate[...], mat_a[span, :]) + dot_nt(grad_up[...], mat_b[span, :])
        ).astype(BF16)


def feed_grad_kernel(grad_out, inner, ffn_in, grad_gate, grad_up, total):
    units = inner.shape[1]
    step = 256
    for index, (left, right) in enumerate(
        ((ffn_in, grad_gate), (ffn_in, grad_up), (grad_out, inner))
    ):
        for first in range(0, units, step):
            out = slice(index * units + first, index * units + first + step)
            total[:, out] = dot_tn(left[...], right[:, first : first + step]).astype(BF16)


def feed_out_kernel(inner, whole_f, partial, mat, sem):
    units = inner.shape[1]
    copy = load(whole_f.at[:, 2 * units : 3 * units], mat, sem)
    copy.wait()
    for first in range(0, partial.shape[1], 512):
        span = slice(first, first + 512)
        partial[:, span] = dot_nt(inner[...], mat[span, :]).astype(BF16)


def modulate_back(values, gain, shift, grad):
    scale = row_scale(values)
    normed = values * scale
    inner = grad * gain * (1.0 + shift)
    mean = jnp.mean(inner * normed, axis=1, keepdims=True)
    return scale * (inner - normed * mean), grad * normed


def mixed_grad_kernel(
    hidden, member, gain, cotangent, mods, grad_in, whole_b,
    grad_hidden, grad_out, grad_mixed, mat_b, mod_1, mod_2, sem
):
    copies = [load(whole_b, mat_b, sem)]
    token_columns(member, mods, 1, mod_1)
    token_columns(member, mods, 2, mod_2)

    def step(at):
        back, _ = modulate_back(
            hidden[at, :], gain[...], mod_2[at, :].astype(F32), grad_in[at, :].astype(F32)
        )
        total = cotangent[at, :].astype(F32) + back
        grad_hidden[at, :] = total
        grad_out[at, :] = (jnp.tanh(mod_1[at, :].astype(F32)) * total).astype(BF16)

    over_strips(hidden.shape[0], step)
    wait_all(copies)
    width = grad_mixed.shape[1]
    grad_mixed[...] = dot_nn(grad_out[...], mat_b[:, width:])


def feed_exchange_kernel(
    n_tensor, tokens, member, gain, cotangent, mods, attn_out, whole_f, whole_ko,
    hidden, grad_hidden, grad_attn_out, grad_mixed, result_rows, gate_part, ffn_mod, gain_sum, *rest
):
    outs, rest = rest[:3], rest[3:]
    (
        ffn_in, inner, grad_gate, grad_up, grad_out, ffn_part, out_part,
        mat, mod_1, mod_2, mod_3, grad_in, ffn_rows, wide_grad, rows_grad, *rest
    ) = rest
    totals, rest = rest[:3], rest[3:]
    buffers, (arrived_1, arrived_2, sem, mat_sem, sems, tensor_sems) = rest[:15], rest[15:]
    announce((PAIR, ALONG_X, ALONG_Y), range(1, n_tensor), n_tensor)
    feed_kernel(
        tokens, member, gain, cotangent, mods, attn_out, whole_f,
        hidden, ffn_in, inner, grad_gate, grad_up, grad_out, ffn_part,
        mat, mod_1, mod_2, mod_3, sem,
    )
    pl.semaphore_wait(pltpu.get_barrier_semaphore(), 3 + n_tensor - 1)
    sum_in = TensorSum(0, n_tensor, arrived_1, tensor_sems)
    sum_in.scatter(ffn_part)
    size = outs[0].shape[0]
    reduces, firsts = [], []
    for number, (left, right) in enumerate(
        ((ffn_in, grad_gate), (ffn_in, grad_up), (grad_out, inner))
    ):
        total = totals[number]
        for first in range(0, total.shape[1], 256):
            span = slice(first, first + 256)
            total[:, span] = dot_tn(left[...], right[:, span]).astype(BF16)
        reduce = Reduce(
            number, piece_reader(total, size), outs[number],
            *buffers[5 * number : 5 * number + 5], sems,
        )
        reduces.append(reduce)
        firsts.append(reduce_firsts(reduce, total, size))
    units = inner.shape[1]
    for first in range(0, out_part.shape[1], 512):
        span = slice(first, first + 512)
        out_part[:, span] = dot_nt(inner[...], mat[span, 2 * units :]).astype(BF16)
    sum_out = TensorSum(1, n_tensor, arrived_2, tensor_sems)
    for piece in (3, 2, 1, 0):
        for number in range(3):
            reduces[number].second(piece, firsts[number][piece])
    sum_in.add(grad_in, True)
    sum_in.gather(grad_in)
    for reduce in reduces:
        reduce.third()
    sum_in.finish()
    sum_out.scatter(out_part)
    head_width = grad_mixed.shape[1]
    copy = load(whole_ko.at[:, head_width:], mat.at[:, :head_width], mat_sem)

    def step(at):
        back, _ = modulate_back(
            hidden[at, :], gain[...], mod_2[at, :].astype(F32), grad_in[at, :].astype(F32)
        )
        total = cotangent[at, :].astype(F32) + back
        grad_hidden[at, :] = total
        grad_attn_out[at, :] = (jnp.tanh(mod_1[at, :].astype(F32)) * total).astype(BF16)

    over_strips(hidden.shape[0], step)
    copy.wait()
    grad_mixed[...] = dot_nn(grad_attn_out[...], mat[:, :head_width])
    gain_sum[...] = jnp.zeros_like(gain_sum)

    def scale_step(at):
        state = hidden[at, :]
        product = grad_in[at, :].astype(F32) * state * row_scale(state)
        gain_sum[...] += jnp.sum(
            product * (1.0 + mod_2[at, :].astype(F32)), axis=0, keepdims=True
        )
        wide_grad[at, :] = product * gain[...]

    over_strips(hidden.shape[0], scale_step)
    ffn_mod[...] = segment_sum(member[...], wide_grad[...])
    for reduce in reduces:
        reduce.last()
    sum_out.add(ffn_rows, False)
    first = sum_out.rank * sum_out.size

    def row_step(here):
        at = pl.ds(pl.multiple_of(first + here.start, STRIP), STRIP)
        gate = jnp.tanh(mod_3[at, :].astype(F32))
        out = ffn_rows[here, :].astype(F32)
        result_rows[here, :] = (hidden[at, :] + gate * out).astype(BF16)
        rows_grad[here, :] = cotangent[at, :].astype(F32) * out * (1.0 - gate * gate)

    over_strips(sum_out.size, row_step)
    gate_part[...] = segment_sum(member[sum_out.block(sum_out.rank), :], rows_grad[...]).astype(BF16)


def attend_back_kernel(
    micro, scale, live, text_len, grad_mixed, cross_out, query, key, value, text_key_far,
    text_value_far, text_raw_far, query_raw, key_raw, q_gain, k_gain, t_gain, cosine, sine, self_id, self_row, segment,
    gate, grad_query_b, grad_key_b, grad_value_b, grad_text, gain_sums,
    grad_query, grad_key, grad_cross, grad_turned, gain_turned, text_key, text_value, text_raw, sems,
    *held
):
    held, held_sems = held[:-1], held[-1]
    early = (grad_mixed, cross_out, query, key, value, query_raw, key_raw, cosine, sine)
    copies = [load(far, here, held_sems.at[i]) for i, (far, here) in enumerate(zip(early, held))]
    grad_mixed, cross_out, query, key, value, query_raw, key_raw, cosine, sine = held
    text_copies = [
        load(far, here, sems.at[index])
        for index, (far, here) in enumerate(
            ((text_key_far, text_key), (text_value_far, text_value), (text_raw_far, text_raw))
        )
    ]
    rows, width = query.shape
    count = rows // micro
    slots = text_key.shape[0] // micro
    heads = width // HEAD_DIM
    blocks = head_blocks(width)
    wait_all(copies)
    gate_sum = jnp.sum(grad_mixed[...] * cross_out[...], axis=0, keepdims=True)
    gain_sums[...] = jnp.zeros_like(gain_sums)
    gain_sums[3:4, :] = gate_sum * (1.0 - gate[...] * gate[...])
    grad_cross[...] = (gate[...] * grad_mixed[...]).astype(BF16)
    gain_turned[...] = jnp.zeros_like(gain_turned)
    gain_column = jnp.transpose(jnp.broadcast_to(t_gain[...], (8, width)))[:, :1]
    for batch in range(micro):
        at = slice(batch * count, (batch + 1) * count)
        allowed = twice(self_id[at, :]) == self_row[batch : batch + 1, :]
        for first in range(0, width, 2 * HEAD_DIM):
            lanes = slice(first, first + 2 * HEAD_DIM)
            q, k = stack_pair(query[at, lanes]), key[at, lanes]
            grad = stack_pair(grad_mixed[at, lanes].astype(BF16))
            probs = softmax(dot_nt(q, k) * scale, allowed, None)
            grad_probs = dot_nt(grad, value[at, lanes])
            mean = jnp.sum(probs * grad_probs, axis=1, keepdims=True)
            scaled = (probs * (grad_probs - mean) * scale).astype(BF16)
            grad_query[at, lanes] = unstack_pair(dot_nn(scaled, k))
            grad_key[at, lanes] = dot_tn(scaled, q)
            grad_value_b[at, lanes] = dot_tn(probs.astype(BF16), grad).astype(BF16)

    wait_all(text_copies)

    @pl.loop(0, micro * slots)
    def _(image):
        @pl.when(live[image] == 0)
        def _():
            grad_text[:, pl.ds(pl.multiple_of(image * TXT, TXT), TXT)] = jnp.zeros(
                (2 * width, TXT), BF16
            )

        @pl.when(live[image] > 0)
        def _():
            at = pl.ds(pl.multiple_of((image // slots) * count, count), count)
            tokens = pl.ds(pl.multiple_of(image * TXT, TXT), TXT)
            mine = twice(segment[at, :]) == lax.rem(image, slots)
            column = lax.broadcasted_iota(jnp.int32, (2 * count, TXT), 1)
            allowed = mine & (column < text_len[image])
            for first in range(0, width, 2 * HEAD_DIM):
                lanes = slice(first, first + 2 * HEAD_DIM)
                q, k = stack_pair(query[at, lanes]), text_key[image, :, lanes]
                grad = stack_pair(grad_cross[at, lanes])
                probs = softmax(dot_nt(q, k) * scale, allowed, mine)
                grad_probs = dot_nt(grad, text_value[image, :, lanes])
                mean = jnp.sum(probs * grad_probs, axis=1, keepdims=True)
                scaled = (probs * (grad_probs - mean) * scale).astype(BF16)
                grad_query[at, lanes] += unstack_pair(dot_nn(scaled, k))
                grad_turned[lanes, :] = dot_tn(q, scaled)
                grad_text[width + first : width + first + 2 * HEAD_DIM, tokens] = dot_tn(
                    grad, probs.astype(BF16)
                ).astype(BF16)
            by_head = (heads, HEAD_DIM, TXT)
            raw = jnp.transpose(text_raw[image].astype(F32)).reshape(by_head)
            norm = lax.rsqrt(jnp.mean(raw * raw, axis=1, keepdims=True) + EPSILON)
            normed = raw * norm
            upper = grad_turned[...].reshape(by_head)
            gain_turned[...] += (upper * normed).reshape(width, TXT)
            inner = upper * gain_column.reshape(heads, HEAD_DIM, 1)
            mean = jnp.mean(inner * normed, axis=1, keepdims=True)
            back = norm * (inner - normed * mean)
            grad_text[:width, tokens] = back.reshape(width, TXT).astype(BF16)

    for index, (grad, raw, gain, out) in enumerate(
        (
            (grad_query, query_raw, q_gain, grad_query_b),
            (grad_key, key_raw, k_gain, grad_key_b),
        )
    ):
        turned = grad[...] * cosine[...] + swap_pairs(grad[...] * sine[...])
        back, gain_sum = head_norm_back(raw[...], gain[...], turned, blocks)
        out[...] = back.astype(BF16)
        gain_sums[index : index + 1, :] = gain_sum
    text_sums = jnp.sum(gain_turned[...], axis=1, keepdims=True)
    gain_sums[2:3, :] = jnp.transpose(jnp.broadcast_to(text_sums, (width, 128)))[:1, :]


def attn_grad_kernel(
    attn_in, grad_query, grad_key, grad_value, grad_out, mixed, whole_a, whole_b,
    total_a, total_b, whole, mat_a, mat_b, pair, sems
):
    copies = [load(whole_a, mat_a, sems.at[0]), load(whole_b, mat_b, sems.at[1])]
    width = grad_query.shape[1]
    pair[:, :width] = grad_query[...]
    pair[:, width:] = grad_value[...]
    wait_all(copies)
    for first in range(0, whole.shape[1], 512):
        span = slice(first, first + 512)
        whole[:, span] = (
            dot_nt(pair[...], mat_a[span, :]) + dot_nt(grad_key[...], mat_b[span, :width])
        ).astype(BF16)
    for first in range(0, 2 * width, 256):
        span = slice(first, first + 256)
        total_a[:, span] = dot_tn(attn_in[...], pair[:, span]).astype(BF16)
    total_b[:, :width] = dot_tn(attn_in[...], grad_key[...]).astype(BF16)
    total_b[:, width:] = dot_tn(grad_out[...], mixed[...]).astype(BF16)


def last_exchange_kernel(
    n_tensor, captions, grad_text_far, qv_far, ko_far, tokens_far, hidden_far, attn_far, attn_part,
    member, attn_gain, mods, cond_act, gain_sums, result_rows, gate_part, ffn_mod, ffn_gain_sum,
    out_qv, out_ko, out_text, result, grad_tokens, grad_adaln,
    own_attn, own_ffn, own_query, own_key, own_text, own_gate, *rest
):
    buffers, rest = rest[:15], rest[15:]
    (
        text_total, block, grad_in, gate_parts, other_mod, grad_mod, arrived, mod_a, mod_b, work_grad,
        sums, attn_sum, all_mod, all_sums, all_attn, heads_turned,
        block_sems, sems, tensor_sems, small_sems,
        grad_text, total_qv, total_ko, tokens, grad_hidden, attn_out, load_sems,
    ) = rest
    masks = range(1, 8)
    announce(masks, range(1, n_tensor), n_tensor)
    loads = [
        load(far, here, load_sems.at[i])
        for i, (far, here) in enumerate(
            (
                (grad_text_far, grad_text), (qv_far, total_qv), (ko_far, total_ko),
                (tokens_far, tokens), (hidden_far, grad_hidden), (attn_far, attn_out),
            )
        )
    ]
    pl.semaphore_wait(pltpu.get_barrier_semaphore(), 7 + n_tensor - 1)
    sum_in = TensorSum(0, n_tensor, arrived, tensor_sems)
    sum_in.scatter(attn_part)
    head_width = gain_sums.shape[1]
    sums[0:1, :] = ffn_gain_sum[...]
    for row in range(4):
        sums[1:2, row * head_width : (row + 1) * head_width] = gain_sums[row : row + 1, :]
    rank = lax.axis_index("dp")
    copies = [
        send(sums, all_sums.at[mask], small_sems, (1, mask), {"dp": partner(mask)})
        for mask in masks
    ]
    sum_out = TensorSum(1, n_tensor, arrived, tensor_sems)
    result[sum_out.block(sum_out.rank), :] = result_rows[...]
    gate_parts[0] = gate_part[...]
    gate_copies = [
        send(gate_part, gate_parts.at[place + 1], tensor_sems, (2, place), {"tensor": other})
        for place, other in sum_in.others
    ]
    size = out_qv.shape[0]
    depth = out_text.shape[1]
    reduces, firsts = [], []
    for number, (far, total, out) in enumerate(
        ((qv_far, total_qv, out_qv), (ko_far, total_ko, out_ko))
    ):
        reduce = Reduce(
            number, piece_reader(total, size), out, *buffers[5 * number : 5 * number + 5], sems
        )
        reduces.append(reduce)
        firsts.append(reduce_firsts(reduce, far, size))

    def fetch(mask, slot):
        columns = pl.ds(pl.multiple_of(partner(mask) * depth, 128), depth)
        return pltpu.make_async_copy(
            captions.at[:, columns], block.at[slot], block_sems.at[slot]
        )

    def mask_at(place):
        return 7 - 2 * place + 7 * (place // 4)

    fetch(7, 0).start()

    def read_text(piece, low):
        return text_total[2 * piece, pl.ds(low, REDUCE_STRIP), :].astype(F32)

    text = Reduce(2, read_text, out_text, *buffers[10:], sems)

    def work(low, high):
        @pl.loop(low, high)
        def _(place):
            slot = lax.rem(place, 2)
            mask = mask_at(place)

            @pl.when(place < 7)
            def _():
                fetch(mask_at(place + 1), 1 - slot).start()

            fetch(mask, slot).wait()
            for first in range(0, grad_text.shape[0], 256):
                span = slice(first, first + 256)
                text_total[mask, span, :] = dot_nn(grad_text[span, :], block[slot]).astype(BF16)

    wait_all(loads[:3])
    work(0, 2)
    for piece in (3, 2):
        text.first(piece, text_total.at[2 * piece + 1]).start()
    for piece in (3, 2, 1, 0):
        for number in range(2):
            reduces[number].second(piece, firsts[number][piece])
    work(2, 4)
    text_firsts = {}
    for piece in (3, 2, 1, 0):
        text_firsts[piece] = text.first(piece, text_total.at[2 * piece + 1])
    text_firsts[1].start()
    text_firsts[0].start()
    sum_in.add(grad_in, True)
    sum_in.gather(grad_in)
    for reduce in reduces:
        reduce.third()
    work(4, 5)
    text.second(3, text_firsts[3])
    work(5, 6)
    text.second(2, text_firsts[2])
    work(6, 7)
    text.second(1, text_firsts[1])
    work(7, 8)
    text.second(0, text_firsts[0])
    text.third()
    for copy in gate_copies:
        copy.wait()
    gate_mod = gate_parts[0].astype(F32)
    for place, _ in sum_in.others:
        gate_mod = gate_mod + gate_parts[place + 1].astype(F32)
    other_mod[...] = jnp.where(sum_in.rank == 3, gate_mod, ffn_mod[...])
    wait_all(loads[3:])
    sum_in.finish()
    sum_out.gather(result)
    input_kernel(
        tokens, member, attn_gain, grad_hidden, other_mod, mods, grad_in, attn_out,
        grad_tokens, grad_mod, attn_sum, mod_a, mod_b, work_grad,
    )
    for mask in masks:
        device = {"dp": partner(mask)}
        copies.append(send(grad_mod, all_mod.at[rank], small_sems, (0, mask), device))
        copies.append(send(attn_sum, all_attn.at[mask], small_sems, (2, mask), device))
    all_mod[rank] = grad_mod[...]
    for reduce in reduces:
        reduce.last()
    text.last()
    for copy in copies:
        copy.wait_recv()
    added, attn_added = sums[...], attn_sum[...]
    for mask in masks:
        added = added + all_sums[mask]
        attn_added = attn_added + all_attn[mask]
    grad_adaln[...] = dot_tn(cond_act[...], all_mod[...].reshape(8 * 16, all_mod.shape[2]))
    gain_size = own_attn.shape[1]
    for whole, out in ((attn_added, own_attn), (added[0:1, :], own_ffn)):
        out[...] = whole[:, :gain_size]
        for index in range(1, 8):
            part = whole[:, index * gain_size : (index + 1) * gain_size]
            out[...] = jnp.where(rank == index, part, out[...])
    heads = own_query.shape[1]
    for place, out in enumerate((own_query, own_key, own_text)):
        for head in range(heads):
            first = place * head_width + head * HEAD_DIM
            heads_turned[head : head + 1, :HEAD_DIM] = added[1:2, first : first + HEAD_DIM]
        turned = jnp.transpose(heads_turned[...])
        part = out.shape[0]
        out[...] = turned[:part, :heads]
        for index in range(1, 8):
            here = turned[index * part : (index + 1) * part, :heads]
            out[...] = jnp.where(rank == index, here, out[...])
    for head in range(heads):
        first = 3 * head_width + head * HEAD_DIM
        own_gate[:, head : head + 1] = jnp.sum(
            added[1:2, first : first + HEAD_DIM], axis=1, keepdims=True
        )
    for copy in copies:
        copy.wait_send()
    sum_out.finish()


def segment_sum(member, values):
    high = values.astype(BF16)
    rest = values - high.astype(F32)
    middle = rest.astype(BF16)
    low = (rest - middle.astype(F32)).astype(BF16)
    return dot_tn(member, high) + dot_tn(member, middle) + dot_tn(member, low)


def output_kernel(
    hidden, member, gain, cotangent, mods, ffn_out, grad_in,
    result, grad_mod, grad_gain, mod_2, mod_3, grad
):
    token_columns(member, mods, 2, mod_2)
    token_columns(member, mods, 3, mod_3)
    rank = lax.axis_index("tensor")
    grad_gain[...] = jnp.zeros_like(grad_gain)

    def step(at):
        state = hidden[at, :]
        gate = jnp.tanh(mod_3[at, :].astype(F32))
        out = ffn_out[at, :].astype(F32)
        result[at, :] = (state + gate * out).astype(BF16)
        up = grad_in[at, :].astype(F32)
        product = up * state * row_scale(state)
        grad_gain[...] += jnp.sum(
            product * (1.0 + mod_2[at, :].astype(F32)), axis=0, keepdims=True
        )
        grad_gate = cotangent[at, :].astype(F32) * out * (1.0 - gate * gate)
        grad[at, :] = jnp.where(rank == 2, product * gain[...], grad_gate)

    over_strips(hidden.shape[0], step)
    grad_mod[...] = segment_sum(member[...], grad[...])


def input_kernel(
    tokens, member, gain, grad_hidden, other_mod, mods, grad_in, attn_out,
    grad_tokens, grad_mod, grad_gain, mod_0, mod_1, grad
):
    token_columns(member, mods, 0, mod_0)
    token_columns(member, mods, 1, mod_1)
    rank = lax.axis_index("tensor")
    grad_gain[...] = jnp.zeros_like(grad_gain)

    def step(at):
        shift = mod_0[at, :].astype(F32)
        upper = grad_hidden[at, :]
        back, product = modulate_back(
            tokens[at, :].astype(F32), gain[...], shift, grad_in[at, :].astype(F32)
        )
        grad_tokens[at, :] = (upper + back).astype(BF16)
        grad_gain[...] += jnp.sum(product * (1.0 + shift), axis=0, keepdims=True)
        gate = jnp.tanh(mod_1[at, :].astype(F32))
        grad_gate = upper * attn_out[at, :].astype(F32) * (1.0 - gate * gate)
        grad[at, :] = jnp.where(rank == 0, product * gain[...], grad_gate)

    over_strips(tokens.shape[0], step)
    own = segment_sum(member[...], grad[...])
    grad_mod[...] = jnp.where(rank < 2, own, other_mod[...]).astype(BF16)


def shards(
    n_dp,
    n_tensor,
    tokens,
    context,
    captions,
    shapes,
    text_len,
    w_query,
    w_key,
    w_value,
    w_out,
    w_text_key,
    w_text_value,
    w_gate,
    w_up,
    w_down,
    w_adaln,
    gain_attn,
    gain_ffn,
    gain_query,
    gain_key,
    gain_text,
    cross_gate,
    cotangent,
):
    parts = 8 if n_dp == 8 else 1
    micro, count, width = tokens.shape
    slots = shapes.shape[1]
    rows = micro * count
    images = micro * slots
    heads = w_query.shape[1] // HEAD_DIM
    local = heads * HEAD_DIM
    units = w_gate.shape[1]
    scale = HEAD_DIM ** (-0.5)
    dp_rank = lax.axis_index("dp")
    padded = 16
    vmem, smem, anywhere = pltpu.VMEM, pltpu.SMEM, pl.ANY
    dma = pltpu.SemaphoreType.DMA

    def inside(*arrays):
        return [(array, vmem) for array in arrays]

    def scalars(*arrays):
        return [(array, smem) for array in arrays]

    def outside(*arrays):
        return [(array, anywhere) for array in arrays]

    def after(values, earlier):
        return lax.optimization_barrier((list(values), list(earlier)))[0]

    def gathered(shard):
        return lax.all_gather(shard, "dp", axis=0, tiled=True)

    def scattered(whole):
        return lax.psum_scatter(whole, "dp", scatter_dimension=0, tiled=True).astype(F32)

    part_rows = rows // n_tensor
    arrived = vmem((n_tensor - 1, part_rows, width), BF16)

    def tensor_sum(partial):
        (out,) = exchange(
            functools.partial(tensor_kernel, n_tensor),
            [(struct((rows, width)), vmem)],
            inside(partial),
            [arrived, dma((2, 2, n_tensor - 1))],
            1,
        )
        return out

    gain_list = (gain_attn, gain_ffn, gain_query, gain_key, gain_text)
    cond_rows, span = w_adaln.shape
    shard_qv = jnp.concatenate([w_query, w_value], axis=1)
    shard_ko = jnp.concatenate([w_key, w_out], axis=1)
    shard_f = jnp.concatenate([w_gate, w_up, w_down], axis=1)
    if parts == 1:
        whole_tk, whole_tv = gathered(w_text_key), gathered(w_text_value)
        whole_qv, whole_ko = gathered(shard_qv), gathered(shard_ko)
        gains = [lax.all_gather(gain.astype(F32), "dp", axis=0, tiled=True) for gain in gain_list]
        attn_gain, ffn_gain = [gain.reshape(1, width) for gain in gains[:2]]
        query_gain, key_gain, text_gain = [gain.T.reshape(1, local) for gain in gains[2:]]
        context_all = gathered(context.reshape(images, -1))
        cond_cols = lax.dynamic_slice_in_dim(context_all, dp_rank * cond_rows, cond_rows, 1)
        cond_act = jax.nn.silu(cond_cols.astype(F32)).astype(BF16)
        mod_part = scattered(dot_nn(cond_act, w_adaln)).astype(BF16)
        mods = lax.all_gather(mod_part, "tensor", axis=0)
        mods = jnp.pad(mods, ((0, 0), (0, padded - images), (0, 0)))
    else:
        text_raw, text_key, text_value, whole_qv, whole_ko, cond_act, mods, *gains = exchange(
            functools.partial(gather_kernel, n_tensor),
            [(struct((images, TXT, local)), anywhere)] * 3
            + [(struct((width, 2 * local)), anywhere)] * 2
            + [
                (struct((parts * padded, cond_rows)), vmem),
                (struct((n_tensor, padded, span)), vmem),
            ]
            + [(struct((1, width), F32), vmem)] * 2
            + [(struct((1, local), F32), vmem)] * 3,
            outside(w_text_key, w_text_value, shard_qv, shard_ko)
            + inside(
                context, gain_attn[None], gain_ffn[None], gain_query, gain_key, gain_text, w_adaln
            )
            + outside(captions.reshape(images, TXT, DT)),
            [
                vmem((parts, 2 * padded, cond_rows), BF16),
                vmem((parts, 2 * padded, cond_rows), BF16),
                vmem((parts, padded, span), BF16),
                vmem((parts, padded, span), BF16),
                vmem((DT, local), BF16),
                vmem((DT, local), BF16),
                vmem((local, local), BF16),
                vmem((2, TXT, DT), BF16),
                vmem((2, 3, TXT, local), BF16),
                dma((2,)),
                dma((2, 3)),
                dma((4,)),
                dma((2, 4, 9)),
                dma((2, 8)),
                dma((2, 8)),
                dma((2, n_tensor)),
            ],
            2,
        )
        attn_gain, ffn_gain, query_gain, key_gain, text_gain = gains
        (shard_f,) = after([shard_f], [mods])
    whole_f = gathered(shard_f)
    layouts = [image_layout(shapes[i], count) for i in range(micro)]
    member, segment, inside_any, row_pos, col_pos = [
        jnp.stack([layout[j] for layout in layouts]) for j in range(5)
    ]
    cosine, sine = rope_tables(row_pos.reshape(rows), col_pos.reshape(rows))
    cosine = jnp.tile(jnp.stack([cosine, cosine], axis=2).reshape(rows, HEAD_DIM), (1, heads))
    sine = jnp.tile(jnp.stack([-sine, sine], axis=2).reshape(rows, HEAD_DIM), (1, heads))
    which = jnp.arange(micro, dtype=jnp.int32)
    member = jnp.where(
        (which[:, None] == which[None, :])[:, None, :, None], member[:, :, None, :], 0.0
    )
    member = jnp.pad(member.reshape(rows, images), ((0, 0), (0, padded - images))).astype(BF16)
    self_row = jnp.where(inside_any > 0, segment, slots)
    self_id = self_row.reshape(rows, 1)
    segment = segment.reshape(rows, 1)
    lens = text_len.reshape(images)
    used = shapes[:, :, 0] * (shapes[:, :, 1] + 1) > 0
    used = used | (jnp.arange(slots)[None, :] == 0)
    live = used.reshape(images).astype(jnp.int32)
    at = jnp.arange(images, dtype=jnp.int32)
    source = lax.cummax(jnp.where(live > 0, at, 0))
    gate = jnp.repeat(jnp.tanh(cross_gate.astype(F32)), HEAD_DIM)[None, :]
    token_rows = tokens.reshape(rows, width)
    grad_y = cotangent.reshape(rows, width)
    caption_images = captions.reshape(images, TXT, DT)

    attn_in, query_raw, key_raw, query_rot, key_rot, value = run(
        project_kernel,
        [struct((rows, width))]
        + [struct((rows, local), F32)] * 2
        + [struct((rows, local))] * 3,
        inside(token_rows, member, attn_gain, query_gain, key_gain, cosine, sine, mods)
        + outside(whole_qv, whole_ko),
        [
            vmem((width, 2 * local), BF16),
            vmem((width, 2 * local), BF16),
            vmem((rows, width), BF16),
            dma((2,)),
        ],
        flops=6 * rows * width * local,
        traffic=10 * 2**20,
    )

    if parts == 1:
        text_raw, text_key, text_value = pl.pallas_call(
            text_kernel,
            out_shape=[struct((images, TXT, local))] * 3,
            grid_spec=pltpu.PrefetchScalarGridSpec(
                num_scalar_prefetch=2,
                grid=(images,),
                in_specs=[
                    pl.BlockSpec((1, TXT, DT), lambda i, live, source: (source[i], 0, 0)),
                    pl.BlockSpec((1, local), lambda i, live, source: (0, 0)),
                ]
                + [pl.BlockSpec(memory_space=anywhere)] * 2,
                out_specs=[pl.BlockSpec((1, TXT, local), lambda i, live, source: (i, 0, 0))] * 3,
                scratch_shapes=[vmem((DT, local), BF16), vmem((DT, local), BF16), dma((2,))],
            ),
            compiler_params=pltpu.CompilerParams(vmem_limit_bytes=40 * 2**20),
            cost_estimate=pl.CostEstimate(
                flops=2 * images * TXT * DT * local, bytes_accessed=20 * 2**20, transcendentals=0
            ),
        )(live, source, caption_images, text_gain, whole_tk, whole_tv)

    wide = vmem((rows, width), BF16)
    mixed, cross_out, attn_part = run(
        functools.partial(attend_kernel, micro, scale),
        [struct((rows, local)), struct((rows, local), F32), struct((rows, width))],
        scalars(live, lens)
        + inside(query_rot, key_rot, value)
        + outside(text_key, text_value)
        + inside(self_id, self_row, segment, gate)
        + outside(whole_ko),
        [
            vmem((width, 2 * local), BF16),
            vmem((images, TXT, local), BF16),
            vmem((images, TXT, local), BF16),
            vmem((rows, local), F32),
            dma,
            dma((2,)),
        ],
        flops=2 * 2**30,
        traffic=12 * 2**20,
    )
    attn_out = tensor_sum(attn_part)

    size = width // parts
    if parts == 1:
        mat = vmem((width, 3 * units), BF16)
        hidden, ffn_in, inner, grad_gate, grad_up, grad_ffn_out, ffn_part = run(
            feed_kernel,
            [struct((rows, width), F32), struct((rows, width))]
            + [struct((rows, units))] * 3
            + [struct((rows, width))] * 2,
            inside(token_rows, member, ffn_gain, grad_y, mods, attn_out) + outside(whole_f),
            [mat, wide, wide, wide, dma],
            flops=10 * rows * width * units,
            traffic=20 * 2**20,
        )
        (grad_f,) = run(
            feed_grad_kernel,
            [struct((width, 3 * units))],
            inside(grad_ffn_out, inner, ffn_in, grad_gate, grad_up),
            flops=6 * rows * width * units,
            traffic=12 * 2**20,
        )
        (ffn_part,) = after([ffn_part], [grad_f])
        grad_ffn_in = tensor_sum(ffn_part)
        grad_f = scattered(grad_f)
        (ffn_out_part,) = run(
            feed_out_kernel,
            [struct((rows, width))],
            inside(inner) + outside(whole_f),
            [vmem((width, units), BF16), dma],
            flops=2 * rows * width * units,
            traffic=5 * 2**20,
        )
        ffn_out = lax.psum(ffn_out_part, "tensor")

        grad_hidden, grad_attn_out, grad_mixed = run(
            mixed_grad_kernel,
            [struct((rows, width), F32), struct((rows, width)), struct((rows, local), F32)],
            inside(hidden, member, ffn_gain, grad_y, mods, grad_ffn_in) + outside(whole_ko),
            [vmem((width, 2 * local), BF16), wide, wide, dma],
            flops=2 * rows * width * local,
            traffic=8 * 2**20,
        )
    else:
        (
            hidden, grad_hidden, grad_attn_out, grad_mixed, result_rows, gate_part, ffn_mod,
            ffn_gain_sum, *grad_f
        ) = exchange(
            functools.partial(feed_exchange_kernel, n_tensor),
            [
                (struct((rows, width), F32), vmem),
                (struct((rows, width), F32), vmem),
                (struct((rows, width)), vmem),
                (struct((rows, local), F32), vmem),
                (struct((part_rows, width)), vmem),
                (struct((padded, width)), vmem),
                (struct((padded, width), F32), vmem),
                (struct((1, width), F32), vmem),
            ]
            + [(struct((size, units), F32), vmem)] * 3,
            inside(token_rows, member, ffn_gain, grad_y, mods, attn_out)
            + outside(whole_f, whole_ko),
            [wide]
            + [vmem((rows, units), BF16)] * 3
            + [wide] * 3
            + [vmem((width, 3 * units), BF16), wide, wide, wide, wide]
            + [
                vmem((part_rows, width), BF16),
                vmem((rows, width), F32),
                vmem((part_rows, width), F32),
            ]
            + [vmem((width, units), BF16)] * 3
            + reduce_scratch(size, units) * 3
            + [arrived, arrived, dma, dma, dma((2, 3, 10)), dma((2, 4, n_tensor - 1))],
            5,
            vmem=60,
        )

    tile = struct((rows, local))
    grad_query_b, grad_key_b, grad_value_b, grad_text_all, gain_sums = run(
        functools.partial(attend_back_kernel, micro, scale),
        [tile, tile, tile, struct((2 * local, images * TXT)), struct((8, local), F32)],
        scalars(live, lens)
        + outside(
            grad_mixed, cross_out, query_rot, key_rot, value, text_key, text_value, text_raw,
            query_raw, key_raw,
        )
        + inside(query_gain, key_gain, text_gain)
        + outside(cosine, sine)
        + inside(self_id, self_row, segment, gate),
        [
            vmem((rows, local), F32),
            vmem((rows, local), F32),
            vmem((rows, local), BF16),
            vmem((local, TXT), F32),
            vmem((local, TXT), F32),
            vmem((images, TXT, local), BF16),
            vmem((images, TXT, local), BF16),
            vmem((images, TXT, local), BF16),
            dma((3,)),
        ]
        + [vmem((rows, local), F32)] * 2
        + [vmem((rows, local), BF16)] * 3
        + [vmem((rows, local), F32)] * 4
        + [
            dma((9,)),
        ],
        flops=4 * 2**30,
        traffic=15 * 2**20,
    )

    total_qv, total_ko, attn_in_part = run(
        attn_grad_kernel,
        [struct((width, 2 * local))] * 2 + [struct((rows, width))],
        inside(attn_in, grad_query_b, grad_key_b, grad_value_b, grad_attn_out, mixed)
        + outside(whole_qv, whole_ko),
        [
            vmem((width, 2 * local), BF16),
            vmem((width, 2 * local), BF16),
            vmem((rows, 2 * local), BF16),
            dma((2,)),
        ],
        flops=14 * rows * width * local,
        traffic=15 * 2**20,
    )
    depth = DT // parts
    caption_rows = captions.reshape(images * TXT, DT)
    if parts == 1:
        grad_attn_in = lax.psum(attn_in_part, "tensor")
        grad_text = dot_nn(grad_text_all, caption_rows)
        wholes = (total_qv, total_ko, grad_text.T)
        grad_qv, grad_ko, grad_text = [scattered(whole.astype(F32)) for whole in wholes]
        grad_query, grad_value = grad_qv[:, :local], grad_qv[:, local:]
        grad_key, grad_out = grad_ko[:, :local], grad_ko[:, local:]
        grad_tk, grad_tv = grad_text[:, :local], grad_text[:, local:]
        grad_f = [grad_f[:, i * units : (i + 1) * units] for i in range(3)]
        result, ffn_mod, ffn_gain_sum = run(
            output_kernel,
            [struct((rows, width)), struct((padded, width), F32), struct((1, width), F32)],
            inside(hidden, member, ffn_gain, grad_y, mods, ffn_out, grad_ffn_in),
            [wide, wide, vmem((rows, width), F32)],
        )
        grad_tokens, grad_mod, attn_gain_sum = run(
            input_kernel,
            [struct((rows, width)), struct((padded, width)), struct((1, width), F32)],
            inside(
                token_rows, member, attn_gain, grad_hidden, ffn_mod, mods, grad_attn_in, attn_out
            ),
            [wide, wide, vmem((rows, width), F32)],
        )
        grad_w_adaln = dot_tn(cond_act, gathered(grad_mod[:images]))
        sums = [attn_gain_sum[0], ffn_gain_sum[0]]
        sums += [row.reshape(heads, HEAD_DIM).T for row in gain_sums[:3]]
        sums = lax.psum(sums, "dp")
        own = [
            lax.dynamic_slice_in_dim(whole, dp_rank * (whole.shape[0] // n_dp), whole.shape[0] // n_dp, 0)
            for whole in sums
        ]
        own.append(lax.psum(jnp.sum(gain_sums[3].reshape(heads, HEAD_DIM), axis=1), "dp"))
    else:
        grad_qv, grad_ko, grad_text, result, grad_tokens, grad_w_adaln, *own = exchange(
            functools.partial(last_exchange_kernel, n_tensor),
            [
                (struct((size, 2 * local), F32), vmem),
                (struct((size, 2 * local), F32), vmem),
                (struct((2 * local, depth), F32), vmem),
                (struct((rows, width)), vmem),
                (struct((rows, width)), vmem),
                (struct((cond_rows, span), F32), vmem),
            ]
            + [(struct((1, gain_attn.size), F32), vmem)] * 2
            + [(struct(gain_query.shape, F32), vmem)] * 3
            + [(struct((1, heads), F32), vmem)],
            outside(
                caption_rows, grad_text_all, total_qv, total_ko, token_rows, grad_hidden, attn_out
            )
            + inside(
                attn_in_part, member, attn_gain, mods, cond_act, gain_sums, result_rows, gate_part, ffn_mod,
                ffn_gain_sum,
            ),
            reduce_scratch(size, 2 * local) * 2
            + reduce_scratch(2 * local, depth)
            + [
                vmem((parts, 2 * local, depth), BF16),
                vmem((2, images * TXT, depth), BF16),
                wide,
                vmem((n_tensor, padded, width), BF16),
                vmem((padded, width), F32),
                vmem((padded, width), BF16),
                arrived,
                wide,
                wide,
                vmem((rows, width), F32),
                vmem((2, width), F32),
                vmem((1, width), F32),
                vmem((parts, padded, width), BF16),
                vmem((parts, 2, width), F32),
                vmem((parts, 1, width), F32),
                vmem((8, 128), F32),
                dma((2,)),
                dma((2, 3, 10)),
                dma((2, 4, n_tensor - 1)),
                dma((2, 3, 8)),
                vmem((2 * local, images * TXT), BF16),
                vmem((width, 2 * local), BF16),
                vmem((width, 2 * local), BF16),
                wide,
                vmem((rows, width), F32),
                wide,
                dma((6,)),
            ],
            3,
            vmem=62,
        )
        own[:2] = [part[0] for part in own[:2]]
        own[5] = own[5][0]
        plain = [*grad_f, grad_w_adaln, result, grad_tokens]
        square, tall = struct((size, local), F32), struct((depth, local), F32)
        (
            grad_query, grad_key, grad_value, grad_out, grad_tk, grad_tv, *plain
        ) = pl.pallas_call(
            emit_kernel,
            out_shape=[square] * 4 + [tall] * 2 + [struct(x.shape, x.dtype) for x in plain],
            in_specs=[pl.BlockSpec(memory_space=anywhere)] * (3 + len(plain)),
            out_specs=[pl.BlockSpec(memory_space=anywhere)] * (6 + len(plain)),
            scratch_shapes=[vmem(x.shape, x.dtype) for x in (grad_qv, grad_ko, grad_text, *plain)]
            + [
                vmem((depth, local), F32),
                vmem((depth, local), F32),
                dma((3 + len(plain),)),
                dma((6 + len(plain),)),
            ],
            compiler_params=pltpu.CompilerParams(vmem_limit_bytes=62 * 2**20),
        )(grad_qv, grad_ko, grad_text, *plain)
        *grad_f, grad_w_adaln, result, grad_tokens = plain

    return (
        result.reshape(micro, count, width),
        grad_tokens.reshape(micro, count, width),
        grad_query,
        grad_key,
        grad_value,
        grad_out,
        grad_tk,
        grad_tv,
        *grad_f,
        grad_w_adaln,
        *own,
    )


def solution(mesh):
    return jax.shard_map(
        functools.partial(shards, mesh.shape["dp"], mesh.shape["tensor"]),
        mesh=mesh,
        in_specs=(
            P(None, "dp", None),
            P(None, "dp", None),
            P(None, "dp", None, None),
            P(None, "dp", None),
            P(None, "dp"),
            P("dp", "tensor"),
            P("dp", "tensor"),
            P("dp", "tensor"),
            P("dp", "tensor"),
            P("dp", "tensor"),
            P("dp", "tensor"),
            P("dp", "tensor"),
            P("dp", "tensor"),
            P("dp", "tensor"),
            P("dp", "tensor"),
            P("dp"),
            P("dp"),
            P("dp", "tensor"),
            P("dp", "tensor"),
            P("dp", "tensor"),
            P("tensor"),
            P(None, "dp", None),
        ),
        out_specs=(
            P(None, "dp", None),
            P(None, "dp", None),
            P("dp", "tensor"),
            P("dp", "tensor"),
            P("dp", "tensor"),
            P("dp", "tensor"),
            P("dp", "tensor"),
            P("dp", "tensor"),
            P("dp", "tensor"),
            P("dp", "tensor"),
            P("dp", "tensor"),
            P("dp", "tensor"),
            P("dp"),
            P("dp"),
            P("dp", "tensor"),
            P("dp", "tensor"),
            P("dp", "tensor"),
            P("tensor"),
        ),
        check_vma=False,
    )
```

```python
import functools

import jax
import jax.numpy as jnp
from jax import lax
from jax.experimental import pallas as pl
from jax.experimental.pallas import tpu as pltpu
from jax.sharding import PartitionSpec as P

HEAD_DIM = 64
DT = 4096
TXT = 256


EPSILON = 1e-06
MASKED = -1e30
ROPE_BASE = 10000.0
STRIP = 16
F32 = jnp.float32
BF16 = jnp.bfloat16


def image_layout(shapes, count):
    height = shapes[:, 0]
    stride_all = shapes[:, 1] + 1
    extent = height * stride_all
    finish = jnp.cumsum(extent)
    begin = finish - extent
    places = jnp.arange(count, dtype=jnp.int32)
    member = (places[:, None] >= begin[None, :]) & (places[:, None] < finish[None, :])
    member_int = member.astype(jnp.int32)
    inside = jnp.sum(member_int, axis=1)
    slot_ids = jnp.arange(shapes.shape[0], dtype=jnp.int32)
    segment = jnp.sum(member_int * slot_ids[None, :], axis=1)
    stride = jnp.sum(member_int * stride_all[None, :], axis=1) + 1 - inside
    offset = places - jnp.sum(member_int * begin[None, :], axis=1)
    return (member.astype(jnp.float32), segment, inside, offset // stride, offset % stride)


def rope_tables(row_pos, col_pos):
    quarter = HEAD_DIM // 4
    freq = ROPE_BASE ** (-jnp.arange(quarter, dtype=jnp.float32) / quarter)
    angles = jnp.stack(
        [
            row_pos.astype(jnp.float32)[:, None] * freq[None, :],
            col_pos.astype(jnp.float32)[:, None] * freq[None, :],
        ],
        axis=1,
    )
    return (jnp.cos(angles), jnp.sin(angles))


def dot_nn(left, right):
    return lax.dot_general(left, right, (((1,), (0,)), ((), ())), preferred_element_type=F32)


def dot_nt(left, right):
    return lax.dot_general(left, right, (((1,), (1,)), ((), ())), preferred_element_type=F32)


def dot_tn(left, right):
    return lax.dot_general(left, right, (((0,), (0,)), ((), ())), preferred_element_type=F32)


def struct(shape, dtype=BF16):
    return jax.ShapeDtypeStruct(shape, dtype)


def run(body, outs, ins, scratch=(), flops=0, traffic=0, vmem=48):
    return pl.pallas_call(
        body,
        out_shape=outs,
        in_specs=[pl.BlockSpec(memory_space=space) for _, space in ins],
        out_specs=[pl.BlockSpec(memory_space=pltpu.VMEM)] * len(outs),
        scratch_shapes=list(scratch),
        compiler_params=pltpu.CompilerParams(vmem_limit_bytes=vmem * 2**20),
        cost_estimate=pl.CostEstimate(flops=flops, bytes_accessed=traffic, transcendentals=0),
    )(*[array for array, _ in ins])


def load(source, target, sem):
    copy = pltpu.make_async_copy(source, target, sem)
    copy.start()
    return copy


def wait_all(copies):
    for copy in copies:
        copy.wait()


def token_columns(member, mods, which, target):
    target[...] = dot_nn(member[...], mods[which]).astype(BF16)


def over_strips(rows, step):
    @pl.loop(0, rows // STRIP)
    def _(index):
        step(pl.ds(pl.multiple_of(index * STRIP, STRIP), STRIP))


def head_sum(values, blocks):
    high = values.astype(BF16)
    low = (values - high.astype(F32)).astype(BF16)
    return dot_nn(high, blocks) + dot_nn(low, blocks)


def head_blocks(width):
    row = lax.broadcasted_iota(jnp.int32, (width, width), 0) // HEAD_DIM
    column = lax.broadcasted_iota(jnp.int32, (width, width), 1) // HEAD_DIM
    return jnp.where(row == column, 1.0, 0.0).astype(BF16)


def swap_pairs(values):
    width = values.shape[1]
    quarter = HEAD_DIM // 4
    lane = lax.broadcasted_iota(jnp.int32, values.shape, 1)
    former = lax.rem(lane, 2 * quarter) < quarter
    return jnp.where(
        former, pltpu.roll(values, width - quarter, 1), pltpu.roll(values, quarter, 1)
    )


def head_norm(values, gain, blocks):
    scale = lax.rsqrt(head_sum(values * values, blocks) * (1.0 / HEAD_DIM) + EPSILON)
    return values * scale * gain


def head_norm_back(values, gain, grad, blocks):
    scale = lax.rsqrt(head_sum(values * values, blocks) * (1.0 / HEAD_DIM) + EPSILON)
    normed = values * scale
    grad_gain = jnp.sum(grad * normed, axis=0, keepdims=True)
    inner = grad * gain
    mean = head_sum(inner * normed, blocks) * (1.0 / HEAD_DIM)
    return scale * (inner - normed * mean), grad_gain


def row_scale(values):
    return lax.rsqrt(jnp.mean(values * values, axis=1, keepdims=True) + EPSILON)


MESH = pl.DeviceIdType.MESH
PAIR, ALONG_X, ALONG_Y = 1, 2, 4


def partner(mask):
    rank = lax.axis_index("dp")
    index = rank
    for bit in (1, 2, 4):
        flip = lax.rem(mask // bit, 2)
        index = index + flip * (bit - 2 * bit * lax.rem(rank // bit, 2))
    return index


def announce(masks, shifts, n_tensor):
    barrier = pltpu.get_barrier_semaphore()
    rank = lax.axis_index("tensor")
    for mask in masks:
        pl.semaphore_signal(
            barrier, inc=1, device_id={"dp": partner(mask)}, device_id_type=MESH
        )
    for shift in shifts:
        pl.semaphore_signal(
            barrier,
            inc=1,
            device_id={"tensor": lax.rem(rank + shift, n_tensor)},
            device_id_type=MESH,
        )


def greet(masks, shifts, n_tensor):
    announce(masks, shifts, n_tensor)
    pl.semaphore_wait(pltpu.get_barrier_semaphore(), len(masks) + len(shifts))


def send(source, target, sems, index, device):
    copy = pltpu.make_async_remote_copy(
        src_ref=source,
        dst_ref=target,
        send_sem=sems.at[(0,) + index],
        recv_sem=sems.at[(1,) + index],
        device_id=device,
        device_id_type=MESH,
    )
    copy.start()
    return copy


def gather_kernel(
    n_tensor, shard_tk, shard_tv, shard_qv, shard_ko, context, attn_own, ffn_own, q_own, k_own,
    t_own, w_adaln, captions,
    text_raw, text_key, text_value, qv, ko, cond_act, mods, attn_gain, ffn_gain, q_gain, k_gain, t_gain,
    small, small_all, product, sums, tk, tv, blocks, block, stage, block_sems, stage_sems, own_sems, shard_sems, small_sems, mod_sems, tensor_sems,
):
    rank, tensor_rank = lax.axis_index("dp"), lax.axis_index("tensor")
    masks = range(1, 8)
    shifts = range(1, n_tensor)
    greet(masks, shifts, n_tensor)
    groups = ((shard_tk, tk), (shard_tv, tv), (shard_qv, qv), (shard_ko, ko))

    def rows_of(shard, index, first, size):
        return pl.ds(pl.multiple_of(index * shard.shape[0] + first, 32), size)

    firsts, seconds, pairs, locals_ = {}, {}, {}, []

    def step_1(number):
        shard, whole = groups[number]
        mine = whole.at[rows_of(shard, rank, 0, shard.shape[0])]
        firsts[number] = [
            send(shard, mine, shard_sems, (number, place), {"dp": partner(mask)})
            for place, mask in ((0, ALONG_X), (1, ALONG_Y))
        ]
        pairs[number] = [send(shard, mine, shard_sems, (number, 4), {"dp": partner(PAIR)})]
        local = pltpu.make_async_copy(shard, mine, own_sems.at[number])
        local.start()
        locals_.append(local)

    def step_2(number):
        shard, whole = groups[number]
        size = shard.shape[0]
        half = size // 2
        seconds[number] = []
        for place, mask, onward, start in ((0, ALONG_X, ALONG_Y, half), (1, ALONG_Y, ALONG_X, 0)):
            firsts[number][place].wait_recv()
            part = whole.at[rows_of(shard, partner(mask), start, half)]
            seconds[number].append(
                send(part, part, shard_sems, (number, 2 + place), {"dp": partner(onward)})
            )
            piece = whole.at[rows_of(shard, partner(mask), 0, size)]
            pairs[number].append(
                send(piece, piece, shard_sems, (number, 5 + place), {"dp": partner(PAIR)})
            )

    def step_3(number):
        shard, whole = groups[number]
        half = shard.shape[0] // 2
        for place, start in ((0, half), (1, 0)):
            seconds[number][place].wait_recv()
            part = whole.at[rows_of(shard, partner(ALONG_X + ALONG_Y), start, half)]
            pairs[number].append(
                send(part, part, shard_sems, (number, 7 + place), {"dp": partner(PAIR)})
            )

    def step_4(number):
        for copy in pairs[number]:
            copy.wait_recv()
        locals_[number].wait()

    count = captions.shape[0]

    def fetch(image, slot):
        return pltpu.make_async_copy(captions.at[image], block.at[slot], block_sems.at[slot])

    outputs = (text_raw, text_key, text_value)
    kinds = ((0, 1), (2,))

    def store(image, slot, kind):
        return [
            pltpu.make_async_copy(
                stage.at[slot, index], outputs[index].at[image], stage_sems.at[slot, index]
            )
            for index in kinds[kind]
        ]

    def text_images(low, high, kind):
        @pl.loop(low, high)
        def _(image):
            slot = lax.rem(image, 2)

            @pl.when(image < count - 1)
            def _():
                fetch(image + 1, 1 - slot).start()

            if kind == 0:

                @pl.when(image == count - 1)
                def _():
                    fetch(0, 1 - slot).start()

            fetch(image, slot).wait()

            @pl.when(image >= 2)
            def _():
                wait_all(store(image - 2, slot, kind))

            if kind == 0:
                raw = dot_nn(block[slot], tk[...])
                stage[slot, 0] = raw.astype(BF16)
                stage[slot, 1] = head_norm(raw, t_gain[...], blocks[...]).astype(BF16)
            else:
                stage[slot, 2] = dot_nn(block[slot], tv[...]).astype(BF16)
            for copy in store(image, slot, kind):
                copy.start()

    fetch(0, 0).start()
    step_1(0)
    blocks[...] = head_blocks(tk.shape[1])
    small_copies = []
    images, slots = context.shape[0] * context.shape[1], context.shape[1]
    depth = w_adaln.shape[0]
    gain_size = attn_own.shape[1]
    heads = q_own.shape[1]
    small[...] = jnp.zeros_like(small)
    for index in range(8):
        for first in range(0, images, slots):
            small[index, first : first + slots, :] = context[
                first // slots, :, index * depth : (index + 1) * depth
            ]
        for row, own in ((16, attn_own), (18, ffn_own)):
            for place, first in enumerate(range(0, gain_size, depth)):
                size = min(depth, gain_size - first)
                small[index, row + place : row + place + 1, :size] = own[:, first : first + size]
        for place, own in enumerate((q_own, k_own, t_own)):
            small[index, 24:32, 8 * place : 8 * place + heads] = own[...]
    for mask in masks:
        small_copies.append(
            send(
                small.at[partner(mask)], small_all.at[rank], small_sems, (mask,),
                {"dp": partner(mask)},
            )
        )
    small_all[rank] = small[rank]
    for copy in small_copies:
        copy.wait_recv()
    width = w_adaln.shape[1]
    contexts = small_all[:, 0:16, :].astype(F32).reshape(8 * 16, depth)
    cond_act[...] = jax.nn.silu(contexts).astype(BF16)
    product[...] = dot_nn(cond_act[...], w_adaln[...]).astype(BF16).reshape(8, 16, width)
    mod_copies = [
        send(
            product.at[partner(mask)], sums.at[mask], mod_sems, (mask,), {"dp": partner(mask)}
        )
        for mask in masks
    ]
    step_2(0)
    step_1(1)
    for row, out in ((16, attn_gain), (18, ffn_gain)):
        for index in range(8):
            for place, first in enumerate(range(0, gain_size, depth)):
                size = min(depth, gain_size - first)
                start = index * gain_size + first
                out[:, start : start + size] = small_all[
                    index, row + place : row + place + 1, :size
                ].astype(F32)
    turned = jnp.transpose(small_all[:, 24:32, :].astype(F32).reshape(HEAD_DIM, depth))
    for place, out in enumerate((q_gain, k_gain, t_gain)):
        for head in range(heads):
            out[:, head * HEAD_DIM : (head + 1) * HEAD_DIM] = turned[
                8 * place + head : 8 * place + head + 1, :
            ]
    sums[0] = product[rank]
    for copy in mod_copies:
        copy.wait_recv()
    total = sums[0].astype(F32)
    for mask in masks:
        total = total + sums[mask].astype(F32)
    mods[tensor_rank] = total.astype(BF16)
    tensor_copies = [
        send(
            mods.at[tensor_rank], mods.at[tensor_rank], tensor_sems, (shift,),
            {"tensor": lax.rem(tensor_rank + shift, n_tensor)},
        )
        for shift in shifts
    ]

    step_3(0)
    step_4(0)
    third = count // 3
    text_images(0, third, 0)
    step_2(1)
    step_1(2)
    step_1(3)
    text_images(third, 2 * third, 0)
    step_3(1)
    text_images(2 * third, count, 0)
    step_4(1)
    text_images(0, third, 1)
    step_2(2)
    step_2(3)
    text_images(third, 2 * third, 1)
    text_images(2 * third, count, 1)
    step_3(2)
    step_3(3)
    step_4(2)
    step_4(3)
    for image in (count - 2, count - 1):
        for kind in (0, 1):
            wait_all(store(image, image % 2, kind))
    for copy in tensor_copies:
        copy.wait_recv()
    for number in range(4):
        for copy in firsts[number] + seconds[number] + pairs[number]:
            copy.wait_send()
    for copy in small_copies + mod_copies + tensor_copies:
        copy.wait_send()


ROUTES = ((0, 1, 2, ALONG_X, ALONG_Y), (1, 2, 1, ALONG_Y, ALONG_X))
REDUCE_STRIP = 32


def over_half(half, step):
    @pl.loop(0, half // REDUCE_STRIP)
    def _(index):
        step(pl.multiple_of(index * REDUCE_STRIP, REDUCE_STRIP))


class Reduce:
    def __init__(self, number, read, out, from_pair, out_2, in_2, out_3, in_3, sems):
        self.number, self.read, self.out, self.sems = number, read, out, sems
        self.from_pair, self.out_2, self.in_2, self.out_3, self.in_3 = (
            from_pair, out_2, in_2, out_3, in_3
        )
        self.half = out.shape[0] // 2
        self.copies, self.arriving = [], {}

    def pair_term(self, piece, low):
        there = pl.ds(low, REDUCE_STRIP)
        return self.read(piece, low) + self.from_pair[piece, there, :].astype(F32)

    def move(self, source, target, index, mask):
        return pltpu.make_async_remote_copy(
            src_ref=source,
            dst_ref=target,
            send_sem=self.sems.at[0, self.number, index],
            recv_sem=self.sems.at[1, self.number, index],
            device_id={"dp": partner(mask)},
            device_id_type=MESH,
        )

    def first(self, piece, source):
        return self.move(source, self.from_pair.at[piece], piece, PAIR)

    def second(self, piece, copy):
        copy.wait_recv()
        self.copies.append(copy)
        for side, close, far, first, last in ROUTES:
            if piece not in (close, 3):
                continue
            slot = 1 if piece == 3 else 0

            def step(low):
                self.out_2[side, slot, pl.ds(low, REDUCE_STRIP), :] = self.pair_term(
                    piece, pl.multiple_of(low + side * self.half, REDUCE_STRIP)
                ).astype(BF16)

            over_half(self.half, step)
            moved = self.move(
                self.out_2.at[side, slot], self.in_2.at[side, slot], 4 + 2 * side + slot, first
            )
            moved.start()
            self.arriving[side, slot] = moved
            self.copies.append(moved)

    def third(self):
        for side, close, far, first, last in ROUTES:
            self.arriving[side, 1].wait_recv()

            def step(low):
                here = pl.ds(low, REDUCE_STRIP)
                there = pl.multiple_of(low + side * self.half, REDUCE_STRIP)
                self.out_3[side, here, :] = (
                    self.pair_term(far, there) + self.in_2[side, 1, here, :].astype(F32)
                ).astype(BF16)

            over_half(self.half, step)
            moved = self.move(self.out_3.at[side], self.in_3.at[side], 8 + side, last)
            moved.start()
            self.arriving[side, 2] = moved
            self.copies.append(moved)

    def last(self):
        for side in (0, 1):
            self.arriving[side, 0].wait_recv()
            self.arriving[side, 2].wait_recv()

            def step(low):
                here = pl.ds(low, REDUCE_STRIP)
                there = pl.multiple_of(low + side * self.half, REDUCE_STRIP)
                self.out[pl.ds(there, REDUCE_STRIP), :] = (
                    self.pair_term(0, there)
                    + self.in_2[side, 0, here, :].astype(F32)
                    + self.in_3[side, here, :].astype(F32)
                )

            over_half(self.half, step)
        for copy in self.copies:
            copy.wait_send()


def reduce_scratch(depth, columns):
    half = depth // 2
    return [
        pltpu.VMEM((4, depth, columns), BF16),
        pltpu.VMEM((2, 2, half, columns), BF16),
        pltpu.VMEM((2, 2, half, columns), BF16),
        pltpu.VMEM((2, half, columns), BF16),
        pltpu.VMEM((2, half, columns), BF16),
    ]


def piece_reader(total, size):
    def read(piece, low):
        first = partner(2 * piece) * size + low
        return total[pl.ds(pl.multiple_of(first, 32), REDUCE_STRIP), :].astype(F32)

    return read


def reduce_firsts(reduce, total, size):
    copies = {}
    for piece in (3, 2, 1, 0):
        copies[piece] = reduce.first(piece, piece_of(total, 2 * piece + 1, size))
        copies[piece].start()
    return copies


def piece_of(total, mask, size):
    return total.at[pl.ds(pl.multiple_of(partner(mask) * size, 64), size)]


class TensorSum:
    def __init__(self, number, n_tensor, arrived, sems):
        self.number, self.n_tensor, self.arrived, self.sems = number, n_tensor, arrived, sems
        self.rank = lax.axis_index("tensor")
        self.size = arrived.shape[1]
        self.others = [
            (shift - 1, lax.rem(self.rank + shift, n_tensor)) for shift in range(1, n_tensor)
        ]

    def block(self, index):
        return pl.ds(pl.multiple_of(index * self.size, 16), self.size)

    def scatter(self, partial):
        self.partial = partial
        self.firsts = [
            send(
                partial.at[self.block(other)], self.arrived.at[place], self.sems,
                (2 * self.number, place), {"tensor": other},
            )
            for place, other in self.others
        ]

    def add(self, out, whole):
        for copy in self.firsts:
            copy.wait_recv()

        @pl.loop(0, self.size // STRIP)
        def _(index):
            low = pl.multiple_of(index * STRIP, STRIP)
            there = pl.ds(pl.multiple_of(self.rank * self.size + low, STRIP), STRIP)
            total = self.partial[there, :].astype(F32)
            for place, _ in self.others:
                total = total + self.arrived[place, pl.ds(low, STRIP), :].astype(F32)
            out[there if whole else pl.ds(low, STRIP), :] = total.astype(BF16)

        for copy in self.firsts:
            copy.wait_send()

    def gather(self, out):
        mine = out.at[self.block(self.rank)]
        self.seconds = [
            send(mine, mine, self.sems, (2 * self.number + 1, place), {"tensor": other})
            for place, other in self.others
        ]

    def finish(self):
        for copy in self.seconds:
            copy.wait()


def tensor_kernel(n_tensor, partial, out, arrived, sems):
    greet((), range(1, n_tensor), n_tensor)
    total = TensorSum(0, n_tensor, arrived, sems)
    total.scatter(partial)
    total.add(out, True)
    total.gather(out)
    total.finish()


def emit_kernel(*refs):
    count = (len(refs) - 16) // 3
    sources, refs = refs[: 3 + count], refs[3 + count :]
    outs, refs = refs[: 6 + count], refs[6 + count :]
    held, (turned_key, turned_value, in_sems, sems) = refs[: 3 + count], refs[3 + count :]
    loads = [load(far, here, in_sems.at[i]) for i, (far, here) in enumerate(zip(sources, held))]
    query, key, value, out, text_key, text_value = outs[:6]
    width = query.shape[1]
    copies = []

    def put(here, target):
        copies.append(load(here, target, sems.at[len(copies)]))

    for index in range(3, 3 + count):
        loads[index].wait()
        put(held[index], outs[3 + index])
    for index, first, second in ((0, query, value), (1, key, out)):
        loads[index].wait()
        put(held[index].at[:, :width], first)
        put(held[index].at[:, width:], second)
    loads[2].wait()
    turned_key[...] = jnp.transpose(held[2][:width, :])
    put(turned_key, text_key)
    turned_value[...] = jnp.transpose(held[2][width:, :])
    put(turned_value, text_value)
    wait_all(copies)


def exchange(body, outs, ins, scratch, collective, vmem=48):
    spaces = [space for _, space in outs]
    return pl.pallas_call(
        body,
        out_shape=[shape for shape, _ in outs],
        in_specs=[pl.BlockSpec(memory_space=space) for _, space in ins],
        out_specs=[pl.BlockSpec(memory_space=space) for space in spaces],
        scratch_shapes=scratch,
        compiler_params=pltpu.CompilerParams(
            collective_id=collective, has_side_effects=True, vmem_limit_bytes=vmem * 2**20
        ),
    )(*[array for array, _ in ins])


def project_kernel(
    tokens, member, gain, q_gain, k_gain, cosine, sine, mods, whole_a, whole_b,
    attn_in, query_raw, key_raw, query_rot, key_rot, value, mat_a, mat_b, mod, sems
):
    copies = [load(whole_a, mat_a, sems.at[0]), load(whole_b, mat_b, sems.at[1])]
    width = q_gain.shape[1]
    token_columns(member, mods, 0, mod)
    blocks = head_blocks(width)

    def step(at):
        x = tokens[at, :].astype(F32)
        normed = x * row_scale(x)
        attn_in[at, :] = (normed * gain[...] * (1.0 + mod[at, :].astype(F32))).astype(BF16)

    over_strips(tokens.shape[0], step)
    wait_all(copies)
    query_raw[...] = dot_nn(attn_in[...], mat_a[:, :width])
    key_raw[...] = dot_nn(attn_in[...], mat_b[:, :width])
    value[...] = dot_nn(attn_in[...], mat_a[:, width:]).astype(BF16)
    for raw, head_gain, out in ((query_raw, q_gain, query_rot), (key_raw, k_gain, key_rot)):
        normed = head_norm(raw[...], head_gain[...], blocks)
        out[...] = (normed * cosine[...] + swap_pairs(normed) * sine[...]).astype(BF16)


def text_kernel(
    live, source, captions, gain, whole_k, whole_v,
    text_raw, text_key, text_value, mat_k, mat_v, sems
):
    image = pl.program_id(0)

    @pl.when(image == 0)
    def _():
        wait_all([load(whole_k, mat_k, sems.at[0]), load(whole_v, mat_v, sems.at[1])])

    @pl.when(live[image] > 0)
    def _():
        raw = dot_nn(captions[0], mat_k[...])
        text_raw[0] = raw.astype(BF16)
        text_key[0] = head_norm(raw, gain[...], head_blocks(raw.shape[1])).astype(BF16)
        text_value[0] = dot_nn(captions[0], mat_v[...]).astype(BF16)


def stack_pair(values):
    lane = lax.broadcasted_iota(jnp.int32, (1, 2 * HEAD_DIM), 1)
    first = jnp.where(lane < HEAD_DIM, 1.0, 0.0).astype(values.dtype)
    second = jnp.where(lane < HEAD_DIM, 0.0, 1.0).astype(values.dtype)
    return jnp.concatenate([values * first, values * second], axis=0)


def unstack_pair(values):
    count = values.shape[0] // 2
    lane = lax.broadcasted_iota(jnp.int32, (count, 2 * HEAD_DIM), 1)
    return jnp.where(lane < HEAD_DIM, values[:count], values[count:])


def twice(values):
    return jnp.concatenate([values, values], axis=0)


def softmax(scores, allowed, rows_live):
    scores = jnp.where(allowed, scores, MASKED)
    expo = jnp.where(allowed, jnp.exp(scores - jnp.max(scores, axis=1, keepdims=True)), 0.0)
    total = jnp.sum(expo, axis=1, keepdims=True)
    if rows_live is not None:
        total = jnp.where(rows_live, total, 1.0)
    return expo * (1.0 / total)


def attend_kernel(
    micro, scale, live, text_len, query, key, value, text_key_far, text_value_far,
    self_id, self_row, segment, gate, whole_b, mixed, cross_out, whole,
    mat_b, text_key, text_value, self_out, sem, sems
):
    text_copies = [
        load(text_key_far, text_key, sems.at[0]), load(text_value_far, text_value, sems.at[1])
    ]
    copies = [load(whole_b, mat_b, sem)]
    rows, width = query.shape
    count = rows // micro
    slots = text_key.shape[0] // micro
    heads = width // HEAD_DIM
    cross_out[...] = jnp.zeros_like(cross_out)

    for batch in range(micro):
        at = slice(batch * count, (batch + 1) * count)
        allowed = twice(self_id[at, :]) == self_row[batch : batch + 1, :]
        for first in range(0, width, 2 * HEAD_DIM):
            lanes = slice(first, first + 2 * HEAD_DIM)
            scores = dot_nt(stack_pair(query[at, lanes]), key[at, lanes]) * scale
            probs = softmax(scores, allowed, None).astype(BF16)
            self_out[at, lanes] = unstack_pair(dot_nn(probs, value[at, lanes]))
    wait_all(text_copies)

    @pl.loop(0, micro * slots)
    def _(image):
        @pl.when(live[image] > 0)
        def _():
            at = pl.ds(pl.multiple_of((image // slots) * count, count), count)
            mine = twice(segment[at, :]) == lax.rem(image, slots)
            column = lax.broadcasted_iota(jnp.int32, (2 * count, TXT), 1)
            allowed = mine & (column < text_len[image])
            for first in range(0, width, 2 * HEAD_DIM):
                lanes = slice(first, first + 2 * HEAD_DIM)
                scores = dot_nt(stack_pair(query[at, lanes]), text_key[image, :, lanes]) * scale
                probs = softmax(scores, allowed, mine).astype(BF16)
                cross_out[at, lanes] += unstack_pair(dot_nn(probs, text_value[image, :, lanes]))

    mixed[...] = (self_out[...] + gate[...] * cross_out[...]).astype(BF16)
    wait_all(copies)
    whole[...] = dot_nt(mixed[...], mat_b[:, width:]).astype(BF16)


def feed_kernel(
    tokens, member, gain, cotangent, mods, attn_out, whole_f,
    hidden, ffn_in, inner, grad_gate, grad_up, grad_out, whole,
    mat, mod_1, mod_2, mod_3, sem
):
    copies = [load(whole_f, mat, sem)]
    units = inner.shape[1]
    mat_a, mat_b, mat_c = [mat.at[:, i * units : (i + 1) * units] for i in range(3)]
    token_columns(member, mods, 1, mod_1)
    token_columns(member, mods, 2, mod_2)
    token_columns(member, mods, 3, mod_3)

    def step(at):
        gate_attn = jnp.tanh(mod_1[at, :].astype(F32))
        state = tokens[at, :].astype(F32) + gate_attn * attn_out[at, :].astype(F32)
        hidden[at, :] = state
        normed = state * row_scale(state)
        ffn_in[at, :] = (normed * gain[...] * (1.0 + mod_2[at, :].astype(F32))).astype(BF16)
        gate_ffn = jnp.tanh(mod_3[at, :].astype(F32))
        grad_out[at, :] = (gate_ffn * cotangent[at, :].astype(F32)).astype(BF16)

    rows = tokens.shape[0]
    over_strips(rows, step)
    wait_all(copies)
    chunk = 256
    for first in range(0, units, chunk):
        span = slice(first, first + chunk)
        gate = dot_nn(ffn_in[...], mat_a[:, span])
        up = dot_nn(ffn_in[...], mat_b[:, span])
        grad_inner = dot_nn(grad_out[...], mat_c[:, span])
        turn = jax.nn.sigmoid(gate)
        active = gate * turn
        inner[:, span] = (active * up).astype(BF16)
        grad_up[:, span] = (grad_inner * active).astype(BF16)
        slope = turn * (1.0 + gate * (1.0 - turn))
        grad_gate[:, span] = (grad_inner * up * slope).astype(BF16)
    width = tokens.shape[1]
    for first in range(0, width, 512):
        span = slice(first, first + 512)
        whole[:, span] = (
            dot_nt(grad_gate[...], mat_a[span, :]) + dot_nt(grad_up[...], mat_b[span, :])
        ).astype(BF16)


def feed_grad_kernel(grad_out, inner, ffn_in, grad_gate, grad_up, total):
    units = inner.shape[1]
    step = 256
    for index, (left, right) in enumerate(
        ((ffn_in, grad_gate), (ffn_in, grad_up), (grad_out, inner))
    ):
        for first in range(0, units, step):
            out = slice(index * units + first, index * units + first + step)
            total[:, out] = dot_tn(left[...], right[:, first : first + step]).astype(BF16)


def feed_out_kernel(inner, whole_f, partial, mat, sem):
    units = inner.shape[1]
    copy = load(whole_f.at[:, 2 * units : 3 * units], mat, sem)
    copy.wait()
    for first in range(0, partial.shape[1], 512):
        span = slice(first, first + 512)
        partial[:, span] = dot_nt(inner[...], mat[span, :]).astype(BF16)


def modulate_back(values, gain, shift, grad):
    scale = row_scale(values)
    normed = values * scale
    inner = grad * gain * (1.0 + shift)
    mean = jnp.mean(inner * normed, axis=1, keepdims=True)
    return scale * (inner - normed * mean), grad * normed


def mixed_grad_kernel(
    hidden, member, gain, cotangent, mods, grad_in, whole_b,
    grad_hidden, grad_out, grad_mixed, mat_b, mod_1, mod_2, sem
):
    copies = [load(whole_b, mat_b, sem)]
    token_columns(member, mods, 1, mod_1)
    token_columns(member, mods, 2, mod_2)

    def step(at):
        back, _ = modulate_back(
            hidden[at, :], gain[...], mod_2[at, :].astype(F32), grad_in[at, :].astype(F32)
        )
        total = cotangent[at, :].astype(F32) + back
        grad_hidden[at, :] = total
        grad_out[at, :] = (jnp.tanh(mod_1[at, :].astype(F32)) * total).astype(BF16)

    over_strips(hidden.shape[0], step)
    wait_all(copies)
    width = grad_mixed.shape[1]
    grad_mixed[...] = dot_nn(grad_out[...], mat_b[:, width:])


def feed_exchange_kernel(
    n_tensor, tokens, member, gain, cotangent, mods, attn_out, whole_f, whole_ko,
    hidden, grad_hidden, grad_attn_out, grad_mixed, result_rows, gate_part, ffn_mod, gain_sum, *rest
):
    outs, rest = rest[:3], rest[3:]
    (
        ffn_in, inner, grad_gate, grad_up, grad_out, ffn_part, out_part,
        mat, mod_1, mod_2, mod_3, grad_in, ffn_rows, wide_grad, rows_grad, *rest
    ) = rest
    totals, rest = rest[:3], rest[3:]
    buffers, (arrived_1, arrived_2, sem, mat_sem, sems, tensor_sems) = rest[:15], rest[15:]
    announce((PAIR, ALONG_X, ALONG_Y), range(1, n_tensor), n_tensor)
    feed_kernel(
        tokens, member, gain, cotangent, mods, attn_out, whole_f,
        hidden, ffn_in, inner, grad_gate, grad_up, grad_out, ffn_part,
        mat, mod_1, mod_2, mod_3, sem,
    )
    pl.semaphore_wait(pltpu.get_barrier_semaphore(), 3 + n_tensor - 1)
    sum_in = TensorSum(0, n_tensor, arrived_1, tensor_sems)
    sum_in.scatter(ffn_part)
    size = outs[0].shape[0]
    reduces, firsts = [], []
    for number, (left, right) in enumerate(
        ((ffn_in, grad_gate), (ffn_in, grad_up), (grad_out, inner))
    ):
        total = totals[number]
        for first in range(0, total.shape[1], 256):
            span = slice(first, first + 256)
            total[:, span] = dot_tn(left[...], right[:, span]).astype(BF16)
        reduce = Reduce(
            number, piece_reader(total, size), outs[number],
            *buffers[5 * number : 5 * number + 5], sems,
        )
        reduces.append(reduce)
        firsts.append(reduce_firsts(reduce, total, size))
    units = inner.shape[1]
    for first in range(0, out_part.shape[1], 512):
        span = slice(first, first + 512)
        out_part[:, span] = dot_nt(inner[...], mat[span, 2 * units :]).astype(BF16)
    sum_out = TensorSum(1, n_tensor, arrived_2, tensor_sems)
    for piece in (3, 2, 1, 0):
        for number in range(3):
            reduces[number].second(piece, firsts[number][piece])
    sum_in.add(grad_in, True)
    sum_in.gather(grad_in)
    for reduce in reduces:
        reduce.third()
    sum_in.finish()
    sum_out.scatter(out_part)
    head_width = grad_mixed.shape[1]
    copy = load(whole_ko.at[:, head_width:], mat.at[:, :head_width], mat_sem)

    def step(at):
        back, _ = modulate_back(
            hidden[at, :], gain[...], mod_2[at, :].astype(F32), grad_in[at, :].astype(F32)
        )
        total = cotangent[at, :].astype(F32) + back
        grad_hidden[at, :] = total
        grad_attn_out[at, :] = (jnp.tanh(mod_1[at, :].astype(F32)) * total).astype(BF16)

    over_strips(hidden.shape[0], step)
    copy.wait()
    grad_mixed[...] = dot_nn(grad_attn_out[...], mat[:, :head_width])
    gain_sum[...] = jnp.zeros_like(gain_sum)

    def scale_step(at):
        state = hidden[at, :]
        product = grad_in[at, :].astype(F32) * state * row_scale(state)
        gain_sum[...] += jnp.sum(
            product * (1.0 + mod_2[at, :].astype(F32)), axis=0, keepdims=True
        )
        wide_grad[at, :] = product * gain[...]

    over_strips(hidden.shape[0], scale_step)
    ffn_mod[...] = segment_sum(member[...], wide_grad[...])
    for reduce in reduces:
        reduce.last()
    sum_out.add(ffn_rows, False)
    first = sum_out.rank * sum_out.size

    def row_step(here):
        at = pl.ds(pl.multiple_of(first + here.start, STRIP), STRIP)
        gate = jnp.tanh(mod_3[at, :].astype(F32))
        out = ffn_rows[here, :].astype(F32)
        result_rows[here, :] = (hidden[at, :] + gate * out).astype(BF16)
        rows_grad[here, :] = cotangent[at, :].astype(F32) * out * (1.0 - gate * gate)

    over_strips(sum_out.size, row_step)
    gate_part[...] = segment_sum(member[sum_out.block(sum_out.rank), :], rows_grad[...]).astype(BF16)


def attend_back_kernel(
    micro, scale, live, text_len, grad_mixed, cross_out, query, key, value, text_key_far,
    text_value_far, text_raw_far, query_raw, key_raw, q_gain, k_gain, t_gain, cosine, sine, self_id, self_row, segment,
    gate, grad_query_b, grad_key_b, grad_value_b, grad_text, gain_sums,
    grad_query, grad_key, grad_cross, grad_turned, gain_turned, text_key, text_value, text_raw, sems,
    *held
):
    held, held_sems = held[:-1], held[-1]
    early = (grad_mixed, cross_out, query, key, value, query_raw, key_raw, cosine, sine)
    copies = [load(far, here, held_sems.at[i]) for i, (far, here) in enumerate(zip(early, held))]
    grad_mixed, cross_out, query, key, value, query_raw, key_raw, cosine, sine = held
    text_copies = [
        load(far, here, sems.at[index])
        for index, (far, here) in enumerate(
            ((text_key_far, text_key), (text_value_far, text_value), (text_raw_far, text_raw))
        )
    ]
    rows, width = query.shape
    count = rows // micro
    slots = text_key.shape[0] // micro
    heads = width // HEAD_DIM
    blocks = head_blocks(width)
    wait_all(copies)
    gate_sum = jnp.sum(grad_mixed[...] * cross_out[...], axis=0, keepdims=True)
    gain_sums[...] = jnp.zeros_like(gain_sums)
    gain_sums[3:4, :] = gate_sum * (1.0 - gate[...] * gate[...])
    grad_cross[...] = (gate[...] * grad_mixed[...]).astype(BF16)
    gain_turned[...] = jnp.zeros_like(gain_turned)
    gain_column = jnp.transpose(jnp.broadcast_to(t_gain[...], (8, width)))[:, :1]
    for batch in range(micro):
        at = slice(batch * count, (batch + 1) * count)
        allowed = twice(self_id[at, :]) == self_row[batch : batch + 1, :]
        for first in range(0, width, 2 * HEAD_DIM):
            lanes = slice(first, first + 2 * HEAD_DIM)
            q, k = stack_pair(query[at, lanes]), key[at, lanes]
            grad = stack_pair(grad_mixed[at, lanes].astype(BF16))
            probs = softmax(dot_nt(q, k) * scale, allowed, None)
            grad_probs = dot_nt(grad, value[at, lanes])
            mean = jnp.sum(probs * grad_probs, axis=1, keepdims=True)
            scaled = (probs * (grad_probs - mean) * scale).astype(BF16)
            grad_query[at, lanes] = unstack_pair(dot_nn(scaled, k))
            grad_key[at, lanes] = dot_tn(scaled, q)
            grad_value_b[at, lanes] = dot_tn(probs.astype(BF16), grad).astype(BF16)

    wait_all(text_copies)

    @pl.loop(0, micro * slots)
    def _(image):
        @pl.when(live[image] == 0)
        def _():
            grad_text[:, pl.ds(pl.multiple_of(image * TXT, TXT), TXT)] = jnp.zeros(
                (2 * width, TXT), BF16
            )

        @pl.when(live[image] > 0)
        def _():
            at = pl.ds(pl.multiple_of((image // slots) * count, count), count)
            tokens = pl.ds(pl.multiple_of(image * TXT, TXT), TXT)
            mine = twice(segment[at, :]) == lax.rem(image, slots)
            column = lax.broadcasted_iota(jnp.int32, (2 * count, TXT), 1)
            allowed = mine & (column < text_len[image])
            for first in range(0, width, 2 * HEAD_DIM):
                lanes = slice(first, first + 2 * HEAD_DIM)
                q, k = stack_pair(query[at, lanes]), text_key[image, :, lanes]
                grad = stack_pair(grad_cross[at, lanes])
                probs = softmax(dot_nt(q, k) * scale, allowed, mine)
                grad_probs = dot_nt(grad, text_value[image, :, lanes])
                mean = jnp.sum(probs * grad_probs, axis=1, keepdims=True)
                scaled = (probs * (grad_probs - mean) * scale).astype(BF16)
                grad_query[at, lanes] += unstack_pair(dot_nn(scaled, k))
                grad_turned[lanes, :] = dot_tn(q, scaled)
                grad_text[width + first : width + first + 2 * HEAD_DIM, tokens] = dot_tn(
                    grad, probs.astype(BF16)
                ).astype(BF16)
            by_head = (heads, HEAD_DIM, TXT)
            raw = jnp.transpose(text_raw[image].astype(F32)).reshape(by_head)
            norm = lax.rsqrt(jnp.mean(raw * raw, axis=1, keepdims=True) + EPSILON)
            normed = raw * norm
            upper = grad_turned[...].reshape(by_head)
            gain_turned[...] += (upper * normed).reshape(width, TXT)
            inner = upper * gain_column.reshape(heads, HEAD_DIM, 1)
            mean = jnp.mean(inner * normed, axis=1, keepdims=True)
            back = norm * (inner - normed * mean)
            grad_text[:width, tokens] = back.reshape(width, TXT).astype(BF16)

    for index, (grad, raw, gain, out) in enumerate(
        (
            (grad_query, query_raw, q_gain, grad_query_b),
            (grad_key, key_raw, k_gain, grad_key_b),
        )
    ):
        turned = grad[...] * cosine[...] + swap_pairs(grad[...] * sine[...])
        back, gain_sum = head_norm_back(raw[...], gain[...], turned, blocks)
        out[...] = back.astype(BF16)
        gain_sums[index : index + 1, :] = gain_sum
    text_sums = jnp.sum(gain_turned[...], axis=1, keepdims=True)
    gain_sums[2:3, :] = jnp.transpose(jnp.broadcast_to(text_sums, (width, 128)))[:1, :]


def attn_grad_kernel(
    attn_in, grad_query, grad_key, grad_value, grad_out, mixed, whole_a, whole_b,
    total_a, total_b, whole, mat_a, mat_b, pair, sems
):
    copies = [load(whole_a, mat_a, sems.at[0]), load(whole_b, mat_b, sems.at[1])]
    width = grad_query.shape[1]
    pair[:, :width] = grad_query[...]
    pair[:, width:] = grad_value[...]
    wait_all(copies)
    for first in range(0, whole.shape[1], 512):
        span = slice(first, first + 512)
        whole[:, span] = (
            dot_nt(pair[...], mat_a[span, :]) + dot_nt(grad_key[...], mat_b[span, :width])
        ).astype(BF16)
    for first in range(0, 2 * width, 256):
        span = slice(first, first + 256)
        total_a[:, span] = dot_tn(attn_in[...], pair[:, span]).astype(BF16)
    total_b[:, :width] = dot_tn(attn_in[...], grad_key[...]).astype(BF16)
    total_b[:, width:] = dot_tn(grad_out[...], mixed[...]).astype(BF16)


def last_exchange_kernel(
    n_tensor, captions, grad_text_far, qv_far, ko_far, tokens_far, hidden_far, attn_far, attn_part,
    member, attn_gain, mods, cond_act, gain_sums, result_rows, gate_part, ffn_mod, ffn_gain_sum,
    out_qv, out_ko, out_text, result, grad_tokens, grad_adaln,
    own_attn, own_ffn, own_query, own_key, own_text, own_gate, *rest
):
    buffers, rest = rest[:15], rest[15:]
    (
        text_total, block, grad_in, gate_parts, other_mod, grad_mod, arrived, mod_a, mod_b, work_grad,
        sums, attn_sum, all_mod, all_sums, all_attn, heads_turned,
        block_sems, sems, tensor_sems, small_sems,
        grad_text, total_qv, total_ko, tokens, grad_hidden, attn_out, load_sems,
    ) = rest
    masks = range(1, 8)
    announce(masks, range(1, n_tensor), n_tensor)
    loads = [
        load(far, here, load_sems.at[i])
        for i, (far, here) in enumerate(
            (
                (grad_text_far, grad_text), (qv_far, total_qv), (ko_far, total_ko),
                (tokens_far, tokens), (hidden_far, grad_hidden), (attn_far, attn_out),
            )
        )
    ]
    pl.semaphore_wait(pltpu.get_barrier_semaphore(), 7 + n_tensor - 1)
    sum_in = TensorSum(0, n_tensor, arrived, tensor_sems)
    sum_in.scatter(attn_part)
    head_width = gain_sums.shape[1]
    sums[0:1, :] = ffn_gain_sum[...]
    for row in range(4):
        sums[1:2, row * head_width : (row + 1) * head_width] = gain_sums[row : row + 1, :]
    rank = lax.axis_index("dp")
    copies = [
        send(sums, all_sums.at[mask], small_sems, (1, mask), {"dp": partner(mask)})
        for mask in masks
    ]
    sum_out = TensorSum(1, n_tensor, arrived, tensor_sems)
    result[sum_out.block(sum_out.rank), :] = result_rows[...]
    gate_parts[0] = gate_part[...]
    gate_copies = [
        send(gate_part, gate_parts.at[place + 1], tensor_sems, (2, place), {"tensor": other})
        for place, other in sum_in.others
    ]
    size = out_qv.shape[0]
    depth = out_text.shape[1]
    reduces, firsts = [], []
    for number, (far, total, out) in enumerate(
        ((qv_far, total_qv, out_qv), (ko_far, total_ko, out_ko))
    ):
        reduce = Reduce(
            number, piece_reader(total, size), out, *buffers[5 * number : 5 * number + 5], sems
        )
        reduces.append(reduce)
        firsts.append(reduce_firsts(reduce, far, size))

    def fetch(mask, slot):
        columns = pl.ds(pl.multiple_of(partner(mask) * depth, 128), depth)
        return pltpu.make_async_copy(
            captions.at[:, columns], block.at[slot], block_sems.at[slot]
        )

    def mask_at(place):
        return 7 - 2 * place + 7 * (place // 4)

    fetch(7, 0).start()

    def read_text(piece, low):
        return text_total[2 * piece, pl.ds(low, REDUCE_STRIP), :].astype(F32)

    text = Reduce(2, read_text, out_text, *buffers[10:], sems)

    def work(low, high):
        @pl.loop(low, high)
        def _(place):
            slot = lax.rem(place, 2)
            mask = mask_at(place)

            @pl.when(place < 7)
            def _():
                fetch(mask_at(place + 1), 1 - slot).start()

            fetch(mask, slot).wait()
            for first in range(0, grad_text.shape[0], 256):
                span = slice(first, first + 256)
                text_total[mask, span, :] = dot_nn(grad_text[span, :], block[slot]).astype(BF16)

    wait_all(loads[:3])
    work(0, 2)
    for piece in (3, 2):
        text.first(piece, text_total.at[2 * piece + 1]).start()
    for piece in (3, 2, 1, 0):
        for number in range(2):
            reduces[number].second(piece, firsts[number][piece])
    work(2, 4)
    text_firsts = {}
    for piece in (3, 2, 1, 0):
        text_firsts[piece] = text.first(piece, text_total.at[2 * piece + 1])
    text_firsts[1].start()
    text_firsts[0].start()
    sum_in.add(grad_in, True)
    sum_in.gather(grad_in)
    for reduce in reduces:
        reduce.third()
    work(4, 5)
    text.second(3, text_firsts[3])
    work(5, 6)
    text.second(2, text_firsts[2])
    work(6, 7)
    text.second(1, text_firsts[1])
    work(7, 8)
    text.second(0, text_firsts[0])
    text.third()
    for copy in gate_copies:
        copy.wait()
    gate_mod = gate_parts[0].astype(F32)
    for place, _ in sum_in.others:
        gate_mod = gate_mod + gate_parts[place + 1].astype(F32)
    other_mod[...] = jnp.where(sum_in.rank == 3, gate_mod, ffn_mod[...])
    wait_all(loads[3:])
    sum_in.finish()
    sum_out.gather(result)
    input_kernel(
        tokens, member, attn_gain, grad_hidden, other_mod, mods, grad_in, attn_out,
        grad_tokens, grad_mod, attn_sum, mod_a, mod_b, work_grad,
    )
    for mask in masks:
        device = {"dp": partner(mask)}
        copies.append(send(grad_mod, all_mod.at[rank], small_sems, (0, mask), device))
        copies.append(send(attn_sum, all_attn.at[mask], small_sems, (2, mask), device))
    all_mod[rank] = grad_mod[...]
    for reduce in reduces:
        reduce.last()
    text.last()
    for copy in copies:
        copy.wait_recv()
    added, attn_added = sums[...], attn_sum[...]
    for mask in masks:
        added = added + all_sums[mask]
        attn_added = attn_added + all_attn[mask]
    grad_adaln[...] = dot_tn(cond_act[...], all_mod[...].reshape(8 * 16, all_mod.shape[2]))
    gain_size = own_attn.shape[1]
    for whole, out in ((attn_added, own_attn), (added[0:1, :], own_ffn)):
        out[...] = whole[:, :gain_size]
        for index in range(1, 8):
            part = whole[:, index * gain_size : (index + 1) * gain_size]
            out[...] = jnp.where(rank == index, part, out[...])
    heads = own_query.shape[1]
    for place, out in enumerate((own_query, own_key, own_text)):
        for head in range(heads):
            first = place * head_width + head * HEAD_DIM
            heads_turned[head : head + 1, :HEAD_DIM] = added[1:2, first : first + HEAD_DIM]
        turned = jnp.transpose(heads_turned[...])
        part = out.shape[0]
        out[...] = turned[:part, :heads]
        for index in range(1, 8):
            here = turned[index * part : (index + 1) * part, :heads]
            out[...] = jnp.where(rank == index, here, out[...])
    for head in range(heads):
        first = 3 * head_width + head * HEAD_DIM
        own_gate[:, head : head + 1] = jnp.sum(
            added[1:2, first : first + HEAD_DIM], axis=1, keepdims=True
        )
    for copy in copies:
        copy.wait_send()
    sum_out.finish()


def segment_sum(member, values):
    high = values.astype(BF16)
    rest = values - high.astype(F32)
    middle = rest.astype(BF16)
    low = (rest - middle.astype(F32)).astype(BF16)
    return dot_tn(member, high) + dot_tn(member, middle) + dot_tn(member, low)


def output_kernel(
    hidden, member, gain, cotangent, mods, ffn_out, grad_in,
    result, grad_mod, grad_gain, mod_2, mod_3, grad
):
    token_columns(member, mods, 2, mod_2)
    token_columns(member, mods, 3, mod_3)
    rank = lax.axis_index("tensor")
    grad_gain[...] = jnp.zeros_like(grad_gain)

    def step(at):
        state = hidden[at, :]
        gate = jnp.tanh(mod_3[at, :].astype(F32))
        out = ffn_out[at, :].astype(F32)
        result[at, :] = (state + gate * out).astype(BF16)
        up = grad_in[at, :].astype(F32)
        product = up * state * row_scale(state)
        grad_gain[...] += jnp.sum(
            product * (1.0 + mod_2[at, :].astype(F32)), axis=0, keepdims=True
        )
        grad_gate = cotangent[at, :].astype(F32) * out * (1.0 - gate * gate)
        grad[at, :] = jnp.where(rank == 2, product * gain[...], grad_gate)

    over_strips(hidden.shape[0], step)
    grad_mod[...] = segment_sum(member[...], grad[...])


def input_kernel(
    tokens, member, gain, grad_hidden, other_mod, mods, grad_in, attn_out,
    grad_tokens, grad_mod, grad_gain, mod_0, mod_1, grad
):
    token_columns(member, mods, 0, mod_0)
    token_columns(member, mods, 1, mod_1)
    rank = lax.axis_index("tensor")
    grad_gain[...] = jnp.zeros_like(grad_gain)

    def step(at):
        shift = mod_0[at, :].astype(F32)
        upper = grad_hidden[at, :]
        back, product = modulate_back(
            tokens[at, :].astype(F32), gain[...], shift, grad_in[at, :].astype(F32)
        )
        grad_tokens[at, :] = (upper + back).astype(BF16)
        grad_gain[...] += jnp.sum(product * (1.0 + shift), axis=0, keepdims=True)
        gate = jnp.tanh(mod_1[at, :].astype(F32))
        grad_gate = upper * attn_out[at, :].astype(F32) * (1.0 - gate * gate)
        grad[at, :] = jnp.where(rank == 0, product * gain[...], grad_gate)

    over_strips(tokens.shape[0], step)
    own = segment_sum(member[...], grad[...])
    grad_mod[...] = jnp.where(rank < 2, own, other_mod[...]).astype(BF16)


def shards(
    n_dp,
    n_tensor,
    tokens,
    context,
    captions,
    shapes,
    text_len,
    w_query,
    w_key,
    w_value,
    w_out,
    w_text_key,
    w_text_value,
    w_gate,
    w_up,
    w_down,
    w_adaln,
    gain_attn,
    gain_ffn,
    gain_query,
    gain_key,
    gain_text,
    cross_gate,
    cotangent,
):
    parts = 8 if n_dp == 8 else 1
    micro, count, width = tokens.shape
    slots = shapes.shape[1]
    rows = micro * count
    images = micro * slots
    heads = w_query.shape[1] // HEAD_DIM
    local = heads * HEAD_DIM
    units = w_gate.shape[1]
    scale = HEAD_DIM ** (-0.5)
    dp_rank = lax.axis_index("dp")
    padded = 16
    vmem, smem, anywhere = pltpu.VMEM, pltpu.SMEM, pl.ANY
    dma = pltpu.SemaphoreType.DMA

    def inside(*arrays):
        return [(array, vmem) for array in arrays]

    def scalars(*arrays):
        return [(array, smem) for array in arrays]

    def outside(*arrays):
        return [(array, anywhere) for array in arrays]

    def after(values, earlier):
        return lax.optimization_barrier((list(values), list(earlier)))[0]

    def gathered(shard):
        return lax.all_gather(shard, "dp", axis=0, tiled=True)

    def scattered(whole):
        return lax.psum_scatter(whole, "dp", scatter_dimension=0, tiled=True).astype(F32)

    part_rows = rows // n_tensor
    arrived = vmem((n_tensor - 1, part_rows, width), BF16)

    def tensor_sum(partial):
        (out,) = exchange(
            functools.partial(tensor_kernel, n_tensor),
            [(struct((rows, width)), vmem)],
            inside(partial),
            [arrived, dma((2, 2, n_tensor - 1))],
            1,
        )
        return out

    gain_list = (gain_attn, gain_ffn, gain_query, gain_key, gain_text)
    cond_rows, span = w_adaln.shape
    shard_qv = jnp.concatenate([w_query, w_value], axis=1)
    shard_ko = jnp.concatenate([w_key, w_out], axis=1)
    shard_f = jnp.concatenate([w_gate, w_up, w_down], axis=1)
    if parts == 1:
        whole_tk, whole_tv = gathered(w_text_key), gathered(w_text_value)
        whole_qv, whole_ko = gathered(shard_qv), gathered(shard_ko)
        gains = [lax.all_gather(gain.astype(F32), "dp", axis=0, tiled=True) for gain in gain_list]
        attn_gain, ffn_gain = [gain.reshape(1, width) for gain in gains[:2]]
        query_gain, key_gain, text_gain = [gain.T.reshape(1, local) for gain in gains[2:]]
        context_all = gathered(context.reshape(images, -1))
        cond_cols = lax.dynamic_slice_in_dim(context_all, dp_rank * cond_rows, cond_rows, 1)
        cond_act = jax.nn.silu(cond_cols.astype(F32)).astype(BF16)
        mod_part = scattered(dot_nn(cond_act, w_adaln)).astype(BF16)
        mods = lax.all_gather(mod_part, "tensor", axis=0)
        mods = jnp.pad(mods, ((0, 0), (0, padded - images), (0, 0)))
    else:
        text_raw, text_key, text_value, whole_qv, whole_ko, cond_act, mods, *gains = exchange(
            functools.partial(gather_kernel, n_tensor),
            [(struct((images, TXT, local)), anywhere)] * 3
            + [(struct((width, 2 * local)), anywhere)] * 2
            + [
                (struct((parts * padded, cond_rows)), vmem),
                (struct((n_tensor, padded, span)), vmem),
            ]
            + [(struct((1, width), F32), vmem)] * 2
            + [(struct((1, local), F32), vmem)] * 3,
            outside(w_text_key, w_text_value, shard_qv, shard_ko)
            + inside(
                context, gain_attn[None], gain_ffn[None], gain_query, gain_key, gain_text, w_adaln
            )
            + outside(captions.reshape(images, TXT, DT)),
            [
                vmem((parts, 2 * padded, cond_rows), BF16),
                vmem((parts, 2 * padded, cond_rows), BF16),
                vmem((parts, padded, span), BF16),
                vmem((parts, padded, span), BF16),
                vmem((DT, local), BF16),
                vmem((DT, local), BF16),
                vmem((local, local), BF16),
                vmem((2, TXT, DT), BF16),
                vmem((2, 3, TXT, local), BF16),
                dma((2,)),
                dma((2, 3)),
                dma((4,)),
                dma((2, 4, 9)),
                dma((2, 8)),
                dma((2, 8)),
                dma((2, n_tensor)),
            ],
            2,
        )
        attn_gain, ffn_gain, query_gain, key_gain, text_gain = gains
        (shard_f,) = after([shard_f], [mods])
    whole_f = gathered(shard_f)
    layouts = [image_layout(shapes[i], count) for i in range(micro)]
    member, segment, inside_any, row_pos, col_pos = [
        jnp.stack([layout[j] for layout in layouts]) for j in range(5)
    ]
    cosine, sine = rope_tables(row_pos.reshape(rows), col_pos.reshape(rows))
    cosine = jnp.tile(jnp.stack([cosine, cosine], axis=2).reshape(rows, HEAD_DIM), (1, heads))
    sine = jnp.tile(jnp.stack([-sine, sine], axis=2).reshape(rows, HEAD_DIM), (1, heads))
    which = jnp.arange(micro, dtype=jnp.int32)
    member = jnp.where(
        (which[:, None] == which[None, :])[:, None, :, None], member[:, :, None, :], 0.0
    )
    member = jnp.pad(member.reshape(rows, images), ((0, 0), (0, padded - images))).astype(BF16)
    self_row = jnp.where(inside_any > 0, segment, slots)
    self_id = self_row.reshape(rows, 1)
    segment = segment.reshape(rows, 1)
    lens = text_len.reshape(images)
    used = shapes[:, :, 0] * (shapes[:, :, 1] + 1) > 0
    used = used | (jnp.arange(slots)[None, :] == 0)
    live = used.reshape(images).astype(jnp.int32)
    at = jnp.arange(images, dtype=jnp.int32)
    source = lax.cummax(jnp.where(live > 0, at, 0))
    gate = jnp.repeat(jnp.tanh(cross_gate.astype(F32)), HEAD_DIM)[None, :]
    token_rows = tokens.reshape(rows, width)
    grad_y = cotangent.reshape(rows, width)
    caption_images = captions.reshape(images, TXT, DT)

    attn_in, query_raw, key_raw, query_rot, key_rot, value = run(
        project_kernel,
        [struct((rows, width))]
        + [struct((rows, local), F32)] * 2
        + [struct((rows, local))] * 3,
        inside(token_rows, member, attn_gain, query_gain, key_gain, cosine, sine, mods)
        + outside(whole_qv, whole_ko),
        [
            vmem((width, 2 * local), BF16),
            vmem((width, 2 * local), BF16),
            vmem((rows, width), BF16),
            dma((2,)),
        ],
        flops=6 * rows * width * local,
        traffic=10 * 2**20,
    )

    if parts == 1:
        text_raw, text_key, text_value = pl.pallas_call(
            text_kernel,
            out_shape=[struct((images, TXT, local))] * 3,
            grid_spec=pltpu.PrefetchScalarGridSpec(
                num_scalar_prefetch=2,
                grid=(images,),
                in_specs=[
                    pl.BlockSpec((1, TXT, DT), lambda i, live, source: (source[i], 0, 0)),
                    pl.BlockSpec((1, local), lambda i, live, source: (0, 0)),
                ]
                + [pl.BlockSpec(memory_space=anywhere)] * 2,
                out_specs=[pl.BlockSpec((1, TXT, local), lambda i, live, source: (i, 0, 0))] * 3,
                scratch_shapes=[vmem((DT, local), BF16), vmem((DT, local), BF16), dma((2,))],
            ),
            compiler_params=pltpu.CompilerParams(vmem_limit_bytes=40 * 2**20),
            cost_estimate=pl.CostEstimate(
                flops=2 * images * TXT * DT * local, bytes_accessed=20 * 2**20, transcendentals=0
            ),
        )(live, source, caption_images, text_gain, whole_tk, whole_tv)

    wide = vmem((rows, width), BF16)
    mixed, cross_out, attn_part = run(
        functools.partial(attend_kernel, micro, scale),
        [struct((rows, local)), struct((rows, local), F32), struct((rows, width))],
        scalars(live, lens)
        + inside(query_rot, key_rot, value)
        + outside(text_key, text_value)
        + inside(self_id, self_row, segment, gate)
        + outside(whole_ko),
        [
            vmem((width, 2 * local), BF16),
            vmem((images, TXT, local), BF16),
            vmem((images, TXT, local), BF16),
            vmem((rows, local), F32),
            dma,
            dma((2,)),
        ],
        flops=2 * 2**30,
        traffic=12 * 2**20,
    )
    attn_out = tensor_sum(attn_part)

    size = width // parts
    if parts == 1:
        mat = vmem((width, 3 * units), BF16)
        hidden, ffn_in, inner, grad_gate, grad_up, grad_ffn_out, ffn_part = run(
            feed_kernel,
            [struct((rows, width), F32), struct((rows, width))]
            + [struct((rows, units))] * 3
            + [struct((rows, width))] * 2,
            inside(token_rows, member, ffn_gain, grad_y, mods, attn_out) + outside(whole_f),
            [mat, wide, wide, wide, dma],
            flops=10 * rows * width * units,
            traffic=20 * 2**20,
        )
        (grad_f,) = run(
            feed_grad_kernel,
            [struct((width, 3 * units))],
            inside(grad_ffn_out, inner, ffn_in, grad_gate, grad_up),
            flops=6 * rows * width * units,
            traffic=12 * 2**20,
        )
        (ffn_part,) = after([ffn_part], [grad_f])
        grad_ffn_in = tensor_sum(ffn_part)
        grad_f = scattered(grad_f)
        (ffn_out_part,) = run(
            feed_out_kernel,
            [struct((rows, width))],
            inside(inner) + outside(whole_f),
            [vmem((width, units), BF16), dma],
            flops=2 * rows * width * units,
            traffic=5 * 2**20,
        )
        ffn_out = lax.psum(ffn_out_part, "tensor")

        grad_hidden, grad_attn_out, grad_mixed = run(
            mixed_grad_kernel,
            [struct((rows, width), F32), struct((rows, width)), struct((rows, local), F32)],
            inside(hidden, member, ffn_gain, grad_y, mods, grad_ffn_in) + outside(whole_ko),
            [vmem((width, 2 * local), BF16), wide, wide, dma],
            flops=2 * rows * width * local,
            traffic=8 * 2**20,
        )
    else:
        (
            hidden, grad_hidden, grad_attn_out, grad_mixed, result_rows, gate_part, ffn_mod,
            ffn_gain_sum, *grad_f
        ) = exchange(
            functools.partial(feed_exchange_kernel, n_tensor),
            [
                (struct((rows, width), F32), vmem),
                (struct((rows, width), F32), vmem),
                (struct((rows, width)), vmem),
                (struct((rows, local), F32), vmem),
                (struct((part_rows, width)), vmem),
                (struct((padded, width)), vmem),
                (struct((padded, width), F32), vmem),
                (struct((1, width), F32), vmem),
            ]
            + [(struct((size, units), F32), vmem)] * 3,
            inside(token_rows, member, ffn_gain, grad_y, mods, attn_out)
            + outside(whole_f, whole_ko),
            [wide]
            + [vmem((rows, units), BF16)] * 3
            + [wide] * 3
            + [vmem((width, 3 * units), BF16), wide, wide, wide, wide]
            + [
                vmem((part_rows, width), BF16),
                vmem((rows, width), F32),
                vmem((part_rows, width), F32),
            ]
            + [vmem((width, units), BF16)] * 3
            + reduce_scratch(size, units) * 3
            + [arrived, arrived, dma, dma, dma((2, 3, 10)), dma((2, 4, n_tensor - 1))],
            5,
            vmem=60,
        )

    tile = struct((rows, local))
    grad_query_b, grad_key_b, grad_value_b, grad_text_all, gain_sums = run(
        functools.partial(attend_back_kernel, micro, scale),
        [tile, tile, tile, struct((2 * local, images * TXT)), struct((8, local), F32)],
        scalars(live, lens)
        + outside(
            grad_mixed, cross_out, query_rot, key_rot, value, text_key, text_value, text_raw,
            query_raw, key_raw,
        )
        + inside(query_gain, key_gain, text_gain)
        + outside(cosine, sine)
        + inside(self_id, self_row, segment, gate),
        [
            vmem((rows, local), F32),
            vmem((rows, local), F32),
            vmem((rows, local), BF16),
            vmem((local, TXT), F32),
            vmem((local, TXT), F32),
            vmem((images, TXT, local), BF16),
            vmem((images, TXT, local), BF16),
            vmem((images, TXT, local), BF16),
            dma((3,)),
        ]
        + [vmem((rows, local), F32)] * 2
        + [vmem((rows, local), BF16)] * 3
        + [vmem((rows, local), F32)] * 4
        + [
            dma((9,)),
        ],
        flops=4 * 2**30,
        traffic=15 * 2**20,
        vmem=62,
    )

    total_qv, total_ko, attn_in_part = run(
        attn_grad_kernel,
        [struct((width, 2 * local))] * 2 + [struct((rows, width))],
        inside(attn_in, grad_query_b, grad_key_b, grad_value_b, grad_attn_out, mixed)
        + outside(whole_qv, whole_ko),
        [
            vmem((width, 2 * local), BF16),
            vmem((width, 2 * local), BF16),
            vmem((rows, 2 * local), BF16),
            dma((2,)),
        ],
        flops=14 * rows * width * local,
        traffic=15 * 2**20,
    )
    depth = DT // parts
    caption_rows = captions.reshape(images * TXT, DT)
    if parts == 1:
        grad_attn_in = lax.psum(attn_in_part, "tensor")
        grad_text = dot_nn(grad_text_all, caption_rows)
        wholes = (total_qv, total_ko, grad_text.T)
        grad_qv, grad_ko, grad_text = [scattered(whole.astype(F32)) for whole in wholes]
        grad_query, grad_value = grad_qv[:, :local], grad_qv[:, local:]
        grad_key, grad_out = grad_ko[:, :local], grad_ko[:, local:]
        grad_tk, grad_tv = grad_text[:, :local], grad_text[:, local:]
        grad_f = [grad_f[:, i * units : (i + 1) * units] for i in range(3)]
        result, ffn_mod, ffn_gain_sum = run(
            output_kernel,
            [struct((rows, width)), struct((padded, width), F32), struct((1, width), F32)],
            inside(hidden, member, ffn_gain, grad_y, mods, ffn_out, grad_ffn_in),
            [wide, wide, vmem((rows, width), F32)],
        )
        grad_tokens, grad_mod, attn_gain_sum = run(
            input_kernel,
            [struct((rows, width)), struct((padded, width)), struct((1, width), F32)],
            inside(
                token_rows, member, attn_gain, grad_hidden, ffn_mod, mods, grad_attn_in, attn_out
            ),
            [wide, wide, vmem((rows, width), F32)],
        )
        grad_w_adaln = dot_tn(cond_act, gathered(grad_mod[:images]))
        sums = [attn_gain_sum[0], ffn_gain_sum[0]]
        sums += [row.reshape(heads, HEAD_DIM).T for row in gain_sums[:3]]
        sums = lax.psum(sums, "dp")
        own = [
            lax.dynamic_slice_in_dim(whole, dp_rank * (whole.shape[0] // n_dp), whole.shape[0] // n_dp, 0)
            for whole in sums
        ]
        own.append(lax.psum(jnp.sum(gain_sums[3].reshape(heads, HEAD_DIM), axis=1), "dp"))
    else:
        grad_qv, grad_ko, grad_text, result, grad_tokens, grad_w_adaln, *own = exchange(
            functools.partial(last_exchange_kernel, n_tensor),
            [
                (struct((size, 2 * local), F32), vmem),
                (struct((size, 2 * local), F32), vmem),
                (struct((2 * local, depth), F32), vmem),
                (struct((rows, width)), vmem),
                (struct((rows, width)), vmem),
                (struct((cond_rows, span), F32), vmem),
            ]
            + [(struct((1, gain_attn.size), F32), vmem)] * 2
            + [(struct(gain_query.shape, F32), vmem)] * 3
            + [(struct((1, heads), F32), vmem)],
            outside(
                caption_rows, grad_text_all, total_qv, total_ko, token_rows, grad_hidden, attn_out
            )
            + inside(
                attn_in_part, member, attn_gain, mods, cond_act, gain_sums, result_rows, gate_part, ffn_mod,
                ffn_gain_sum,
            ),
            reduce_scratch(size, 2 * local) * 2
            + reduce_scratch(2 * local, depth)
            + [
                vmem((parts, 2 * local, depth), BF16),
                vmem((2, images * TXT, depth), BF16),
                wide,
                vmem((n_tensor, padded, width), BF16),
                vmem((padded, width), F32),
                vmem((padded, width), BF16),
                arrived,
                wide,
                wide,
                vmem((rows, width), F32),
                vmem((2, width), F32),
                vmem((1, width), F32),
                vmem((parts, padded, width), BF16),
                vmem((parts, 2, width), F32),
                vmem((parts, 1, width), F32),
                vmem((8, 128), F32),
                dma((2,)),
                dma((2, 3, 10)),
                dma((2, 4, n_tensor - 1)),
                dma((2, 3, 8)),
                vmem((2 * local, images * TXT), BF16),
                vmem((width, 2 * local), BF16),
                vmem((width, 2 * local), BF16),
                wide,
                vmem((rows, width), F32),
                wide,
                dma((6,)),
            ],
            3,
            vmem=62,
        )
        own[:2] = [part[0] for part in own[:2]]
        own[5] = own[5][0]
        plain = [*grad_f, grad_w_adaln, result, grad_tokens]
        square, tall = struct((size, local), F32), struct((depth, local), F32)
        (
            grad_query, grad_key, grad_value, grad_out, grad_tk, grad_tv, *plain
        ) = pl.pallas_call(
            emit_kernel,
            out_shape=[square] * 4 + [tall] * 2 + [struct(x.shape, x.dtype) for x in plain],
            in_specs=[pl.BlockSpec(memory_space=anywhere)] * (3 + len(plain)),
            out_specs=[pl.BlockSpec(memory_space=anywhere)] * (6 + len(plain)),
            scratch_shapes=[vmem(x.shape, x.dtype) for x in (grad_qv, grad_ko, grad_text, *plain)]
            + [
                vmem((depth, local), F32),
                vmem((depth, local), F32),
                dma((3 + len(plain),)),
                dma((6 + len(plain),)),
            ],
            compiler_params=pltpu.CompilerParams(vmem_limit_bytes=62 * 2**20),
        )(grad_qv, grad_ko, grad_text, *plain)
        *grad_f, grad_w_adaln, result, grad_tokens = plain

    return (
        result.reshape(micro, count, width),
        grad_tokens.reshape(micro, count, width),
        grad_query,
        grad_key,
        grad_value,
        grad_out,
        grad_tk,
        grad_tv,
        *grad_f,
        grad_w_adaln,
        *own,
    )


def solution(mesh):
    return jax.shard_map(
        functools.partial(shards, mesh.shape["dp"], mesh.shape["tensor"]),
        mesh=mesh,
        in_specs=(
            P(None, "dp", None),
            P(None, "dp", None),
            P(None, "dp", None, None),
            P(None, "dp", None),
            P(None, "dp"),
            P("dp", "tensor"),
            P("dp", "tensor"),
            P("dp", "tensor"),
            P("dp", "tensor"),
            P("dp", "tensor"),
            P("dp", "tensor"),
            P("dp", "tensor"),
            P("dp", "tensor"),
            P("dp", "tensor"),
            P("dp", "tensor"),
            P("dp"),
            P("dp"),
            P("dp", "tensor"),
            P("dp", "tensor"),
            P("dp", "tensor"),
            P("tensor"),
            P(None, "dp", None),
        ),
        out_specs=(
            P(None, "dp", None),
            P(None, "dp", None),
            P("dp", "tensor"),
            P("dp", "tensor"),
            P("dp", "tensor"),
            P("dp", "tensor"),
            P("dp", "tensor"),
            P("dp", "tensor"),
            P("dp", "tensor"),
            P("dp", "tensor"),
            P("dp", "tensor"),
            P("dp", "tensor"),
            P("dp"),
            P("dp"),
            P("dp", "tensor"),
            P("dp", "tensor"),
            P("dp", "tensor"),
            P("tensor"),
        ),
        check_vma=False,
    )
```

```python
import functools

import jax
import jax.numpy as jnp
from jax import lax
from jax.experimental import pallas as pl
from jax.experimental.pallas import tpu as pltpu
from jax.sharding import PartitionSpec as P

HEAD_DIM = 64
DT = 4096
TXT = 256


EPSILON = 1e-06
MASKED = -1e30
ROPE_BASE = 10000.0
STRIP = 16
F32 = jnp.float32
BF16 = jnp.bfloat16


def image_layout(shapes, count):
    height = shapes[:, 0]
    stride_all = shapes[:, 1] + 1
    extent = height * stride_all
    finish = jnp.cumsum(extent)
    begin = finish - extent
    places = jnp.arange(count, dtype=jnp.int32)
    member = (places[:, None] >= begin[None, :]) & (places[:, None] < finish[None, :])
    member_int = member.astype(jnp.int32)
    inside = jnp.sum(member_int, axis=1)
    slot_ids = jnp.arange(shapes.shape[0], dtype=jnp.int32)
    segment = jnp.sum(member_int * slot_ids[None, :], axis=1)
    stride = jnp.sum(member_int * stride_all[None, :], axis=1) + 1 - inside
    offset = places - jnp.sum(member_int * begin[None, :], axis=1)
    return (member.astype(jnp.float32), segment, inside, offset // stride, offset % stride)


def rope_tables(row_pos, col_pos):
    quarter = HEAD_DIM // 4
    freq = ROPE_BASE ** (-jnp.arange(quarter, dtype=jnp.float32) / quarter)
    angles = jnp.stack(
        [
            row_pos.astype(jnp.float32)[:, None] * freq[None, :],
            col_pos.astype(jnp.float32)[:, None] * freq[None, :],
        ],
        axis=1,
    )
    return (jnp.cos(angles), jnp.sin(angles))


def dot_nn(left, right):
    return lax.dot_general(left, right, (((1,), (0,)), ((), ())), preferred_element_type=F32)


def dot_nt(left, right):
    return lax.dot_general(left, right, (((1,), (1,)), ((), ())), preferred_element_type=F32)


def dot_tn(left, right):
    return lax.dot_general(left, right, (((0,), (0,)), ((), ())), preferred_element_type=F32)


def struct(shape, dtype=BF16):
    return jax.ShapeDtypeStruct(shape, dtype)


def run(body, outs, ins, scratch=(), flops=0, traffic=0, vmem=48):
    return pl.pallas_call(
        body,
        out_shape=outs,
        in_specs=[pl.BlockSpec(memory_space=space) for _, space in ins],
        out_specs=[pl.BlockSpec(memory_space=pltpu.VMEM)] * len(outs),
        scratch_shapes=list(scratch),
        compiler_params=pltpu.CompilerParams(vmem_limit_bytes=vmem * 2**20),
        cost_estimate=pl.CostEstimate(flops=flops, bytes_accessed=traffic, transcendentals=0),
    )(*[array for array, _ in ins])


def load(source, target, sem):
    copy = pltpu.make_async_copy(source, target, sem)
    copy.start()
    return copy


def wait_all(copies):
    for copy in copies:
        copy.wait()


def token_columns(member, mods, which, target):
    target[...] = dot_nn(member[...], mods[which]).astype(BF16)


def over_strips(rows, step):
    @pl.loop(0, rows // STRIP)
    def _(index):
        step(pl.ds(pl.multiple_of(index * STRIP, STRIP), STRIP))


def head_sum(values, blocks):
    high = values.astype(BF16)
    low = (values - high.astype(F32)).astype(BF16)
    return dot_nn(high, blocks) + dot_nn(low, blocks)


def head_blocks(width):
    row = lax.broadcasted_iota(jnp.int32, (width, width), 0) // HEAD_DIM
    column = lax.broadcasted_iota(jnp.int32, (width, width), 1) // HEAD_DIM
    return jnp.where(row == column, 1.0, 0.0).astype(BF16)


def swap_pairs(values):
    width = values.shape[1]
    quarter = HEAD_DIM // 4
    lane = lax.broadcasted_iota(jnp.int32, values.shape, 1)
    former = lax.rem(lane, 2 * quarter) < quarter
    return jnp.where(
        former, pltpu.roll(values, width - quarter, 1), pltpu.roll(values, quarter, 1)
    )


def head_norm(values, gain, blocks):
    scale = lax.rsqrt(head_sum(values * values, blocks) * (1.0 / HEAD_DIM) + EPSILON)
    return values * scale * gain


def head_norm_back(values, gain, grad, blocks):
    scale = lax.rsqrt(head_sum(values * values, blocks) * (1.0 / HEAD_DIM) + EPSILON)
    normed = values * scale
    grad_gain = jnp.sum(grad * normed, axis=0, keepdims=True)
    inner = grad * gain
    mean = head_sum(inner * normed, blocks) * (1.0 / HEAD_DIM)
    return scale * (inner - normed * mean), grad_gain


def row_scale(values):
    return lax.rsqrt(jnp.mean(values * values, axis=1, keepdims=True) + EPSILON)


MESH = pl.DeviceIdType.MESH
PAIR, ALONG_X, ALONG_Y = 1, 2, 4


def partner(mask):
    rank = lax.axis_index("dp")
    index = rank
    for bit in (1, 2, 4):
        flip = lax.rem(mask // bit, 2)
        index = index + flip * (bit - 2 * bit * lax.rem(rank // bit, 2))
    return index


def announce(masks, shifts, n_tensor):
    barrier = pltpu.get_barrier_semaphore()
    rank = lax.axis_index("tensor")
    for mask in masks:
        pl.semaphore_signal(
            barrier, inc=1, device_id={"dp": partner(mask)}, device_id_type=MESH
        )
    for shift in shifts:
        pl.semaphore_signal(
            barrier,
            inc=1,
            device_id={"tensor": lax.rem(rank + shift, n_tensor)},
            device_id_type=MESH,
        )


def greet(masks, shifts, n_tensor):
    announce(masks, shifts, n_tensor)
    pl.semaphore_wait(pltpu.get_barrier_semaphore(), len(masks) + len(shifts))


def send(source, target, sems, index, device):
    copy = pltpu.make_async_remote_copy(
        src_ref=source,
        dst_ref=target,
        send_sem=sems.at[(0,) + index],
        recv_sem=sems.at[(1,) + index],
        device_id=device,
        device_id_type=MESH,
    )
    copy.start()
    return copy


def gather_kernel(
    n_tensor, shard_tk, shard_tv, shard_qv, shard_ko, context, attn_own, ffn_own, q_own, k_own,
    t_own, w_adaln, captions,
    text_raw, text_key, text_value, qv, ko, cond_act, mods, attn_gain, ffn_gain, q_gain, k_gain, t_gain,
    small, small_all, product, sums, tk, tv, blocks, block, stage, block_sems, stage_sems, own_sems, shard_sems, small_sems, mod_sems, tensor_sems,
):
    rank, tensor_rank = lax.axis_index("dp"), lax.axis_index("tensor")
    masks = range(1, 8)
    shifts = range(1, n_tensor)
    greet(masks, shifts, n_tensor)
    groups = ((shard_tk, tk), (shard_tv, tv), (shard_qv, qv), (shard_ko, ko))

    def rows_of(shard, index, first, size):
        return pl.ds(pl.multiple_of(index * shard.shape[0] + first, 32), size)

    firsts, seconds, pairs, locals_ = {}, {}, {}, []

    def step_1(number):
        shard, whole = groups[number]
        mine = whole.at[rows_of(shard, rank, 0, shard.shape[0])]
        firsts[number] = [
            send(shard, mine, shard_sems, (number, place), {"dp": partner(mask)})
            for place, mask in ((0, ALONG_X), (1, ALONG_Y))
        ]
        pairs[number] = [send(shard, mine, shard_sems, (number, 4), {"dp": partner(PAIR)})]
        local = pltpu.make_async_copy(shard, mine, own_sems.at[number])
        local.start()
        locals_.append(local)

    def step_2(number):
        shard, whole = groups[number]
        size = shard.shape[0]
        half = size // 2
        seconds[number] = []
        for place, mask, onward, start in ((0, ALONG_X, ALONG_Y, half), (1, ALONG_Y, ALONG_X, 0)):
            firsts[number][place].wait_recv()
            part = whole.at[rows_of(shard, partner(mask), start, half)]
            seconds[number].append(
                send(part, part, shard_sems, (number, 2 + place), {"dp": partner(onward)})
            )
            piece = whole.at[rows_of(shard, partner(mask), 0, size)]
            pairs[number].append(
                send(piece, piece, shard_sems, (number, 5 + place), {"dp": partner(PAIR)})
            )

    def step_3(number):
        shard, whole = groups[number]
        half = shard.shape[0] // 2
        for place, start in ((0, half), (1, 0)):
            seconds[number][place].wait_recv()
            part = whole.at[rows_of(shard, partner(ALONG_X + ALONG_Y), start, half)]
            pairs[number].append(
                send(part, part, shard_sems, (number, 7 + place), {"dp": partner(PAIR)})
            )

    def step_4(number):
        for copy in pairs[number]:
            copy.wait_recv()
        locals_[number].wait()

    count = captions.shape[0]

    def fetch(image, slot):
        return pltpu.make_async_copy(captions.at[image], block.at[slot], block_sems.at[slot])

    outputs = (text_raw, text_key, text_value)
    kinds = ((0, 1), (2,))

    def store(image, slot, kind):
        return [
            pltpu.make_async_copy(
                stage.at[slot, index], outputs[index].at[image], stage_sems.at[slot, index]
            )
            for index in kinds[kind]
        ]

    def text_images(low, high, kind):
        @pl.loop(low, high)
        def _(image):
            slot = lax.rem(image, 2)

            @pl.when(image < count - 1)
            def _():
                fetch(image + 1, 1 - slot).start()

            if kind == 0:

                @pl.when(image == count - 1)
                def _():
                    fetch(0, 1 - slot).start()

            fetch(image, slot).wait()

            @pl.when(image >= 2)
            def _():
                wait_all(store(image - 2, slot, kind))

            if kind == 0:
                raw = dot_nn(block[slot], tk[...])
                stage[slot, 0] = raw.astype(BF16)
                stage[slot, 1] = head_norm(raw, t_gain[...], blocks[...]).astype(BF16)
            else:
                stage[slot, 2] = dot_nn(block[slot], tv[...]).astype(BF16)
            for copy in store(image, slot, kind):
                copy.start()

    fetch(0, 0).start()
    step_1(0)
    blocks[...] = head_blocks(tk.shape[1])
    small_copies = []
    images, slots = context.shape[0] * context.shape[1], context.shape[1]
    depth = w_adaln.shape[0]
    gain_size = attn_own.shape[1]
    heads = q_own.shape[1]
    small[...] = jnp.zeros_like(small)
    for index in range(8):
        for first in range(0, images, slots):
            small[index, first : first + slots, :] = context[
                first // slots, :, index * depth : (index + 1) * depth
            ]
        for row, own in ((16, attn_own), (18, ffn_own)):
            for place, first in enumerate(range(0, gain_size, depth)):
                size = min(depth, gain_size - first)
                small[index, row + place : row + place + 1, :size] = own[:, first : first + size]
        for place, own in enumerate((q_own, k_own, t_own)):
            small[index, 24:32, 8 * place : 8 * place + heads] = own[...]
    for mask in masks:
        small_copies.append(
            send(
                small.at[partner(mask)], small_all.at[rank], small_sems, (mask,),
                {"dp": partner(mask)},
            )
        )
    small_all[rank] = small[rank]
    for copy in small_copies:
        copy.wait_recv()
    width = w_adaln.shape[1]
    contexts = small_all[:, 0:16, :].astype(F32).reshape(8 * 16, depth)
    cond_act[...] = jax.nn.silu(contexts).astype(BF16)
    product[...] = dot_nn(cond_act[...], w_adaln[...]).astype(BF16).reshape(8, 16, width)
    mod_copies = [
        send(
            product.at[partner(mask)], sums.at[mask], mod_sems, (mask,), {"dp": partner(mask)}
        )
        for mask in masks
    ]
    step_2(0)
    step_1(1)
    for row, out in ((16, attn_gain), (18, ffn_gain)):
        for index in range(8):
            for place, first in enumerate(range(0, gain_size, depth)):
                size = min(depth, gain_size - first)
                start = index * gain_size + first
                out[:, start : start + size] = small_all[
                    index, row + place : row + place + 1, :size
                ].astype(F32)
    turned = jnp.transpose(small_all[:, 24:32, :].astype(F32).reshape(HEAD_DIM, depth))
    for place, out in enumerate((q_gain, k_gain, t_gain)):
        for head in range(heads):
            out[:, head * HEAD_DIM : (head + 1) * HEAD_DIM] = turned[
                8 * place + head : 8 * place + head + 1, :
            ]
    sums[0] = product[rank]
    for copy in mod_copies:
        copy.wait_recv()
    total = sums[0].astype(F32)
    for mask in masks:
        total = total + sums[mask].astype(F32)
    mods[tensor_rank] = total.astype(BF16)
    tensor_copies = [
        send(
            mods.at[tensor_rank], mods.at[tensor_rank], tensor_sems, (shift,),
            {"tensor": lax.rem(tensor_rank + shift, n_tensor)},
        )
        for shift in shifts
    ]

    step_3(0)
    step_4(0)
    third = count // 3
    text_images(0, third, 0)
    step_2(1)
    step_1(2)
    step_1(3)
    text_images(third, 2 * third, 0)
    step_3(1)
    text_images(2 * third, count, 0)
    step_4(1)
    text_images(0, third, 1)
    step_2(2)
    step_2(3)
    text_images(third, 2 * third, 1)
    text_images(2 * third, count, 1)
    step_3(2)
    step_3(3)
    step_4(2)
    step_4(3)
    for image in (count - 2, count - 1):
        for kind in (0, 1):
            wait_all(store(image, image % 2, kind))
    for copy in tensor_copies:
        copy.wait_recv()
    for number in range(4):
        for copy in firsts[number] + seconds[number] + pairs[number]:
            copy.wait_send()
    for copy in small_copies + mod_copies + tensor_copies:
        copy.wait_send()


ROUTES = ((0, 1, 2, ALONG_X, ALONG_Y), (1, 2, 1, ALONG_Y, ALONG_X))
REDUCE_STRIP = 32


def over_half(half, step):
    @pl.loop(0, half // REDUCE_STRIP)
    def _(index):
        step(pl.multiple_of(index * REDUCE_STRIP, REDUCE_STRIP))


class Reduce:
    def __init__(self, number, read, out, from_pair, out_2, in_2, out_3, in_3, sems):
        self.number, self.read, self.out, self.sems = number, read, out, sems
        self.from_pair, self.out_2, self.in_2, self.out_3, self.in_3 = (
            from_pair, out_2, in_2, out_3, in_3
        )
        self.half = out.shape[0] // 2
        self.copies, self.arriving = [], {}

    def pair_term(self, piece, low):
        there = pl.ds(low, REDUCE_STRIP)
        return self.read(piece, low) + self.from_pair[piece, there, :].astype(F32)

    def move(self, source, target, index, mask):
        return pltpu.make_async_remote_copy(
            src_ref=source,
            dst_ref=target,
            send_sem=self.sems.at[0, self.number, index],
            recv_sem=self.sems.at[1, self.number, index],
            device_id={"dp": partner(mask)},
            device_id_type=MESH,
        )

    def first(self, piece, source):
        return self.move(source, self.from_pair.at[piece], piece, PAIR)

    def second(self, piece, copy):
        copy.wait_recv()
        self.copies.append(copy)
        for side, close, far, first, last in ROUTES:
            if piece not in (close, 3):
                continue
            slot = 1 if piece == 3 else 0

            def step(low):
                self.out_2[side, slot, pl.ds(low, REDUCE_STRIP), :] = self.pair_term(
                    piece, pl.multiple_of(low + side * self.half, REDUCE_STRIP)
                ).astype(BF16)

            over_half(self.half, step)
            moved = self.move(
                self.out_2.at[side, slot], self.in_2.at[side, slot], 4 + 2 * side + slot, first
            )
            moved.start()
            self.arriving[side, slot] = moved
            self.copies.append(moved)

    def third(self):
        for side, close, far, first, last in ROUTES:
            self.arriving[side, 1].wait_recv()

            def step(low):
                here = pl.ds(low, REDUCE_STRIP)
                there = pl.multiple_of(low + side * self.half, REDUCE_STRIP)
                self.out_3[side, here, :] = (
                    self.pair_term(far, there) + self.in_2[side, 1, here, :].astype(F32)
                ).astype(BF16)

            over_half(self.half, step)
            moved = self.move(self.out_3.at[side], self.in_3.at[side], 8 + side, last)
            moved.start()
            self.arriving[side, 2] = moved
            self.copies.append(moved)

    def last(self):
        for side in (0, 1):
            self.arriving[side, 0].wait_recv()
            self.arriving[side, 2].wait_recv()

            def step(low):
                here = pl.ds(low, REDUCE_STRIP)
                there = pl.multiple_of(low + side * self.half, REDUCE_STRIP)
                self.out[pl.ds(there, REDUCE_STRIP), :] = (
                    self.pair_term(0, there)
                    + self.in_2[side, 0, here, :].astype(F32)
                    + self.in_3[side, here, :].astype(F32)
                )

            over_half(self.half, step)
        for copy in self.copies:
            copy.wait_send()


def reduce_scratch(depth, columns):
    half = depth // 2
    return [
        pltpu.VMEM((4, depth, columns), BF16),
        pltpu.VMEM((2, 2, half, columns), BF16),
        pltpu.VMEM((2, 2, half, columns), BF16),
        pltpu.VMEM((2, half, columns), BF16),
        pltpu.VMEM((2, half, columns), BF16),
    ]


def piece_reader(total, size):
    def read(piece, low):
        first = partner(2 * piece) * size + low
        return total[pl.ds(pl.multiple_of(first, 32), REDUCE_STRIP), :].astype(F32)

    return read


def reduce_firsts(reduce, total, size):
    copies = {}
    for piece in (3, 2, 1, 0):
        copies[piece] = reduce.first(piece, piece_of(total, 2 * piece + 1, size))
        copies[piece].start()
    return copies


def piece_of(total, mask, size):
    return total.at[pl.ds(pl.multiple_of(partner(mask) * size, 64), size)]


class TensorSum:
    def __init__(self, number, n_tensor, arrived, sems):
        self.number, self.n_tensor, self.arrived, self.sems = number, n_tensor, arrived, sems
        self.rank = lax.axis_index("tensor")
        self.size = arrived.shape[1]
        self.others = [
            (shift - 1, lax.rem(self.rank + shift, n_tensor)) for shift in range(1, n_tensor)
        ]

    def block(self, index):
        return pl.ds(pl.multiple_of(index * self.size, 16), self.size)

    def scatter(self, partial):
        self.partial = partial
        self.firsts = [
            send(
                partial.at[self.block(other)], self.arrived.at[place], self.sems,
                (2 * self.number, place), {"tensor": other},
            )
            for place, other in self.others
        ]

    def add(self, out, whole):
        for copy in self.firsts:
            copy.wait_recv()

        @pl.loop(0, self.size // STRIP)
        def _(index):
            low = pl.multiple_of(index * STRIP, STRIP)
            there = pl.ds(pl.multiple_of(self.rank * self.size + low, STRIP), STRIP)
            total = self.partial[there, :].astype(F32)
            for place, _ in self.others:
                total = total + self.arrived[place, pl.ds(low, STRIP), :].astype(F32)
            out[there if whole else pl.ds(low, STRIP), :] = total.astype(BF16)

        for copy in self.firsts:
            copy.wait_send()

    def gather(self, out):
        mine = out.at[self.block(self.rank)]
        self.seconds = [
            send(mine, mine, self.sems, (2 * self.number + 1, place), {"tensor": other})
            for place, other in self.others
        ]

    def finish(self):
        for copy in self.seconds:
            copy.wait()


def tensor_kernel(n_tensor, partial, out, arrived, sems):
    greet((), range(1, n_tensor), n_tensor)
    total = TensorSum(0, n_tensor, arrived, sems)
    total.scatter(partial)
    total.add(out, True)
    total.gather(out)
    total.finish()


def emit_kernel(*refs):
    count = (len(refs) - 16) // 3
    sources, refs = refs[: 3 + count], refs[3 + count :]
    outs, refs = refs[: 6 + count], refs[6 + count :]
    held, (turned_key, turned_value, in_sems, sems) = refs[: 3 + count], refs[3 + count :]
    loads = [load(far, here, in_sems.at[i]) for i, (far, here) in enumerate(zip(sources, held))]
    query, key, value, out, text_key, text_value = outs[:6]
    width = query.shape[1]
    copies = []

    def put(here, target):
        copies.append(load(here, target, sems.at[len(copies)]))

    for index in range(3, 3 + count):
        loads[index].wait()
        put(held[index], outs[3 + index])
    for index, first, second in ((0, query, value), (1, key, out)):
        loads[index].wait()
        put(held[index].at[:, :width], first)
        put(held[index].at[:, width:], second)
    loads[2].wait()
    turned_key[...] = jnp.transpose(held[2][:width, :])
    put(turned_key, text_key)
    turned_value[...] = jnp.transpose(held[2][width:, :])
    put(turned_value, text_value)
    wait_all(copies)


def exchange(body, outs, ins, scratch, collective, vmem=48):
    spaces = [space for _, space in outs]
    return pl.pallas_call(
        body,
        out_shape=[shape for shape, _ in outs],
        in_specs=[pl.BlockSpec(memory_space=space) for _, space in ins],
        out_specs=[pl.BlockSpec(memory_space=space) for space in spaces],
        scratch_shapes=scratch,
        compiler_params=pltpu.CompilerParams(
            collective_id=collective, has_side_effects=True, vmem_limit_bytes=vmem * 2**20
        ),
    )(*[array for array, _ in ins])


def project_kernel(
    tokens, member, gain, q_gain, k_gain, cosine, sine, mods, whole_a, whole_b,
    attn_in, query_raw, key_raw, query_rot, key_rot, value, mat_a, mat_b, mod, sems
):
    copies = [load(whole_a, mat_a, sems.at[0]), load(whole_b, mat_b, sems.at[1])]
    width = q_gain.shape[1]
    token_columns(member, mods, 0, mod)
    blocks = head_blocks(width)

    def step(at):
        x = tokens[at, :].astype(F32)
        normed = x * row_scale(x)
        attn_in[at, :] = (normed * gain[...] * (1.0 + mod[at, :].astype(F32))).astype(BF16)

    over_strips(tokens.shape[0], step)
    wait_all(copies)
    query_raw[...] = dot_nn(attn_in[...], mat_a[:, :width])
    key_raw[...] = dot_nn(attn_in[...], mat_b[:, :width])
    value[...] = dot_nn(attn_in[...], mat_a[:, width:]).astype(BF16)
    for raw, head_gain, out in ((query_raw, q_gain, query_rot), (key_raw, k_gain, key_rot)):
        normed = head_norm(raw[...], head_gain[...], blocks)
        out[...] = (normed * cosine[...] + swap_pairs(normed) * sine[...]).astype(BF16)


def text_kernel(
    live, source, captions, gain, whole_k, whole_v,
    text_raw, text_key, text_value, mat_k, mat_v, sems
):
    image = pl.program_id(0)

    @pl.when(image == 0)
    def _():
        wait_all([load(whole_k, mat_k, sems.at[0]), load(whole_v, mat_v, sems.at[1])])

    @pl.when(live[image] > 0)
    def _():
        raw = dot_nn(captions[0], mat_k[...])
        text_raw[0] = raw.astype(BF16)
        text_key[0] = head_norm(raw, gain[...], head_blocks(raw.shape[1])).astype(BF16)
        text_value[0] = dot_nn(captions[0], mat_v[...]).astype(BF16)


def stack_pair(values):
    lane = lax.broadcasted_iota(jnp.int32, (1, 2 * HEAD_DIM), 1)
    first = jnp.where(lane < HEAD_DIM, 1.0, 0.0).astype(values.dtype)
    second = jnp.where(lane < HEAD_DIM, 0.0, 1.0).astype(values.dtype)
    return jnp.concatenate([values * first, values * second], axis=0)


def unstack_pair(values):
    count = values.shape[0] // 2
    lane = lax.broadcasted_iota(jnp.int32, (count, 2 * HEAD_DIM), 1)
    return jnp.where(lane < HEAD_DIM, values[:count], values[count:])


def twice(values):
    return jnp.concatenate([values, values], axis=0)


def softmax(scores, allowed, rows_live):
    scores = jnp.where(allowed, scores, MASKED)
    expo = jnp.where(allowed, jnp.exp(scores - jnp.max(scores, axis=1, keepdims=True)), 0.0)
    total = jnp.sum(expo, axis=1, keepdims=True)
    if rows_live is not None:
        total = jnp.where(rows_live, total, 1.0)
    return expo * (1.0 / total)


def attend_kernel(
    micro, scale, live, text_len, query, key, value, text_key_far, text_value_far,
    self_id, self_row, segment, gate, whole_b, mixed, cross_out, whole,
    mat_b, text_key, text_value, self_out, sem, sems
):
    text_copies = [
        load(text_key_far, text_key, sems.at[0]), load(text_value_far, text_value, sems.at[1])
    ]
    copies = [load(whole_b, mat_b, sem)]
    rows, width = query.shape
    count = rows // micro
    slots = text_key.shape[0] // micro
    heads = width // HEAD_DIM
    cross_out[...] = jnp.zeros_like(cross_out)

    for batch in range(micro):
        at = slice(batch * count, (batch + 1) * count)
        allowed = twice(self_id[at, :]) == self_row[batch : batch + 1, :]
        for first in range(0, width, 2 * HEAD_DIM):
            lanes = slice(first, first + 2 * HEAD_DIM)
            scores = dot_nt(stack_pair(query[at, lanes]), key[at, lanes]) * scale
            probs = softmax(scores, allowed, None).astype(BF16)
            self_out[at, lanes] = unstack_pair(dot_nn(probs, value[at, lanes]))
    wait_all(text_copies)

    @pl.loop(0, micro * slots)
    def _(image):
        @pl.when(live[image] > 0)
        def _():
            at = pl.ds(pl.multiple_of((image // slots) * count, count), count)
            mine = twice(segment[at, :]) == lax.rem(image, slots)
            column = lax.broadcasted_iota(jnp.int32, (2 * count, TXT), 1)
            allowed = mine & (column < text_len[image])
            for first in range(0, width, 2 * HEAD_DIM):
                lanes = slice(first, first + 2 * HEAD_DIM)
                scores = dot_nt(stack_pair(query[at, lanes]), text_key[image, :, lanes]) * scale
                probs = softmax(scores, allowed, mine).astype(BF16)
                cross_out[at, lanes] += unstack_pair(dot_nn(probs, text_value[image, :, lanes]))

    mixed[...] = (self_out[...] + gate[...] * cross_out[...]).astype(BF16)
    wait_all(copies)
    whole[...] = dot_nt(mixed[...], mat_b[:, width:]).astype(BF16)


def feed_kernel(
    tokens, member, gain, cotangent, mods, attn_out, whole_f,
    hidden, ffn_in, inner, grad_gate, grad_up, grad_out, whole,
    mat, mod_1, mod_2, mod_3, sem
):
    copies = [load(whole_f, mat, sem)]
    units = inner.shape[1]
    mat_a, mat_b, mat_c = [mat.at[:, i * units : (i + 1) * units] for i in range(3)]
    token_columns(member, mods, 1, mod_1)
    token_columns(member, mods, 2, mod_2)
    token_columns(member, mods, 3, mod_3)

    def step(at):
        gate_attn = jnp.tanh(mod_1[at, :].astype(F32))
        state = tokens[at, :].astype(F32) + gate_attn * attn_out[at, :].astype(F32)
        hidden[at, :] = state
        normed = state * row_scale(state)
        ffn_in[at, :] = (normed * gain[...] * (1.0 + mod_2[at, :].astype(F32))).astype(BF16)
        gate_ffn = jnp.tanh(mod_3[at, :].astype(F32))
        grad_out[at, :] = (gate_ffn * cotangent[at, :].astype(F32)).astype(BF16)

    rows = tokens.shape[0]
    over_strips(rows, step)
    wait_all(copies)
    chunk = 256
    for first in range(0, units, chunk):
        span = slice(first, first + chunk)
        gate = dot_nn(ffn_in[...], mat_a[:, span])
        up = dot_nn(ffn_in[...], mat_b[:, span])
        grad_inner = dot_nn(grad_out[...], mat_c[:, span])
        turn = jax.nn.sigmoid(gate)
        active = gate * turn
        inner[:, span] = (active * up).astype(BF16)
        grad_up[:, span] = (grad_inner * active).astype(BF16)
        slope = turn * (1.0 + gate * (1.0 - turn))
        grad_gate[:, span] = (grad_inner * up * slope).astype(BF16)
    width = tokens.shape[1]
    for first in range(0, width, 512):
        span = slice(first, first + 512)
        whole[:, span] = (
            dot_nt(grad_gate[...], mat_a[span, :]) + dot_nt(grad_up[...], mat_b[span, :])
        ).astype(BF16)


def feed_grad_kernel(grad_out, inner, ffn_in, grad_gate, grad_up, total):
    units = inner.shape[1]
    step = 256
    for index, (left, right) in enumerate(
        ((ffn_in, grad_gate), (ffn_in, grad_up), (grad_out, inner))
    ):
        for first in range(0, units, step):
            out = slice(index * units + first, index * units + first + step)
            total[:, out] = dot_tn(left[...], right[:, first : first + step]).astype(BF16)


def feed_out_kernel(inner, whole_f, partial, mat, sem):
    units = inner.shape[1]
    copy = load(whole_f.at[:, 2 * units : 3 * units], mat, sem)
    copy.wait()
    for first in range(0, partial.shape[1], 512):
        span = slice(first, first + 512)
        partial[:, span] = dot_nt(inner[...], mat[span, :]).astype(BF16)


def modulate_back(values, gain, shift, grad):
    scale = row_scale(values)
    normed = values * scale
    inner = grad * gain * (1.0 + shift)
    mean = jnp.mean(inner * normed, axis=1, keepdims=True)
    return scale * (inner - normed * mean), grad * normed


def mixed_grad_kernel(
    hidden, member, gain, cotangent, mods, grad_in, whole_b,
    grad_hidden, grad_out, grad_mixed, mat_b, mod_1, mod_2, sem
):
    copies = [load(whole_b, mat_b, sem)]
    token_columns(member, mods, 1, mod_1)
    token_columns(member, mods, 2, mod_2)

    def step(at):
        back, _ = modulate_back(
            hidden[at, :], gain[...], mod_2[at, :].astype(F32), grad_in[at, :].astype(F32)
        )
        total = cotangent[at, :].astype(F32) + back
        grad_hidden[at, :] = total
        grad_out[at, :] = (jnp.tanh(mod_1[at, :].astype(F32)) * total).astype(BF16)

    over_strips(hidden.shape[0], step)
    wait_all(copies)
    width = grad_mixed.shape[1]
    grad_mixed[...] = dot_nn(grad_out[...], mat_b[:, width:])


def feed_exchange_kernel(
    n_tensor, tokens, member, gain, cotangent, mods, attn_out, whole_f, whole_ko,
    hidden, grad_hidden, grad_attn_out, grad_mixed, result_rows, gate_part, ffn_mod, gain_sum, *rest
):
    outs, rest = rest[:3], rest[3:]
    (
        ffn_in, inner, grad_gate, grad_up, grad_out, ffn_part, out_part,
        mat, mod_1, mod_2, mod_3, grad_in, ffn_rows, wide_grad, rows_grad, *rest
    ) = rest
    totals, rest = rest[:3], rest[3:]
    buffers, (arrived_1, arrived_2, sem, mat_sem, sems, tensor_sems) = rest[:15], rest[15:]
    announce((PAIR, ALONG_X, ALONG_Y), range(1, n_tensor), n_tensor)
    feed_kernel(
        tokens, member, gain, cotangent, mods, attn_out, whole_f,
        hidden, ffn_in, inner, grad_gate, grad_up, grad_out, ffn_part,
        mat, mod_1, mod_2, mod_3, sem,
    )
    pl.semaphore_wait(pltpu.get_barrier_semaphore(), 3 + n_tensor - 1)
    sum_in = TensorSum(0, n_tensor, arrived_1, tensor_sems)
    sum_in.scatter(ffn_part)
    size = outs[0].shape[0]
    reduces, firsts = [], []
    for number, (left, right) in enumerate(
        ((ffn_in, grad_gate), (ffn_in, grad_up), (grad_out, inner))
    ):
        total = totals[number]
        for first in range(0, total.shape[1], 256):
            span = slice(first, first + 256)
            total[:, span] = dot_tn(left[...], right[:, span]).astype(BF16)
        reduce = Reduce(
            number, piece_reader(total, size), outs[number],
            *buffers[5 * number : 5 * number + 5], sems,
        )
        reduces.append(reduce)
        firsts.append(reduce_firsts(reduce, total, size))
    units = inner.shape[1]
    for first in range(0, out_part.shape[1], 512):
        span = slice(first, first + 512)
        out_part[:, span] = dot_nt(inner[...], mat[span, 2 * units :]).astype(BF16)
    sum_out = TensorSum(1, n_tensor, arrived_2, tensor_sems)
    for piece in (3, 2, 1, 0):
        for number in range(3):
            reduces[number].second(piece, firsts[number][piece])
    sum_in.add(grad_in, True)
    sum_in.gather(grad_in)
    for reduce in reduces:
        reduce.third()
    sum_in.finish()
    sum_out.scatter(out_part)
    head_width = grad_mixed.shape[1]
    copy = load(whole_ko.at[:, head_width:], mat.at[:, :head_width], mat_sem)

    def step(at):
        back, _ = modulate_back(
            hidden[at, :], gain[...], mod_2[at, :].astype(F32), grad_in[at, :].astype(F32)
        )
        total = cotangent[at, :].astype(F32) + back
        grad_hidden[at, :] = total
        grad_attn_out[at, :] = (jnp.tanh(mod_1[at, :].astype(F32)) * total).astype(BF16)

    over_strips(hidden.shape[0], step)
    copy.wait()
    grad_mixed[...] = dot_nn(grad_attn_out[...], mat[:, :head_width])
    gain_sum[...] = jnp.zeros_like(gain_sum)

    def scale_step(at):
        state = hidden[at, :]
        product = grad_in[at, :].astype(F32) * state * row_scale(state)
        gain_sum[...] += jnp.sum(
            product * (1.0 + mod_2[at, :].astype(F32)), axis=0, keepdims=True
        )
        wide_grad[at, :] = product * gain[...]

    over_strips(hidden.shape[0], scale_step)
    ffn_mod[...] = segment_sum(member[...], wide_grad[...])
    for reduce in reduces:
        reduce.last()
    sum_out.add(ffn_rows, False)
    first = sum_out.rank * sum_out.size

    def row_step(here):
        at = pl.ds(pl.multiple_of(first + here.start, STRIP), STRIP)
        gate = jnp.tanh(mod_3[at, :].astype(F32))
        out = ffn_rows[here, :].astype(F32)
        result_rows[here, :] = (hidden[at, :] + gate * out).astype(BF16)
        rows_grad[here, :] = cotangent[at, :].astype(F32) * out * (1.0 - gate * gate)

    over_strips(sum_out.size, row_step)
    gate_part[...] = segment_sum(member[sum_out.block(sum_out.rank), :], rows_grad[...]).astype(BF16)


def attend_back_kernel(
    micro, scale, live, text_len, grad_mixed, cross_out, query, key, value, text_key_far,
    text_value_far, text_raw_far, query_raw, key_raw, q_gain, k_gain, t_gain, cosine, sine, self_id, self_row, segment,
    gate, grad_query_b, grad_key_b, grad_value_b, grad_text, gain_sums,
    grad_query, grad_key, grad_cross, grad_turned, gain_turned, text_key, text_value, text_raw, sems,
    *held
):
    held, held_sems = held[:-1], held[-1]
    early = (grad_mixed, cross_out, query, key, value, query_raw, key_raw, cosine, sine)
    copies = [load(far, here, held_sems.at[i]) for i, (far, here) in enumerate(zip(early, held))]
    grad_mixed, cross_out, query, key, value, query_raw, key_raw, cosine, sine = held
    text_copies = [
        load(far, here, sems.at[index])
        for index, (far, here) in enumerate(
            ((text_key_far, text_key), (text_value_far, text_value), (text_raw_far, text_raw))
        )
    ]
    rows, width = query.shape
    count = rows // micro
    slots = text_key.shape[0] // micro
    heads = width // HEAD_DIM
    blocks = head_blocks(width)
    wait_all(copies)
    gate_sum = jnp.sum(grad_mixed[...] * cross_out[...], axis=0, keepdims=True)
    gain_sums[...] = jnp.zeros_like(gain_sums)
    gain_sums[3:4, :] = gate_sum * (1.0 - gate[...] * gate[...])
    grad_cross[...] = (gate[...] * grad_mixed[...]).astype(BF16)
    gain_turned[...] = jnp.zeros_like(gain_turned)
    gain_column = jnp.transpose(jnp.broadcast_to(t_gain[...], (8, width)))[:, :1]
    for batch in range(micro):
        at = slice(batch * count, (batch + 1) * count)
        allowed = twice(self_id[at, :]) == self_row[batch : batch + 1, :]
        for first in range(0, width, 2 * HEAD_DIM):
            lanes = slice(first, first + 2 * HEAD_DIM)
            q, k = stack_pair(query[at, lanes]), key[at, lanes]
            grad = stack_pair(grad_mixed[at, lanes].astype(BF16))
            probs = softmax(dot_nt(q, k) * scale, allowed, None)
            grad_probs = dot_nt(grad, value[at, lanes])
            mean = jnp.sum(probs * grad_probs, axis=1, keepdims=True)
            scaled = (probs * (grad_probs - mean) * scale).astype(BF16)
            grad_query[at, lanes] = unstack_pair(dot_nn(scaled, k))
            grad_key[at, lanes] = dot_tn(scaled, q)
            grad_value_b[at, lanes] = dot_tn(probs.astype(BF16), grad).astype(BF16)

    wait_all(text_copies)

    @pl.loop(0, micro * slots)
    def _(image):
        @pl.when(live[image] == 0)
        def _():
            grad_text[:, pl.ds(pl.multiple_of(image * TXT, TXT), TXT)] = jnp.zeros(
                (2 * width, TXT), BF16
            )

        @pl.when(live[image] > 0)
        def _():
            at = pl.ds(pl.multiple_of((image // slots) * count, count), count)
            tokens = pl.ds(pl.multiple_of(image * TXT, TXT), TXT)
            mine = twice(segment[at, :]) == lax.rem(image, slots)
            column = lax.broadcasted_iota(jnp.int32, (2 * count, TXT), 1)
            allowed = mine & (column < text_len[image])
            for first in range(0, width, 2 * HEAD_DIM):
                lanes = slice(first, first + 2 * HEAD_DIM)
                q, k = stack_pair(query[at, lanes]), text_key[image, :, lanes]
                grad = stack_pair(grad_cross[at, lanes])
                probs = softmax(dot_nt(q, k) * scale, allowed, mine)
                grad_probs = dot_nt(grad, text_value[image, :, lanes])
                mean = jnp.sum(probs * grad_probs, axis=1, keepdims=True)
                scaled = (probs * (grad_probs - mean) * scale).astype(BF16)
                grad_query[at, lanes] += unstack_pair(dot_nn(scaled, k))
                grad_turned[lanes, :] = dot_tn(q, scaled)
                grad_text[width + first : width + first + 2 * HEAD_DIM, tokens] = dot_tn(
                    grad, probs.astype(BF16)
                ).astype(BF16)
            by_head = (heads, HEAD_DIM, TXT)
            raw = jnp.transpose(text_raw[image].astype(F32)).reshape(by_head)
            norm = lax.rsqrt(jnp.mean(raw * raw, axis=1, keepdims=True) + EPSILON)
            normed = raw * norm
            upper = grad_turned[...].reshape(by_head)
            gain_turned[...] += (upper * normed).reshape(width, TXT)
            inner = upper * gain_column.reshape(heads, HEAD_DIM, 1)
            mean = jnp.mean(inner * normed, axis=1, keepdims=True)
            back = norm * (inner - normed * mean)
            grad_text[:width, tokens] = back.reshape(width, TXT).astype(BF16)

    for index, (grad, raw, gain, out) in enumerate(
        (
            (grad_query, query_raw, q_gain, grad_query_b),
            (grad_key, key_raw, k_gain, grad_key_b),
        )
    ):
        turned = grad[...] * cosine[...] + swap_pairs(grad[...] * sine[...])
        back, gain_sum = head_norm_back(raw[...], gain[...], turned, blocks)
        out[...] = back.astype(BF16)
        gain_sums[index : index + 1, :] = gain_sum
    text_sums = jnp.sum(gain_turned[...], axis=1, keepdims=True)
    gain_sums[2:3, :] = jnp.transpose(jnp.broadcast_to(text_sums, (width, 128)))[:1, :]


def attn_grad_kernel(
    attn_in, grad_query, grad_key, grad_value, grad_out, mixed, whole_a, whole_b,
    total_a, total_b, whole, mat_a, mat_b, pair, sems
):
    copies = [load(whole_a, mat_a, sems.at[0]), load(whole_b, mat_b, sems.at[1])]
    width = grad_query.shape[1]
    pair[:, :width] = grad_query[...]
    pair[:, width:] = grad_value[...]
    wait_all(copies)
    for first in range(0, whole.shape[1], 512):
        span = slice(first, first + 512)
        whole[:, span] = (
            dot_nt(pair[...], mat_a[span, :]) + dot_nt(grad_key[...], mat_b[span, :width])
        ).astype(BF16)
    for first in range(0, 2 * width, 256):
        span = slice(first, first + 256)
        total_a[:, span] = dot_tn(attn_in[...], pair[:, span]).astype(BF16)
    total_b[:, :width] = dot_tn(attn_in[...], grad_key[...]).astype(BF16)
    total_b[:, width:] = dot_tn(grad_out[...], mixed[...]).astype(BF16)


def last_exchange_kernel(
    n_tensor, captions, grad_text_far, qv_far, ko_far, tokens_far, hidden_far, attn_far, attn_part,
    member, attn_gain, mods, cond_act, gain_sums, result_rows, gate_part, ffn_mod, ffn_gain_sum,
    out_qv, out_ko, out_text, result, grad_tokens, grad_adaln,
    own_attn, own_ffn, own_query, own_key, own_text, own_gate, *rest
):
    buffers, rest = rest[:15], rest[15:]
    (
        text_total, block, grad_in, gate_parts, other_mod, grad_mod, arrived, mod_a, mod_b, work_grad,
        sums, attn_sum, all_mod, all_sums, all_attn, heads_turned,
        block_sems, sems, tensor_sems, small_sems,
        grad_text, total_qv, total_ko, tokens, grad_hidden, attn_out, load_sems,
    ) = rest
    masks = range(1, 8)
    announce(masks, range(1, n_tensor), n_tensor)
    loads = [
        load(far, here, load_sems.at[i])
        for i, (far, here) in enumerate(
            (
                (grad_text_far, grad_text), (qv_far, total_qv), (ko_far, total_ko),
                (tokens_far, tokens), (hidden_far, grad_hidden), (attn_far, attn_out),
            )
        )
    ]
    pl.semaphore_wait(pltpu.get_barrier_semaphore(), 7 + n_tensor - 1)
    sum_in = TensorSum(0, n_tensor, arrived, tensor_sems)
    sum_in.scatter(attn_part)
    head_width = gain_sums.shape[1]
    sums[0:1, :] = ffn_gain_sum[...]
    for row in range(4):
        sums[1:2, row * head_width : (row + 1) * head_width] = gain_sums[row : row + 1, :]
    rank = lax.axis_index("dp")
    copies = [
        send(sums, all_sums.at[mask], small_sems, (1, mask), {"dp": partner(mask)})
        for mask in masks
    ]
    sum_out = TensorSum(1, n_tensor, arrived, tensor_sems)
    result[sum_out.block(sum_out.rank), :] = result_rows[...]
    gate_parts[0] = gate_part[...]
    gate_copies = [
        send(gate_part, gate_parts.at[place + 1], tensor_sems, (2, place), {"tensor": other})
        for place, other in sum_in.others
    ]
    size = out_qv.shape[0]
    depth = out_text.shape[1]
    reduces, firsts = [], []
    for number, (far, total, out) in enumerate(
        ((qv_far, total_qv, out_qv), (ko_far, total_ko, out_ko))
    ):
        reduce = Reduce(
            number, piece_reader(total, size), out, *buffers[5 * number : 5 * number + 5], sems
        )
        reduces.append(reduce)
        firsts.append(reduce_firsts(reduce, far, size))

    def fetch(mask, slot):
        columns = pl.ds(pl.multiple_of(partner(mask) * depth, 128), depth)
        return pltpu.make_async_copy(
            captions.at[:, columns], block.at[slot], block_sems.at[slot]
        )

    def mask_at(place):
        return 7 - 2 * place + 7 * (place // 4)

    fetch(7, 0).start()

    def read_text(piece, low):
        return text_total[2 * piece, pl.ds(low, REDUCE_STRIP), :].astype(F32)

    text = Reduce(2, read_text, out_text, *buffers[10:], sems)

    def work(low, high):
        @pl.loop(low, high)
        def _(place):
            slot = lax.rem(place, 2)
            mask = mask_at(place)

            @pl.when(place < 7)
            def _():
                fetch(mask_at(place + 1), 1 - slot).start()

            fetch(mask, slot).wait()
            for first in range(0, grad_text.shape[0], 256):
                span = slice(first, first + 256)
                text_total[mask, span, :] = dot_nn(grad_text[span, :], block[slot]).astype(BF16)

    wait_all(loads[:3])
    work(0, 2)
    for piece in (3, 2):
        text.first(piece, text_total.at[2 * piece + 1]).start()
    for piece in (3, 2, 1, 0):
        for number in range(2):
            reduces[number].second(piece, firsts[number][piece])
    work(2, 4)
    text_firsts = {}
    for piece in (3, 2, 1, 0):
        text_firsts[piece] = text.first(piece, text_total.at[2 * piece + 1])
    text_firsts[1].start()
    text_firsts[0].start()
    sum_in.add(grad_in, True)
    sum_in.gather(grad_in)
    for reduce in reduces:
        reduce.third()
    work(4, 5)
    text.second(3, text_firsts[3])
    work(5, 6)
    text.second(2, text_firsts[2])
    work(6, 7)
    text.second(1, text_firsts[1])
    work(7, 8)
    text.second(0, text_firsts[0])
    text.third()
    for copy in gate_copies:
        copy.wait()
    gate_mod = gate_parts[0].astype(F32)
    for place, _ in sum_in.others:
        gate_mod = gate_mod + gate_parts[place + 1].astype(F32)
    other_mod[...] = jnp.where(sum_in.rank == 3, gate_mod, ffn_mod[...])
    wait_all(loads[3:])
    sum_in.finish()
    sum_out.gather(result)
    input_kernel(
        tokens, member, attn_gain, grad_hidden, other_mod, mods, grad_in, attn_out,
        grad_tokens, grad_mod, attn_sum, mod_a, mod_b, work_grad,
    )
    for mask in masks:
        device = {"dp": partner(mask)}
        copies.append(send(grad_mod, all_mod.at[rank], small_sems, (0, mask), device))
        copies.append(send(attn_sum, all_attn.at[mask], small_sems, (2, mask), device))
    all_mod[rank] = grad_mod[...]
    for reduce in reduces:
        reduce.last()
    text.last()
    for copy in copies:
        copy.wait_recv()
    added, attn_added = sums[...], attn_sum[...]
    for mask in masks:
        added = added + all_sums[mask]
        attn_added = attn_added + all_attn[mask]
    grad_adaln[...] = dot_tn(cond_act[...], all_mod[...].reshape(8 * 16, all_mod.shape[2]))
    gain_size = own_attn.shape[1]
    for whole, out in ((attn_added, own_attn), (added[0:1, :], own_ffn)):
        out[...] = whole[:, :gain_size]
        for index in range(1, 8):
            part = whole[:, index * gain_size : (index + 1) * gain_size]
            out[...] = jnp.where(rank == index, part, out[...])
    heads = own_query.shape[1]
    for place, out in enumerate((own_query, own_key, own_text)):
        for head in range(heads):
            first = place * head_width + head * HEAD_DIM
            heads_turned[head : head + 1, :HEAD_DIM] = added[1:2, first : first + HEAD_DIM]
        turned = jnp.transpose(heads_turned[...])
        part = out.shape[0]
        out[...] = turned[:part, :heads]
        for index in range(1, 8):
            here = turned[index * part : (index + 1) * part, :heads]
            out[...] = jnp.where(rank == index, here, out[...])
    for head in range(heads):
        first = 3 * head_width + head * HEAD_DIM
        own_gate[:, head : head + 1] = jnp.sum(
            added[1:2, first : first + HEAD_DIM], axis=1, keepdims=True
        )
    for copy in copies:
        copy.wait_send()
    sum_out.finish()


def segment_sum(member, values):
    high = values.astype(BF16)
    rest = values - high.astype(F32)
    middle = rest.astype(BF16)
    low = (rest - middle.astype(F32)).astype(BF16)
    return dot_tn(member, high) + dot_tn(member, middle) + dot_tn(member, low)


def output_kernel(
    hidden, member, gain, cotangent, mods, ffn_out, grad_in,
    result, grad_mod, grad_gain, mod_2, mod_3, grad
):
    token_columns(member, mods, 2, mod_2)
    token_columns(member, mods, 3, mod_3)
    rank = lax.axis_index("tensor")
    grad_gain[...] = jnp.zeros_like(grad_gain)

    def step(at):
        state = hidden[at, :]
        gate = jnp.tanh(mod_3[at, :].astype(F32))
        out = ffn_out[at, :].astype(F32)
        result[at, :] = (state + gate * out).astype(BF16)
        up = grad_in[at, :].astype(F32)
        product = up * state * row_scale(state)
        grad_gain[...] += jnp.sum(
            product * (1.0 + mod_2[at, :].astype(F32)), axis=0, keepdims=True
        )
        grad_gate = cotangent[at, :].astype(F32) * out * (1.0 - gate * gate)
        grad[at, :] = jnp.where(rank == 2, product * gain[...], grad_gate)

    over_strips(hidden.shape[0], step)
    grad_mod[...] = segment_sum(member[...], grad[...])


def input_kernel(
    tokens, member, gain, grad_hidden, other_mod, mods, grad_in, attn_out,
    grad_tokens, grad_mod, grad_gain, mod_0, mod_1, grad
):
    token_columns(member, mods, 0, mod_0)
    token_columns(member, mods, 1, mod_1)
    rank = lax.axis_index("tensor")
    grad_gain[...] = jnp.zeros_like(grad_gain)

    def step(at):
        shift = mod_0[at, :].astype(F32)
        upper = grad_hidden[at, :]
        back, product = modulate_back(
            tokens[at, :].astype(F32), gain[...], shift, grad_in[at, :].astype(F32)
        )
        grad_tokens[at, :] = (upper + back).astype(BF16)
        grad_gain[...] += jnp.sum(product * (1.0 + shift), axis=0, keepdims=True)
        gate = jnp.tanh(mod_1[at, :].astype(F32))
        grad_gate = upper * attn_out[at, :].astype(F32) * (1.0 - gate * gate)
        grad[at, :] = jnp.where(rank == 0, product * gain[...], grad_gate)

    over_strips(tokens.shape[0], step)
    own = segment_sum(member[...], grad[...])
    grad_mod[...] = jnp.where(rank < 2, own, other_mod[...]).astype(BF16)


def shards(
    n_dp,
    n_tensor,
    tokens,
    context,
    captions,
    shapes,
    text_len,
    w_query,
    w_key,
    w_value,
    w_out,
    w_text_key,
    w_text_value,
    w_gate,
    w_up,
    w_down,
    w_adaln,
    gain_attn,
    gain_ffn,
    gain_query,
    gain_key,
    gain_text,
    cross_gate,
    cotangent,
):
    parts = 8 if n_dp == 8 else 1
    micro, count, width = tokens.shape
    slots = shapes.shape[1]
    rows = micro * count
    images = micro * slots
    heads = w_query.shape[1] // HEAD_DIM
    local = heads * HEAD_DIM
    units = w_gate.shape[1]
    scale = HEAD_DIM ** (-0.5)
    dp_rank = lax.axis_index("dp")
    padded = 16
    vmem, smem, anywhere = pltpu.VMEM, pltpu.SMEM, pl.ANY
    dma = pltpu.SemaphoreType.DMA

    def inside(*arrays):
        return [(array, vmem) for array in arrays]

    def scalars(*arrays):
        return [(array, smem) for array in arrays]

    def outside(*arrays):
        return [(array, anywhere) for array in arrays]

    def after(values, earlier):
        return lax.optimization_barrier((list(values), list(earlier)))[0]

    def gathered(shard):
        return lax.all_gather(shard, "dp", axis=0, tiled=True)

    def scattered(whole):
        return lax.psum_scatter(whole, "dp", scatter_dimension=0, tiled=True).astype(F32)

    part_rows = rows // n_tensor
    arrived = vmem((n_tensor - 1, part_rows, width), BF16)

    def tensor_sum(partial):
        (out,) = exchange(
            functools.partial(tensor_kernel, n_tensor),
            [(struct((rows, width)), vmem)],
            inside(partial),
            [arrived, dma((2, 2, n_tensor - 1))],
            1,
        )
        return out

    gain_list = (gain_attn, gain_ffn, gain_query, gain_key, gain_text)
    cond_rows, span = w_adaln.shape
    shard_qv = jnp.concatenate([w_query, w_value], axis=1)
    shard_ko = jnp.concatenate([w_key, w_out], axis=1)
    shard_f = jnp.concatenate([w_gate, w_up, w_down], axis=1)
    if parts == 1:
        whole_tk, whole_tv = gathered(w_text_key), gathered(w_text_value)
        whole_qv, whole_ko = gathered(shard_qv), gathered(shard_ko)
        gains = [lax.all_gather(gain.astype(F32), "dp", axis=0, tiled=True) for gain in gain_list]
        attn_gain, ffn_gain = [gain.reshape(1, width) for gain in gains[:2]]
        query_gain, key_gain, text_gain = [gain.T.reshape(1, local) for gain in gains[2:]]
        context_all = gathered(context.reshape(images, -1))
        cond_cols = lax.dynamic_slice_in_dim(context_all, dp_rank * cond_rows, cond_rows, 1)
        cond_act = jax.nn.silu(cond_cols.astype(F32)).astype(BF16)
        mod_part = scattered(dot_nn(cond_act, w_adaln)).astype(BF16)
        mods = lax.all_gather(mod_part, "tensor", axis=0)
        mods = jnp.pad(mods, ((0, 0), (0, padded - images), (0, 0)))
    else:
        text_raw, text_key, text_value, whole_qv, whole_ko, cond_act, mods, *gains = exchange(
            functools.partial(gather_kernel, n_tensor),
            [(struct((images, TXT, local)), anywhere)] * 3
            + [(struct((width, 2 * local)), anywhere)] * 2
            + [
                (struct((parts * padded, cond_rows)), vmem),
                (struct((n_tensor, padded, span)), vmem),
            ]
            + [(struct((1, width), F32), vmem)] * 2
            + [(struct((1, local), F32), vmem)] * 3,
            outside(w_text_key, w_text_value, shard_qv, shard_ko)
            + inside(
                context, gain_attn[None], gain_ffn[None], gain_query, gain_key, gain_text, w_adaln
            )
            + outside(captions.reshape(images, TXT, DT)),
            [
                vmem((parts, 2 * padded, cond_rows), BF16),
                vmem((parts, 2 * padded, cond_rows), BF16),
                vmem((parts, padded, span), BF16),
                vmem((parts, padded, span), BF16),
                vmem((DT, local), BF16),
                vmem((DT, local), BF16),
                vmem((local, local), BF16),
                vmem((2, TXT, DT), BF16),
                vmem((2, 3, TXT, local), BF16),
                dma((2,)),
                dma((2, 3)),
                dma((4,)),
                dma((2, 4, 9)),
                dma((2, 8)),
                dma((2, 8)),
                dma((2, n_tensor)),
            ],
            2,
        )
        attn_gain, ffn_gain, query_gain, key_gain, text_gain = gains
        (shard_f,) = after([shard_f], [mods])
    whole_f = gathered(shard_f)
    layouts = [image_layout(shapes[i], count) for i in range(micro)]
    member, segment, inside_any, row_pos, col_pos = [
        jnp.stack([layout[j] for layout in layouts]) for j in range(5)
    ]
    cosine, sine = rope_tables(row_pos.reshape(rows), col_pos.reshape(rows))
    cosine = jnp.tile(jnp.stack([cosine, cosine], axis=2).reshape(rows, HEAD_DIM), (1, heads))
    sine = jnp.tile(jnp.stack([-sine, sine], axis=2).reshape(rows, HEAD_DIM), (1, heads))
    which = jnp.arange(micro, dtype=jnp.int32)
    member = jnp.where(
        (which[:, None] == which[None, :])[:, None, :, None], member[:, :, None, :], 0.0
    )
    member = jnp.pad(member.reshape(rows, images), ((0, 0), (0, padded - images))).astype(BF16)
    self_row = jnp.where(inside_any > 0, segment, slots)
    self_id = self_row.reshape(rows, 1)
    segment = segment.reshape(rows, 1)
    lens = text_len.reshape(images)
    used = shapes[:, :, 0] * (shapes[:, :, 1] + 1) > 0
    used = used | (jnp.arange(slots)[None, :] == 0)
    live = used.reshape(images).astype(jnp.int32)
    at = jnp.arange(images, dtype=jnp.int32)
    source = lax.cummax(jnp.where(live > 0, at, 0))
    gate = jnp.repeat(jnp.tanh(cross_gate.astype(F32)), HEAD_DIM)[None, :]
    token_rows = tokens.reshape(rows, width)
    grad_y = cotangent.reshape(rows, width)
    caption_images = captions.reshape(images, TXT, DT)

    attn_in, query_raw, key_raw, query_rot, key_rot, value = run(
        project_kernel,
        [struct((rows, width))]
        + [struct((rows, local), F32)] * 2
        + [struct((rows, local))] * 3,
        inside(token_rows, member, attn_gain, query_gain, key_gain, cosine, sine, mods)
        + outside(whole_qv, whole_ko),
        [
            vmem((width, 2 * local), BF16),
            vmem((width, 2 * local), BF16),
            vmem((rows, width), BF16),
            dma((2,)),
        ],
        flops=6 * rows * width * local,
        traffic=10 * 2**20,
    )

    if parts == 1:
        text_raw, text_key, text_value = pl.pallas_call(
            text_kernel,
            out_shape=[struct((images, TXT, local))] * 3,
            grid_spec=pltpu.PrefetchScalarGridSpec(
                num_scalar_prefetch=2,
                grid=(images,),
                in_specs=[
                    pl.BlockSpec((1, TXT, DT), lambda i, live, source: (source[i], 0, 0)),
                    pl.BlockSpec((1, local), lambda i, live, source: (0, 0)),
                ]
                + [pl.BlockSpec(memory_space=anywhere)] * 2,
                out_specs=[pl.BlockSpec((1, TXT, local), lambda i, live, source: (i, 0, 0))] * 3,
                scratch_shapes=[vmem((DT, local), BF16), vmem((DT, local), BF16), dma((2,))],
            ),
            compiler_params=pltpu.CompilerParams(vmem_limit_bytes=40 * 2**20),
            cost_estimate=pl.CostEstimate(
                flops=2 * images * TXT * DT * local, bytes_accessed=20 * 2**20, transcendentals=0
            ),
        )(live, source, caption_images, text_gain, whole_tk, whole_tv)

    wide = vmem((rows, width), BF16)
    mixed, cross_out, attn_part = run(
        functools.partial(attend_kernel, micro, scale),
        [struct((rows, local)), struct((rows, local), F32), struct((rows, width))],
        scalars(live, lens)
        + inside(query_rot, key_rot, value)
        + outside(text_key, text_value)
        + inside(self_id, self_row, segment, gate)
        + outside(whole_ko),
        [
            vmem((width, 2 * local), BF16),
            vmem((images, TXT, local), BF16),
            vmem((images, TXT, local), BF16),
            vmem((rows, local), F32),
            dma,
            dma((2,)),
        ],
        flops=2 * 2**30,
        traffic=12 * 2**20,
    )
    attn_out = tensor_sum(attn_part)

    size = width // parts
    if parts == 1:
        mat = vmem((width, 3 * units), BF16)
        hidden, ffn_in, inner, grad_gate, grad_up, grad_ffn_out, ffn_part = run(
            feed_kernel,
            [struct((rows, width), F32), struct((rows, width))]
            + [struct((rows, units))] * 3
            + [struct((rows, width))] * 2,
            inside(token_rows, member, ffn_gain, grad_y, mods, attn_out) + outside(whole_f),
            [mat, wide, wide, wide, dma],
            flops=10 * rows * width * units,
            traffic=20 * 2**20,
        )
        (grad_f,) = run(
            feed_grad_kernel,
            [struct((width, 3 * units))],
            inside(grad_ffn_out, inner, ffn_in, grad_gate, grad_up),
            flops=6 * rows * width * units,
            traffic=12 * 2**20,
        )
        (ffn_part,) = after([ffn_part], [grad_f])
        grad_ffn_in = tensor_sum(ffn_part)
        grad_f = scattered(grad_f)
        (ffn_out_part,) = run(
            feed_out_kernel,
            [struct((rows, width))],
            inside(inner) + outside(whole_f),
            [vmem((width, units), BF16), dma],
            flops=2 * rows * width * units,
            traffic=5 * 2**20,
        )
        ffn_out = lax.psum(ffn_out_part, "tensor")

        grad_hidden, grad_attn_out, grad_mixed = run(
            mixed_grad_kernel,
            [struct((rows, width), F32), struct((rows, width)), struct((rows, local), F32)],
            inside(hidden, member, ffn_gain, grad_y, mods, grad_ffn_in) + outside(whole_ko),
            [vmem((width, 2 * local), BF16), wide, wide, dma],
            flops=2 * rows * width * local,
            traffic=8 * 2**20,
        )
    else:
        (
            hidden, grad_hidden, grad_attn_out, grad_mixed, result_rows, gate_part, ffn_mod,
            ffn_gain_sum, *grad_f
        ) = exchange(
            functools.partial(feed_exchange_kernel, n_tensor),
            [
                (struct((rows, width), F32), vmem),
                (struct((rows, width), F32), vmem),
                (struct((rows, width)), vmem),
                (struct((rows, local), F32), vmem),
                (struct((part_rows, width)), vmem),
                (struct((padded, width)), vmem),
                (struct((padded, width), F32), vmem),
                (struct((1, width), F32), vmem),
            ]
            + [(struct((size, units), F32), vmem)] * 3,
            inside(token_rows, member, ffn_gain, grad_y, mods, attn_out)
            + outside(whole_f, whole_ko),
            [wide]
            + [vmem((rows, units), BF16)] * 3
            + [wide] * 3
            + [vmem((width, 3 * units), BF16), wide, wide, wide, wide]
            + [
                vmem((part_rows, width), BF16),
                vmem((rows, width), F32),
                vmem((part_rows, width), F32),
            ]
            + [vmem((width, units), BF16)] * 3
            + reduce_scratch(size, units) * 3
            + [arrived, arrived, dma, dma, dma((2, 3, 10)), dma((2, 4, n_tensor - 1))],
            5,
            vmem=60,
        )

    tile = struct((rows, local))
    grad_query_b, grad_key_b, grad_value_b, grad_text_all, gain_sums = run(
        functools.partial(attend_back_kernel, micro, scale),
        [tile, tile, tile, struct((2 * local, images * TXT)), struct((8, local), F32)],
        scalars(live, lens)
        + outside(
            grad_mixed, cross_out, query_rot, key_rot, value, text_key, text_value, text_raw,
            query_raw, key_raw,
        )
        + inside(query_gain, key_gain, text_gain)
        + outside(cosine, sine)
        + inside(self_id, self_row, segment, gate),
        [
            vmem((rows, local), F32),
            vmem((rows, local), F32),
            vmem((rows, local), BF16),
            vmem((local, TXT), F32),
            vmem((local, TXT), F32),
            vmem((images, TXT, local), BF16),
            vmem((images, TXT, local), BF16),
            vmem((images, TXT, local), BF16),
            dma((3,)),
        ]
        + [vmem((rows, local), F32)] * 2
        + [vmem((rows, local), BF16)] * 3
        + [vmem((rows, local), F32)] * 4
        + [
            dma((9,)),
        ],
        flops=4 * 2**30,
        traffic=15 * 2**20,
        vmem=62,
    )

    total_qv, total_ko, attn_in_part = run(
        attn_grad_kernel,
        [struct((width, 2 * local))] * 2 + [struct((rows, width))],
        inside(attn_in, grad_query_b, grad_key_b, grad_value_b, grad_attn_out, mixed)
        + outside(whole_qv, whole_ko),
        [
            vmem((width, 2 * local), BF16),
            vmem((width, 2 * local), BF16),
            vmem((rows, 2 * local), BF16),
            dma((2,)),
        ],
        flops=14 * rows * width * local,
        traffic=15 * 2**20,
        vmem=62,
    )
    depth = DT // parts
    caption_rows = captions.reshape(images * TXT, DT)
    if parts == 1:
        grad_attn_in = lax.psum(attn_in_part, "tensor")
        grad_text = dot_nn(grad_text_all, caption_rows)
        wholes = (total_qv, total_ko, grad_text.T)
        grad_qv, grad_ko, grad_text = [scattered(whole.astype(F32)) for whole in wholes]
        grad_query, grad_value = grad_qv[:, :local], grad_qv[:, local:]
        grad_key, grad_out = grad_ko[:, :local], grad_ko[:, local:]
        grad_tk, grad_tv = grad_text[:, :local], grad_text[:, local:]
        grad_f = [grad_f[:, i * units : (i + 1) * units] for i in range(3)]
        result, ffn_mod, ffn_gain_sum = run(
            output_kernel,
            [struct((rows, width)), struct((padded, width), F32), struct((1, width), F32)],
            inside(hidden, member, ffn_gain, grad_y, mods, ffn_out, grad_ffn_in),
            [wide, wide, vmem((rows, width), F32)],
        )
        grad_tokens, grad_mod, attn_gain_sum = run(
            input_kernel,
            [struct((rows, width)), struct((padded, width)), struct((1, width), F32)],
            inside(
                token_rows, member, attn_gain, grad_hidden, ffn_mod, mods, grad_attn_in, attn_out
            ),
            [wide, wide, vmem((rows, width), F32)],
        )
        grad_w_adaln = dot_tn(cond_act, gathered(grad_mod[:images]))
        sums = [attn_gain_sum[0], ffn_gain_sum[0]]
        sums += [row.reshape(heads, HEAD_DIM).T for row in gain_sums[:3]]
        sums = lax.psum(sums, "dp")
        own = [
            lax.dynamic_slice_in_dim(whole, dp_rank * (whole.shape[0] // n_dp), whole.shape[0] // n_dp, 0)
            for whole in sums
        ]
        own.append(lax.psum(jnp.sum(gain_sums[3].reshape(heads, HEAD_DIM), axis=1), "dp"))
    else:
        grad_qv, grad_ko, grad_text, result, grad_tokens, grad_w_adaln, *own = exchange(
            functools.partial(last_exchange_kernel, n_tensor),
            [
                (struct((size, 2 * local), F32), vmem),
                (struct((size, 2 * local), F32), vmem),
                (struct((2 * local, depth), F32), vmem),
                (struct((rows, width)), vmem),
                (struct((rows, width)), vmem),
                (struct((cond_rows, span), F32), vmem),
            ]
            + [(struct((1, gain_attn.size), F32), vmem)] * 2
            + [(struct(gain_query.shape, F32), vmem)] * 3
            + [(struct((1, heads), F32), vmem)],
            outside(
                caption_rows, grad_text_all, total_qv, total_ko, token_rows, grad_hidden, attn_out
            )
            + inside(
                attn_in_part, member, attn_gain, mods, cond_act, gain_sums, result_rows, gate_part, ffn_mod,
                ffn_gain_sum,
            ),
            reduce_scratch(size, 2 * local) * 2
            + reduce_scratch(2 * local, depth)
            + [
                vmem((parts, 2 * local, depth), BF16),
                vmem((2, images * TXT, depth), BF16),
                wide,
                vmem((n_tensor, padded, width), BF16),
                vmem((padded, width), F32),
                vmem((padded, width), BF16),
                arrived,
                wide,
                wide,
                vmem((rows, width), F32),
                vmem((2, width), F32),
                vmem((1, width), F32),
                vmem((parts, padded, width), BF16),
                vmem((parts, 2, width), F32),
                vmem((parts, 1, width), F32),
                vmem((8, 128), F32),
                dma((2,)),
                dma((2, 3, 10)),
                dma((2, 4, n_tensor - 1)),
                dma((2, 3, 8)),
                vmem((2 * local, images * TXT), BF16),
                vmem((width, 2 * local), BF16),
                vmem((width, 2 * local), BF16),
                wide,
                vmem((rows, width), F32),
                wide,
                dma((6,)),
            ],
            3,
            vmem=62,
        )
        own[:2] = [part[0] for part in own[:2]]
        own[5] = own[5][0]
        plain = [*grad_f, grad_w_adaln, result, grad_tokens]
        square, tall = struct((size, local), F32), struct((depth, local), F32)
        (
            grad_query, grad_key, grad_value, grad_out, grad_tk, grad_tv, *plain
        ) = pl.pallas_call(
            emit_kernel,
            out_shape=[square] * 4 + [tall] * 2 + [struct(x.shape, x.dtype) for x in plain],
            in_specs=[pl.BlockSpec(memory_space=anywhere)] * (3 + len(plain)),
            out_specs=[pl.BlockSpec(memory_space=anywhere)] * (6 + len(plain)),
            scratch_shapes=[vmem(x.shape, x.dtype) for x in (grad_qv, grad_ko, grad_text, *plain)]
            + [
                vmem((depth, local), F32),
                vmem((depth, local), F32),
                dma((3 + len(plain),)),
                dma((6 + len(plain),)),
            ],
            compiler_params=pltpu.CompilerParams(vmem_limit_bytes=62 * 2**20),
        )(grad_qv, grad_ko, grad_text, *plain)
        *grad_f, grad_w_adaln, result, grad_tokens = plain

    return (
        result.reshape(micro, count, width),
        grad_tokens.reshape(micro, count, width),
        grad_query,
        grad_key,
        grad_value,
        grad_out,
        grad_tk,
        grad_tv,
        *grad_f,
        grad_w_adaln,
        *own,
    )


def solution(mesh):
    return jax.shard_map(
        functools.partial(shards, mesh.shape["dp"], mesh.shape["tensor"]),
        mesh=mesh,
        in_specs=(
            P(None, "dp", None),
            P(None, "dp", None),
            P(None, "dp", None, None),
            P(None, "dp", None),
            P(None, "dp"),
            P("dp", "tensor"),
            P("dp", "tensor"),
            P("dp", "tensor"),
            P("dp", "tensor"),
            P("dp", "tensor"),
            P("dp", "tensor"),
            P("dp", "tensor"),
            P("dp", "tensor"),
            P("dp", "tensor"),
            P("dp", "tensor"),
            P("dp"),
            P("dp"),
            P("dp", "tensor"),
            P("dp", "tensor"),
            P("dp", "tensor"),
            P("tensor"),
            P(None, "dp", None),
        ),
        out_specs=(
            P(None, "dp", None),
            P(None, "dp", None),
            P("dp", "tensor"),
            P("dp", "tensor"),
            P("dp", "tensor"),
            P("dp", "tensor"),
            P("dp", "tensor"),
            P("dp", "tensor"),
            P("dp", "tensor"),
            P("dp", "tensor"),
            P("dp", "tensor"),
            P("dp", "tensor"),
            P("dp"),
            P("dp"),
            P("dp", "tensor"),
            P("dp", "tensor"),
            P("dp", "tensor"),
            P("tensor"),
        ),
        check_vma=False,
    )
```

```python
import functools

import jax
import jax.numpy as jnp
from jax import lax
from jax.experimental import pallas as pl
from jax.experimental.pallas import tpu as pltpu
from jax.sharding import PartitionSpec as P

HEAD_DIM = 64
DT = 4096
TXT = 256


EPSILON = 1e-06
MASKED = -1e30
ROPE_BASE = 10000.0
STRIP = 16
F32 = jnp.float32
BF16 = jnp.bfloat16


def image_layout(shapes, count):
    height = shapes[:, 0]
    stride_all = shapes[:, 1] + 1
    extent = height * stride_all
    finish = jnp.cumsum(extent)
    begin = finish - extent
    places = jnp.arange(count, dtype=jnp.int32)
    member = (places[:, None] >= begin[None, :]) & (places[:, None] < finish[None, :])
    member_int = member.astype(jnp.int32)
    inside = jnp.sum(member_int, axis=1)
    slot_ids = jnp.arange(shapes.shape[0], dtype=jnp.int32)
    segment = jnp.sum(member_int * slot_ids[None, :], axis=1)
    stride = jnp.sum(member_int * stride_all[None, :], axis=1) + 1 - inside
    offset = places - jnp.sum(member_int * begin[None, :], axis=1)
    return (member.astype(jnp.float32), segment, inside, offset // stride, offset % stride)


def rope_tables(row_pos, col_pos):
    quarter = HEAD_DIM // 4
    freq = ROPE_BASE ** (-jnp.arange(quarter, dtype=jnp.float32) / quarter)
    angles = jnp.stack(
        [
            row_pos.astype(jnp.float32)[:, None] * freq[None, :],
            col_pos.astype(jnp.float32)[:, None] * freq[None, :],
        ],
        axis=1,
    )
    return (jnp.cos(angles), jnp.sin(angles))


def dot_nn(left, right):
    return lax.dot_general(left, right, (((1,), (0,)), ((), ())), preferred_element_type=F32)


def dot_nt(left, right):
    return lax.dot_general(left, right, (((1,), (1,)), ((), ())), preferred_element_type=F32)


def dot_tn(left, right):
    return lax.dot_general(left, right, (((0,), (0,)), ((), ())), preferred_element_type=F32)


def struct(shape, dtype=BF16):
    return jax.ShapeDtypeStruct(shape, dtype)


def run(body, outs, ins, scratch=(), flops=0, traffic=0, vmem=48):
    return pl.pallas_call(
        body,
        out_shape=outs,
        in_specs=[pl.BlockSpec(memory_space=space) for _, space in ins],
        out_specs=[pl.BlockSpec(memory_space=pltpu.VMEM)] * len(outs),
        scratch_shapes=list(scratch),
        compiler_params=pltpu.CompilerParams(vmem_limit_bytes=vmem * 2**20),
        cost_estimate=pl.CostEstimate(flops=flops, bytes_accessed=traffic, transcendentals=0),
    )(*[array for array, _ in ins])


def load(source, target, sem):
    copy = pltpu.make_async_copy(source, target, sem)
    copy.start()
    return copy


def wait_all(copies):
    for copy in copies:
        copy.wait()


def token_columns(member, mods, which, target):
    target[...] = dot_nn(member[...], mods[which]).astype(BF16)


def over_strips(rows, step):
    @pl.loop(0, rows // STRIP)
    def _(index):
        step(pl.ds(pl.multiple_of(index * STRIP, STRIP), STRIP))


def head_sum(values, blocks):
    high = values.astype(BF16)
    low = (values - high.astype(F32)).astype(BF16)
    return dot_nn(high, blocks) + dot_nn(low, blocks)


def head_blocks(width):
    row = lax.broadcasted_iota(jnp.int32, (width, width), 0) // HEAD_DIM
    column = lax.broadcasted_iota(jnp.int32, (width, width), 1) // HEAD_DIM
    return jnp.where(row == column, 1.0, 0.0).astype(BF16)


def swap_pairs(values):
    width = values.shape[1]
    quarter = HEAD_DIM // 4
    lane = lax.broadcasted_iota(jnp.int32, values.shape, 1)
    former = lax.rem(lane, 2 * quarter) < quarter
    return jnp.where(
        former, pltpu.roll(values, width - quarter, 1), pltpu.roll(values, quarter, 1)
    )


def head_norm(values, gain, blocks):
    scale = lax.rsqrt(head_sum(values * values, blocks) * (1.0 / HEAD_DIM) + EPSILON)
    return values * scale * gain


def head_norm_back(values, gain, grad, blocks):
    scale = lax.rsqrt(head_sum(values * values, blocks) * (1.0 / HEAD_DIM) + EPSILON)
    normed = values * scale
    grad_gain = jnp.sum(grad * normed, axis=0, keepdims=True)
    inner = grad * gain
    mean = head_sum(inner * normed, blocks) * (1.0 / HEAD_DIM)
    return scale * (inner - normed * mean), grad_gain


def row_scale(values):
    return lax.rsqrt(jnp.mean(values * values, axis=1, keepdims=True) + EPSILON)


MESH = pl.DeviceIdType.MESH
PAIR, ALONG_X, ALONG_Y = 1, 2, 4


def partner(mask):
    rank = lax.axis_index("dp")
    index = rank
    for bit in (1, 2, 4):
        flip = lax.rem(mask // bit, 2)
        index = index + flip * (bit - 2 * bit * lax.rem(rank // bit, 2))
    return index


def announce(masks, shifts, n_tensor):
    barrier = pltpu.get_barrier_semaphore()
    rank = lax.axis_index("tensor")
    for mask in masks:
        pl.semaphore_signal(
            barrier, inc=1, device_id={"dp": partner(mask)}, device_id_type=MESH
        )
    for shift in shifts:
        pl.semaphore_signal(
            barrier,
            inc=1,
            device_id={"tensor": lax.rem(rank + shift, n_tensor)},
            device_id_type=MESH,
        )


def greet(masks, shifts, n_tensor):
    announce(masks, shifts, n_tensor)
    pl.semaphore_wait(pltpu.get_barrier_semaphore(), len(masks) + len(shifts))


def send(source, target, sems, index, device):
    copy = pltpu.make_async_remote_copy(
        src_ref=source,
        dst_ref=target,
        send_sem=sems.at[(0,) + index],
        recv_sem=sems.at[(1,) + index],
        device_id=device,
        device_id_type=MESH,
    )
    copy.start()
    return copy


def gather_kernel(
    n_tensor, shard_tk, shard_tv, shard_qv, shard_ko, context, attn_own, ffn_own, q_own, k_own,
    t_own, w_adaln, captions,
    text_raw, text_key, text_value, qv, ko, cond_act, mods, attn_gain, ffn_gain, q_gain, k_gain, t_gain,
    small, small_all, product, sums, tk, tv, blocks, block, stage, block_sems, stage_sems, own_sems, shard_sems, small_sems, mod_sems, tensor_sems,
):
    rank, tensor_rank = lax.axis_index("dp"), lax.axis_index("tensor")
    masks = range(1, 8)
    shifts = range(1, n_tensor)
    greet(masks, shifts, n_tensor)
    groups = ((shard_tk, tk), (shard_tv, tv), (shard_qv, qv), (shard_ko, ko))

    def rows_of(shard, index, first, size):
        return pl.ds(pl.multiple_of(index * shard.shape[0] + first, 32), size)

    firsts, seconds, pairs, locals_ = {}, {}, {}, []

    def step_1(number):
        shard, whole = groups[number]
        mine = whole.at[rows_of(shard, rank, 0, shard.shape[0])]
        firsts[number] = [
            send(shard, mine, shard_sems, (number, place), {"dp": partner(mask)})
            for place, mask in ((0, ALONG_X), (1, ALONG_Y))
        ]
        pairs[number] = [send(shard, mine, shard_sems, (number, 4), {"dp": partner(PAIR)})]
        local = pltpu.make_async_copy(shard, mine, own_sems.at[number])
        local.start()
        locals_.append(local)

    def step_2(number):
        shard, whole = groups[number]
        size = shard.shape[0]
        half = size // 2
        seconds[number] = []
        for place, mask, onward, start in ((0, ALONG_X, ALONG_Y, half), (1, ALONG_Y, ALONG_X, 0)):
            firsts[number][place].wait_recv()
            part = whole.at[rows_of(shard, partner(mask), start, half)]
            seconds[number].append(
                send(part, part, shard_sems, (number, 2 + place), {"dp": partner(onward)})
            )
            piece = whole.at[rows_of(shard, partner(mask), 0, size)]
            pairs[number].append(
                send(piece, piece, shard_sems, (number, 5 + place), {"dp": partner(PAIR)})
            )

    def step_3(number):
        shard, whole = groups[number]
        half = shard.shape[0] // 2
        for place, start in ((0, half), (1, 0)):
            seconds[number][place].wait_recv()
            part = whole.at[rows_of(shard, partner(ALONG_X + ALONG_Y), start, half)]
            pairs[number].append(
                send(part, part, shard_sems, (number, 7 + place), {"dp": partner(PAIR)})
            )

    def step_4(number):
        for copy in pairs[number]:
            copy.wait_recv()
        locals_[number].wait()

    count = captions.shape[0]

    def fetch(image, slot):
        return pltpu.make_async_copy(captions.at[image], block.at[slot], block_sems.at[slot])

    outputs = (text_raw, text_key, text_value)
    kinds = ((0, 1), (2,))

    def store(image, slot, kind):
        return [
            pltpu.make_async_copy(
                stage.at[slot, index], outputs[index].at[image], stage_sems.at[slot, index]
            )
            for index in kinds[kind]
        ]

    def text_images(low, high, kind):
        @pl.loop(low, high)
        def _(image):
            slot = lax.rem(image, 2)

            @pl.when(image < count - 1)
            def _():
                fetch(image + 1, 1 - slot).start()

            if kind == 0:

                @pl.when(image == count - 1)
                def _():
                    fetch(0, 1 - slot).start()

            fetch(image, slot).wait()

            @pl.when(image >= 2)
            def _():
                wait_all(store(image - 2, slot, kind))

            if kind == 0:
                raw = dot_nn(block[slot], tk[...])
                stage[slot, 0] = raw.astype(BF16)
                stage[slot, 1] = head_norm(raw, t_gain[...], blocks[...]).astype(BF16)
            else:
                stage[slot, 2] = dot_nn(block[slot], tv[...]).astype(BF16)
            for copy in store(image, slot, kind):
                copy.start()

    fetch(0, 0).start()
    step_1(0)
    blocks[...] = head_blocks(tk.shape[1])
    small_copies = []
    images, slots = context.shape[0] * context.shape[1], context.shape[1]
    depth = w_adaln.shape[0]
    gain_size = attn_own.shape[1]
    heads = q_own.shape[1]
    small[...] = jnp.zeros_like(small)
    for index in range(8):
        for first in range(0, images, slots):
            small[index, first : first + slots, :] = context[
                first // slots, :, index * depth : (index + 1) * depth
            ]
        for row, own in ((16, attn_own), (18, ffn_own)):
            for place, first in enumerate(range(0, gain_size, depth)):
                size = min(depth, gain_size - first)
                small[index, row + place : row + place + 1, :size] = own[:, first : first + size]
        for place, own in enumerate((q_own, k_own, t_own)):
            small[index, 24:32, 8 * place : 8 * place + heads] = own[...]
    for mask in masks:
        small_copies.append(
            send(
                small.at[partner(mask)], small_all.at[rank], small_sems, (mask,),
                {"dp": partner(mask)},
            )
        )
    small_all[rank] = small[rank]
    for copy in small_copies:
        copy.wait_recv()
    width = w_adaln.shape[1]
    contexts = small_all[:, 0:16, :].astype(F32).reshape(8 * 16, depth)
    cond_act[...] = jax.nn.silu(contexts).astype(BF16)
    product[...] = dot_nn(cond_act[...], w_adaln[...]).astype(BF16).reshape(8, 16, width)
    mod_copies = [
        send(
            product.at[partner(mask)], sums.at[mask], mod_sems, (mask,), {"dp": partner(mask)}
        )
        for mask in masks
    ]
    step_2(0)
    step_1(1)
    for row, out in ((16, attn_gain), (18, ffn_gain)):
        for index in range(8):
            for place, first in enumerate(range(0, gain_size, depth)):
                size = min(depth, gain_size - first)
                start = index * gain_size + first
                out[:, start : start + size] = small_all[
                    index, row + place : row + place + 1, :size
                ].astype(F32)
    turned = jnp.transpose(small_all[:, 24:32, :].astype(F32).reshape(HEAD_DIM, depth))
    for place, out in enumerate((q_gain, k_gain, t_gain)):
        for head in range(heads):
            out[:, head * HEAD_DIM : (head + 1) * HEAD_DIM] = turned[
                8 * place + head : 8 * place + head + 1, :
            ]
    sums[0] = product[rank]
    for copy in mod_copies:
        copy.wait_recv()
    total = sums[0].astype(F32)
    for mask in masks:
        total = total + sums[mask].astype(F32)
    mods[tensor_rank] = total.astype(BF16)
    tensor_copies = [
        send(
            mods.at[tensor_rank], mods.at[tensor_rank], tensor_sems, (shift,),
            {"tensor": lax.rem(tensor_rank + shift, n_tensor)},
        )
        for shift in shifts
    ]

    step_3(0)
    step_4(0)
    third = count // 3
    text_images(0, third, 0)
    step_2(1)
    step_1(2)
    step_1(3)
    text_images(third, 2 * third, 0)
    step_3(1)
    text_images(2 * third, count, 0)
    step_4(1)
    text_images(0, third, 1)
    step_2(2)
    step_2(3)
    text_images(third, 2 * third, 1)
    text_images(2 * third, count, 1)
    step_3(2)
    step_3(3)
    step_4(2)
    step_4(3)
    for image in (count - 2, count - 1):
        for kind in (0, 1):
            wait_all(store(image, image % 2, kind))
    for copy in tensor_copies:
        copy.wait_recv()
    for number in range(4):
        for copy in firsts[number] + seconds[number] + pairs[number]:
            copy.wait_send()
    for copy in small_copies + mod_copies + tensor_copies:
        copy.wait_send()


ROUTES = ((0, 1, 2, ALONG_X, ALONG_Y), (1, 2, 1, ALONG_Y, ALONG_X))
REDUCE_STRIP = 32


def over_half(half, step):
    @pl.loop(0, half // REDUCE_STRIP)
    def _(index):
        step(pl.multiple_of(index * REDUCE_STRIP, REDUCE_STRIP))


class Reduce:
    def __init__(self, number, read, out, from_pair, out_2, in_2, out_3, in_3, sems):
        self.number, self.read, self.out, self.sems = number, read, out, sems
        self.from_pair, self.out_2, self.in_2, self.out_3, self.in_3 = (
            from_pair, out_2, in_2, out_3, in_3
        )
        self.half = out.shape[0] // 2
        self.copies, self.arriving = [], {}

    def pair_term(self, piece, low):
        there = pl.ds(low, REDUCE_STRIP)
        return self.read(piece, low) + self.from_pair[piece, there, :].astype(F32)

    def move(self, source, target, index, mask):
        return pltpu.make_async_remote_copy(
            src_ref=source,
            dst_ref=target,
            send_sem=self.sems.at[0, self.number, index],
            recv_sem=self.sems.at[1, self.number, index],
            device_id={"dp": partner(mask)},
            device_id_type=MESH,
        )

    def first(self, piece, source):
        return self.move(source, self.from_pair.at[piece], piece, PAIR)

    def second(self, piece, copy):
        copy.wait_recv()
        self.copies.append(copy)
        for side, close, far, first, last in ROUTES:
            if piece not in (close, 3):
                continue
            slot = 1 if piece == 3 else 0

            def step(low):
                self.out_2[side, slot, pl.ds(low, REDUCE_STRIP), :] = self.pair_term(
                    piece, pl.multiple_of(low + side * self.half, REDUCE_STRIP)
                ).astype(BF16)

            over_half(self.half, step)
            moved = self.move(
                self.out_2.at[side, slot], self.in_2.at[side, slot], 4 + 2 * side + slot, first
            )
            moved.start()
            self.arriving[side, slot] = moved
            self.copies.append(moved)

    def third(self):
        for side, close, far, first, last in ROUTES:
            self.arriving[side, 1].wait_recv()

            def step(low):
                here = pl.ds(low, REDUCE_STRIP)
                there = pl.multiple_of(low + side * self.half, REDUCE_STRIP)
                self.out_3[side, here, :] = (
                    self.pair_term(far, there) + self.in_2[side, 1, here, :].astype(F32)
                ).astype(BF16)

            over_half(self.half, step)
            moved = self.move(self.out_3.at[side], self.in_3.at[side], 8 + side, last)
            moved.start()
            self.arriving[side, 2] = moved
            self.copies.append(moved)

    def last(self):
        for side in (0, 1):
            self.arriving[side, 0].wait_recv()
            self.arriving[side, 2].wait_recv()

            def step(low):
                here = pl.ds(low, REDUCE_STRIP)
                there = pl.multiple_of(low + side * self.half, REDUCE_STRIP)
                self.out[pl.ds(there, REDUCE_STRIP), :] = (
                    self.pair_term(0, there)
                    + self.in_2[side, 0, here, :].astype(F32)
                    + self.in_3[side, here, :].astype(F32)
                )

            over_half(self.half, step)
        for copy in self.copies:
            copy.wait_send()


def reduce_scratch(depth, columns):
    half = depth // 2
    return [
        pltpu.VMEM((4, depth, columns), BF16),
        pltpu.VMEM((2, 2, half, columns), BF16),
        pltpu.VMEM((2, 2, half, columns), BF16),
        pltpu.VMEM((2, half, columns), BF16),
        pltpu.VMEM((2, half, columns), BF16),
    ]


def piece_reader(total, size):
    def read(piece, low):
        first = partner(2 * piece) * size + low
        return total[pl.ds(pl.multiple_of(first, 32), REDUCE_STRIP), :].astype(F32)

    return read


def reduce_firsts(reduce, total, size):
    copies = {}
    for piece in (3, 2, 1, 0):
        copies[piece] = reduce.first(piece, piece_of(total, 2 * piece + 1, size))
        copies[piece].start()
    return copies


def piece_of(total, mask, size):
    return total.at[pl.ds(pl.multiple_of(partner(mask) * size, 64), size)]


class TensorSum:
    def __init__(self, number, n_tensor, arrived, sems):
        self.number, self.n_tensor, self.arrived, self.sems = number, n_tensor, arrived, sems
        self.rank = lax.axis_index("tensor")
        self.size = arrived.shape[1]
        self.others = [
            (shift - 1, lax.rem(self.rank + shift, n_tensor)) for shift in range(1, n_tensor)
        ]

    def block(self, index):
        return pl.ds(pl.multiple_of(index * self.size, 16), self.size)

    def scatter(self, partial):
        self.partial = partial
        self.firsts = [
            send(
                partial.at[self.block(other)], self.arrived.at[place], self.sems,
                (2 * self.number, place), {"tensor": other},
            )
            for place, other in self.others
        ]

    def add(self, out, whole):
        for copy in self.firsts:
            copy.wait_recv()

        @pl.loop(0, self.size // STRIP)
        def _(index):
            low = pl.multiple_of(index * STRIP, STRIP)
            there = pl.ds(pl.multiple_of(self.rank * self.size + low, STRIP), STRIP)
            total = self.partial[there, :].astype(F32)
            for place, _ in self.others:
                total = total + self.arrived[place, pl.ds(low, STRIP), :].astype(F32)
            out[there if whole else pl.ds(low, STRIP), :] = total.astype(BF16)

        for copy in self.firsts:
            copy.wait_send()

    def gather(self, out):
        mine = out.at[self.block(self.rank)]
        self.seconds = [
            send(mine, mine, self.sems, (2 * self.number + 1, place), {"tensor": other})
            for place, other in self.others
        ]

    def finish(self):
        for copy in self.seconds:
            copy.wait()


def tensor_kernel(n_tensor, partial, out, arrived, sems):
    greet((), range(1, n_tensor), n_tensor)
    total = TensorSum(0, n_tensor, arrived, sems)
    total.scatter(partial)
    total.add(out, True)
    total.gather(out)
    total.finish()


def emit_kernel(*refs):
    count = (len(refs) - 16) // 3
    sources, refs = refs[: 3 + count], refs[3 + count :]
    outs, refs = refs[: 6 + count], refs[6 + count :]
    held, (turned_key, turned_value, in_sems, sems) = refs[: 3 + count], refs[3 + count :]
    loads = [load(far, here, in_sems.at[i]) for i, (far, here) in enumerate(zip(sources, held))]
    query, key, value, out, text_key, text_value = outs[:6]
    width = query.shape[1]
    copies = []

    def put(here, target):
        copies.append(load(here, target, sems.at[len(copies)]))

    for index in range(3, 3 + count):
        loads[index].wait()
        put(held[index], outs[3 + index])
    for index, first, second in ((0, query, value), (1, key, out)):
        loads[index].wait()
        put(held[index].at[:, :width], first)
        put(held[index].at[:, width:], second)
    loads[2].wait()
    turned_key[...] = jnp.transpose(held[2][:width, :])
    put(turned_key, text_key)
    turned_value[...] = jnp.transpose(held[2][width:, :])
    put(turned_value, text_value)
    wait_all(copies)


def exchange(body, outs, ins, scratch, collective, vmem=48):
    spaces = [space for _, space in outs]
    return pl.pallas_call(
        body,
        out_shape=[shape for shape, _ in outs],
        in_specs=[pl.BlockSpec(memory_space=space) for _, space in ins],
        out_specs=[pl.BlockSpec(memory_space=space) for space in spaces],
        scratch_shapes=scratch,
        compiler_params=pltpu.CompilerParams(
            collective_id=collective, has_side_effects=True, vmem_limit_bytes=vmem * 2**20
        ),
    )(*[array for array, _ in ins])


def project_kernel(
    tokens, member, gain, q_gain, k_gain, cosine, sine, mods, whole_a, whole_b,
    attn_in, query_raw, key_raw, query_rot, key_rot, value, mat_a, mat_b, mod, sems
):
    copies = [load(whole_a, mat_a, sems.at[0]), load(whole_b, mat_b, sems.at[1])]
    width = q_gain.shape[1]
    token_columns(member, mods, 0, mod)
    blocks = head_blocks(width)

    def step(at):
        x = tokens[at, :].astype(F32)
        normed = x * row_scale(x)
        attn_in[at, :] = (normed * gain[...] * (1.0 + mod[at, :].astype(F32))).astype(BF16)

    over_strips(tokens.shape[0], step)
    wait_all(copies)
    query_raw[...] = dot_nn(attn_in[...], mat_a[:, :width])
    key_raw[...] = dot_nn(attn_in[...], mat_b[:, :width])
    value[...] = dot_nn(attn_in[...], mat_a[:, width:]).astype(BF16)
    for raw, head_gain, out in ((query_raw, q_gain, query_rot), (key_raw, k_gain, key_rot)):
        normed = head_norm(raw[...], head_gain[...], blocks)
        out[...] = (normed * cosine[...] + swap_pairs(normed) * sine[...]).astype(BF16)


def text_kernel(
    live, source, captions, gain, whole_k, whole_v,
    text_raw, text_key, text_value, mat_k, mat_v, sems
):
    image = pl.program_id(0)

    @pl.when(image == 0)
    def _():
        wait_all([load(whole_k, mat_k, sems.at[0]), load(whole_v, mat_v, sems.at[1])])

    @pl.when(live[image] > 0)
    def _():
        raw = dot_nn(captions[0], mat_k[...])
        text_raw[0] = raw.astype(BF16)
        text_key[0] = head_norm(raw, gain[...], head_blocks(raw.shape[1])).astype(BF16)
        text_value[0] = dot_nn(captions[0], mat_v[...]).astype(BF16)


def stack_pair(values):
    lane = lax.broadcasted_iota(jnp.int32, (1, 2 * HEAD_DIM), 1)
    first = jnp.where(lane < HEAD_DIM, 1.0, 0.0).astype(values.dtype)
    second = jnp.where(lane < HEAD_DIM, 0.0, 1.0).astype(values.dtype)
    return jnp.concatenate([values * first, values * second], axis=0)


def unstack_pair(values):
    count = values.shape[0] // 2
    lane = lax.broadcasted_iota(jnp.int32, (count, 2 * HEAD_DIM), 1)
    return jnp.where(lane < HEAD_DIM, values[:count], values[count:])


def twice(values):
    return jnp.concatenate([values, values], axis=0)


def softmax(scores, allowed, rows_live):
    scores = jnp.where(allowed, scores, MASKED)
    expo = jnp.where(allowed, jnp.exp(scores - jnp.max(scores, axis=1, keepdims=True)), 0.0)
    total = jnp.sum(expo, axis=1, keepdims=True)
    if rows_live is not None:
        total = jnp.where(rows_live, total, 1.0)
    return expo * (1.0 / total)


def attend_kernel(
    micro, scale, live, text_len, query, key, value, text_key_far, text_value_far,
    self_id, self_row, segment, gate, whole_b, mixed, cross_out, whole,
    mat_b, text_key, text_value, self_out, sem, sems
):
    text_copies = [
        load(text_key_far, text_key, sems.at[0]), load(text_value_far, text_value, sems.at[1])
    ]
    copies = [load(whole_b, mat_b, sem)]
    rows, width = query.shape
    count = rows // micro
    slots = text_key.shape[0] // micro
    heads = width // HEAD_DIM
    cross_out[...] = jnp.zeros_like(cross_out)

    for batch in range(micro):
        at = slice(batch * count, (batch + 1) * count)
        allowed = twice(self_id[at, :]) == self_row[batch : batch + 1, :]
        for first in range(0, width, 2 * HEAD_DIM):
            lanes = slice(first, first + 2 * HEAD_DIM)
            scores = dot_nt(stack_pair(query[at, lanes]), key[at, lanes]) * scale
            probs = softmax(scores, allowed, None).astype(BF16)
            self_out[at, lanes] = unstack_pair(dot_nn(probs, value[at, lanes]))
    wait_all(text_copies)

    @pl.loop(0, micro * slots)
    def _(image):
        @pl.when(live[image] > 0)
        def _():
            at = pl.ds(pl.multiple_of((image // slots) * count, count), count)
            mine = twice(segment[at, :]) == lax.rem(image, slots)
            column = lax.broadcasted_iota(jnp.int32, (2 * count, TXT), 1)
            allowed = mine & (column < text_len[image])
            for first in range(0, width, 2 * HEAD_DIM):
                lanes = slice(first, first + 2 * HEAD_DIM)
                scores = dot_nt(stack_pair(query[at, lanes]), text_key[image, :, lanes]) * scale
                probs = softmax(scores, allowed, mine).astype(BF16)
                cross_out[at, lanes] += unstack_pair(dot_nn(probs, text_value[image, :, lanes]))

    mixed[...] = (self_out[...] + gate[...] * cross_out[...]).astype(BF16)
    wait_all(copies)
    whole[...] = dot_nt(mixed[...], mat_b[:, width:]).astype(BF16)


def feed_kernel(
    tokens, member, gain, cotangent, mods, attn_out, whole_f,
    hidden, ffn_in, inner, grad_gate, grad_up, grad_out, whole,
    mat, mod_1, mod_2, mod_3, sem
):
    copies = [load(whole_f, mat, sem)]
    units = inner.shape[1]
    mat_a, mat_b, mat_c = [mat.at[:, i * units : (i + 1) * units] for i in range(3)]
    token_columns(member, mods, 1, mod_1)
    token_columns(member, mods, 2, mod_2)
    token_columns(member, mods, 3, mod_3)

    def step(at):
        gate_attn = jnp.tanh(mod_1[at, :].astype(F32))
        state = tokens[at, :].astype(F32) + gate_attn * attn_out[at, :].astype(F32)
        hidden[at, :] = state
        normed = state * row_scale(state)
        ffn_in[at, :] = (normed * gain[...] * (1.0 + mod_2[at, :].astype(F32))).astype(BF16)
        gate_ffn = jnp.tanh(mod_3[at, :].astype(F32))
        grad_out[at, :] = (gate_ffn * cotangent[at, :].astype(F32)).astype(BF16)

    rows = tokens.shape[0]
    over_strips(rows, step)
    wait_all(copies)
    chunk = 256
    for first in range(0, units, chunk):
        span = slice(first, first + chunk)
        gate = dot_nn(ffn_in[...], mat_a[:, span])
        up = dot_nn(ffn_in[...], mat_b[:, span])
        grad_inner = dot_nn(grad_out[...], mat_c[:, span])
        turn = jax.nn.sigmoid(gate)
        active = gate * turn
        inner[:, span] = (active * up).astype(BF16)
        grad_up[:, span] = (grad_inner * active).astype(BF16)
        slope = turn * (1.0 + gate * (1.0 - turn))
        grad_gate[:, span] = (grad_inner * up * slope).astype(BF16)
    width = tokens.shape[1]
    for first in range(0, width, 512):
        span = slice(first, first + 512)
        whole[:, span] = (
            dot_nt(grad_gate[...], mat_a[span, :]) + dot_nt(grad_up[...], mat_b[span, :])
        ).astype(BF16)


def feed_grad_kernel(grad_out, inner, ffn_in, grad_gate, grad_up, total):
    units = inner.shape[1]
    step = 256
    for index, (left, right) in enumerate(
        ((ffn_in, grad_gate), (ffn_in, grad_up), (grad_out, inner))
    ):
        for first in range(0, units, step):
            out = slice(index * units + first, index * units + first + step)
            total[:, out] = dot_tn(left[...], right[:, first : first + step]).astype(BF16)


def feed_out_kernel(inner, whole_f, partial, mat, sem):
    units = inner.shape[1]
    copy = load(whole_f.at[:, 2 * units : 3 * units], mat, sem)
    copy.wait()
    for first in range(0, partial.shape[1], 512):
        span = slice(first, first + 512)
        partial[:, span] = dot_nt(inner[...], mat[span, :]).astype(BF16)


def modulate_back(values, gain, shift, grad):
    scale = row_scale(values)
    normed = values * scale
    inner = grad * gain * (1.0 + shift)
    mean = jnp.mean(inner * normed, axis=1, keepdims=True)
    return scale * (inner - normed * mean), grad * normed


def mixed_grad_kernel(
    hidden, member, gain, cotangent, mods, grad_in, whole_b,
    grad_hidden, grad_out, grad_mixed, mat_b, mod_1, mod_2, sem
):
    copies = [load(whole_b, mat_b, sem)]
    token_columns(member, mods, 1, mod_1)
    token_columns(member, mods, 2, mod_2)

    def step(at):
        back, _ = modulate_back(
            hidden[at, :], gain[...], mod_2[at, :].astype(F32), grad_in[at, :].astype(F32)
        )
        total = cotangent[at, :].astype(F32) + back
        grad_hidden[at, :] = total
        grad_out[at, :] = (jnp.tanh(mod_1[at, :].astype(F32)) * total).astype(BF16)

    over_strips(hidden.shape[0], step)
    wait_all(copies)
    width = grad_mixed.shape[1]
    grad_mixed[...] = dot_nn(grad_out[...], mat_b[:, width:])


def feed_exchange_kernel(
    n_tensor, tokens, member, gain, cotangent, mods, attn_out, whole_f, whole_ko,
    hidden, grad_hidden, grad_attn_out, grad_mixed, result_rows, gate_part, ffn_mod, gain_sum, *rest
):
    outs, rest = rest[:3], rest[3:]
    (
        ffn_in, inner, grad_gate, grad_up, grad_out, ffn_part, out_part,
        mat, mod_1, mod_2, mod_3, grad_in, ffn_rows, wide_grad, rows_grad, *rest
    ) = rest
    totals, rest = rest[:3], rest[3:]
    buffers, (arrived_1, arrived_2, sem, mat_sem, sems, tensor_sems) = rest[:15], rest[15:]
    announce((PAIR, ALONG_X, ALONG_Y), range(1, n_tensor), n_tensor)
    feed_kernel(
        tokens, member, gain, cotangent, mods, attn_out, whole_f,
        hidden, ffn_in, inner, grad_gate, grad_up, grad_out, ffn_part,
        mat, mod_1, mod_2, mod_3, sem,
    )
    pl.semaphore_wait(pltpu.get_barrier_semaphore(), 3 + n_tensor - 1)
    sum_in = TensorSum(0, n_tensor, arrived_1, tensor_sems)
    sum_in.scatter(ffn_part)
    size = outs[0].shape[0]
    reduces, firsts = [], []
    for number, (left, right) in enumerate(
        ((ffn_in, grad_gate), (ffn_in, grad_up), (grad_out, inner))
    ):
        total = totals[number]
        for first in range(0, total.shape[1], 256):
            span = slice(first, first + 256)
            total[:, span] = dot_tn(left[...], right[:, span]).astype(BF16)
        reduce = Reduce(
            number, piece_reader(total, size), outs[number],
            *buffers[5 * number : 5 * number + 5], sems,
        )
        reduces.append(reduce)
        firsts.append(reduce_firsts(reduce, total, size))
    units = inner.shape[1]
    for first in range(0, out_part.shape[1], 512):
        span = slice(first, first + 512)
        out_part[:, span] = dot_nt(inner[...], mat[span, 2 * units :]).astype(BF16)
    sum_out = TensorSum(1, n_tensor, arrived_2, tensor_sems)
    for piece in (3, 2, 1, 0):
        for number in range(3):
            reduces[number].second(piece, firsts[number][piece])
    sum_in.add(grad_in, True)
    sum_in.gather(grad_in)
    for reduce in reduces:
        reduce.third()
    sum_in.finish()
    sum_out.scatter(out_part)
    head_width = grad_mixed.shape[1]
    copy = load(whole_ko.at[:, head_width:], mat.at[:, :head_width], mat_sem)

    def step(at):
        back, _ = modulate_back(
            hidden[at, :], gain[...], mod_2[at, :].astype(F32), grad_in[at, :].astype(F32)
        )
        total = cotangent[at, :].astype(F32) + back
        grad_hidden[at, :] = total
        grad_attn_out[at, :] = (jnp.tanh(mod_1[at, :].astype(F32)) * total).astype(BF16)

    over_strips(hidden.shape[0], step)
    copy.wait()
    grad_mixed[...] = dot_nn(grad_attn_out[...], mat[:, :head_width])
    gain_sum[...] = jnp.zeros_like(gain_sum)

    def scale_step(at):
        state = hidden[at, :]
        product = grad_in[at, :].astype(F32) * state * row_scale(state)
        gain_sum[...] += jnp.sum(
            product * (1.0 + mod_2[at, :].astype(F32)), axis=0, keepdims=True
        )
        wide_grad[at, :] = product * gain[...]

    over_strips(hidden.shape[0], scale_step)
    ffn_mod[...] = segment_sum(member[...], wide_grad[...])
    for reduce in reduces:
        reduce.last()
    sum_out.add(ffn_rows, False)
    first = sum_out.rank * sum_out.size

    def row_step(here):
        at = pl.ds(pl.multiple_of(first + here.start, STRIP), STRIP)
        gate = jnp.tanh(mod_3[at, :].astype(F32))
        out = ffn_rows[here, :].astype(F32)
        result_rows[here, :] = (hidden[at, :] + gate * out).astype(BF16)
        rows_grad[here, :] = cotangent[at, :].astype(F32) * out * (1.0 - gate * gate)

    over_strips(sum_out.size, row_step)
    gate_part[...] = segment_sum(member[sum_out.block(sum_out.rank), :], rows_grad[...]).astype(BF16)


def attend_back_kernel(
    micro, scale, live, text_len, grad_mixed, cross_out, query, key, value, text_key_far,
    text_value_far, text_raw_far, query_raw, key_raw, q_gain, k_gain, t_gain, cosine, sine, self_id, self_row, segment,
    gate, grad_query_b, grad_key_b, grad_value_b, grad_text, gain_sums,
    grad_query, grad_key, grad_cross, grad_turned, gain_turned, text_key, text_value, text_raw, sems,
    *held
):
    held, held_sems = held[:-1], held[-1]
    early = (grad_mixed, cross_out, query, key, value, query_raw, key_raw, cosine, sine)
    copies = [load(far, here, held_sems.at[i]) for i, (far, here) in enumerate(zip(early, held))]
    grad_mixed, cross_out, query, key, value, query_raw, key_raw, cosine, sine = held
    text_copies = [
        load(far, here, sems.at[index])
        for index, (far, here) in enumerate(
            ((text_key_far, text_key), (text_value_far, text_value), (text_raw_far, text_raw))
        )
    ]
    rows, width = query.shape
    count = rows // micro
    slots = text_key.shape[0] // micro
    heads = width // HEAD_DIM
    blocks = head_blocks(width)
    wait_all(copies)
    gate_sum = jnp.sum(grad_mixed[...] * cross_out[...], axis=0, keepdims=True)
    gain_sums[...] = jnp.zeros_like(gain_sums)
    gain_sums[3:4, :] = gate_sum * (1.0 - gate[...] * gate[...])
    grad_cross[...] = (gate[...] * grad_mixed[...]).astype(BF16)
    gain_turned[...] = jnp.zeros_like(gain_turned)
    gain_column = jnp.transpose(jnp.broadcast_to(t_gain[...], (8, width)))[:, :1]
    for batch in range(micro):
        at = slice(batch * count, (batch + 1) * count)
        allowed = twice(self_id[at, :]) == self_row[batch : batch + 1, :]
        for first in range(0, width, 2 * HEAD_DIM):
            lanes = slice(first, first + 2 * HEAD_DIM)
            q, k = stack_pair(query[at, lanes]), key[at, lanes]
            grad = stack_pair(grad_mixed[at, lanes].astype(BF16))
            probs = softmax(dot_nt(q, k) * scale, allowed, None)
            grad_probs = dot_nt(grad, value[at, lanes])
            mean = jnp.sum(probs * grad_probs, axis=1, keepdims=True)
            scaled = (probs * (grad_probs - mean) * scale).astype(BF16)
            grad_query[at, lanes] = unstack_pair(dot_nn(scaled, k))
            grad_key[at, lanes] = dot_tn(scaled, q)
            grad_value_b[at, lanes] = dot_tn(probs.astype(BF16), grad).astype(BF16)

    wait_all(text_copies)

    @pl.loop(0, micro * slots)
    def _(image):
        @pl.when(live[image] == 0)
        def _():
            grad_text[:, pl.ds(pl.multiple_of(image * TXT, TXT), TXT)] = jnp.zeros(
                (2 * width, TXT), BF16
            )

        @pl.when(live[image] > 0)
        def _():
            at = pl.ds(pl.multiple_of((image // slots) * count, count), count)
            tokens = pl.ds(pl.multiple_of(image * TXT, TXT), TXT)
            mine = twice(segment[at, :]) == lax.rem(image, slots)
            column = lax.broadcasted_iota(jnp.int32, (2 * count, TXT), 1)
            allowed = mine & (column < text_len[image])
            for first in range(0, width, 2 * HEAD_DIM):
                lanes = slice(first, first + 2 * HEAD_DIM)
                q, k = stack_pair(query[at, lanes]), text_key[image, :, lanes]
                grad = stack_pair(grad_cross[at, lanes])
                probs = softmax(dot_nt(q, k) * scale, allowed, mine)
                grad_probs = dot_nt(grad, text_value[image, :, lanes])
                mean = jnp.sum(probs * grad_probs, axis=1, keepdims=True)
                scaled = (probs * (grad_probs - mean) * scale).astype(BF16)
                grad_query[at, lanes] += unstack_pair(dot_nn(scaled, k))
                grad_turned[lanes, :] = dot_tn(q, scaled)
                grad_text[width + first : width + first + 2 * HEAD_DIM, tokens] = dot_tn(
                    grad, probs.astype(BF16)
                ).astype(BF16)
            by_head = (heads, HEAD_DIM, TXT)
            raw = jnp.transpose(text_raw[image].astype(F32)).reshape(by_head)
            norm = lax.rsqrt(jnp.mean(raw * raw, axis=1, keepdims=True) + EPSILON)
            normed = raw * norm
            upper = grad_turned[...].reshape(by_head)
            gain_turned[...] += (upper * normed).reshape(width, TXT)
            inner = upper * gain_column.reshape(heads, HEAD_DIM, 1)
            mean = jnp.mean(inner * normed, axis=1, keepdims=True)
            back = norm * (inner - normed * mean)
            grad_text[:width, tokens] = back.reshape(width, TXT).astype(BF16)

    for index, (grad, raw, gain, out) in enumerate(
        (
            (grad_query, query_raw, q_gain, grad_query_b),
            (grad_key, key_raw, k_gain, grad_key_b),
        )
    ):
        turned = grad[...] * cosine[...] + swap_pairs(grad[...] * sine[...])
        back, gain_sum = head_norm_back(raw[...], gain[...], turned, blocks)
        out[...] = back.astype(BF16)
        gain_sums[index : index + 1, :] = gain_sum
    text_sums = jnp.sum(gain_turned[...], axis=1, keepdims=True)
    gain_sums[2:3, :] = jnp.transpose(jnp.broadcast_to(text_sums, (width, 128)))[:1, :]


def attn_grad_kernel(
    attn_in, grad_query, grad_key, grad_value, grad_out, mixed, whole_a, whole_b,
    total_a, total_b, whole, mat_a, mat_b, pair, sems
):
    copies = [load(whole_a, mat_a, sems.at[0]), load(whole_b, mat_b, sems.at[1])]
    width = grad_query.shape[1]
    pair[:, :width] = grad_query[...]
    pair[:, width:] = grad_value[...]
    wait_all(copies)
    for first in range(0, whole.shape[1], 512):
        span = slice(first, first + 512)
        whole[:, span] = (
            dot_nt(pair[...], mat_a[span, :]) + dot_nt(grad_key[...], mat_b[span, :width])
        ).astype(BF16)
    for first in range(0, 2 * width, 256):
        span = slice(first, first + 256)
        total_a[:, span] = dot_tn(attn_in[...], pair[:, span]).astype(BF16)
    total_b[:, :width] = dot_tn(attn_in[...], grad_key[...]).astype(BF16)
    total_b[:, width:] = dot_tn(grad_out[...], mixed[...]).astype(BF16)


def last_exchange_kernel(
    n_tensor, captions, grad_text_far, qv_far, ko_far, tokens_far, hidden_far, attn_far, attn_part,
    member, attn_gain, mods, cond_act, gain_sums, result_rows, gate_part, ffn_mod, ffn_gain_sum,
    out_qv, out_ko, out_text, result, grad_tokens, grad_adaln,
    own_attn, own_ffn, own_query, own_key, own_text, own_gate, *rest
):
    buffers, rest = rest[:15], rest[15:]
    (
        text_total, block, grad_in, gate_parts, other_mod, grad_mod, arrived, mod_a, mod_b, work_grad,
        sums, attn_sum, all_mod, all_sums, all_attn, heads_turned,
        block_sems, sems, tensor_sems, small_sems,
        grad_text, total_qv, total_ko, tokens, grad_hidden, attn_out, load_sems,
    ) = rest
    masks = range(1, 8)
    announce(masks, range(1, n_tensor), n_tensor)
    loads = [
        load(far, here, load_sems.at[i])
        for i, (far, here) in enumerate(
            (
                (grad_text_far, grad_text), (qv_far, total_qv), (ko_far, total_ko),
                (tokens_far, tokens), (hidden_far, grad_hidden), (attn_far, attn_out),
            )
        )
    ]
    pl.semaphore_wait(pltpu.get_barrier_semaphore(), 7 + n_tensor - 1)
    sum_in = TensorSum(0, n_tensor, arrived, tensor_sems)
    sum_in.scatter(attn_part)
    head_width = gain_sums.shape[1]
    sums[0:1, :] = ffn_gain_sum[...]
    for row in range(4):
        sums[1:2, row * head_width : (row + 1) * head_width] = gain_sums[row : row + 1, :]
    rank = lax.axis_index("dp")
    copies = [
        send(sums, all_sums.at[mask], small_sems, (1, mask), {"dp": partner(mask)})
        for mask in masks
    ]
    sum_out = TensorSum(1, n_tensor, arrived, tensor_sems)
    result[sum_out.block(sum_out.rank), :] = result_rows[...]
    gate_parts[0] = gate_part[...]
    gate_copies = [
        send(gate_part, gate_parts.at[place + 1], tensor_sems, (2, place), {"tensor": other})
        for place, other in sum_in.others
    ]
    size = out_qv.shape[0]
    depth = out_text.shape[1]
    reduces, firsts = [], []
    for number, (far, total, out) in enumerate(
        ((qv_far, total_qv, out_qv), (ko_far, total_ko, out_ko))
    ):
        reduce = Reduce(
            number, piece_reader(total, size), out, *buffers[5 * number : 5 * number + 5], sems
        )
        reduces.append(reduce)
        firsts.append(reduce_firsts(reduce, far, size))

    def fetch(mask, slot):
        columns = pl.ds(pl.multiple_of(partner(mask) * depth, 128), depth)
        return pltpu.make_async_copy(
            captions.at[:, columns], block.at[slot], block_sems.at[slot]
        )

    def mask_at(place):
        return 7 - 2 * place + 7 * (place // 4)

    fetch(7, 0).start()

    def read_text(piece, low):
        return text_total[2 * piece, pl.ds(low, REDUCE_STRIP), :].astype(F32)

    text = Reduce(2, read_text, out_text, *buffers[10:], sems)

    def work(low, high):
        @pl.loop(low, high)
        def _(place):
            slot = lax.rem(place, 2)
            mask = mask_at(place)

            @pl.when(place < 7)
            def _():
                fetch(mask_at(place + 1), 1 - slot).start()

            fetch(mask, slot).wait()
            for first in range(0, grad_text.shape[0], 256):
                span = slice(first, first + 256)
                text_total[mask, span, :] = dot_nn(grad_text[span, :], block[slot]).astype(BF16)

    wait_all(loads[:3])
    work(0, 2)
    for piece in (3, 2):
        text.first(piece, text_total.at[2 * piece + 1]).start()
    for piece in (3, 2, 1, 0):
        for number in range(2):
            reduces[number].second(piece, firsts[number][piece])
    work(2, 3)
    sum_in.add(grad_in, True)
    sum_in.gather(grad_in)
    work(3, 4)
    text_firsts = {}
    for piece in (3, 2, 1, 0):
        text_firsts[piece] = text.first(piece, text_total.at[2 * piece + 1])
    text_firsts[1].start()
    text_firsts[0].start()
    for reduce in reduces:
        reduce.third()
    work(4, 5)
    text.second(3, text_firsts[3])
    work(5, 6)
    text.second(2, text_firsts[2])
    work(6, 7)
    text.second(1, text_firsts[1])
    work(7, 8)
    text.second(0, text_firsts[0])
    text.third()
    for copy in gate_copies:
        copy.wait()
    gate_mod = gate_parts[0].astype(F32)
    for place, _ in sum_in.others:
        gate_mod = gate_mod + gate_parts[place + 1].astype(F32)
    other_mod[...] = jnp.where(sum_in.rank == 3, gate_mod, ffn_mod[...])
    wait_all(loads[3:])
    sum_in.finish()
    sum_out.gather(result)
    input_kernel(
        tokens, member, attn_gain, grad_hidden, other_mod, mods, grad_in, attn_out,
        grad_tokens, grad_mod, attn_sum, mod_a, mod_b, work_grad,
    )
    for mask in masks:
        device = {"dp": partner(mask)}
        copies.append(send(grad_mod, all_mod.at[rank], small_sems, (0, mask), device))
        copies.append(send(attn_sum, all_attn.at[mask], small_sems, (2, mask), device))
    all_mod[rank] = grad_mod[...]
    for reduce in reduces:
        reduce.last()
    text.last()
    for copy in copies:
        copy.wait_recv()
    added, attn_added = sums[...], attn_sum[...]
    for mask in masks:
        added = added + all_sums[mask]
        attn_added = attn_added + all_attn[mask]
    grad_adaln[...] = dot_tn(cond_act[...], all_mod[...].reshape(8 * 16, all_mod.shape[2]))
    gain_size = own_attn.shape[1]
    for whole, out in ((attn_added, own_attn), (added[0:1, :], own_ffn)):
        out[...] = whole[:, :gain_size]
        for index in range(1, 8):
            part = whole[:, index * gain_size : (index + 1) * gain_size]
            out[...] = jnp.where(rank == index, part, out[...])
    heads = own_query.shape[1]
    for place, out in enumerate((own_query, own_key, own_text)):
        for head in range(heads):
            first = place * head_width + head * HEAD_DIM
            heads_turned[head : head + 1, :HEAD_DIM] = added[1:2, first : first + HEAD_DIM]
        turned = jnp.transpose(heads_turned[...])
        part = out.shape[0]
        out[...] = turned[:part, :heads]
        for index in range(1, 8):
            here = turned[index * part : (index + 1) * part, :heads]
            out[...] = jnp.where(rank == index, here, out[...])
    for head in range(heads):
        first = 3 * head_width + head * HEAD_DIM
        own_gate[:, head : head + 1] = jnp.sum(
            added[1:2, first : first + HEAD_DIM], axis=1, keepdims=True
        )
    for copy in copies:
        copy.wait_send()
    sum_out.finish()


def segment_sum(member, values):
    high = values.astype(BF16)
    rest = values - high.astype(F32)
    middle = rest.astype(BF16)
    low = (rest - middle.astype(F32)).astype(BF16)
    return dot_tn(member, high) + dot_tn(member, middle) + dot_tn(member, low)


def output_kernel(
    hidden, member, gain, cotangent, mods, ffn_out, grad_in,
    result, grad_mod, grad_gain, mod_2, mod_3, grad
):
    token_columns(member, mods, 2, mod_2)
    token_columns(member, mods, 3, mod_3)
    rank = lax.axis_index("tensor")
    grad_gain[...] = jnp.zeros_like(grad_gain)

    def step(at):
        state = hidden[at, :]
        gate = jnp.tanh(mod_3[at, :].astype(F32))
        out = ffn_out[at, :].astype(F32)
        result[at, :] = (state + gate * out).astype(BF16)
        up = grad_in[at, :].astype(F32)
        product = up * state * row_scale(state)
        grad_gain[...] += jnp.sum(
            product * (1.0 + mod_2[at, :].astype(F32)), axis=0, keepdims=True
        )
        grad_gate = cotangent[at, :].astype(F32) * out * (1.0 - gate * gate)
        grad[at, :] = jnp.where(rank == 2, product * gain[...], grad_gate)

    over_strips(hidden.shape[0], step)
    grad_mod[...] = segment_sum(member[...], grad[...])


def input_kernel(
    tokens, member, gain, grad_hidden, other_mod, mods, grad_in, attn_out,
    grad_tokens, grad_mod, grad_gain, mod_0, mod_1, grad
):
    token_columns(member, mods, 0, mod_0)
    token_columns(member, mods, 1, mod_1)
    rank = lax.axis_index("tensor")
    grad_gain[...] = jnp.zeros_like(grad_gain)

    def step(at):
        shift = mod_0[at, :].astype(F32)
        upper = grad_hidden[at, :]
        back, product = modulate_back(
            tokens[at, :].astype(F32), gain[...], shift, grad_in[at, :].astype(F32)
        )
        grad_tokens[at, :] = (upper + back).astype(BF16)
        grad_gain[...] += jnp.sum(product * (1.0 + shift), axis=0, keepdims=True)
        gate = jnp.tanh(mod_1[at, :].astype(F32))
        grad_gate = upper * attn_out[at, :].astype(F32) * (1.0 - gate * gate)
        grad[at, :] = jnp.where(rank == 0, product * gain[...], grad_gate)

    over_strips(tokens.shape[0], step)
    own = segment_sum(member[...], grad[...])
    grad_mod[...] = jnp.where(rank < 2, own, other_mod[...]).astype(BF16)


def shards(
    n_dp,
    n_tensor,
    tokens,
    context,
    captions,
    shapes,
    text_len,
    w_query,
    w_key,
    w_value,
    w_out,
    w_text_key,
    w_text_value,
    w_gate,
    w_up,
    w_down,
    w_adaln,
    gain_attn,
    gain_ffn,
    gain_query,
    gain_key,
    gain_text,
    cross_gate,
    cotangent,
):
    parts = 8 if n_dp == 8 else 1
    micro, count, width = tokens.shape
    slots = shapes.shape[1]
    rows = micro * count
    images = micro * slots
    heads = w_query.shape[1] // HEAD_DIM
    local = heads * HEAD_DIM
    units = w_gate.shape[1]
    scale = HEAD_DIM ** (-0.5)
    dp_rank = lax.axis_index("dp")
    padded = 16
    vmem, smem, anywhere = pltpu.VMEM, pltpu.SMEM, pl.ANY
    dma = pltpu.SemaphoreType.DMA

    def inside(*arrays):
        return [(array, vmem) for array in arrays]

    def scalars(*arrays):
        return [(array, smem) for array in arrays]

    def outside(*arrays):
        return [(array, anywhere) for array in arrays]

    def after(values, earlier):
        return lax.optimization_barrier((list(values), list(earlier)))[0]

    def gathered(shard):
        return lax.all_gather(shard, "dp", axis=0, tiled=True)

    def scattered(whole):
        return lax.psum_scatter(whole, "dp", scatter_dimension=0, tiled=True).astype(F32)

    part_rows = rows // n_tensor
    arrived = vmem((n_tensor - 1, part_rows, width), BF16)

    def tensor_sum(partial):
        (out,) = exchange(
            functools.partial(tensor_kernel, n_tensor),
            [(struct((rows, width)), vmem)],
            inside(partial),
            [arrived, dma((2, 2, n_tensor - 1))],
            1,
        )
        return out

    gain_list = (gain_attn, gain_ffn, gain_query, gain_key, gain_text)
    cond_rows, span = w_adaln.shape
    shard_qv = jnp.concatenate([w_query, w_value], axis=1)
    shard_ko = jnp.concatenate([w_key, w_out], axis=1)
    shard_f = jnp.concatenate([w_gate, w_up, w_down], axis=1)
    if parts == 1:
        whole_tk, whole_tv = gathered(w_text_key), gathered(w_text_value)
        whole_qv, whole_ko = gathered(shard_qv), gathered(shard_ko)
        gains = [lax.all_gather(gain.astype(F32), "dp", axis=0, tiled=True) for gain in gain_list]
        attn_gain, ffn_gain = [gain.reshape(1, width) for gain in gains[:2]]
        query_gain, key_gain, text_gain = [gain.T.reshape(1, local) for gain in gains[2:]]
        context_all = gathered(context.reshape(images, -1))
        cond_cols = lax.dynamic_slice_in_dim(context_all, dp_rank * cond_rows, cond_rows, 1)
        cond_act = jax.nn.silu(cond_cols.astype(F32)).astype(BF16)
        mod_part = scattered(dot_nn(cond_act, w_adaln)).astype(BF16)
        mods = lax.all_gather(mod_part, "tensor", axis=0)
        mods = jnp.pad(mods, ((0, 0), (0, padded - images), (0, 0)))
    else:
        text_raw, text_key, text_value, whole_qv, whole_ko, cond_act, mods, *gains = exchange(
            functools.partial(gather_kernel, n_tensor),
            [(struct((images, TXT, local)), anywhere)] * 3
            + [(struct((width, 2 * local)), anywhere)] * 2
            + [
                (struct((parts * padded, cond_rows)), vmem),
                (struct((n_tensor, padded, span)), vmem),
            ]
            + [(struct((1, width), F32), vmem)] * 2
            + [(struct((1, local), F32), vmem)] * 3,
            outside(w_text_key, w_text_value, shard_qv, shard_ko)
            + inside(
                context, gain_attn[None], gain_ffn[None], gain_query, gain_key, gain_text, w_adaln
            )
            + outside(captions.reshape(images, TXT, DT)),
            [
                vmem((parts, 2 * padded, cond_rows), BF16),
                vmem((parts, 2 * padded, cond_rows), BF16),
                vmem((parts, padded, span), BF16),
                vmem((parts, padded, span), BF16),
                vmem((DT, local), BF16),
                vmem((DT, local), BF16),
                vmem((local, local), BF16),
                vmem((2, TXT, DT), BF16),
                vmem((2, 3, TXT, local), BF16),
                dma((2,)),
                dma((2, 3)),
                dma((4,)),
                dma((2, 4, 9)),
                dma((2, 8)),
                dma((2, 8)),
                dma((2, n_tensor)),
            ],
            2,
        )
        attn_gain, ffn_gain, query_gain, key_gain, text_gain = gains
        (shard_f,) = after([shard_f], [mods])
    whole_f = gathered(shard_f)
    layouts = [image_layout(shapes[i], count) for i in range(micro)]
    member, segment, inside_any, row_pos, col_pos = [
        jnp.stack([layout[j] for layout in layouts]) for j in range(5)
    ]
    cosine, sine = rope_tables(row_pos.reshape(rows), col_pos.reshape(rows))
    cosine = jnp.tile(jnp.stack([cosine, cosine], axis=2).reshape(rows, HEAD_DIM), (1, heads))
    sine = jnp.tile(jnp.stack([-sine, sine], axis=2).reshape(rows, HEAD_DIM), (1, heads))
    which = jnp.arange(micro, dtype=jnp.int32)
    member = jnp.where(
        (which[:, None] == which[None, :])[:, None, :, None], member[:, :, None, :], 0.0
    )
    member = jnp.pad(member.reshape(rows, images), ((0, 0), (0, padded - images))).astype(BF16)
    self_row = jnp.where(inside_any > 0, segment, slots)
    self_id = self_row.reshape(rows, 1)
    segment = segment.reshape(rows, 1)
    lens = text_len.reshape(images)
    used = shapes[:, :, 0] * (shapes[:, :, 1] + 1) > 0
    used = used | (jnp.arange(slots)[None, :] == 0)
    live = used.reshape(images).astype(jnp.int32)
    at = jnp.arange(images, dtype=jnp.int32)
    source = lax.cummax(jnp.where(live > 0, at, 0))
    gate = jnp.repeat(jnp.tanh(cross_gate.astype(F32)), HEAD_DIM)[None, :]
    token_rows = tokens.reshape(rows, width)
    grad_y = cotangent.reshape(rows, width)
    caption_images = captions.reshape(images, TXT, DT)

    attn_in, query_raw, key_raw, query_rot, key_rot, value = run(
        project_kernel,
        [struct((rows, width))]
        + [struct((rows, local), F32)] * 2
        + [struct((rows, local))] * 3,
        inside(token_rows, member, attn_gain, query_gain, key_gain, cosine, sine, mods)
        + outside(whole_qv, whole_ko),
        [
            vmem((width, 2 * local), BF16),
            vmem((width, 2 * local), BF16),
            vmem((rows, width), BF16),
            dma((2,)),
        ],
        flops=6 * rows * width * local,
        traffic=10 * 2**20,
    )

    if parts == 1:
        text_raw, text_key, text_value = pl.pallas_call(
            text_kernel,
            out_shape=[struct((images, TXT, local))] * 3,
            grid_spec=pltpu.PrefetchScalarGridSpec(
                num_scalar_prefetch=2,
                grid=(images,),
                in_specs=[
                    pl.BlockSpec((1, TXT, DT), lambda i, live, source: (source[i], 0, 0)),
                    pl.BlockSpec((1, local), lambda i, live, source: (0, 0)),
                ]
                + [pl.BlockSpec(memory_space=anywhere)] * 2,
                out_specs=[pl.BlockSpec((1, TXT, local), lambda i, live, source: (i, 0, 0))] * 3,
                scratch_shapes=[vmem((DT, local), BF16), vmem((DT, local), BF16), dma((2,))],
            ),
            compiler_params=pltpu.CompilerParams(vmem_limit_bytes=40 * 2**20),
            cost_estimate=pl.CostEstimate(
                flops=2 * images * TXT * DT * local, bytes_accessed=20 * 2**20, transcendentals=0
            ),
        )(live, source, caption_images, text_gain, whole_tk, whole_tv)

    wide = vmem((rows, width), BF16)
    mixed, cross_out, attn_part = run(
        functools.partial(attend_kernel, micro, scale),
        [struct((rows, local)), struct((rows, local), F32), struct((rows, width))],
        scalars(live, lens)
        + inside(query_rot, key_rot, value)
        + outside(text_key, text_value)
        + inside(self_id, self_row, segment, gate)
        + outside(whole_ko),
        [
            vmem((width, 2 * local), BF16),
            vmem((images, TXT, local), BF16),
            vmem((images, TXT, local), BF16),
            vmem((rows, local), F32),
            dma,
            dma((2,)),
        ],
        flops=2 * 2**30,
        traffic=12 * 2**20,
    )
    attn_out = tensor_sum(attn_part)

    size = width // parts
    if parts == 1:
        mat = vmem((width, 3 * units), BF16)
        hidden, ffn_in, inner, grad_gate, grad_up, grad_ffn_out, ffn_part = run(
            feed_kernel,
            [struct((rows, width), F32), struct((rows, width))]
            + [struct((rows, units))] * 3
            + [struct((rows, width))] * 2,
            inside(token_rows, member, ffn_gain, grad_y, mods, attn_out) + outside(whole_f),
            [mat, wide, wide, wide, dma],
            flops=10 * rows * width * units,
            traffic=20 * 2**20,
        )
        (grad_f,) = run(
            feed_grad_kernel,
            [struct((width, 3 * units))],
            inside(grad_ffn_out, inner, ffn_in, grad_gate, grad_up),
            flops=6 * rows * width * units,
            traffic=12 * 2**20,
        )
        (ffn_part,) = after([ffn_part], [grad_f])
        grad_ffn_in = tensor_sum(ffn_part)
        grad_f = scattered(grad_f)
        (ffn_out_part,) = run(
            feed_out_kernel,
            [struct((rows, width))],
            inside(inner) + outside(whole_f),
            [vmem((width, units), BF16), dma],
            flops=2 * rows * width * units,
            traffic=5 * 2**20,
        )
        ffn_out = lax.psum(ffn_out_part, "tensor")

        grad_hidden, grad_attn_out, grad_mixed = run(
            mixed_grad_kernel,
            [struct((rows, width), F32), struct((rows, width)), struct((rows, local), F32)],
            inside(hidden, member, ffn_gain, grad_y, mods, grad_ffn_in) + outside(whole_ko),
            [vmem((width, 2 * local), BF16), wide, wide, dma],
            flops=2 * rows * width * local,
            traffic=8 * 2**20,
        )
    else:
        (
            hidden, grad_hidden, grad_attn_out, grad_mixed, result_rows, gate_part, ffn_mod,
            ffn_gain_sum, *grad_f
        ) = exchange(
            functools.partial(feed_exchange_kernel, n_tensor),
            [
                (struct((rows, width), F32), vmem),
                (struct((rows, width), F32), vmem),
                (struct((rows, width)), vmem),
                (struct((rows, local), F32), vmem),
                (struct((part_rows, width)), vmem),
                (struct((padded, width)), vmem),
                (struct((padded, width), F32), vmem),
                (struct((1, width), F32), vmem),
            ]
            + [(struct((size, units), F32), vmem)] * 3,
            inside(token_rows, member, ffn_gain, grad_y, mods, attn_out)
            + outside(whole_f, whole_ko),
            [wide]
            + [vmem((rows, units), BF16)] * 3
            + [wide] * 3
            + [vmem((width, 3 * units), BF16), wide, wide, wide, wide]
            + [
                vmem((part_rows, width), BF16),
                vmem((rows, width), F32),
                vmem((part_rows, width), F32),
            ]
            + [vmem((width, units), BF16)] * 3
            + reduce_scratch(size, units) * 3
            + [arrived, arrived, dma, dma, dma((2, 3, 10)), dma((2, 4, n_tensor - 1))],
            5,
            vmem=60,
        )

    tile = struct((rows, local))
    grad_query_b, grad_key_b, grad_value_b, grad_text_all, gain_sums = run(
        functools.partial(attend_back_kernel, micro, scale),
        [tile, tile, tile, struct((2 * local, images * TXT)), struct((8, local), F32)],
        scalars(live, lens)
        + outside(
            grad_mixed, cross_out, query_rot, key_rot, value, text_key, text_value, text_raw,
            query_raw, key_raw,
        )
        + inside(query_gain, key_gain, text_gain)
        + outside(cosine, sine)
        + inside(self_id, self_row, segment, gate),
        [
            vmem((rows, local), F32),
            vmem((rows, local), F32),
            vmem((rows, local), BF16),
            vmem((local, TXT), F32),
            vmem((local, TXT), F32),
            vmem((images, TXT, local), BF16),
            vmem((images, TXT, local), BF16),
            vmem((images, TXT, local), BF16),
            dma((3,)),
        ]
        + [vmem((rows, local), F32)] * 2
        + [vmem((rows, local), BF16)] * 3
        + [vmem((rows, local), F32)] * 4
        + [
            dma((9,)),
        ],
        flops=4 * 2**30,
        traffic=15 * 2**20,
        vmem=62,
    )

    total_qv, total_ko, attn_in_part = run(
        attn_grad_kernel,
        [struct((width, 2 * local))] * 2 + [struct((rows, width))],
        inside(attn_in, grad_query_b, grad_key_b, grad_value_b, grad_attn_out, mixed)
        + outside(whole_qv, whole_ko),
        [
            vmem((width, 2 * local), BF16),
            vmem((width, 2 * local), BF16),
            vmem((rows, 2 * local), BF16),
            dma((2,)),
        ],
        flops=14 * rows * width * local,
        traffic=15 * 2**20,
        vmem=62,
    )
    depth = DT // parts
    caption_rows = captions.reshape(images * TXT, DT)
    if parts == 1:
        grad_attn_in = lax.psum(attn_in_part, "tensor")
        grad_text = dot_nn(grad_text_all, caption_rows)
        wholes = (total_qv, total_ko, grad_text.T)
        grad_qv, grad_ko, grad_text = [scattered(whole.astype(F32)) for whole in wholes]
        grad_query, grad_value = grad_qv[:, :local], grad_qv[:, local:]
        grad_key, grad_out = grad_ko[:, :local], grad_ko[:, local:]
        grad_tk, grad_tv = grad_text[:, :local], grad_text[:, local:]
        grad_f = [grad_f[:, i * units : (i + 1) * units] for i in range(3)]
        result, ffn_mod, ffn_gain_sum = run(
            output_kernel,
            [struct((rows, width)), struct((padded, width), F32), struct((1, width), F32)],
            inside(hidden, member, ffn_gain, grad_y, mods, ffn_out, grad_ffn_in),
            [wide, wide, vmem((rows, width), F32)],
        )
        grad_tokens, grad_mod, attn_gain_sum = run(
            input_kernel,
            [struct((rows, width)), struct((padded, width)), struct((1, width), F32)],
            inside(
                token_rows, member, attn_gain, grad_hidden, ffn_mod, mods, grad_attn_in, attn_out
            ),
            [wide, wide, vmem((rows, width), F32)],
        )
        grad_w_adaln = dot_tn(cond_act, gathered(grad_mod[:images]))
        sums = [attn_gain_sum[0], ffn_gain_sum[0]]
        sums += [row.reshape(heads, HEAD_DIM).T for row in gain_sums[:3]]
        sums = lax.psum(sums, "dp")
        own = [
            lax.dynamic_slice_in_dim(whole, dp_rank * (whole.shape[0] // n_dp), whole.shape[0] // n_dp, 0)
            for whole in sums
        ]
        own.append(lax.psum(jnp.sum(gain_sums[3].reshape(heads, HEAD_DIM), axis=1), "dp"))
    else:
        grad_qv, grad_ko, grad_text, result, grad_tokens, grad_w_adaln, *own = exchange(
            functools.partial(last_exchange_kernel, n_tensor),
            [
                (struct((size, 2 * local), F32), vmem),
                (struct((size, 2 * local), F32), vmem),
                (struct((2 * local, depth), F32), vmem),
                (struct((rows, width)), vmem),
                (struct((rows, width)), vmem),
                (struct((cond_rows, span), F32), vmem),
            ]
            + [(struct((1, gain_attn.size), F32), vmem)] * 2
            + [(struct(gain_query.shape, F32), vmem)] * 3
            + [(struct((1, heads), F32), vmem)],
            outside(
                caption_rows, grad_text_all, total_qv, total_ko, token_rows, grad_hidden, attn_out
            )
            + inside(
                attn_in_part, member, attn_gain, mods, cond_act, gain_sums, result_rows, gate_part, ffn_mod,
                ffn_gain_sum,
            ),
            reduce_scratch(size, 2 * local) * 2
            + reduce_scratch(2 * local, depth)
            + [
                vmem((parts, 2 * local, depth), BF16),
                vmem((2, images * TXT, depth), BF16),
                wide,
                vmem((n_tensor, padded, width), BF16),
                vmem((padded, width), F32),
                vmem((padded, width), BF16),
                arrived,
                wide,
                wide,
                vmem((rows, width), F32),
                vmem((2, width), F32),
                vmem((1, width), F32),
                vmem((parts, padded, width), BF16),
                vmem((parts, 2, width), F32),
                vmem((parts, 1, width), F32),
                vmem((8, 128), F32),
                dma((2,)),
                dma((2, 3, 10)),
                dma((2, 4, n_tensor - 1)),
                dma((2, 3, 8)),
                vmem((2 * local, images * TXT), BF16),
                vmem((width, 2 * local), BF16),
                vmem((width, 2 * local), BF16),
                wide,
                vmem((rows, width), F32),
                wide,
                dma((6,)),
            ],
            3,
            vmem=62,
        )
        own[:2] = [part[0] for part in own[:2]]
        own[5] = own[5][0]
        plain = [*grad_f, grad_w_adaln, result, grad_tokens]
        square, tall = struct((size, local), F32), struct((depth, local), F32)
        (
            grad_query, grad_key, grad_value, grad_out, grad_tk, grad_tv, *plain
        ) = pl.pallas_call(
            emit_kernel,
            out_shape=[square] * 4 + [tall] * 2 + [struct(x.shape, x.dtype) for x in plain],
            in_specs=[pl.BlockSpec(memory_space=anywhere)] * (3 + len(plain)),
            out_specs=[pl.BlockSpec(memory_space=anywhere)] * (6 + len(plain)),
            scratch_shapes=[vmem(x.shape, x.dtype) for x in (grad_qv, grad_ko, grad_text, *plain)]
            + [
                vmem((depth, local), F32),
                vmem((depth, local), F32),
                dma((3 + len(plain),)),
                dma((6 + len(plain),)),
            ],
            compiler_params=pltpu.CompilerParams(vmem_limit_bytes=62 * 2**20),
        )(grad_qv, grad_ko, grad_text, *plain)
        *grad_f, grad_w_adaln, result, grad_tokens = plain

    return (
        result.reshape(micro, count, width),
        grad_tokens.reshape(micro, count, width),
        grad_query,
        grad_key,
        grad_value,
        grad_out,
        grad_tk,
        grad_tv,
        *grad_f,
        grad_w_adaln,
        *own,
    )


def solution(mesh):
    return jax.shard_map(
        functools.partial(shards, mesh.shape["dp"], mesh.shape["tensor"]),
        mesh=mesh,
        in_specs=(
            P(None, "dp", None),
            P(None, "dp", None),
            P(None, "dp", None, None),
            P(None, "dp", None),
            P(None, "dp"),
            P("dp", "tensor"),
            P("dp", "tensor"),
            P("dp", "tensor"),
            P("dp", "tensor"),
            P("dp", "tensor"),
            P("dp", "tensor"),
            P("dp", "tensor"),
            P("dp", "tensor"),
            P("dp", "tensor"),
            P("dp", "tensor"),
            P("dp"),
            P("dp"),
            P("dp", "tensor"),
            P("dp", "tensor"),
            P("dp", "tensor"),
            P("tensor"),
            P(None, "dp", None),
        ),
        out_specs=(
            P(None, "dp", None),
            P(None, "dp", None),
            P("dp", "tensor"),
            P("dp", "tensor"),
            P("dp", "tensor"),
            P("dp", "tensor"),
            P("dp", "tensor"),
            P("dp", "tensor"),
            P("dp", "tensor"),
            P("dp", "tensor"),
            P("dp", "tensor"),
            P("dp", "tensor"),
            P("dp"),
            P("dp"),
            P("dp", "tensor"),
            P("dp", "tensor"),
            P("dp", "tensor"),
            P("tensor"),
        ),
        check_vma=False,
    )
```
